32 devices in a mesh: dp: 8 (over y, x, core), tensor: 4 (over z).
Axes of the slice: x: 2, y: 2, z: 4, core: 2. Of those that a mesh axis runs over, the one named last changes fastest.
Arguments:
- token_ids: int32 [2, 2048], P(None, 'dp'), may hold values from 0 to 50287
- labels: int32 [2, 2048], P(None, 'dp'), may hold values from 0 to 50287, as said below
- seq_lengths: int32 [2], replicated, may hold values from 1024 to 2048, as said below
- micro_batch: int32 [2], replicated, may hold values from 0 to 1, as said below
- step_count: int32 [1], replicated, may hold values from 1 to 20
- block_slot: int32 [4, 192], P('tensor'), may hold values from 0 to 191, as said below
- vocab_table: float32 [25144, 2048], P('tensor', 'dp'), may hold values from -0.375 to 0.375
- vocab_first: float32 [25144, 2048], P('tensor', 'dp'), may hold values from -2.7621359e-06 to 2.7621359e-06
- vocab_second: float32 [25144, 2048], P('tensor', 'dp'), may hold values from 1.0251999e-12 to 4.1246416e-12
- layer_blocks: float32 [8, 4, 24, 128, 128], P('dp', 'tensor'), may hold values from -0.1875 to 0.1875
- block_bases: float32 [8, 4, 24, 2, 128, 128], P('dp', 'tensor'), may hold values from -0.5 to 0.5
- block_first: float32 [8, 4, 24, 128, 128], P('dp', 'tensor'), may hold values from -1.8887924e-06 to 1.8887924e-06
- block_second: float32 [8, 4, 24, 128, 128], P('dp', 'tensor'), may hold values from 4.7683716e-13 to 1.9073486e-12
- side_proj: float32 [2, 1024, 288], P(None, ('dp', 'tensor')), may hold values from -0.1875 to 0.1875
- side_first: float32 [2, 1024, 288], P(None, ('dp', 'tensor')), may hold values from -5.2083333e-06 to 5.2083333e-06
- side_second: float32 [2, 1024, 288], P(None, ('dp', 'tensor')), may hold values from 3.729926e-12 to 1.4580621e-11
- shared_params: float32 [5632], P(('dp', 'tensor')), may hold values from 0.1 to 1.9
- shared_first: float32 [5632], P(('dp', 'tensor')), may hold values from -5.330018e-05 to 5.330018e-05
- shared_second: float32 [5632], P(('dp', 'tensor')), may hold values from 3.90625e-10 to 1.5269886e-09
- channel_params: float32 [2, 6, 2048], P(None, None, 'tensor'), may hold values from 0.1 to 1.9
- channel_first: float32 [2, 6, 2048], P(None, None, 'tensor'), may hold values from -2.5515517e-05 to 2.5515517e-05
- channel_second: float32 [2, 6, 2048], P(None, None, 'tensor'), may hold values from 8.951823e-12 to 3.499349e-11
- head_params: float32 [2, 3, 32], P(None, None, 'tensor'), may hold values from -7 to 2.5, as said below
- head_first: float32 [2, 3, 32], P(None, None, 'tensor'), may hold values from -0.00019485572 to 0.00019485572
- head_second: float32 [2, 3, 32], P(None, None, 'tensor'), may hold values from 1.9791667e-10 to 7.8125e-10
Outputs:
- seq_loss: float32 [2], replicated
- clip_norm: float32 [], replicated
- table_next: float32 [25144, 2048], P('tensor', 'dp')
- table_first_next: float32 [25144, 2048], P('tensor', 'dp')
- table_second_next: float32 [25144, 2048], P('tensor', 'dp')
- blocks_next: float32 [8, 4, 24, 128, 128], P('dp', 'tensor')
- blocks_copy: bfloat16 [8, 4, 24, 128, 128], P('dp', 'tensor')
- block_first_next: float32 [8, 4, 24, 128, 128], P('dp', 'tensor')
- block_second_next: float32 [8, 4, 24, 128, 128], P('dp', 'tensor')
- side_next: float32 [2, 1024, 288], P(None, ('dp', 'tensor'))
- side_first_next: float32 [2, 1024, 288], P(None, ('dp', 'tensor'))
- side_second_next: float32 [2, 1024, 288], P(None, ('dp', 'tensor'))
- shared_step: float32 [5632], P(('dp', 'tensor'))
- shared_first_next: float32 [5632], P(('dp', 'tensor'))
- shared_second_next: float32 [5632], P(('dp', 'tensor'))
- channel_step: float32 [2, 6, 2048], P(None, None, 'tensor')
- channel_first_next: float32 [2, 6, 2048], P(None, None, 'tensor')
- channel_second_next: float32 [2, 6, 2048], P(None, None, 'tensor')
- head_step: float32 [2, 3, 32], P(None, None, 'tensor')
- head_first_next: float32 [2, 3, 32], P(None, None, 'tensor')
- head_second_next: float32 [2, 3, 32], P(None, None, 'tensor')
The draws below stay inside these ranges and needn't reach their ends.
Inputs may be any that keep to these rules, and one draw needn't show every extreme that they name: Some labels equal the input token at the same position. `seq_lengths`: one sequence in every draw is exactly 2048 long. `micro_batch`: each micro-batch holds exactly 1 sequence. `block_slot`: each row is a permutation of 0 to 191. `head_params`: row 0 lies in -7 to -2, row 1 in -3 to 2.5, row 2 in 0.5 to 1.5.
All inputs are finite; a program needn't handle non-finite values.
Results may differ from the reference program's by a relative error of at most 0.015.
Values may be sent and summed in bfloat16 or wider, within the bound.
A program may use at most 384 MiB of HBM per device.

```python
import math
import jax
import jax.numpy as jnp
from jax import lax

D = 1024
DI = 2048
H = 32
P_SIZE = 64
N = 128
V = 50288
SPAN = 256
L = 2
MB = 2
BLK = 128
SEQS = 2
MINLEN = 1024
LEN = 2048
NB_T = 192
BPD = 24
SHARED = 5632
N_DP = 8
N_TENSOR = 4


def token_pair(key):
    base_key = jax.random.fold_in(key, 7)
    first_key, second_key, third_key, fourth_key, fifth_key = jax.random.split(base_key, 5)
    input_ids = jnp.minimum(jax.random.randint(first_key, (SEQS, LEN), 0, V, dtype=jnp.int32), jax.random.randint(second_key, (SEQS, LEN), 0, V, dtype=jnp.int32))
    other_ids = jnp.minimum(jax.random.randint(third_key, (SEQS, LEN), 0, V, dtype=jnp.int32), jax.random.randint(fourth_key, (SEQS, LEN), 0, V, dtype=jnp.int32))
    repeat_pick = jax.random.randint(fifth_key, (SEQS, LEN), 0, 16, dtype=jnp.int32) == 0
    target_ids = jnp.where(repeat_pick, input_ids, other_ids)
    return (input_ids.astype(jnp.int32), target_ids.astype(jnp.int32))


def draw_token_ids(key, part):
    return token_pair(key)[0]


def draw_labels(key, part):
    return token_pair(key)[1]


def draw_seq_lengths(key, part):
    first_key, second_key = jax.random.split(key)
    values = jax.random.randint(first_key, (SEQS,), MINLEN, LEN + 1, dtype=jnp.int32)
    chosen = jax.random.randint(second_key, (), 0, SEQS, dtype=jnp.int32)
    return jnp.where(jnp.arange(SEQS, dtype=jnp.int32) == chosen, LEN, values).astype(jnp.int32)


def draw_micro_batch(key, part):
    return (jax.random.permutation(key, SEQS) % MB).astype(jnp.int32)


def draw_block_slot(key, part):
    row_keys = jax.random.split(key, N_TENSOR)
    return jax.vmap(lambda row_key: jax.random.permutation(row_key, NB_T))(row_keys).astype(jnp.int32)


def draw_head_params(key, part):
    key_bias, key_rate, key_skip = jax.random.split(key, 3)
    bias_rows = jax.random.uniform(key_bias, (L, 1, H), jnp.float32, -7.0, -2.0)
    rate_rows = jax.random.uniform(key_rate, (L, 1, H), jnp.float32, -3.0, 2.5)
    skip_rows = jax.random.uniform(key_skip, (L, 1, H), jnp.float32, 0.5, 1.5)
    return jnp.concatenate([bias_rows, rate_rows, skip_rows], axis=1)


def block_scale(key, extent, cuts, least, high):
    factor_of, own = 1.0, jax.random.fold_in(key, 6)
    for position, blocks in cuts:
        steps = jnp.exp(jax.random.uniform(jax.random.fold_in(own, position), (blocks,), jnp.float32, least / len(cuts), high / len(cuts)))
        factor_of = factor_of * jnp.repeat(steps, extent[position] // blocks).reshape([-1 if axis == position else 1 for axis in range(len(extent))])
    return factor_of


def scatter_about(rng, extent, width, bound, cuts=(), held_as=jnp.bfloat16):
    loudness = block_scale(rng, extent, cuts, -0.22, 0.18) if cuts else 1.0
    values = jax.random.normal(rng, extent, jnp.float32) * width * loudness
    return jnp.minimum(jnp.maximum(values, -bound), bound).astype(held_as)


def setup_inputs(seed: int = 0) -> dict:
    key_of = jax.random.split(jax.random.key(seed), 26)
    return {
        "token_ids": draw_token_ids(jax.random.fold_in(key_of[25], 71), 0),
        "labels": draw_labels(jax.random.fold_in(key_of[25], 71), 0),
        "seq_lengths": draw_seq_lengths(jax.random.fold_in(key_of[25], 71), 0),
        "micro_batch": draw_micro_batch(jax.random.fold_in(key_of[25], 71), 0),
        "step_count": jax.random.randint(key_of[4], (1,), 1, 21).astype(jnp.int32),
        "block_slot": draw_block_slot(jax.random.fold_in(key_of[25], 71), 0),
        "vocab_table": scatter_about(key_of[6], (V // 2, 2 * D), (2.0 * D ** -0.5), 0.375, ((0, 4), (1, 8)), jnp.float32),
        "vocab_first": scatter_about(key_of[7], (V // 2, 2 * D), (0.00133 * (min(V, 2 * SEQS * LEN) * D) ** -0.5), 2.762135864031734e-06, ((0, 4), (1, 8)), jnp.float32),
        "vocab_second": jnp.clip(jnp.exp(math.log(4.124641600489198e-12) - 1.3920915 * jax.random.uniform(key_of[8], (V // 2, 2 * D), jnp.float32) ** block_scale(key_of[8], (V // 2, 2 * D), ((0, 4), (1, 8)), -0.2, 0.2)), 1.0251998902588433e-12, 4.124641600489198e-12),
        "layer_blocks": scatter_about(key_of[9], (N_DP, N_TENSOR, BPD, BLK, BLK), (D ** -0.5), 0.1875, ((0, 8), (1, 4)), jnp.float32),
        "block_bases": scatter_about(key_of[10], (N_DP, N_TENSOR, BPD, 2, BLK, BLK), BLK ** -0.5, 0.5, ((0, 8), (1, 4)), jnp.float32),
        "block_first": scatter_about(key_of[11], (N_DP, N_TENSOR, BPD, BLK, BLK), (0.00111 * (3 * L * D * DI) ** -0.5), 1.8887924397859024e-06, ((0, 8), (1, 4)), jnp.float32),
        "block_second": jnp.clip(jnp.exp(math.log(1.9073486279969076e-12) - 1.3862944 * jax.random.uniform(key_of[12], (N_DP, N_TENSOR, BPD, BLK, BLK), jnp.float32) ** block_scale(key_of[12], (N_DP, N_TENSOR, BPD, BLK, BLK), ((0, 8), (1, 4)), -0.2, 0.2)), 4.768371569992269e-13, 1.9073486279969076e-12),
        "side_proj": scatter_about(key_of[13], (L, D, 2 * N + H), D ** -0.5, 0.1875, ((1, 32),), jnp.float32),
        "side_first": scatter_about(key_of[14], (L, D, 2 * N + H), (0.00067 * (L * D * (2 * N + H)) ** -0.5), 5.208333277550992e-06, ((1, 32),), jnp.float32),
        "side_second": jnp.clip(jnp.exp(math.log(1.4580621432447316e-11) - 1.363305 * jax.random.uniform(key_of[15], (L, D, 2 * N + H), jnp.float32) ** block_scale(key_of[15], (L, D, 2 * N + H), ((1, 32),), -0.2, 0.2)), 3.729926090212388e-12, 1.4580621432447316e-11),
        "shared_params": jnp.clip(1.0 + 0.18 * jax.random.normal(key_of[16], (SHARED,), jnp.float32), 0.1, 1.9),
        "shared_first": scatter_about(key_of[17], (SHARED,), (0.00067 * SHARED ** -0.5), 5.3300180297810584e-05, ((0, 32),), jnp.float32),
        "shared_second": jnp.clip(jnp.exp(math.log(1.5269886466384719e-09) - 1.3633048 * jax.random.uniform(key_of[18], (SHARED,), jnp.float32) ** block_scale(key_of[18], (SHARED,), ((0, 32),), -0.2, 0.2)), 3.906250045648818e-10, 1.5269886466384719e-09),
        "channel_params": jnp.clip(1.0 + 0.18 * jax.random.normal(key_of[19], (L, 6, DI), jnp.float32), 0.1, 1.9),
        "channel_first": scatter_about(key_of[20], (L, 6, DI), (0.00067 * (6 * L * DI) ** -0.5), 2.5515517336316407e-05, ((2, 4),), jnp.float32),
        "channel_second": jnp.clip(jnp.exp(math.log(3.499349074398417e-11) - 1.3633049 * jax.random.uniform(key_of[21], (L, 6, DI), jnp.float32) ** block_scale(key_of[21], (L, 6, DI), ((2, 4),), -0.2, 0.2)), 8.951822789982078e-12, 3.499349074398417e-11),
        "head_params": draw_head_params(jax.random.fold_in(key_of[25], 71), 0),
        "head_first": scatter_about(key_of[23], (L, 3, H), (0.00044 * (3 * L * H) ** -0.5), 0.00019485572, ((2, 4),), jnp.float32),
        "head_second": jnp.clip(jnp.exp(math.log(7.812500091297636e-10) - 1.3730491 * jax.random.uniform(key_of[24], (L, 3, H), jnp.float32) ** block_scale(key_of[24], (L, 3, H), ((2, 4),), -0.2, 0.2)), 1.9791666916457729e-10, 7.812500091297636e-10),
    }


@jax.custom_vjp
def low(v):
    return lax.optimization_barrier(v.astype(jnp.bfloat16)).astype(jnp.float32)

@jax.custom_vjp
def low_back(v):
    return v

def low_keep(v):
    return (low(v), None)

def low_pass(kept, grad):
    return (grad,)

def back_keep(v):
    return (v, None)

def back_low(kept, grad):
    return (low(grad),)
low.defvjp(low_keep, low_pass)
low_back.defvjp(back_keep, back_low)
HIGHEST = lax.Precision.HIGHEST
NORM_EPS = 1e-05
SMOOTHING = 0.1
ZLOSS_WEIGHT = 0.005
CLIP_LIMIT = 0.02
BETA_FIRST = 0.9
BETA_SECOND = 0.95
ADAM_EPS = 1e-08
LEARN_RATE = 0.03
WEIGHT_DECAY = 0.01

def rms_scale(values):
    return lax.rsqrt(lax.optimization_barrier(jnp.mean(values * values, axis=-1, keepdims=True)) + NORM_EPS)

def causal_conv(raw_rows, conv_taps, offset):
    row_count = raw_rows.shape[0]
    padded = jnp.concatenate([jnp.zeros((3, raw_rows.shape[1]), jnp.float32), raw_rows], axis=0)
    summed = offset[None, :] + conv_taps[0][None, :] * padded[0:row_count]
    for tap_index in range(1, 4):
        summed = summed + conv_taps[tap_index][None, :] * padded[tap_index:tap_index + row_count]
    return jax.nn.silu(summed)

def span_step(carry_state, pieces):
    inputs, keys_b, queries_c, step_sizes, decay_rates = pieces
    cumulative = jnp.cumsum(decay_rates, axis=0)
    spread = cumulative[:, None, :] - cumulative[None, :, :]
    positions = jnp.arange(cumulative.shape[0])
    lower_mask = (positions[:, None] >= positions[None, :])[:, :, None]
    decay_weights = jnp.where(lower_mask, jnp.exp(jnp.where(lower_mask, spread, 0.0)), 0.0)
    scores = jnp.dot(queries_c, keys_b.T, precision=HIGHEST)
    scaled = inputs * step_sizes[:, :, None]
    mixing = scores[:, :, None] * decay_weights
    within = jnp.einsum('qrh,rhp->qhp', mixing, scaled, precision=HIGHEST)
    carried = jnp.exp(cumulative)[:, :, None] * jnp.einsum('qn,hpn->qhp', queries_c, carry_state, precision=HIGHEST)
    tail_decay = jnp.exp(cumulative[-1][None, :] - cumulative)
    fresh_state = jnp.einsum('rhp,rn->hpn', scaled * tail_decay[:, :, None], keys_b, precision=HIGHEST)
    new_state = jnp.exp(cumulative[-1])[:, None, None] * carry_state + fresh_state
    return (new_state, within + carried)

def assemble(blocks_low, block_slot):
    inner_part = DI // N_TENSOR
    zx_count = D * 2 * inner_part // (BLK * BLK)
    per_layer = 3 * D * inner_part // (BLK * BLK)
    zx_weights = []
    out_weights = []
    for layer_index in range(L):
        zx_shards = []
        out_shards = []
        for shard_index in range(N_TENSOR):
            ordered = blocks_low[:, shard_index].reshape(NB_T, BLK, BLK)[block_slot[shard_index]]
            base_index = layer_index * per_layer
            zx_shards.append(ordered[base_index:base_index + zx_count].reshape(D // BLK, 2 * inner_part // BLK, BLK, BLK).transpose(0, 2, 1, 3).reshape(D, 2, inner_part))
            out_shards.append(ordered[base_index + zx_count:base_index + per_layer].reshape(inner_part // BLK, D // BLK, BLK, BLK).transpose(0, 2, 1, 3).reshape(inner_part, D))
        zx_weights.append(jnp.stack(zx_shards))
        out_weights.append(jnp.stack(out_shards))
    return (zx_weights, out_weights)

def mixer(residual, layer_index, zx_weights, out_weights, side_used, shared_used, channels, head_rows):
    base_index = layer_index * (D + 10 * N)
    gain_in = shared_used[base_index:base_index + D]
    bc_taps = shared_used[base_index + D:base_index + D + 8 * N].reshape(4, 2 * N)
    bc_offset = shared_used[base_index + D + 8 * N:base_index + D + 10 * N]
    normed = low(residual * rms_scale(residual) * gain_in[None, :])
    gate_in = low_back(jnp.einsum('td,jdkc->tjkc', normed, zx_weights[layer_index], precision=HIGHEST))
    gate_z = gate_in[:, :, 0, :].reshape(-1, DI)
    raw_x = gate_in[:, :, 1, :].reshape(-1, DI)
    side_out = jnp.dot(normed, side_used[layer_index], precision=HIGHEST)
    raw_rows = jnp.concatenate([raw_x, side_out[:, :2 * N]], axis=1)
    conv_taps = jnp.concatenate([channels[layer_index, 0:4], bc_taps], axis=1)
    offset = jnp.concatenate([channels[layer_index, 4], bc_offset])
    conv_out = causal_conv(raw_rows, conv_taps, offset)
    inputs = conv_out[:, :DI].reshape(-1, H, P_SIZE)
    keys_b = conv_out[:, DI:DI + N]
    queries_c = conv_out[:, DI + N:]
    step_sizes = jax.nn.softplus(side_out[:, 2 * N:] + head_rows[layer_index, 0][None, :])
    decay_rates = -step_sizes * jnp.exp(head_rows[layer_index, 1])[None, :]
    span_count = inputs.shape[0] // SPAN
    pieces = (inputs.reshape(span_count, SPAN, H, P_SIZE), keys_b.reshape(span_count, SPAN, N), queries_c.reshape(span_count, SPAN, N), step_sizes.reshape(span_count, SPAN, H), decay_rates.reshape(span_count, SPAN, H))
    start_state = jnp.zeros((H, P_SIZE, N), jnp.float32)
    final_state, outputs = lax.scan(jax.checkpoint(span_step), start_state, pieces)
    mixed_out = outputs.reshape(-1, H, P_SIZE) + head_rows[layer_index, 2][None, :, None] * inputs
    gated_out = mixed_out.reshape(-1, DI) * jax.nn.silu(gate_z)
    scaled_out = low(gated_out * rms_scale(gated_out) * channels[layer_index, 5][None, :])
    branch = low_back(jnp.einsum('tjc,jcd->td', scaled_out.reshape(-1, N_TENSOR, DI // N_TENSOR), out_weights[layer_index], precision=HIGHEST))
    return residual + branch

def block_loss(table_used, rows_in, targets, keep_part):
    logits = low_back(jnp.dot(rows_in, table_used.T, precision=HIGHEST))
    top_value = lax.optimization_barrier(jnp.max(logits, axis=1, keepdims=True))
    log_total = top_value[:, 0] + jnp.log(lax.optimization_barrier(jnp.sum(jnp.exp(logits - top_value), axis=1)))
    target_logit = jnp.take_along_axis(logits, targets[:, None], axis=1)[:, 0]
    token_loss = log_total - (1.0 - SMOOTHING) * target_logit - SMOOTHING / V * lax.optimization_barrier(jnp.sum(logits, axis=1)) + ZLOSS_WEIGHT * log_total * log_total
    return jnp.sum(keep_part * token_loss)

def adam_update(weight_in, gradient, moment_one, moment_two, factor, fix_one, fix_two, decay_rate):
    gradient = gradient * factor
    one_next = BETA_FIRST * moment_one + (1.0 - BETA_FIRST) * gradient
    two_next = BETA_SECOND * moment_two + (1.0 - BETA_SECOND) * gradient * gradient
    direction = one_next / fix_one / (jnp.sqrt(two_next / fix_two) + ADAM_EPS)
    return (weight_in - LEARN_RATE * (direction + decay_rate * weight_in), one_next, two_next)

def soap_update(weight_in, gradient, bases, moment_one, moment_two, factor, fix_one, fix_two):
    gradient = gradient * factor
    left_basis = bases[..., 0, :, :]
    right_basis = bases[..., 1, :, :]
    half_turn = jnp.einsum('...ab,...ac->...bc', left_basis, gradient, precision=HIGHEST)
    rotated = jnp.einsum('...bc,...cd->...bd', half_turn, right_basis, precision=HIGHEST)
    one_next = BETA_FIRST * moment_one + (1.0 - BETA_FIRST) * rotated
    two_next = BETA_SECOND * moment_two + (1.0 - BETA_SECOND) * rotated * rotated
    direction = one_next / fix_one / (jnp.sqrt(two_next / fix_two) + ADAM_EPS)
    back_half = jnp.einsum('...ab,...bc->...ac', left_basis, direction, precision=HIGHEST)
    turned = jnp.einsum('...ac,...dc->...ad', back_half, right_basis, precision=HIGHEST)
    weight_next = weight_in - LEARN_RATE * (turned + WEIGHT_DECAY * weight_in)
    return (weight_next, weight_next.astype(jnp.bfloat16), one_next, two_next)

def reference(token_ids, labels, seq_lengths, micro_batch, step_count, block_slot, vocab_table, vocab_first, vocab_second, layer_blocks, block_bases, block_first, block_second, side_proj, side_first, side_second, shared_params, shared_first, shared_second, channel_params, channel_first, channel_second, head_params, head_first, head_second):
    member = micro_batch[:, None] == jnp.arange(MB, dtype=jnp.int32)[None, :]
    batch_tokens = lax.optimization_barrier(jnp.sum(jnp.where(member, seq_lengths[:, None], 0), axis=0)).astype(jnp.float32)
    seq_weight = 1.0 / (MB * lax.optimization_barrier(jnp.sum(jnp.where(member, batch_tokens[None, :], 0.0), axis=1)))
    positions = jnp.arange(LEN, dtype=jnp.int32)
    keep_rows = (positions[None, :] < seq_lengths[:, None]).astype(jnp.float32) * seq_weight[:, None]
    row_block = 512 if LEN % 512 == 0 else LEN
    block_total = LEN // row_block

    def forward_loss(table_f, blocks_f, side_f, shared_f, channels, head_rows):
        table_used = low(table_f.reshape(V, D))
        zx_weights, out_weights = assemble(low(blocks_f), block_slot)
        side_used = low(side_f)
        shared_used = low(shared_f)
        final_gain = shared_used[L * (D + 10 * N):]

        def one_sequence(running, seq_item):
            ids_row, target_row, keep_row = seq_item
            residual = low_back(table_used[ids_row])
            for layer_index in range(L):
                residual = mixer(residual, layer_index, zx_weights, out_weights, side_used, shared_used, channels, head_rows)
            final_rows = low(residual * rms_scale(residual) * final_gain[None, :])
            block_parts = lax.map(jax.checkpoint(lambda block_item: block_loss(table_used, block_item[0], block_item[1], block_item[2])), (final_rows.reshape(block_total, row_block, D), target_row.reshape(block_total, row_block), keep_row.reshape(block_total, row_block)))
            return (running, jnp.sum(block_parts))
        unused, seq_values = lax.scan(jax.checkpoint(one_sequence), jnp.zeros((), jnp.float32), (token_ids, labels, keep_rows))
        return seq_values
    seq_loss, backward = jax.vjp(forward_loss, vocab_table, layer_blocks, side_proj, shared_params, channel_params, head_params)
    all_grads = backward(jnp.ones_like(seq_loss))
    square_sum = jnp.zeros((), jnp.float32)
    for gradient in all_grads:
        square_sum = square_sum + jnp.sum(gradient * gradient)
    clip_norm = jnp.sqrt(square_sum)
    factor = jnp.minimum(1.0, CLIP_LIMIT / (clip_norm + 1e-06))
    steps_done = step_count[0].astype(jnp.float32)
    fix_one = 1.0 - jnp.power(BETA_FIRST, steps_done)
    fix_two = 1.0 - jnp.power(BETA_SECOND, steps_done)
    table_out = adam_update(vocab_table, all_grads[0], vocab_first, vocab_second, factor, fix_one, fix_two, WEIGHT_DECAY)
    block_out = soap_update(layer_blocks, all_grads[1], block_bases, block_first, block_second, factor, fix_one, fix_two)
    side_out = adam_update(side_proj, all_grads[2], side_first, side_second, factor, fix_one, fix_two, WEIGHT_DECAY)
    shared_out = adam_update(shared_params, all_grads[3], shared_first, shared_second, factor, fix_one, fix_two, 0.0)
    channel_out = adam_update(channel_params, all_grads[4], channel_first, channel_second, factor, fix_one, fix_two, 0.0)
    head_out = adam_update(head_params, all_grads[5], head_first, head_second, factor, fix_one, fix_two, 0.0)
    shared_step = shared_out[0] - shared_params
    channel_step = channel_out[0] - channel_params
    head_step = head_out[0] - head_params
    return (seq_loss, clip_norm, table_out[0], table_out[1], table_out[2], block_out[0], block_out[1], block_out[2], block_out[3], side_out[0], side_out[1], side_out[2], shared_step, shared_out[1], shared_out[2], channel_step, channel_out[1], channel_out[2], head_step, head_out[1], head_out[2])
```

```python
import functools

import jax
import jax.numpy as jnp
from jax import lax
from jax.experimental import pallas as pl
from jax.experimental.pallas import tpu as pltpu
from jax.sharding import PartitionSpec as P

D = 1024
DI = 2048
H = 32
P_SIZE = 64
N = 128
V = 50288
SPAN = 256
L = 2
MB = 2
BLK = 128
RIM = 16
PAIRS = 640
LANES = 128

HIGHEST = lax.Precision.HIGHEST
NORM_EPS = 1e-05
SMOOTHING = 0.1
ZLOSS_WEIGHT = 0.005
CLIP_LIMIT = 0.02
BETA_FIRST = 0.9
BETA_SECOND = 0.95
ADAM_EPS = 1e-08
LEARN_RATE = 0.03
WEIGHT_DECAY = 0.01

BF = jnp.bfloat16
F32 = jnp.float32
MIB = 1 << 20


def nn(a, b, precision=None):
    return lax.dot_general(
        a, b, (((1,), (0,)), ((), ())), precision=precision, preferred_element_type=F32
    )


def nt_dot(a, b, precision=None):
    return lax.dot_general(
        a, b, (((1,), (1,)), ((), ())), precision=precision, preferred_element_type=F32
    )


def tn(a, b, precision=None):
    return lax.dot_general(
        a, b, (((0,), (0,)), ((), ())), precision=precision, preferred_element_type=F32
    )


def iota(shape, dim):
    return lax.broadcasted_iota(jnp.int32, shape, dim)


def head_map(inner):
    return (iota((LANES, inner), 0) == iota((LANES, inner), 1) // P_SIZE).astype(F32)


def swap(x, axis, offset):
    size = lax.axis_size(axis)
    return lax.ppermute(x, axis, [(i, i ^ offset) for i in range(size)])


def sigmoid(x):
    return 1.0 / (1.0 + jnp.exp(-x))


def softplus(x):
    return jnp.maximum(x, 0.0) + jnp.log1p(jnp.exp(-jnp.abs(x)))


def call(kernel, name, out_shape, args, smem=(), scratch=(), mib=48, flops=0, moved=0, **extra):
    specs = [
        pl.BlockSpec(memory_space=pltpu.SMEM if i in smem else pltpu.VMEM)
        for i in range(len(args))
    ]
    return pl.pallas_call(
        kernel,
        out_shape=out_shape,
        in_specs=specs,
        out_specs=jax.tree.map(lambda _: pl.BlockSpec(memory_space=pltpu.VMEM), out_shape),
        scratch_shapes=list(scratch),
        compiler_params=pltpu.CompilerParams(vmem_limit_bytes=mib * MIB),
        cost_estimate=pl.CostEstimate(flops=flops, bytes_accessed=moved, transcendentals=0),
        name=name,
        **extra,
    )(*args)


def sds(shape, dtype):
    return jax.ShapeDtypeStruct(shape, dtype)


def look_kernel(groups, rows, scal, idx, mask_ref, table, *rest):
    outs, work = rest[:groups], rest[groups]
    place = scal[0]
    for off in range(groups):
        base = (place ^ off) * rows

        def turn(step, carry):
            for lane in range(8):
                at = step * 8 + lane
                work[pl.ds(at, 1), :] = table[pl.ds(idx[base + at], 1), :]
            return carry

        lax.fori_loop(0, rows // 8, turn, 0)
        keep = mask_ref[pl.ds(pl.multiple_of(base, rows), rows), :]
        outs[off][...] = jnp.where(keep > 0, work[...], 0.0).astype(BF)


def gather_rows(scal, idx, keep, table, groups, rows):
    cols = table.shape[1]
    return call(
        functools.partial(look_kernel, groups, rows),
        "look",
        [sds((rows, cols), BF)] * groups,
        (scal, idx, keep, table),
        smem=(0, 1),
        scratch=[pltpu.VMEM((rows, cols), F32)],
        moved=30 * MIB,
    )


def join_kernel(groups, shards, own, scal, *rest):
    parts, outs, work = rest[:groups], rest[groups : groups + shards], rest[-1]
    place, shard = scal[0], scal[1]
    half = groups // 2
    cols = parts[0].shape[1]
    for off in range(half):
        at = ((place ^ off) % half) * cols
        work[:, pl.ds(pl.multiple_of(at, cols), cols)] = parts[off][...] + parts[off + half][...]
    for off in range(shards):
        at = pl.multiple_of((shard ^ off) * own, own)
        outs[off][...] = work[pl.ds(at, own), :]


def join_parts(scal, parts, shards, own):
    rows = parts[0].shape[0]
    return call(
        functools.partial(join_kernel, len(parts), shards, own),
        "join",
        [sds((own, D), BF)] * shards,
        (scal, *parts),
        smem=(0,),
        scratch=[pltpu.VMEM((rows, D), BF)],
        moved=4 * MIB,
    )


def cut_kernel(groups, shards, own, scal, *rest):
    parts, outs, work = rest[:shards], rest[shards : shards + groups], rest[-1]
    place, shard = scal[0], scal[1]
    half = groups // 2
    cols = outs[0].shape[1]
    for off in range(shards):
        at = pl.multiple_of((shard ^ off) * own, own)
        work[pl.ds(at, own), :] = parts[off][...]
    for off in range(groups):
        at = ((place ^ off) % half) * cols
        outs[off][...] = work[:, pl.ds(pl.multiple_of(at, cols), cols)]


def cut_parts(scal, parts, groups):
    own = parts[0].shape[0]
    shards = len(parts)
    cols = 2 * D // groups
    return call(
        functools.partial(cut_kernel, groups, shards, own),
        "cut",
        [sds((own * shards, cols), BF)] * groups,
        (scal, *parts),
        smem=(0,),
        scratch=[pltpu.VMEM((own * shards, D), BF)],
        moved=4 * MIB,
    )


def add_kernel(groups, rows, vrows, scal, idx, share, *rest):
    parts, out, square, work, bins = (rest[:groups], rest[groups], rest[groups + 1], rest[-2], rest[-1])
    place = scal[0]
    bins[0:vrows, :] = share[0:vrows, :].astype(F32)
    for off in range(groups):
        base = (place ^ off) * rows
        work[...] = parts[off][...].astype(F32)

        def turn(step, carry):
            for lane in range(8):
                at = step * 8 + lane
                to = pl.ds(idx[base + at], 1)
                bins[to, :] = bins[to, :] + work[pl.ds(at, 1), :]
            return carry

        lax.fori_loop(0, rows // 8, turn, 0)
    total = bins[0:vrows, :]
    out[...] = total
    square[...] = jnp.sum(total * total, axis=0, keepdims=True)


def add_rows(scal, idx, share, parts, vrows):
    cols = share.shape[1]
    rows = parts[0].shape[0]
    return call(
        functools.partial(add_kernel, len(parts), rows, vrows),
        "addrows",
        [sds((vrows, cols), F32), sds((1, cols), F32)],
        (scal, idx, share, *parts),
        smem=(0, 1),
        scratch=[pltpu.VMEM((rows, cols), F32), pltpu.VMEM((vrows + 8, cols), F32)],
        moved=30 * MIB,
    )


def conv_sum(raw, params, rows, lanes):
    total = params[4:5, :] + params[0:1, :] * raw[pl.ds(RIM - 3, rows), lanes]
    for k in range(1, 4):
        total = total + params[k : k + 1, :] * raw[pl.ds(RIM - 3 + k, rows), lanes]
    return total


def front_kernel(shards, own, scal, *rest):
    blocks, rest = rest[:shards], rest[shards:]
    rims, rest = rest[:shards], rest[shards:]
    wzx, wside, chan, bcp, head = rest[:5]
    normed, zx, side, yloc, final, tot_out, c_out, cum_out, xs_scr = rest[5:]
    shard = scal[0]
    rows = own * shards
    inner = chan.shape[1]
    rim = rims[0][...]
    for other in rims[1:]:
        rim = rim + other[...]
    normed[0:RIM, :] = rim
    for off in range(shards):
        at = pl.multiple_of(RIM + (shard ^ off) * own, RIM)
        normed[pl.ds(at, own), :] = blocks[off][...]
    zx[...] = nn(normed[...], wzx[...])
    side[...] = nn(normed[...], wside[...])
    pre = conv_sum(zx, chan, rows, pl.ds(inner, inner))
    xs_scr[...] = pre * sigmoid(pre)
    pre = conv_sum(side, bcp, rows, pl.ds(0, 2 * N))
    bc = (pre * sigmoid(pre)).astype(BF)
    c_out[...] = bc[:, N:]
    dt = softplus(side[RIM:, 2 * N :] + head[0:1, :])
    rate = -dt * jnp.exp(head[1:2, :])
    expand = head_map(inner)
    skip = nn(head[...], expand, HIGHEST)[2:3, :]
    lower = (iota((SPAN, SPAN), 0) >= iota((SPAN, SPAN), 1)).astype(F32)
    first_half = iota((SPAN, LANES), 1) < P_SIZE
    state = None
    base = jnp.zeros((1, LANES), F32)
    for span in range(rows // SPAN):
        here = slice(span * SPAN, (span + 1) * SPAN)
        cum = nn(lower, rate[here], HIGHEST)
        cum_t = cum.T
        tot = cum[SPAN - 1 : SPAN, :]
        keys = bc[here, :N]
        queries = bc[here, N:]
        scores = nt_dot(queries, keys)
        xs = xs_scr[here, :]
        scaled = xs * nn(dt[here], expand, HIGHEST)
        scaled_low = scaled.astype(BF)
        pieces = []
        for pair in range(inner // LANES):
            values = scaled_low[:, pair * LANES : (pair + 1) * LANES]
            both = []
            for h in (2 * pair, 2 * pair + 1):
                gap = cum[:, h : h + 1] - cum_t[h : h + 1, :]
                decay = jnp.exp(jnp.minimum(gap, 0.0)) * lower
                both.append(nn((scores * decay).astype(BF), values))
            pieces.append(jnp.where(first_half, both[0], both[1]))
        y = jnp.concatenate(pieces, axis=1) + skip * xs
        if state is not None:
            y = y + nn(jnp.exp(cum), expand, HIGHEST) * nn(queries, state.astype(BF))
        yloc[here, :] = y
        tail = nn(jnp.exp(tot - cum), expand, HIGHEST)
        fresh = tn(keys, (scaled * tail).astype(BF))
        if state is not None:
            fresh = fresh + nn(jnp.exp(tot), expand, HIGHEST) * state
        state = fresh
        cum_out[here, :] = cum + base
        base = base + tot
    final[...] = state.astype(BF)
    tot_out[...] = jnp.broadcast_to(base, tot_out.shape)


def mixer_front(scal, blocks, rims, wzx, wside, chan, bcp, head):
    shards = len(blocks)
    own = blocks[0].shape[0]
    rows = own * shards
    inner = chan.shape[1]
    return call(
        functools.partial(front_kernel, shards, own),
        "front",
        [
            sds((rows + RIM, D), BF),
            sds((rows + RIM, 2 * inner), F32),
            sds((rows + RIM, 2 * N + LANES), F32),
            sds((rows, inner), F32),
            sds((N, inner), BF),
            sds((8, LANES), F32),
            sds((rows, N), BF),
            sds((rows, LANES), F32),
        ],
        (scal, *blocks, *rims, wzx, wside, chan, bcp, head),
        smem=(0,),
        scratch=[pltpu.VMEM((rows, inner), F32)],
        flops=8 * rows * D * inner,
        moved=12 * MIB,
    )


def chain(parts, tots, expand):
    total = None
    past = jnp.zeros((1, LANES), F32)
    for part, tot in zip(parts, tots):
        term = nn(jnp.exp(past), expand, HIGHEST) * part[...].astype(F32)
        total = term if total is None else total + term
        past = past + tot[0:1, :]
    return total


def middle_kernel(shards, own, hops, scal, *rest):
    states, tots, rest = rest[:hops], rest[hops : 2 * hops], rest[2 * hops :]
    yloc, zx, c_in, cum, wout, chan = rest[:6]
    y_out, s_out, square = rest[6:9]
    parts, work = rest[9 : 9 + shards], rest[-1]
    shard = scal[0]
    rows, inner = yloc.shape
    expand = head_map(inner)
    state = chain(states, tots, expand)
    s_out[...] = state
    y = yloc[...] + nn(jnp.exp(cum[...]), expand, HIGHEST) * nn(c_in[...], state.astype(BF))
    y_out[...] = y
    z = zx[RIM:, :inner]
    gated = y * (z * sigmoid(z))
    square[...] = nt_dot(jnp.ones((8, inner), F32), gated * gated, HIGHEST)
    work[...] = nn((gated * chan[5:6, :]).astype(BF), wout[...]).astype(BF)
    for off in range(shards):
        at = pl.multiple_of((shard ^ off) * own, own)
        parts[off][...] = work[pl.ds(at, own), :]


def mixer_middle(scal, states, tots, yloc, zx, c_in, cum, wout, chan, shards):
    rows, inner = yloc.shape
    own = rows // shards
    return call(
        functools.partial(middle_kernel, shards, own, len(states)),
        "middle",
        [sds((rows, inner), F32), sds((N, inner), F32), sds((8, rows), F32)]
        + [sds((own, D), BF)] * shards,
        (scal, *states, *tots, yloc, zx, c_in, cum, wout, chan),
        smem=(0,),
        scratch=[pltpu.VMEM((rows, D), BF)],
        flops=2 * rows * D * inner,
        moved=8 * MIB,
    )


def gate_back_kernel(shards, own, scal, *rest):
    blocks, rest = rest[:shards], rest[shards:]
    coef, wout, y_in, zx, c_in, cum, chan = rest[:7]
    grads, u_out, dy_out, dz_out, state_out, gain_out = rest[7:]
    shard = scal[0]
    inner = chan.shape[1]
    for off in range(shards):
        at = pl.multiple_of((shard ^ off) * own, own)
        grads[pl.ds(at, own), :] = blocks[off][...]
    du = nt_dot(grads[...], wout[...])
    z = zx[RIM:, :inner]
    y = y_in[...]
    sig = sigmoid(z)
    silu = z * sig
    gated = y * silu
    gain_out[...] = jnp.sum(du * gated, axis=0, keepdims=True)
    gain = chan[5:6, :]
    u_out[...] = (gated * gain).astype(BF)
    dgated = du * gain - gated * coef[...]
    dy = dgated * silu
    dy_out[...] = dy
    dz_out[...] = (dgated * y * (sig * (1.0 + z * (1.0 - sig)))).astype(BF)
    grown = nn(jnp.exp(cum[...]), head_map(inner), HIGHEST)
    state_out[...] = tn(c_in[...], (dy * grown).astype(BF)).astype(BF)


def gate_back(scal, blocks, coef, wout, y, zx, c_in, cum, chan):
    shards = len(blocks)
    own = blocks[0].shape[0]
    rows, inner = y.shape
    return call(
        functools.partial(gate_back_kernel, shards, own),
        "gateback",
        [
            sds((rows, D), BF),
            sds((rows, inner), BF),
            sds((rows, inner), F32),
            sds((rows, inner), BF),
            sds((N, inner), BF),
            sds((1, inner), F32),
        ],
        (scal, *blocks, coef, wout, y, zx, c_in, cum, chan),
        smem=(0,),
        flops=2 * rows * D * inner,
        moved=10 * MIB,
    )


def silu_slope(pre):
    sig = sigmoid(pre)
    return sig * (1.0 + pre * (1.0 - sig))


def conv_back(ds_scr, raw, params, rows, lanes, width, low_out, out_lanes):
    ext = rows + RIM
    total = params[0:1, :] * ds_scr[pl.ds(3, ext), :]
    for k in range(1, 4):
        total = total + params[k : k + 1, :] * ds_scr[pl.ds(3 - k, ext), :]
    low_out[:, out_lanes] = total.astype(BF)
    ds = ds_scr[pl.ds(RIM, rows), :]
    grads = [
        jnp.sum(ds * raw[pl.ds(RIM - 3 + k, rows), lanes], axis=0, keepdims=True) for k in range(4)
    ]
    grads.append(jnp.sum(ds, axis=0, keepdims=True))
    grads.append(jnp.zeros((3, width), F32))
    return jnp.concatenate(grads, axis=0)


def back_kernel(shards, own, hops, scal, *rest):
    states, tots, rest = rest[:hops], rest[hops : 2 * hops], rest[2 * hops :]
    s_in, zx, side, dy_in, dz_in, y_in, wzx, wside, chan, bcp, head = rest[:11]
    dzx, dside, chan_out, bcp_out, head_out, rim_out = rest[11:17]
    parts, rest = rest[17 : 17 + shards], rest[17 + shards :]
    xs_scr, dsx, dsbc, work = rest
    shard = scal[0]
    rows, inner = dy_in.shape
    expand = head_map(inner)
    pre_x = conv_sum(zx, chan, rows, pl.ds(inner, inner))
    xs_scr[...] = pre_x * sigmoid(pre_x)
    pre_bc = conv_sum(side, bcp, rows, pl.ds(0, 2 * N))
    bc = (pre_bc * sigmoid(pre_bc)).astype(BF)
    raw_dt = side[RIM:, 2 * N :] + head[0:1, :]
    dt = softplus(raw_dt)
    grow = jnp.exp(head[1:2, :])
    rate = -dt * grow
    skip = nn(head[...], expand, HIGHEST)[2:3, :]
    lower = (iota((SPAN, SPAN), 0) >= iota((SPAN, SPAN), 1)).astype(F32)
    upper = (iota((SPAN, SPAN), 0) <= iota((SPAN, SPAN), 1)).astype(F32)
    first_half = iota((SPAN, LANES), 1) < P_SIZE
    spans = rows // SPAN
    cums, starts = [], [s_in[...]]
    for span in range(spans):
        here = slice(span * SPAN, (span + 1) * SPAN)
        cum = nn(lower, rate[here], HIGHEST)
        cums.append(cum)
        if span + 1 < spans:
            tot = cum[SPAN - 1 : SPAN, :]
            scale = nn(dt[here] * jnp.exp(tot - cum), expand, HIGHEST)
            fresh = tn(bc[here, :N], (xs_scr[here, :] * scale).astype(BF))
            starts.append(nn(jnp.exp(tot), expand, HIGHEST) * starts[-1] + fresh)
    dstate = chain(states, tots, expand)
    dsx[0:RIM, :] = jnp.zeros((RIM, inner), F32)
    dsx[RIM + rows :, :] = jnp.zeros((RIM, inner), F32)
    dsbc[0:RIM, :] = jnp.zeros((RIM, 2 * N), F32)
    dsbc[RIM + rows :, :] = jnp.zeros((RIM, 2 * N), F32)
    dside[0:RIM, 2 * N :] = jnp.zeros((RIM, LANES), BF)
    dzx[0:RIM, :inner] = jnp.zeros((RIM, inner), BF)
    dzx[RIM:, :inner] = dz_in[...]
    dbias = jnp.zeros((1, LANES), F32)
    dgrow = jnp.zeros((1, LANES), F32)
    dskip = jnp.zeros((1, LANES), F32)
    for span in reversed(range(spans)):
        here = slice(span * SPAN, (span + 1) * SPAN)
        there = slice(RIM + span * SPAN, RIM + (span + 1) * SPAN)
        cum = cums[span]
        cum_t = cum.T
        tot = cum[SPAN - 1 : SPAN, :]
        keys = bc[here, :N]
        queries = bc[here, N:]
        start = starts[span]
        scores_t = nt_dot(keys, queries)
        xs = xs_scr[here, :]
        dy = dy_in[here, :]
        dy_low = dy.astype(BF)
        dt_wide = nn(dt[here], expand, HIGHEST)
        scaled = xs * dt_wide
        scaled_low = scaled.astype(BF)
        dscores_t = jnp.zeros((SPAN, SPAN), F32)
        pieces = []
        for pair in range(inner // LANES):
            values = scaled_low[:, pair * LANES : (pair + 1) * LANES]
            dpair = dy_low[:, pair * LANES : (pair + 1) * LANES]
            both = []
            for h in (2 * pair, 2 * pair + 1):
                gap = cum_t[h : h + 1, :] - cum[:, h : h + 1]
                decay = jnp.exp(jnp.minimum(gap, 0.0)) * upper
                mine = first_half if h % 2 == 0 else jnp.logical_not(first_half)
                outer = nt_dot(jnp.where(mine, values, jnp.zeros_like(values)), dpair)
                dscores_t = dscores_t + outer * decay
                both.append(nn((scores_t * decay).astype(BF), dpair))
            pieces.append(jnp.where(first_half, both[0], both[1]))
        dscaled = jnp.concatenate(pieces, axis=1)
        dscores_low = dscores_t.astype(BF)
        grown = nn(jnp.exp(cum), expand, HIGHEST)
        tail = nn(jnp.exp(tot - cum), expand, HIGHEST)
        dy_grown = (dy * grown).astype(BF)
        dstate_low = dstate.astype(BF)
        through = tail * nn(keys, dstate_low)
        dscaled = dscaled + through
        dqueries = tn(dscores_low, keys) + nt_dot(dy_grown, start.astype(BF))
        dkeys = nn(dscores_low, queries) + nt_dot((scaled * tail).astype(BF), dstate_low)
        plain = y_in[here, :] - skip * xs
        held = scaled_low.astype(F32)
        dcum = nt_dot(dy_low.astype(F32) * plain - held * dscaled, expand, HIGHEST)
        tot_wide = nn(jnp.exp(tot), expand, HIGHEST)
        over = jnp.sum(held * through, axis=0, keepdims=True) + jnp.sum(
            tot_wide * dstate * start, axis=0, keepdims=True
        )
        dtot = nt_dot(jnp.broadcast_to(over, (8, inner)), expand, HIGHEST)[0:1, :]
        drate = nn(upper, dcum, HIGHEST) + dtot
        ddt = nt_dot(dscaled * xs, expand, HIGHEST) - drate * grow
        dgrow = dgrow + jnp.sum(drate * rate[here], axis=0, keepdims=True)
        draw = ddt * sigmoid(raw_dt[here])
        dbias = dbias + jnp.sum(draw, axis=0, keepdims=True)
        dside[there, 2 * N :] = draw.astype(BF)
        over = jnp.sum(dy * xs, axis=0, keepdims=True)
        dskip = dskip + nt_dot(jnp.broadcast_to(over, (8, inner)), expand, HIGHEST)[0:1, :]
        dsx[there, :] = dscaled * dt_wide + skip * dy
        dsbc[there, :N] = dkeys
        dsbc[there, N:] = dqueries
        if span > 0:
            dstate = tot_wide * dstate + tn(queries, dy_grown)
    body = pl.ds(RIM, rows)
    pre_x = conv_sum(zx, chan, rows, pl.ds(inner, inner))
    dsx[body, :] = dsx[body, :] * silu_slope(pre_x)
    pre_bc = conv_sum(side, bcp, rows, pl.ds(0, 2 * N))
    dsbc[body, :] = dsbc[body, :] * silu_slope(pre_bc)
    chan_out[...] = conv_back(
        dsx, zx, chan, rows, pl.ds(inner, inner), inner, dzx, pl.ds(inner, inner)
    )
    bcp_out[...] = conv_back(dsbc, side, bcp, rows, pl.ds(0, 2 * N), 2 * N, dside, pl.ds(0, 2 * N))
    head_out[...] = jnp.concatenate([dbias, dgrow, dskip, jnp.zeros((5, LANES), F32)], axis=0)
    work[...] = (nt_dot(dzx[...], wzx[...]) + nt_dot(dside[...], wside[...])).astype(BF)
    rim_out[...] = work[0:RIM, :]
    for off in range(shards):
        at = pl.multiple_of(RIM + (shard ^ off) * own, RIM)
        parts[off][...] = work[pl.ds(at, own), :]


def mixer_back(scal, states, tots, s_in, zx, side, dy, dz, y, wzx, wside, chan, bcp, head, shards):
    rows, inner = dy.shape
    own = rows // shards
    ext = rows + RIM
    return call(
        functools.partial(back_kernel, shards, own, len(states)),
        "back",
        [
            sds((ext, 2 * inner), BF),
            sds((ext, 2 * N + LANES), BF),
            sds((8, inner), F32),
            sds((8, 2 * N), F32),
            sds((8, LANES), F32),
            sds((RIM, D), BF),
        ]
        + [sds((own, D), BF)] * shards,
        (scal, *states, *tots, s_in, zx, side, dy, dz, y, wzx, wside, chan, bcp, head),
        smem=(0,),
        scratch=[
            pltpu.VMEM((rows, inner), F32),
            pltpu.VMEM((ext + RIM, inner), F32),
            pltpu.VMEM((ext + RIM, 2 * N), F32),
            pltpu.VMEM((ext, D), BF),
        ],
        flops=8 * rows * D * inner,
        moved=16 * MIB,
    )


def logits_kernel(shards, own, vrows, label, table, *rest):
    blocks, rest = rest[:shards], rest[shards:]
    p_out, tops, stats, rows_scr, top, total, target, plain = rest
    step = pl.program_id(0)
    rows = own * shards

    @pl.when(step == 0)
    def _():
        for off in range(shards):
            rows_scr[off * own : (off + 1) * own, :] = blocks[off][...]
        top[...] = jnp.full((1, rows), -1e30, F32)
        total[...] = jnp.zeros((1, rows), F32)
        target[...] = jnp.zeros((1, rows), F32)
        plain[...] = jnp.zeros((1, rows), F32)

    at = step * PAIRS + iota((PAIRS, rows), 0)
    valid = at < vrows
    logits = []
    highest = top[...]
    for half in range(2):
        raw = nt_dot(table[:, half * D : (half + 1) * D], rows_scr[...])
        highest = jnp.maximum(
            highest, jnp.max(jnp.where(valid, raw, -1e30), axis=0, keepdims=True)
        )
        logits.append(raw)
    summed = total[...] * jnp.exp(top[...] - highest)
    hit = target[...]
    whole = plain[...]
    for half in range(2):
        raw = logits[half]
        part = jnp.where(valid, jnp.exp(raw - highest), 0.0)
        summed = summed + jnp.sum(part, axis=0, keepdims=True)
        hit = hit + jnp.sum(
            jnp.where(2 * at + half == label[...], raw, 0.0), axis=0, keepdims=True
        )
        whole = whole + jnp.sum(raw, axis=0, keepdims=True)
        p_out[half] = part.astype(BF)
    top[...] = highest
    total[...] = summed
    target[...] = hit
    plain[...] = whole
    tops[...] = jnp.broadcast_to(highest, (1, 8, rows))
    stats[...] = jnp.concatenate([highest, summed, hit, whole, jnp.zeros((4, rows), F32)], axis=0)


def vocab_logits(label, table, blocks, vrows):
    shards = len(blocks)
    own = blocks[0].shape[0]
    rows = own * shards
    padded = table.shape[0]
    steps = padded // PAIRS
    whole = lambda i: (0, 0)
    return pl.pallas_call(
        functools.partial(logits_kernel, shards, own, vrows),
        grid=(steps,),
        out_shape=[
            sds((2, padded, rows), BF),
            sds((steps, 8, rows), F32),
            sds((8, rows), F32),
        ],
        in_specs=[
            pl.BlockSpec((1, rows), whole),
            pl.BlockSpec((PAIRS, 2 * D), lambda i: (i, 0)),
        ]
        + [pl.BlockSpec((own, D), whole)] * shards,
        out_specs=[
            pl.BlockSpec((2, PAIRS, rows), lambda i: (0, i, 0)),
            pl.BlockSpec((1, 8, rows), lambda i: (i, 0, 0)),
            pl.BlockSpec((8, rows), whole),
        ],
        scratch_shapes=[pltpu.VMEM((rows, D), BF)] + [pltpu.VMEM((1, rows), F32)] * 4,
        compiler_params=pltpu.CompilerParams(
            dimension_semantics=("arbitrary",), vmem_limit_bytes=48 * MIB
        ),
        cost_estimate=pl.CostEstimate(
            flops=4 * rows * D * padded, bytes_accessed=40 * MIB, transcendentals=2 * rows * padded
        ),
        name="logits",
    )(label, table, *blocks)


def rows_kernel(shards, own, vrows, label, scale, weight, p_in, table, *rest):
    q_out, parts, acc = rest[0], rest[1 : 1 + shards], rest[-1]
    step = pl.program_id(0)
    rows = own * shards

    @pl.when(step == 0)
    def _():
        acc[...] = jnp.zeros_like(acc)

    at = step * PAIRS + iota((PAIRS, rows), 0)
    keep = jnp.where(at < vrows, weight[...], 0.0)
    factor = scale[0, 0:1, :]
    term = None
    for half in range(2):
        share = jnp.where(2 * at + half == label[...], 1.0 - SMOOTHING + SMOOTHING / V, SMOOTHING / V)
        q = (p_in[half].astype(F32) * factor - keep * share).astype(BF)
        q_out[half] = q
        part = tn(q, table[:, half * D : (half + 1) * D])
        term = part if term is None else term + part
    acc[...] += term

    @pl.when(step == pl.num_programs(0) - 1)
    def _():
        for off in range(shards):
            parts[off][...] = acc[off * own : (off + 1) * own, :].astype(BF)


def vocab_rows(label, scale, weight, p_in, table, vrows, shards):
    _, padded, rows = p_in.shape
    steps = padded // PAIRS
    own = rows // shards
    whole = lambda i: (0, 0)
    return pl.pallas_call(
        functools.partial(rows_kernel, shards, own, vrows),
        grid=(steps,),
        out_shape=[sds((2, padded, rows), BF)] + [sds((own, D), BF)] * shards,
        in_specs=[
            pl.BlockSpec((1, rows), whole),
            pl.BlockSpec((1, 8, rows), lambda i: (i, 0, 0)),
            pl.BlockSpec((1, rows), whole),
            pl.BlockSpec((2, PAIRS, rows), lambda i: (0, i, 0)),
            pl.BlockSpec((PAIRS, 2 * D), lambda i: (i, 0)),
        ],
        out_specs=[pl.BlockSpec((2, PAIRS, rows), lambda i: (0, i, 0))]
        + [pl.BlockSpec((own, D), whole)] * shards,
        scratch_shapes=[pltpu.VMEM((rows, D), F32)],
        compiler_params=pltpu.CompilerParams(
            dimension_semantics=("arbitrary",), vmem_limit_bytes=48 * MIB
        ),
        cost_estimate=pl.CostEstimate(
            flops=4 * rows * D * padded, bytes_accessed=52 * MIB, transcendentals=0
        ),
        name="rowgrads",
    )(label, scale, weight, p_in, table)


def table_kernel(shards, own, q_in, *rest):
    blocks, out, rows_scr = rest[:shards], rest[shards], rest[-1]

    @pl.when(pl.program_id(0) == 0)
    def _():
        for off in range(shards):
            rows_scr[off * own : (off + 1) * own, :] = blocks[off][...]

    for half in range(2):
        out[:, half * D : (half + 1) * D] = nn(q_in[half], rows_scr[...]).astype(BF)


def vocab_table_grad(q_in, blocks):
    _, padded, rows = q_in.shape
    shards = len(blocks)
    own = blocks[0].shape[0]
    whole = lambda i: (0, 0)
    return pl.pallas_call(
        functools.partial(table_kernel, shards, own),
        grid=(padded // PAIRS,),
        out_shape=sds((padded, 2 * D), BF),
        in_specs=[pl.BlockSpec((2, PAIRS, rows), lambda i: (0, i, 0))]
        + [pl.BlockSpec((own, D), whole)] * shards,
        out_specs=pl.BlockSpec((PAIRS, 2 * D), lambda i: (i, 0)),
        scratch_shapes=[pltpu.VMEM((rows, D), BF)],
        compiler_params=pltpu.CompilerParams(
            dimension_semantics=("arbitrary",), vmem_limit_bytes=48 * MIB
        ),
        cost_estimate=pl.CostEstimate(
            flops=4 * rows * D * padded, bytes_accessed=40 * MIB, transcendentals=0
        ),
        name="tablegrads",
    )(q_in, *blocks)


def adam_update(weight_in, gradient, moment_one, moment_two, factor, fix_one, fix_two, decay_rate):
    gradient = gradient * factor
    one_next = BETA_FIRST * moment_one + (1.0 - BETA_FIRST) * gradient
    two_next = BETA_SECOND * moment_two + (1.0 - BETA_SECOND) * gradient * gradient
    direction = one_next / fix_one / (jnp.sqrt(two_next / fix_two) + ADAM_EPS)
    return (weight_in - LEARN_RATE * (direction + decay_rate * weight_in), one_next, two_next)


def soap_update(weight_in, gradient, bases, moment_one, moment_two, factor, fix_one, fix_two):
    gradient = gradient * factor
    left_basis = bases[..., 0, :, :]
    right_basis = bases[..., 1, :, :]
    half_turn = jnp.einsum("...ab,...ac->...bc", left_basis, gradient, precision=HIGHEST)
    rotated = jnp.einsum("...bc,...cd->...bd", half_turn, right_basis, precision=HIGHEST)
    one_next = BETA_FIRST * moment_one + (1.0 - BETA_FIRST) * rotated
    two_next = BETA_SECOND * moment_two + (1.0 - BETA_SECOND) * rotated * rotated
    direction = one_next / fix_one / (jnp.sqrt(two_next / fix_two) + ADAM_EPS)
    back_half = jnp.einsum("...ab,...bc->...ac", left_basis, direction, precision=HIGHEST)
    turned = jnp.einsum("...ac,...dc->...ad", back_half, right_basis, precision=HIGHEST)
    weight_next = weight_in - LEARN_RATE * (turned + WEIGHT_DECAY * weight_in)
    return (weight_next, weight_next.astype(BF), one_next, two_next)


def to_blocks(matrix):
    row_count, col_count = matrix.shape
    return (
        matrix.reshape(row_count // BLK, BLK, col_count // BLK, BLK)
        .transpose(0, 2, 1, 3)
        .reshape(-1, BLK, BLK)
    )


def total_over(x, axis):
    out = x
    for off in range(1, lax.axis_size(axis)):
        out = out + swap(x, axis, off)
    return out


def rms_scale(values):
    return lax.rsqrt(jnp.mean(values * values, axis=-1, keepdims=True) + NORM_EPS)


def shards(
    token_ids,
    labels,
    seq_lengths,
    micro_batch,
    step_count,
    block_slot,
    vocab_table,
    vocab_first,
    vocab_second,
    layer_blocks,
    block_bases,
    block_first,
    block_second,
    side_proj,
    side_first,
    side_second,
    shared_params,
    shared_first,
    shared_second,
    channel_params,
    channel_first,
    channel_second,
    head_params,
    head_first,
    head_second,
):
    nt = lax.axis_size("tensor")
    nd = lax.axis_size("dp")
    shard = lax.axis_index("tensor")
    place = lax.axis_index("dp")
    seqs = token_ids.shape[0]
    length = token_ids.shape[1] * nd
    chunks = nd // seqs
    rows = seqs * length // nd
    own = rows // nt
    vrows = vocab_table.shape[0]
    padded = -(-vrows // PAIRS) * PAIRS
    half = nd // 2
    inner = channel_params.shape[2]
    heads = head_params.shape[2]
    tiles = block_slot.shape[1]
    zx_count = D * 2 * inner // (BLK * BLK)
    per_layer = 3 * D * inner // (BLK * BLK)
    stride = D + 10 * N
    both = ("dp", "tensor")
    side_rows = side_proj.shape[1]
    share_size = shared_params.shape[0]
    share_pad = -(-share_size // 2048) * 2048

    piece = jnp.concatenate(
        [
            jnp.pad(side_proj.astype(BF), ((0, 0), (0, 0), (0, LANES - H))).reshape(-1, LANES),
            jnp.pad(shared_params.astype(BF), (0, share_pad - share_size)).reshape(-1, LANES),
        ],
        axis=0,
    )
    piece_rows = piece.shape[0]
    side_part = piece_rows - share_pad // LANES
    pieces = jnp.zeros((nt, piece_rows, LANES), BF)
    for off in range(nt):
        pieces = lax.dynamic_update_index_in_dim(
            pieces, piece if off == 0 else swap(piece, "tensor", off), shard ^ off, 0
        )
    own_tiles = layer_blocks.shape[2]
    carried = jnp.concatenate(
        [layer_blocks.astype(BF).reshape(own_tiles * BLK, BLK), pieces.reshape(-1, LANES)], axis=0
    )
    gathered = lax.all_gather(carried, "dp", axis=0, tiled=False)
    ids_all = lax.all_gather(jnp.concatenate([token_ids, labels], axis=0), "dp", axis=1, tiled=True)
    table_low = jnp.pad(vocab_table.astype(BF), ((0, padded - vrows), (0, 0)))

    slot_tiles = gathered[:, : own_tiles * BLK].reshape(tiles, BLK, BLK)
    ordered = slot_tiles[block_slot[0]]
    small = gathered[:, own_tiles * BLK :].reshape(nd, nt, piece_rows, LANES)
    side_full = (
        small[:, :, :side_part]
        .reshape(nd, nt, L, side_rows, 2 * N + LANES)
        .transpose(2, 0, 1, 3, 4)
        .reshape(L, D, 2 * N + LANES)
    )
    shared_full = small[:, :, side_part:].reshape(nd * nt, share_pad)[:, :share_size].reshape(-1)
    shared_full = shared_full.astype(F32)

    all_ids = ids_all[:seqs].reshape(-1)
    local_row = all_ids // 2 - shard * vrows
    held = (local_row >= 0) & (local_row < vrows) & (all_ids % 2 == place // half)
    scal = jnp.stack([place, shard]).astype(jnp.int32)
    scal_shard = shard.astype(jnp.int32).reshape(1)
    parts = gather_rows(
        scal,
        jnp.where(held, local_row, 0),
        jnp.broadcast_to(held[:, None], (held.shape[0], 1)).astype(F32),
        vocab_table,
        nd,
        rows,
    )
    parts = [parts[0]] + [swap(parts[off], "dp", off) for off in range(1, nd)]
    parts = join_parts(scal, parts, nt, own)
    residual = parts[0]
    for off in range(1, nt):
        residual = residual + swap(parts[off], "tensor", off)
    residual = residual.astype(F32)
    table_all = lax.all_gather(table_low, "dp", axis=1, tiled=True)

    def layer_mats(layer_index):
        base_index = layer_index * per_layer
        zx_part = (
            ordered[base_index : base_index + zx_count]
            .reshape(D // BLK, 2 * inner // BLK, BLK, BLK)
            .transpose(0, 2, 1, 3)
            .reshape(D, 2 * inner)
        )
        out_part = (
            ordered[base_index + zx_count : base_index + per_layer]
            .reshape(inner // BLK, D // BLK, BLK, BLK)
            .transpose(0, 2, 1, 3)
            .reshape(inner, D)
        )
        dt_part = lax.dynamic_slice_in_dim(
            side_full[layer_index], 2 * N + shard * heads, heads, 1
        )
        side_here = jnp.concatenate(
            [
                side_full[layer_index][:, : 2 * N],
                jnp.pad(dt_part, ((0, 0), (0, LANES - heads))),
            ],
            axis=1,
        )
        base = layer_index * stride
        gain = shared_full[base : base + D]
        taps = shared_full[base + D : base + D + 8 * N].reshape(4, 2 * N)
        bias = shared_full[base + D + 8 * N : base + stride].reshape(1, 2 * N)
        bcp = jnp.concatenate([taps, bias, jnp.zeros((3, 2 * N), F32)], axis=0)
        chan = jnp.pad(channel_params[layer_index], ((0, 2), (0, 0)))
        head = jnp.pad(head_params[layer_index], ((0, 5), (0, LANES - heads)))
        return (zx_part, out_part, side_here, gain, bcp, chan, head)

    def spread(x):
        return [x] + [swap(x, "tensor", off) for off in range(1, nt)]

    def rim_pairs(to):
        return [
            (k * nt + nt - 1, (k + 1) * nt + to) for k in range(nd) if k % chunks + 1 < chunks
        ]

    def hop(x, distance):
        pairs = [
            (k, k + distance)
            for k in range(nd)
            if 0 <= k % chunks + distance < chunks
        ]
        return lax.ppermute(x, "dp", pairs)

    def collect(parts):
        total = parts[0].astype(F32)
        for off in range(1, nt):
            total = total + swap(parts[off], "tensor", off).astype(F32)
        return total

    hops = range(1, chunks)
    mats = [layer_mats(layer_index) for layer_index in range(L)]
    saved = []
    for layer_index in range(L):
        wzx, wout, wside, gain, bcp, chan, head = mats[layer_index]
        normed_own = (residual * rms_scale(residual) * gain[None, :]).astype(BF)
        edge = normed_own[own - RIM :]
        rims = [lax.ppermute(edge, both, rim_pairs(to)) for to in range(nt)]
        normed, zx, side, yloc, final, tot, c_out, cum = mixer_front(
            scal_shard, spread(normed_own), rims, wzx, wside, chan, bcp, head
        )
        states = [hop(final, k) for k in hops]
        tots = [hop(tot, k) for k in hops]
        result = mixer_middle(scal_shard, states, tots, yloc, zx, c_out, cum, wout, chan, nt)
        y, s_in, square = result[:3]
        square = total_over(square, "tensor")[0]
        square = lax.dynamic_slice_in_dim(square, shard * own, own)
        factor = lax.rsqrt(square / DI + NORM_EPS)[:, None]
        branch = collect(result[3:])
        saved.append((residual, normed, zx, side, tot, c_out, cum, y, s_in, factor, branch))
        residual = residual + factor * branch
    final_gain = shared_full[L * stride :]
    final_scale = rms_scale(residual)
    final_rows = spread((residual * final_scale * final_gain[None, :]).astype(BF))

    member = micro_batch[:, None] == jnp.arange(MB, dtype=jnp.int32)[None, :]
    batch_tokens = jnp.sum(jnp.where(member, seq_lengths[:, None], 0), axis=0).astype(F32)
    seq_weight = 1.0 / (MB * jnp.sum(jnp.where(member, batch_tokens[None, :], 0.0), axis=1))
    block_order = shard ^ jnp.arange(nt, dtype=jnp.int32)
    row_at = (
        place * rows + block_order[:, None] * own + jnp.arange(own, dtype=jnp.int32)[None, :]
    ).reshape(rows)
    my_seq = place // chunks
    weight = jnp.where(row_at % length < seq_lengths[my_seq], seq_weight[my_seq], 0.0)
    all_labels = ids_all[seqs:].reshape(-1)
    label = (all_labels[row_at] - 2 * shard * vrows).reshape(1, rows)

    p_low, tops, stats = vocab_logits(label, table_all, final_rows, vrows)
    stats = stats.reshape(8, nt, own)
    merged = (stats[0], stats[1], stats[2], stats[3])
    others = [swap(stats, "tensor", off) for off in range(1, nt)]
    best = stats[0]
    for off in range(1, nt):
        best = jnp.maximum(best, jnp.stack([others[off - 1][0, o ^ off] for o in range(nt)]))
    summed = stats[1] * jnp.exp(stats[0] - best)
    target = stats[2]
    plain = stats[3]
    for off in range(1, nt):
        them = jnp.stack([others[off - 1][:, o ^ off] for o in range(nt)], axis=1)
        summed = summed + them[1] * jnp.exp(them[0] - best)
        target = target + them[2]
        plain = plain + them[3]
    log_total = best + jnp.log(summed)
    token_loss = (
        log_total
        - (1.0 - SMOOTHING) * target
        - SMOOTHING / V * plain
        + ZLOSS_WEIGHT * log_total * log_total
    )
    loss_here = jnp.sum(weight[:own] * token_loss[0])
    seq_part = jnp.where(jnp.arange(seqs) == my_seq, loss_here, 0.0)
    soft = (weight.reshape(nt, own) * (1.0 + 2.0 * ZLOSS_WEIGHT * log_total)).reshape(1, 1, rows)
    scale = soft * jnp.exp(tops - log_total.reshape(1, 1, rows))
    result = vocab_rows(label, scale, weight.reshape(1, rows), p_low, table_all, vrows, nt)
    q_low = result[0]
    grad_final = collect(result[1:])
    table_grad = vocab_table_grad(q_low, final_rows)
    table_share = lax.psum_scatter(table_grad, "dp", scatter_dimension=1, tiled=True)

    grad_final_gain = jnp.sum(grad_final * residual * final_scale, axis=0)
    scaled_grad = grad_final * final_gain[None, :]
    grad_res = final_scale * scaled_grad - residual * (
        final_scale * final_scale * final_scale
    ) * jnp.mean(scaled_grad * residual, axis=1, keepdims=True)

    block_pieces = [None] * (2 * L)
    side_pieces = [None] * L
    channel_pieces = [None] * L
    head_pieces = [None] * L
    shared_pieces = [None] * L
    for layer_index in reversed(range(L)):
        wzx, wout, wside, gain, bcp, chan, head = mats[layer_index]
        residual_in, normed, zx, side, tot, c_out, cum, y, s_in, factor, branch = saved[layer_index]
        inner_rows = jnp.sum(grad_res * branch, axis=1)
        coef_own = factor[:, 0] * factor[:, 0] * factor[:, 0] * inner_rows / DI
        coef = jnp.zeros((rows,), F32)
        for off in range(nt):
            coef = lax.dynamic_update_slice_in_dim(
                coef, coef_own if off == 0 else swap(coef_own, "tensor", off), (shard ^ off) * own, 0
            )
        grads, u_low, dy, dz, dstate, gain_grad = gate_back(
            scal_shard,
            spread((factor * grad_res).astype(BF)),
            coef[:, None],
            wout,
            y,
            zx,
            c_out,
            cum,
            chan,
        )
        states = [hop(dstate, -k) for k in hops]
        tots = [hop(tot, -k) for k in hops]
        grad_out_w = tn(u_low, grads)
        result = mixer_back(
            scal_shard, states, tots, s_in, zx, side, dy, dz, y, wzx, wside, chan, bcp, head, nt
        )
        dzx, dside, chan_grad, bcp_grad, head_grad, rim_grad = result[:6]
        grad_local = collect(result[6:])
        rim_sum = jnp.zeros((RIM, D), F32)
        for to in range(nt):
            pairs = [(b, a) for a, b in rim_pairs(to)]
            rim_sum = rim_sum + lax.ppermute(rim_grad, both, pairs).astype(F32)
        grad_local = grad_local + jnp.pad(rim_sum, ((own - RIM, 0), (0, 0)))
        grad_zx_w = tn(normed, dzx)
        grad_side_w = tn(normed, dside)
        inv_scale = rms_scale(residual_in)
        grad_gain_in = jnp.sum(grad_local * residual_in * inv_scale, axis=0)
        scaled_in = grad_local * gain[None, :]
        grad_res = (
            grad_res
            + inv_scale * scaled_in
            - residual_in
            * (inv_scale * inv_scale * inv_scale)
            * jnp.mean(scaled_in * residual_in, axis=1, keepdims=True)
        )
        block_pieces[2 * layer_index] = to_blocks(grad_zx_w.astype(BF))
        block_pieces[2 * layer_index + 1] = to_blocks(grad_out_w.astype(BF))
        spaced = lax.dynamic_update_slice(
            jnp.zeros((D, LANES), F32),
            grad_side_w[:, 2 * N : 2 * N + heads],
            (jnp.zeros((), jnp.int32), shard * heads),
        )
        side_pieces[layer_index] = jnp.concatenate([grad_side_w[:, : 2 * N], spaced], axis=1)
        channel_pieces[layer_index] = jnp.concatenate([chan_grad[:5], gain_grad], axis=0)
        head_pieces[layer_index] = head_grad[:3, :heads]
        shared_pieces[layer_index] = jnp.concatenate(
            [grad_gain_in, bcp_grad[:4].reshape(-1), bcp_grad[4]]
        )

    embed = cut_parts(scal, spread(grad_res.astype(BF)), nd)
    embed = [embed[0]] + [swap(embed[off], "dp", off) for off in range(1, nd)]

    inverse = jnp.zeros((tiles,), jnp.int32).at[block_slot[0]].set(jnp.arange(tiles, dtype=jnp.int32))
    ordered_grads = jnp.concatenate(block_pieces, axis=0)
    slot_grads = ordered_grads[inverse].reshape(nd, own_tiles * BLK, BLK)
    side_grads = (
        jnp.stack(side_pieces)
        .astype(BF)
        .reshape(L, nd, nt, side_rows, 2 * N + LANES)
        .transpose(1, 2, 0, 3, 4)
        .reshape(nd, nt, side_part, LANES)
    )
    shared_grads = jnp.concatenate(shared_pieces + [grad_final_gain]).astype(BF)
    shared_grads = jnp.pad(
        shared_grads.reshape(nd, nt, share_size), ((0, 0), (0, 0), (0, share_pad - share_size))
    ).reshape(nd, nt, share_pad // LANES, LANES)
    small_grads = jnp.concatenate([side_grads, shared_grads], axis=2).reshape(nd, -1, LANES)
    block_share = lax.psum_scatter(
        jnp.concatenate([slot_grads, small_grads], axis=1), "dp", scatter_dimension=0, tiled=True
    )[0]
    block_grads = block_share[: own_tiles * BLK].astype(F32)
    small_share = block_share[own_tiles * BLK :].reshape(nt, piece_rows, LANES)
    mine = jnp.zeros((piece_rows, LANES), F32)
    for off in range(nt):
        sent = lax.dynamic_index_in_dim(small_share, shard ^ off, 0, False)
        mine = mine + (sent if off == 0 else swap(sent, "tensor", off)).astype(F32)
    side_share = mine[:side_part].reshape(L, side_rows, 2 * N + LANES)[:, :, : 2 * N + H]
    shared_share = mine[side_part:].reshape(-1)[:share_size]
    lines = jnp.concatenate(
        [
            jnp.stack(channel_pieces).reshape(-1, LANES),
            jnp.pad(jnp.stack(head_pieces).reshape(-1), (0, LANES - L * 3 * heads)).reshape(1, LANES),
        ],
        axis=0,
    )
    lines = total_over(lines, "dp")
    channel_sum = lines[:-1].reshape(channel_params.shape)
    head_sum = lines[-1, : L * 3 * heads].reshape(head_params.shape)

    grad_table, table_square = add_rows(
        scal, jnp.where(held, local_row, vrows), table_share, embed, vrows
    )
    first_copy = (place == 0).astype(F32)
    square_part = (
        jnp.sum(block_grads * block_grads)
        + jnp.sum(table_square)
        + jnp.sum(side_share * side_share)
        + jnp.sum(shared_share * shared_share)
        + first_copy * (jnp.sum(channel_sum * channel_sum) + jnp.sum(head_sum * head_sum))
    )
    packed = jnp.concatenate([seq_part, square_part[None]])
    packed = total_over(total_over(packed, "tensor"), "dp")
    seq_loss = packed[:seqs]
    clip_norm = jnp.sqrt(packed[seqs])
    factor = jnp.minimum(1.0, CLIP_LIMIT / (clip_norm + 1e-06))
    steps_done = step_count[0].astype(F32)
    fix_one = 1.0 - jnp.power(BETA_FIRST, steps_done)
    fix_two = 1.0 - jnp.power(BETA_SECOND, steps_done)
    table_out = adam_update(
        vocab_table, grad_table, vocab_first, vocab_second, factor, fix_one, fix_two, WEIGHT_DECAY
    )
    block_out = soap_update(
        layer_blocks,
        block_grads.reshape(layer_blocks.shape),
        block_bases,
        block_first,
        block_second,
        factor,
        fix_one,
        fix_two,
    )
    side_next = adam_update(
        side_proj, side_share, side_first, side_second, factor, fix_one, fix_two, WEIGHT_DECAY
    )
    shared_next = adam_update(
        shared_params, shared_share, shared_first, shared_second, factor, fix_one, fix_two, 0.0
    )
    channel_next = adam_update(
        channel_params, channel_sum, channel_first, channel_second, factor, fix_one, fix_two, 0.0
    )
    head_next = adam_update(
        head_params, head_sum, head_first, head_second, factor, fix_one, fix_two, 0.0
    )
    return (
        seq_loss,
        clip_norm,
        table_out[0],
        table_out[1],
        table_out[2],
        block_out[0],
        block_out[1],
        block_out[2],
        block_out[3],
        side_next[0],
        side_next[1],
        side_next[2],
        shared_next[0] - shared_params,
        shared_next[1],
        shared_next[2],
        channel_next[0] - channel_params,
        channel_next[1],
        channel_next[2],
        head_next[0] - head_params,
        head_next[1],
        head_next[2],
    )


def solution(mesh):
    table = P("tensor", "dp")
    block = P("dp", "tensor", None, None, None)
    side = P(None, ("dp", "tensor"), None)
    shared = P(("dp", "tensor"))
    channel = P(None, None, "tensor")
    in_specs = (
        P(None, "dp"),
        P(None, "dp"),
        P(),
        P(),
        P(),
        P("tensor", None),
        *[table] * 3,
        block,
        P("dp", "tensor", None, None, None, None),
        block,
        block,
        *[side] * 3,
        *[shared] * 3,
        *[channel] * 6,
    )
    out_specs = (
        P(),
        P(),
        *[table] * 3,
        *[block] * 4,
        *[side] * 3,
        *[shared] * 3,
        *[channel] * 6,
    )
    return jax.shard_map(shards, mesh=mesh, in_specs=in_specs, out_specs=out_specs, check_vma=False)
```

```python
import functools

import jax
import jax.numpy as jnp
from jax import lax
from jax.experimental import pallas as pl
from jax.experimental.pallas import tpu as pltpu
from jax.sharding import PartitionSpec as P

D = 1024
DI = 2048
H = 32
P_SIZE = 64
N = 128
V = 50288
SPAN = 256
L = 2
MB = 2
BLK = 128
RIM = 16
PAIRS = 640
LANES = 128

HIGHEST = lax.Precision.HIGHEST
NORM_EPS = 1e-05
SMOOTHING = 0.1
ZLOSS_WEIGHT = 0.005
CLIP_LIMIT = 0.02
BETA_FIRST = 0.9
BETA_SECOND = 0.95
ADAM_EPS = 1e-08
LEARN_RATE = 0.03
WEIGHT_DECAY = 0.01

BF = jnp.bfloat16
F32 = jnp.float32
MIB = 1 << 20


def nn(a, b, precision=None):
    return lax.dot_general(
        a, b, (((1,), (0,)), ((), ())), precision=precision, preferred_element_type=F32
    )


def nt_dot(a, b, precision=None):
    return lax.dot_general(
        a, b, (((1,), (1,)), ((), ())), precision=precision, preferred_element_type=F32
    )


def tn(a, b, precision=None):
    return lax.dot_general(
        a, b, (((0,), (0,)), ((), ())), precision=precision, preferred_element_type=F32
    )


def iota(shape, dim):
    return lax.broadcasted_iota(jnp.int32, shape, dim)


def head_map(inner):
    return (iota((LANES, inner), 0) == iota((LANES, inner), 1) // P_SIZE).astype(F32).astype(BF)


def swap(x, axis, offset):
    size = lax.axis_size(axis)
    return lax.ppermute(x, axis, [(i, i ^ offset) for i in range(size)])


def halves(x):
    high = x.astype(BF)
    return high, (x - high.astype(F32)).astype(BF)


def thirds(x):
    high = x.astype(BF)
    rest = x - high.astype(F32)
    mid = rest.astype(BF)
    return high, mid, (rest - mid.astype(F32)).astype(BF)


def widen(x, expand):
    high, low = halves(x)
    twice = jnp.concatenate([expand, expand], axis=0)
    return nn(jnp.concatenate([high, low], axis=1), twice)


def narrow(x, expand):
    high, low = halves(x)
    return nt_dot(high, expand) + nt_dot(low, expand)


def tri_sum(tri, x):
    wide = nn(tri, jnp.concatenate(thirds(x), axis=1))
    size = x.shape[1]
    return wide[:, :size] + wide[:, size : 2 * size] + wide[:, 2 * size :]


def lanes3(column):
    high, mid, low = thirds(column)
    lane = iota((column.shape[0], LANES), 1)
    zero = jnp.zeros((column.shape[0], LANES), F32)
    wide = jnp.where(lane == 0, high.astype(F32), zero)
    wide = jnp.where(lane == 1, mid.astype(F32), wide)
    return jnp.where(lane == 2, low.astype(F32), wide).astype(BF)


def column3(wide):
    return wide[:, 0:1] + wide[:, 1:2] + wide[:, 2:3]


def rows3(line, inner):
    high, mid, low = thirds(line)
    at = iota((RIM, LANES), 0)
    wide = jnp.where(at == 0, high.astype(F32), 0.0)
    wide = jnp.where(at == 1, mid.astype(F32), wide)
    wide = jnp.where(at == 2, low.astype(F32), wide)
    if inner > LANES:
        wide = jnp.concatenate([wide, jnp.zeros((RIM, inner - LANES), F32)], axis=1)
    return wide.astype(BF)


def sigmoid(x):
    return 1.0 / (1.0 + jnp.exp(-x))


def softplus(x):
    return jnp.maximum(x, 0.0) + jnp.log1p(jnp.exp(-jnp.abs(x)))


def call(kernel, name, out_shape, args, smem=(), scratch=(), mib=48, flops=0, moved=0, **extra):
    specs = [
        pl.BlockSpec(memory_space=pltpu.SMEM if i in smem else pltpu.VMEM)
        for i in range(len(args))
    ]
    return pl.pallas_call(
        kernel,
        out_shape=out_shape,
        in_specs=specs,
        out_specs=jax.tree.map(lambda _: pl.BlockSpec(memory_space=pltpu.VMEM), out_shape),
        scratch_shapes=list(scratch),
        compiler_params=pltpu.CompilerParams(vmem_limit_bytes=mib * MIB),
        cost_estimate=pl.CostEstimate(flops=flops, bytes_accessed=moved, transcendentals=0),
        name=name,
        **extra,
    )(*args)


def sds(shape, dtype):
    return jax.ShapeDtypeStruct(shape, dtype)


def look_kernel(groups, rows, scal, code, table, *rest):
    outs, listed, count, work = rest[:groups], rest[groups], rest[groups + 1], rest[groups + 2]
    place = scal[0]
    total = groups * rows

    def fill(step, carry):
        work[pl.ds(pl.multiple_of(step * rows, rows), rows), :] = jnp.zeros((rows, table.shape[1]), F32)
        return carry

    lax.fori_loop(0, groups, fill, 0)

    def note(step, found):
        for lane in range(8):
            at = step * 8 + lane
            listed[found] = at
            found = found + 1 + lax.shift_right_arithmetic(code[at], 31)
        return found

    found = lax.fori_loop(0, total // 8, note, 0)
    for lane in range(8):
        listed[found + lane] = total
    count[0] = found

    def turn(step, carry):
        for lane in range(8):
            at = listed[step * 8 + lane]
            work[pl.ds(at, 1), :] = table[pl.ds(code[at], 1), :]
        return carry

    lax.fori_loop(0, (found + 7) // 8, turn, 0)
    for off in range(groups):
        base = pl.multiple_of((place ^ off) * rows, rows)
        outs[off][...] = work[pl.ds(base, rows), :].astype(BF)


def gather_rows(scal, code, table, groups, rows):
    cols = table.shape[1]
    total = groups * rows
    vmem = pl.BlockSpec(memory_space=pltpu.VMEM)
    smem = pl.BlockSpec(memory_space=pltpu.SMEM)
    return pl.pallas_call(
        functools.partial(look_kernel, groups, rows),
        out_shape=[sds((rows, cols), BF)] * groups + [sds((total + 8,), jnp.int32), sds((1,), jnp.int32)],
        in_specs=[smem, smem, vmem],
        out_specs=[vmem] * groups + [smem, smem],
        scratch_shapes=[pltpu.VMEM((total + 8, cols), F32)],
        compiler_params=pltpu.CompilerParams(vmem_limit_bytes=48 * MIB),
        cost_estimate=pl.CostEstimate(flops=0, bytes_accessed=30 * MIB, transcendentals=0),
        name="look",
    )(scal, code, table)


def join_kernel(groups, shards, own, scal, *rest):
    parts, outs, work = rest[:groups], rest[groups : groups + shards], rest[-1]
    place, shard = scal[0], scal[1]
    half = groups // 2
    cols = parts[0].shape[1]
    for off in range(half):
        at = ((place ^ off) % half) * cols
        work[:, pl.ds(pl.multiple_of(at, cols), cols)] = parts[off][...] + parts[off + half][...]
    for off in range(shards):
        at = pl.multiple_of((shard ^ off) * own, own)
        outs[off][...] = work[pl.ds(at, own), :]


def join_parts(scal, parts, shards, own):
    rows = parts[0].shape[0]
    return call(
        functools.partial(join_kernel, len(parts), shards, own),
        "join",
        [sds((own, D), BF)] * shards,
        (scal, *parts),
        smem=(0,),
        scratch=[pltpu.VMEM((rows, D), BF)],
        moved=4 * MIB,
    )


def cut_kernel(groups, shards, own, scal, *rest):
    parts, outs, work = rest[:shards], rest[shards : shards + groups], rest[-1]
    place, shard = scal[0], scal[1]
    half = groups // 2
    cols = outs[0].shape[1]
    for off in range(shards):
        at = pl.multiple_of((shard ^ off) * own, own)
        work[pl.ds(at, own), :] = parts[off][...]
    for off in range(groups):
        at = ((place ^ off) % half) * cols
        outs[off][...] = work[:, pl.ds(pl.multiple_of(at, cols), cols)]


def cut_parts(scal, parts, groups):
    own = parts[0].shape[0]
    shards = len(parts)
    cols = 2 * D // groups
    return call(
        functools.partial(cut_kernel, groups, shards, own),
        "cut",
        [sds((own * shards, cols), BF)] * groups,
        (scal, *parts),
        smem=(0,),
        scratch=[pltpu.VMEM((own * shards, D), BF)],
        moved=4 * MIB,
    )


def add_kernel(groups, rows, vrows, scal, code, listed, count, share, *rest):
    parts, out, square, work = rest[:groups], rest[groups], rest[groups + 1], rest[groups + 2]
    place = scal[0]
    out[...] = share[0:vrows, :].astype(F32)
    for off in range(groups):
        base = pl.multiple_of((place ^ off) * rows, rows)
        work[pl.ds(base, rows), :] = parts[off][...].astype(F32)
    work[groups * rows :, :] = jnp.zeros((8, work.shape[1]), F32)

    def turn(step, carry):
        for lane in range(8):
            at = listed[step * 8 + lane]
            to = pl.ds(code[at], 1)
            out[to, :] = out[to, :] + work[pl.ds(at, 1), :]
        return carry

    lax.fori_loop(0, (count[0] + 7) // 8, turn, 0)
    total = out[...]
    square[...] = jnp.sum(total * total, axis=0, keepdims=True)


def add_rows(scal, code, listed, count, share, parts, vrows):
    cols = share.shape[1]
    rows = parts[0].shape[0]
    return call(
        functools.partial(add_kernel, len(parts), rows, vrows),
        "addrows",
        [sds((vrows, cols), F32), sds((1, cols), F32)],
        (scal, code, listed, count, share, *parts),
        smem=(0, 1, 2, 3),
        scratch=[pltpu.VMEM((rows * len(parts) + 8, cols), F32)],
        moved=30 * MIB,
    )


def tiles_kernel(slots_each, zx_count, per_layer, layers, slot, tiles, *outs):
    for layer in range(layers):
        for at in range(per_layer):
            where = slot[0, layer * per_layer + at]
            owner = where // slots_each
            first = pl.multiple_of((where % slots_each) * BLK, BLK)
            tile = tiles[owner, pl.ds(first, BLK), :]
            if at < zx_count:
                wide = outs[2 * layer].shape[1] // BLK
                row, col = at // wide, at % wide
                out = outs[2 * layer]
            else:
                wide = D // BLK
                row, col = (at - zx_count) // wide, (at - zx_count) % wide
                out = outs[2 * layer + 1]
            out[row * BLK : (row + 1) * BLK, col * BLK : (col + 1) * BLK] = tile


def place_tiles(slot, tiles, slots_each, inner, zx_count, per_layer):
    return call(
        functools.partial(tiles_kernel, slots_each, zx_count, per_layer, L),
        "placetiles",
        [sds((D, 2 * inner), BF), sds((inner, D), BF)] * L,
        (slot, tiles),
        smem=(0,),
        moved=14 * MIB,
    )


def norm_rows(values, gain):
    return values * lax.rsqrt(jnp.mean(values * values, axis=-1, keepdims=True) + NORM_EPS) * gain


def total_of(parts):
    total = parts[0][...].astype(F32)
    for part in parts[1:]:
        total = total + part[...].astype(F32)
    return total


def enter_kernel(count, *refs):
    parts, (gain, residual, normed) = refs[:count], refs[count:]
    total = total_of(parts)
    residual[...] = total
    normed[...] = norm_rows(total, gain[...]).astype(BF)


def enter(parts, gain):
    own = parts[0].shape[0]
    return call(
        functools.partial(enter_kernel, len(parts)),
        "enter",
        [sds((own, D), F32), sds((own, D), BF)],
        (*parts, gain),
        moved=2 * MIB,
    )


def join_residual_kernel(count, *refs):
    parts, (before, gain, residual, branch, factor, normed) = refs[:count], refs[count:]
    total = total_of(parts)
    scale = lax.rsqrt(column3(total[:, D:]) / DI + NORM_EPS)
    branch[...] = total[:, :D]
    factor[...] = scale
    after = before[...] + scale * total[:, :D]
    residual[...] = after
    normed[...] = norm_rows(after, gain[...]).astype(BF)


def join_residual(parts, before, gain):
    own = before.shape[0]
    return call(
        functools.partial(join_residual_kernel, len(parts)),
        "residual",
        [sds((own, D), F32), sds((own, D), F32), sds((own, 1), F32), sds((own, D), BF)],
        (*parts, before, gain),
        moved=3 * MIB,
    )


def back_rows_kernel(count, rim_count, last, *refs):
    parts, refs = refs[:count], refs[count:]
    rims, refs = refs[:rim_count], refs[rim_count:]
    residual, gain, refs = refs[0], refs[1], refs[2:]
    grad_in = None
    if rim_count:
        grad_in, refs = refs[0], refs[1:]
    if not last:
        branch, factor, refs = refs[0], refs[1], refs[2:]
    if rim_count:
        grad_out, payload, gain_grad, work = refs
    else:
        grad_out, payload, gain_grad = refs
    grad = total_of(parts)
    if rim_count:
        work[...] = grad
        own = work.shape[0]
        work[own - RIM :, :] += total_of(rims)
        grad = work[...]
    values = residual[...]
    inv = lax.rsqrt(jnp.mean(values * values, axis=-1, keepdims=True) + NORM_EPS)
    gain_grad[...] = jnp.sum(grad * values * inv, axis=0, keepdims=True)
    scaled = grad * gain[...]
    result = inv * scaled - values * (inv * inv * inv) * jnp.mean(
        scaled * values, axis=-1, keepdims=True
    )
    if grad_in is not None:
        result = grad_in[...] + result
    grad_out[...] = result
    if last:
        payload[...] = result.astype(BF)
    else:
        scale = factor[...]
        payload[:, :D] = (scale * result).astype(BF)
        inner_rows = jnp.sum(result * branch[...], axis=-1, keepdims=True)
        payload[:, D:] = lanes3(scale * scale * scale * inner_rows / DI)


def back_rows(parts, rims, residual, gain, grad_in, below):
    own = residual.shape[0]
    last = below is None
    args = (*parts, *rims, residual, gain)
    if rims:
        args = (*args, grad_in)
    if not last:
        args = (*args, *below)
    return call(
        functools.partial(back_rows_kernel, len(parts), len(rims), last),
        "backrows",
        [
            sds((own, D), F32),
            sds((own, D if last else D + LANES), BF),
            sds((1, D), F32),
        ],
        args,
        scratch=[pltpu.VMEM((own, D), F32)] if rims else [],
        moved=4 * MIB,
    )


def sum_kernel(groups, shards, x_ref, o_ref, mid, from_shards, from_groups, send, recv):
    place, shard = lax.axis_index("dp"), lax.axis_index("tensor")
    peers = [(place, shard ^ off) for off in range(1, shards)]
    peers += [(place ^ off, shard) for off in range(1, groups)]
    barrier = pltpu.get_barrier_semaphore()
    for peer in peers:
        pl.semaphore_signal(barrier, inc=1, device_id=peer, device_id_type=pl.DeviceIdType.MESH)
    pl.semaphore_wait(barrier, len(peers))

    def exchange(source, slots, first, some):
        copies = []
        for i, peer in enumerate(some):
            copy = pltpu.make_async_remote_copy(
                src_ref=source,
                dst_ref=slots.at[i],
                send_sem=send.at[first + i],
                recv_sem=recv.at[first + i],
                device_id=peer,
                device_id_type=pl.DeviceIdType.MESH,
            )
            copy.start()
            copies.append(copy)
        for copy in copies:
            copy.wait()
        total = source[...]
        for i in range(len(some)):
            total = total + slots[i]
        return total

    mid[...] = exchange(x_ref, from_shards, 0, peers[: shards - 1])
    o_ref[...] = exchange(mid, from_groups, shards - 1, peers[shards - 1 :])


def sum_everywhere(x, groups, shards):
    count = groups + shards - 2
    return pl.pallas_call(
        functools.partial(sum_kernel, groups, shards),
        out_shape=sds((8, LANES), F32),
        in_specs=[pl.BlockSpec(memory_space=pltpu.VMEM)],
        out_specs=pl.BlockSpec(memory_space=pltpu.VMEM),
        scratch_shapes=[
            pltpu.VMEM((8, LANES), F32),
            pltpu.VMEM((shards - 1, 8, LANES), F32),
            pltpu.VMEM((groups - 1, 8, LANES), F32),
            pltpu.SemaphoreType.DMA((count,)),
            pltpu.SemaphoreType.DMA((count,)),
        ],
        compiler_params=pltpu.CompilerParams(
            collective_id=1, has_side_effects=True, vmem_limit_bytes=8 * MIB
        ),
        name="sumall",
    )(x)


def conv_sum(raw, params, rows, lanes):
    total = params[4:5, :] + params[0:1, :] * raw[pl.ds(RIM - 3, rows), lanes]
    for k in range(1, 4):
        total = total + params[k : k + 1, :] * raw[pl.ds(RIM - 3 + k, rows), lanes]
    return total


def front_kernel(shards, own, scal, *rest):
    blocks, rest = rest[:shards], rest[shards:]
    rims, rest = rest[:shards], rest[shards:]
    wzx, wside, chan, bcp, head = rest[:5]
    normed, zx, side, yloc, final, c_out, cum_out, xs_scr = rest[5:]
    shard = scal[0]
    rows = own * shards
    inner = chan.shape[1]
    rim = rims[0][...]
    for other in rims[1:]:
        rim = rim + other[...]
    normed[0:RIM, :] = rim
    for off in range(shards):
        at = pl.multiple_of(RIM + (shard ^ off) * own, RIM)
        normed[pl.ds(at, own), :] = blocks[off][...]
    zx[...] = nn(normed[...], wzx[...])
    side[...] = nn(normed[...], wside[...])
    pre = conv_sum(zx, chan, rows, pl.ds(inner, inner))
    xs_scr[...] = pre * sigmoid(pre)
    pre = conv_sum(side, bcp, rows, pl.ds(0, 2 * N))
    bc = (pre * sigmoid(pre)).astype(BF)
    c_out[...] = bc[:, N:]
    dt = softplus(side[RIM:, 2 * N :] + head[0:1, :])
    rate = -dt * jnp.exp(head[1:2, :])
    expand = head_map(inner)
    skip = widen(head[...], expand)[2:3, :]
    lower = (iota((SPAN, SPAN), 0) >= iota((SPAN, SPAN), 1)).astype(F32)
    lower_low = lower.astype(BF)
    first_half = iota((SPAN, LANES), 1) < P_SIZE
    state = None
    base = jnp.zeros((1, LANES), F32)
    for span in range(rows // SPAN):
        here = slice(span * SPAN, (span + 1) * SPAN)
        cum = tri_sum(lower_low, rate[here])
        cum_t = cum.T
        tot = cum[SPAN - 1 : SPAN, :]
        keys = bc[here, :N]
        queries = bc[here, N:]
        scores = nt_dot(queries, keys)
        xs = xs_scr[here, :]
        scaled = xs * widen(dt[here], expand)
        scaled_low = scaled.astype(BF)
        pieces = []
        for pair in range(inner // LANES):
            values = scaled_low[:, pair * LANES : (pair + 1) * LANES]
            both = []
            for h in (2 * pair, 2 * pair + 1):
                gap = cum[:, h : h + 1] - cum_t[h : h + 1, :]
                decay = jnp.exp(jnp.minimum(gap, 0.0)) * lower
                both.append(nn((scores * decay).astype(BF), values))
            pieces.append(jnp.where(first_half, both[0], both[1]))
        y = jnp.concatenate(pieces, axis=1) + skip * xs
        if state is not None:
            y = y + widen(jnp.exp(cum), expand) * nn(queries, state.astype(BF))
        yloc[here, :] = y
        tail = widen(jnp.exp(tot - cum), expand)
        fresh = tn(keys, (scaled * tail).astype(BF))
        if state is not None:
            fresh = fresh + widen(jnp.exp(tot), expand) * state
        state = fresh
        cum_out[here, :] = cum + base
        base = base + tot
    final[0:N, :] = state.astype(BF)
    final[N:, :] = rows3(base, inner)


def mixer_front(scal, blocks, rims, wzx, wside, chan, bcp, head):
    shards = len(blocks)
    own = blocks[0].shape[0]
    rows = own * shards
    inner = chan.shape[1]
    return call(
        functools.partial(front_kernel, shards, own),
        "front",
        [
            sds((rows + RIM, D), BF),
            sds((rows + RIM, 2 * inner), F32),
            sds((rows + RIM, 2 * N + LANES), F32),
            sds((rows, inner), F32),
            sds((N + RIM, inner), BF),
            sds((rows, N), BF),
            sds((rows, LANES), F32),
        ],
        (scal, *blocks, *rims, wzx, wside, chan, bcp, head),
        smem=(0,),
        scratch=[pltpu.VMEM((rows, inner), F32)],
        flops=8 * rows * D * inner,
        moved=12 * MIB,
    )


def chain(parts, expand):
    total = None
    past = jnp.zeros((1, LANES), F32)
    for part in parts:
        term = widen(jnp.exp(past), expand) * part[0:N, :].astype(F32)
        total = term if total is None else total + term
        past = past + jnp.sum(part[N:, :LANES].astype(F32), axis=0, keepdims=True)
    return total


def middle_kernel(shards, own, hops, scal, *rest):
    states, rest = rest[:hops], rest[hops:]
    yloc, zx, c_in, cum, wout, chan = rest[:6]
    y_out, s_out = rest[6:8]
    parts, work = rest[8 : 8 + shards], rest[-1]
    shard = scal[0]
    rows, inner = yloc.shape
    expand = head_map(inner)
    state = chain(states, expand)
    s_out[...] = state
    y = yloc[...] + widen(jnp.exp(cum[...]), expand) * nn(c_in[...], state.astype(BF))
    y_out[...] = y
    z = zx[RIM:, :inner]
    gated = y * (z * sigmoid(z))
    work[:, :D] = nn((gated * chan[5:6, :]).astype(BF), wout[...]).astype(BF)
    work[:, D:] = lanes3(jnp.sum(gated * gated, axis=1, keepdims=True))
    for off in range(shards):
        at = pl.multiple_of((shard ^ off) * own, own)
        parts[off][...] = work[pl.ds(at, own), :]


def mixer_middle(scal, states, yloc, zx, c_in, cum, wout, chan, shards):
    rows, inner = yloc.shape
    own = rows // shards
    return call(
        functools.partial(middle_kernel, shards, own, len(states)),
        "middle",
        [sds((rows, inner), F32), sds((N, inner), F32)]
        + [sds((own, D + LANES), BF)] * shards,
        (scal, *states, yloc, zx, c_in, cum, wout, chan),
        smem=(0,),
        scratch=[pltpu.VMEM((rows, D + LANES), BF)],
        flops=2 * rows * D * inner,
        moved=8 * MIB,
    )


def gate_back_kernel(shards, own, scal, *rest):
    blocks, rest = rest[:shards], rest[shards:]
    wout, y_in, zx, c_in, cum, chan = rest[:6]
    grads, u_out, dy_out, dz_out, state_out, gain_out, coef = rest[6:]
    shard = scal[0]
    inner = chan.shape[1]
    for off in range(shards):
        at = pl.multiple_of((shard ^ off) * own, own)
        grads[pl.ds(at, own), :] = blocks[off][:, :D]
        coef[pl.ds(at, own), :] = column3(blocks[off][:, D:].astype(F32))
    du = nt_dot(grads[...], wout[...])
    z = zx[RIM:, :inner]
    y = y_in[...]
    sig = sigmoid(z)
    silu = z * sig
    gated = y * silu
    gain_out[...] = jnp.sum(du * gated, axis=0, keepdims=True)
    gain = chan[5:6, :]
    u_out[...] = (gated * gain).astype(BF)
    dgated = du * gain - gated * coef[...]
    dy = dgated * silu
    dy_out[...] = dy
    dz_out[...] = (dgated * y * (sig * (1.0 + z * (1.0 - sig)))).astype(BF)
    grown = widen(jnp.exp(cum[...]), head_map(inner))
    state_out[0:N, :] = tn(c_in[...], (dy * grown).astype(BF)).astype(BF)
    rows = dy.shape[0]
    state_out[N:, :] = rows3(cum[rows - 1 : rows, :], inner)


def gate_back(scal, blocks, wout, y, zx, c_in, cum, chan):
    shards = len(blocks)
    own = blocks[0].shape[0]
    rows, inner = y.shape
    return call(
        functools.partial(gate_back_kernel, shards, own),
        "gateback",
        [
            sds((rows, D), BF),
            sds((rows, inner), BF),
            sds((rows, inner), F32),
            sds((rows, inner), BF),
            sds((N + RIM, inner), BF),
            sds((1, inner), F32),
        ],
        (scal, *blocks, wout, y, zx, c_in, cum, chan),
        smem=(0,),
        scratch=[pltpu.VMEM((rows, 1), F32)],
        flops=2 * rows * D * inner,
        moved=10 * MIB,
    )


def silu_slope(pre):
    sig = sigmoid(pre)
    return sig * (1.0 + pre * (1.0 - sig))


def conv_back(ds_scr, raw, params, rows, lanes, width, low_out, out_lanes):
    ext = rows + RIM
    total = params[0:1, :] * ds_scr[pl.ds(3, ext), :]
    for k in range(1, 4):
        total = total + params[k : k + 1, :] * ds_scr[pl.ds(3 - k, ext), :]
    low_out[:, out_lanes] = total.astype(BF)
    ds = ds_scr[pl.ds(RIM, rows), :]
    grads = [
        jnp.sum(ds * raw[pl.ds(RIM - 3 + k, rows), lanes], axis=0, keepdims=True) for k in range(4)
    ]
    grads.append(jnp.sum(ds, axis=0, keepdims=True))
    grads.append(jnp.zeros((3, width), F32))
    return jnp.concatenate(grads, axis=0)


def back_kernel(shards, own, hops, scal, *rest):
    states, rest = rest[:hops], rest[hops:]
    s_in, zx, side, dy_in, dz_in, y_in, wzx, wside, chan, bcp, head = rest[:11]
    dzx, dside, chan_out, bcp_out, head_out, rim_out = rest[11:17]
    parts, rest = rest[17 : 17 + shards], rest[17 + shards :]
    xs_scr, dsx, dsbc, work = rest
    shard = scal[0]
    rows, inner = dy_in.shape
    expand = head_map(inner)
    pre_x = conv_sum(zx, chan, rows, pl.ds(inner, inner))
    xs_scr[...] = pre_x * sigmoid(pre_x)
    pre_bc = conv_sum(side, bcp, rows, pl.ds(0, 2 * N))
    bc = (pre_bc * sigmoid(pre_bc)).astype(BF)
    raw_dt = side[RIM:, 2 * N :] + head[0:1, :]
    dt = softplus(raw_dt)
    grow = jnp.exp(head[1:2, :])
    rate = -dt * grow
    skip = widen(head[...], expand)[2:3, :]
    lower_low = (iota((SPAN, SPAN), 0) >= iota((SPAN, SPAN), 1)).astype(F32).astype(BF)
    upper = (iota((SPAN, SPAN), 0) <= iota((SPAN, SPAN), 1)).astype(F32)
    upper_low = upper.astype(BF)
    first_half = iota((SPAN, LANES), 1) < P_SIZE
    spans = rows // SPAN
    cums, starts = [], [s_in[...]]
    for span in range(spans):
        here = slice(span * SPAN, (span + 1) * SPAN)
        cum = tri_sum(lower_low, rate[here])
        cums.append(cum)
        if span + 1 < spans:
            tot = cum[SPAN - 1 : SPAN, :]
            scale = widen(dt[here] * jnp.exp(tot - cum), expand)
            fresh = tn(bc[here, :N], (xs_scr[here, :] * scale).astype(BF))
            starts.append(widen(jnp.exp(tot), expand) * starts[-1] + fresh)
    dstate = chain(states, expand)
    dsx[0:RIM, :] = jnp.zeros((RIM, inner), F32)
    dsx[RIM + rows :, :] = jnp.zeros((RIM, inner), F32)
    dsbc[0:RIM, :] = jnp.zeros((RIM, 2 * N), F32)
    dsbc[RIM + rows :, :] = jnp.zeros((RIM, 2 * N), F32)
    dside[0:RIM, 2 * N :] = jnp.zeros((RIM, LANES), BF)
    dzx[0:RIM, :inner] = jnp.zeros((RIM, inner), BF)
    dzx[RIM:, :inner] = dz_in[...]
    dbias = jnp.zeros((1, LANES), F32)
    dgrow = jnp.zeros((1, LANES), F32)
    dskip = jnp.zeros((1, LANES), F32)
    for span in reversed(range(spans)):
        here = slice(span * SPAN, (span + 1) * SPAN)
        there = slice(RIM + span * SPAN, RIM + (span + 1) * SPAN)
        cum = cums[span]
        cum_t = cum.T
        tot = cum[SPAN - 1 : SPAN, :]
        keys = bc[here, :N]
        queries = bc[here, N:]
        start = starts[span]
        scores_t = nt_dot(keys, queries)
        xs = xs_scr[here, :]
        dy = dy_in[here, :]
        dy_low = dy.astype(BF)
        dt_wide = widen(dt[here], expand)
        scaled = xs * dt_wide
        scaled_low = scaled.astype(BF)
        dscores_t = jnp.zeros((SPAN, SPAN), F32)
        pieces = []
        for pair in range(inner // LANES):
            values = scaled_low[:, pair * LANES : (pair + 1) * LANES]
            dpair = dy_low[:, pair * LANES : (pair + 1) * LANES]
            both = []
            for h in (2 * pair, 2 * pair + 1):
                gap = cum_t[h : h + 1, :] - cum[:, h : h + 1]
                decay = jnp.exp(jnp.minimum(gap, 0.0)) * upper
                mine = first_half if h % 2 == 0 else jnp.logical_not(first_half)
                outer = nt_dot(jnp.where(mine, values, jnp.zeros_like(values)), dpair)
                dscores_t = dscores_t + outer * decay
                both.append(nn((scores_t * decay).astype(BF), dpair))
            pieces.append(jnp.where(first_half, both[0], both[1]))
        dscaled = jnp.concatenate(pieces, axis=1)
        dscores_low = dscores_t.astype(BF)
        grown = widen(jnp.exp(cum), expand)
        tail = widen(jnp.exp(tot - cum), expand)
        dy_grown = (dy * grown).astype(BF)
        dstate_low = dstate.astype(BF)
        through = tail * nn(keys, dstate_low)
        dscaled = dscaled + through
        dqueries = tn(dscores_low, keys) + nt_dot(dy_grown, start.astype(BF))
        dkeys = nn(dscores_low, queries) + nt_dot((scaled * tail).astype(BF), dstate_low)
        plain = y_in[here, :] - skip * xs
        held = scaled_low.astype(F32)
        dcum = narrow(dy_low.astype(F32) * plain - held * dscaled, expand)
        tot_wide = widen(jnp.exp(tot), expand)
        over = jnp.sum(held * through, axis=0, keepdims=True) + jnp.sum(
            tot_wide * dstate * start, axis=0, keepdims=True
        )
        dtot = narrow(jnp.broadcast_to(over, (8, inner)), expand)[0:1, :]
        drate = tri_sum(upper_low, dcum) + dtot
        ddt = narrow(dscaled * xs, expand) - drate * grow
        dgrow = dgrow + jnp.sum(drate * rate[here], axis=0, keepdims=True)
        draw = ddt * sigmoid(raw_dt[here])
        dbias = dbias + jnp.sum(draw, axis=0, keepdims=True)
        dside[there, 2 * N :] = draw.astype(BF)
        over = jnp.sum(dy * xs, axis=0, keepdims=True)
        dskip = dskip + narrow(jnp.broadcast_to(over, (8, inner)), expand)[0:1, :]
        dsx[there, :] = dscaled * dt_wide + skip * dy
        dsbc[there, :N] = dkeys
        dsbc[there, N:] = dqueries
        if span > 0:
            dstate = tot_wide * dstate + tn(queries, dy_grown)
    body = pl.ds(RIM, rows)
    pre_x = conv_sum(zx, chan, rows, pl.ds(inner, inner))
    dsx[body, :] = dsx[body, :] * silu_slope(pre_x)
    pre_bc = conv_sum(side, bcp, rows, pl.ds(0, 2 * N))
    dsbc[body, :] = dsbc[body, :] * silu_slope(pre_bc)
    chan_out[...] = conv_back(
        dsx, zx, chan, rows, pl.ds(inner, inner), inner, dzx, pl.ds(inner, inner)
    )
    bcp_out[...] = conv_back(dsbc, side, bcp, rows, pl.ds(0, 2 * N), 2 * N, dside, pl.ds(0, 2 * N))
    head_out[...] = jnp.concatenate([dbias, dgrow, dskip, jnp.zeros((5, LANES), F32)], axis=0)
    work[...] = (nt_dot(dzx[...], wzx[...]) + nt_dot(dside[...], wside[...])).astype(BF)
    rim_out[...] = work[0:RIM, :]
    for off in range(shards):
        at = pl.multiple_of(RIM + (shard ^ off) * own, RIM)
        parts[off][...] = work[pl.ds(at, own), :]


def mixer_back(scal, states, s_in, zx, side, dy, dz, y, wzx, wside, chan, bcp, head, shards):
    rows, inner = dy.shape
    own = rows // shards
    ext = rows + RIM
    return call(
        functools.partial(back_kernel, shards, own, len(states)),
        "back",
        [
            sds((ext, 2 * inner), BF),
            sds((ext, 2 * N + LANES), BF),
            sds((8, inner), F32),
            sds((8, 2 * N), F32),
            sds((8, LANES), F32),
            sds((RIM, D), BF),
        ]
        + [sds((own, D), BF)] * shards,
        (scal, *states, s_in, zx, side, dy, dz, y, wzx, wside, chan, bcp, head),
        smem=(0,),
        scratch=[
            pltpu.VMEM((rows, inner), F32),
            pltpu.VMEM((ext + RIM, inner), F32),
            pltpu.VMEM((ext + RIM, 2 * N), F32),
            pltpu.VMEM((ext, D), BF),
        ],
        flops=8 * rows * D * inner,
        moved=16 * MIB,
    )


def logits_kernel(shards, own, vrows, label, table, *rest):
    blocks, rest = rest[:shards], rest[shards:]
    p_out, tops, stats, rows_scr, top, total, target, plain = rest
    step = pl.program_id(0)
    rows = own * shards

    @pl.when(step == 0)
    def _():
        for off in range(shards):
            rows_scr[:, off * own : (off + 1) * own] = blocks[off][...].T
        top[...] = jnp.full((1, rows), -1e30, F32)
        total[...] = jnp.zeros((1, rows), F32)
        target[...] = jnp.zeros((1, rows), F32)
        plain[...] = jnp.zeros((1, rows), F32)

    padding = jnp.where(step * PAIRS + iota((PAIRS, LANES), 0) < vrows, 0.0, -1e30)
    padding = jnp.concatenate([padding] * (rows // LANES), axis=1)
    highest, summed, hit, whole = top[...], total[...], target[...], plain[...]
    wanted = label[...] - 2 * step * PAIRS
    line = 2 * iota((PAIRS, rows), 0)
    for half in range(2):
        raw = nn(table[:, half * D : (half + 1) * D], rows_scr[...])
        shown = raw + padding
        before = highest
        highest = jnp.maximum(before, jnp.max(shown, axis=0, keepdims=True))
        part = jnp.exp(shown - highest)
        summed = summed * jnp.exp(before - highest) + jnp.sum(part, axis=0, keepdims=True)
        hit = hit + jnp.sum(jnp.where(line == wanted - half, raw, 0.0), axis=0, keepdims=True)
        whole = whole + jnp.sum(raw, axis=0, keepdims=True)
        p_out[half] = part.astype(BF)
        tops[0, 8 * half : 8 * half + 8, :] = jnp.broadcast_to(highest, (8, rows))
    top[...] = highest
    total[...] = summed
    target[...] = hit
    plain[...] = whole
    stats[...] = jnp.concatenate([highest, summed, hit, whole, jnp.zeros((4, rows), F32)], axis=0)


def vocab_logits(label, table, blocks, vrows):
    shards = len(blocks)
    own = blocks[0].shape[0]
    rows = own * shards
    padded = table.shape[0]
    steps = padded // PAIRS
    whole = lambda i: (0, 0)
    return pl.pallas_call(
        functools.partial(logits_kernel, shards, own, vrows),
        grid=(steps,),
        out_shape=[
            sds((2, padded, rows), BF),
            sds((steps, 16, rows), F32),
            sds((8, rows), F32),
        ],
        in_specs=[
            pl.BlockSpec((1, rows), whole),
            pl.BlockSpec((PAIRS, 2 * D), lambda i: (i, 0)),
        ]
        + [pl.BlockSpec((own, D), whole)] * shards,
        out_specs=[
            pl.BlockSpec((2, PAIRS, rows), lambda i: (0, i, 0)),
            pl.BlockSpec((1, 16, rows), lambda i: (i, 0, 0)),
            pl.BlockSpec((8, rows), whole),
        ],
        scratch_shapes=[pltpu.VMEM((D, rows), BF)] + [pltpu.VMEM((1, rows), F32)] * 4,
        compiler_params=pltpu.CompilerParams(
            dimension_semantics=("arbitrary",), vmem_limit_bytes=48 * MIB
        ),
        cost_estimate=pl.CostEstimate(
            flops=4 * rows * D * padded, bytes_accessed=40 * MIB, transcendentals=2 * rows * padded
        ),
        name="logits",
    )(label, table, *blocks)


def rows_kernel(shards, own, vrows, label, scale, weight, p_in, table, *rest):
    q_out, parts, acc = rest[0], rest[1 : 1 + shards], rest[-1]
    step = pl.program_id(0)
    rows = own * shards

    @pl.when(step == 0)
    def _():
        acc[...] = jnp.zeros_like(acc)

    wanted = label[...] - 2 * step * PAIRS
    line = 2 * iota((PAIRS, rows), 0)
    usual = (SMOOTHING / V) * weight[...]
    special = (1.0 - SMOOTHING + SMOOTHING / V) * weight[...]
    term = None
    for half in range(2):
        share = jnp.where(line == wanted - half, special, usual)
        q = (p_in[half].astype(F32) * scale[0, 8 * half : 8 * half + 1, :] - share).astype(BF)
        q_out[half] = q
        part = tn(q, table[:, half * D : (half + 1) * D])
        term = part if term is None else term + part
    acc[...] += term

    @pl.when(step == pl.num_programs(0) - 1)
    def _():
        for off in range(shards):
            parts[off][...] = acc[off * own : (off + 1) * own, :].astype(BF)


def vocab_rows(label, scale, weight, p_in, table, vrows, shards):
    _, padded, rows = p_in.shape
    steps = padded // PAIRS
    own = rows // shards
    whole = lambda i: (0, 0)
    return pl.pallas_call(
        functools.partial(rows_kernel, shards, own, vrows),
        grid=(steps,),
        out_shape=[sds((2, padded, rows), BF)] + [sds((own, D), BF)] * shards,
        in_specs=[
            pl.BlockSpec((1, rows), whole),
            pl.BlockSpec((1, 16, rows), lambda i: (i, 0, 0)),
            pl.BlockSpec((1, rows), whole),
            pl.BlockSpec((2, PAIRS, rows), lambda i: (0, i, 0)),
            pl.BlockSpec((PAIRS, 2 * D), lambda i: (i, 0)),
        ],
        out_specs=[pl.BlockSpec((2, PAIRS, rows), lambda i: (0, i, 0))]
        + [pl.BlockSpec((own, D), whole)] * shards,
        scratch_shapes=[pltpu.VMEM((rows, D), F32)],
        compiler_params=pltpu.CompilerParams(
            dimension_semantics=("arbitrary",), vmem_limit_bytes=48 * MIB
        ),
        cost_estimate=pl.CostEstimate(
            flops=4 * rows * D * padded, bytes_accessed=52 * MIB, transcendentals=0
        ),
        name="rowgrads",
    )(label, scale, weight, p_in, table)


def table_kernel(shards, own, q_in, *rest):
    blocks, out, rows_scr = rest[:shards], rest[shards], rest[-1]

    @pl.when(pl.program_id(0) == 0)
    def _():
        for off in range(shards):
            rows_scr[off * own : (off + 1) * own, :] = blocks[off][...]

    for half in range(2):
        out[:, half * D : (half + 1) * D] = nn(q_in[half], rows_scr[...]).astype(BF)


def vocab_table_grad(q_in, blocks):
    _, padded, rows = q_in.shape
    shards = len(blocks)
    own = blocks[0].shape[0]
    whole = lambda i: (0, 0)
    return pl.pallas_call(
        functools.partial(table_kernel, shards, own),
        grid=(padded // PAIRS,),
        out_shape=sds((padded, 2 * D), BF),
        in_specs=[pl.BlockSpec((2, PAIRS, rows), lambda i: (0, i, 0))]
        + [pl.BlockSpec((own, D), whole)] * shards,
        out_specs=pl.BlockSpec((PAIRS, 2 * D), lambda i: (i, 0)),
        scratch_shapes=[pltpu.VMEM((rows, D), BF)],
        compiler_params=pltpu.CompilerParams(
            dimension_semantics=("arbitrary",), vmem_limit_bytes=48 * MIB
        ),
        cost_estimate=pl.CostEstimate(
            flops=4 * rows * D * padded, bytes_accessed=40 * MIB, transcendentals=0
        ),
        name="tablegrads",
    )(q_in, *blocks)


def adam_update(weight_in, gradient, moment_one, moment_two, factor, fix_one, fix_two, decay_rate):
    gradient = gradient * factor
    one_next = BETA_FIRST * moment_one + (1.0 - BETA_FIRST) * gradient
    two_next = BETA_SECOND * moment_two + (1.0 - BETA_SECOND) * gradient * gradient
    direction = one_next / fix_one / (jnp.sqrt(two_next / fix_two) + ADAM_EPS)
    return (weight_in - LEARN_RATE * (direction + decay_rate * weight_in), one_next, two_next)


def soap_turn(gradient, bases):
    left_basis = bases[..., 0, :, :]
    right_basis = bases[..., 1, :, :]
    half_turn = jnp.einsum("...ab,...ac->...bc", left_basis, gradient, precision=HIGHEST)
    return jnp.einsum("...bc,...cd->...bd", half_turn, right_basis, precision=HIGHEST)


def soap_update(weight_in, turned_grad, bases, moment_one, moment_two, factor, fix_one, fix_two):
    left_basis = bases[..., 0, :, :]
    right_basis = bases[..., 1, :, :]
    rotated = turned_grad * factor
    one_next = BETA_FIRST * moment_one + (1.0 - BETA_FIRST) * rotated
    two_next = BETA_SECOND * moment_two + (1.0 - BETA_SECOND) * rotated * rotated
    direction = one_next / fix_one / (jnp.sqrt(two_next / fix_two) + ADAM_EPS)
    back_half = jnp.einsum("...ab,...bc->...ac", left_basis, direction, precision=HIGHEST)
    turned = jnp.einsum("...ac,...dc->...ad", back_half, right_basis, precision=HIGHEST)
    weight_next = weight_in - LEARN_RATE * (turned + WEIGHT_DECAY * weight_in)
    return (weight_next, weight_next.astype(BF), one_next, two_next)


def to_blocks(matrix):
    row_count, col_count = matrix.shape
    return (
        matrix.reshape(row_count // BLK, BLK, col_count // BLK, BLK)
        .transpose(0, 2, 1, 3)
        .reshape(-1, BLK, BLK)
    )


def total_over(x, axis):
    out = x
    for off in range(1, lax.axis_size(axis)):
        out = out + swap(x, axis, off)
    return out


def rms_scale(values):
    return lax.rsqrt(jnp.mean(values * values, axis=-1, keepdims=True) + NORM_EPS)


def shards(
    token_ids,
    labels,
    seq_lengths,
    micro_batch,
    step_count,
    block_slot,
    vocab_table,
    vocab_first,
    vocab_second,
    layer_blocks,
    block_bases,
    block_first,
    block_second,
    side_proj,
    side_first,
    side_second,
    shared_params,
    shared_first,
    shared_second,
    channel_params,
    channel_first,
    channel_second,
    head_params,
    head_first,
    head_second,
):
    nt = lax.axis_size("tensor")
    nd = lax.axis_size("dp")
    shard = lax.axis_index("tensor")
    place = lax.axis_index("dp")
    seqs = token_ids.shape[0]
    length = token_ids.shape[1] * nd
    chunks = nd // seqs
    rows = seqs * length // nd
    own = rows // nt
    vrows = vocab_table.shape[0]
    padded = -(-vrows // PAIRS) * PAIRS
    half = nd // 2
    inner = channel_params.shape[2]
    heads = head_params.shape[2]
    tiles = block_slot.shape[1]
    zx_count = D * 2 * inner // (BLK * BLK)
    per_layer = 3 * D * inner // (BLK * BLK)
    stride = D + 10 * N
    both = ("dp", "tensor")
    side_rows = side_proj.shape[1]
    share_size = shared_params.shape[0]
    share_pad = -(-share_size // 2048) * 2048

    piece = jnp.concatenate(
        [
            jnp.pad(side_proj.astype(BF), ((0, 0), (0, 0), (0, LANES - H))).reshape(-1, LANES),
            jnp.pad(shared_params.astype(BF), (0, share_pad - share_size)).reshape(-1, LANES),
        ],
        axis=0,
    )
    piece_rows = piece.shape[0]
    side_part = piece_rows - share_pad // LANES
    pieces = jnp.zeros((nt, piece_rows, LANES), BF)
    for off in range(nt):
        pieces = lax.dynamic_update_index_in_dim(
            pieces, piece if off == 0 else swap(piece, "tensor", off), shard ^ off, 0
        )
    own_tiles = layer_blocks.shape[2]
    carried = jnp.concatenate(
        [layer_blocks.astype(BF).reshape(own_tiles * BLK, BLK), pieces.reshape(-1, LANES)], axis=0
    )
    gathered = lax.all_gather(carried, "dp", axis=0, tiled=False)
    ids_all = lax.all_gather(jnp.concatenate([token_ids, labels], axis=0), "dp", axis=1, tiled=True)
    table_low = jnp.pad(vocab_table.astype(BF), ((0, padded - vrows), (0, 0)))

    placed = place_tiles(block_slot, gathered, own_tiles, inner, zx_count, per_layer)
    small = gathered[:, own_tiles * BLK :].reshape(nd, nt, piece_rows, LANES)
    side_full = (
        small[:, :, :side_part]
        .reshape(nd, nt, L, side_rows, 2 * N + LANES)
        .transpose(2, 0, 1, 3, 4)
        .reshape(L, D, 2 * N + LANES)
    )
    shared_full = small[:, :, side_part:].reshape(nd * nt, share_pad)[:, :share_size].reshape(-1)
    shared_full = shared_full.astype(F32)

    all_ids = ids_all[:seqs].reshape(-1)
    local_row = all_ids // 2 - shard * vrows
    held = (local_row >= 0) & (local_row < vrows) & (all_ids % 2 == place // half)
    scal = jnp.stack([place, shard]).astype(jnp.int32)
    scal_shard = shard.astype(jnp.int32).reshape(1)
    code = jnp.concatenate([jnp.where(held, local_row, -1), jnp.zeros((8,), jnp.int32)])
    parts = gather_rows(scal, code, vocab_table, nd, rows)
    listed, count = parts[nd], parts[nd + 1]
    parts = [parts[0]] + [swap(parts[off], "dp", off) for off in range(1, nd)]
    parts = join_parts(scal, parts, nt, own)
    table_all = lax.all_gather(table_low, "dp", axis=1, tiled=True)

    def layer_mats(layer_index):
        zx_part, out_part = placed[2 * layer_index], placed[2 * layer_index + 1]
        dt_part = lax.dynamic_slice_in_dim(
            side_full[layer_index], 2 * N + shard * heads, heads, 1
        )
        side_here = jnp.concatenate(
            [
                side_full[layer_index][:, : 2 * N],
                jnp.pad(dt_part, ((0, 0), (0, LANES - heads))),
            ],
            axis=1,
        )
        base = layer_index * stride
        gain = shared_full[base : base + D]
        taps = shared_full[base + D : base + D + 8 * N].reshape(4, 2 * N)
        bias = shared_full[base + D + 8 * N : base + stride].reshape(1, 2 * N)
        bcp = jnp.concatenate([taps, bias, jnp.zeros((3, 2 * N), F32)], axis=0)
        chan = jnp.pad(channel_params[layer_index], ((0, 2), (0, 0)))
        head = jnp.pad(head_params[layer_index], ((0, 5), (0, LANES - heads)))
        return (zx_part, out_part, side_here, gain, bcp, chan, head)

    def spread(x):
        return [x] + [swap(x, "tensor", off) for off in range(1, nt)]

    def rim_pairs(to):
        return [
            (k * nt + nt - 1, (k + 1) * nt + to) for k in range(nd) if k % chunks + 1 < chunks
        ]

    def hop(x, distance):
        pairs = [
            (k, k + distance)
            for k in range(nd)
            if 0 <= k % chunks + distance < chunks
        ]
        return lax.ppermute(x, "dp", pairs)

    def returned(parts):
        return [parts[0]] + [swap(parts[off], "tensor", off) for off in range(1, nt)]

    hops = range(1, chunks)
    mats = [layer_mats(layer_index) for layer_index in range(L)]
    final_gain = shared_full[L * stride :][None, :]
    gains = [mats[layer_index][3][None, :] for layer_index in range(L)] + [final_gain]
    saved = []
    residual, normed_own = enter(returned(parts), gains[0])
    for layer_index in range(L):
        wzx, wout, wside, gain, bcp, chan, head = mats[layer_index]
        edge = normed_own[own - RIM :]
        rims = [lax.ppermute(edge, both, rim_pairs(to)) for to in range(nt)]
        normed, zx, side, yloc, final, c_out, cum = mixer_front(
            scal_shard, spread(normed_own), rims, wzx, wside, chan, bcp, head
        )
        states = [hop(final, k) for k in hops]
        result = mixer_middle(scal_shard, states, yloc, zx, c_out, cum, wout, chan, nt)
        y, s_in = result[:2]
        before = residual
        residual, branch, factor, normed_own = join_residual(
            returned(result[2:]), before, gains[layer_index + 1]
        )
        saved.append((before, normed, zx, side, c_out, cum, y, s_in, factor, branch))
    final_rows = spread(normed_own)

    member = micro_batch[:, None] == jnp.arange(MB, dtype=jnp.int32)[None, :]
    batch_tokens = jnp.sum(jnp.where(member, seq_lengths[:, None], 0), axis=0).astype(F32)
    seq_weight = 1.0 / (MB * jnp.sum(jnp.where(member, batch_tokens[None, :], 0.0), axis=1))
    block_order = shard ^ jnp.arange(nt, dtype=jnp.int32)
    row_at = (
        place * rows + block_order[:, None] * own + jnp.arange(own, dtype=jnp.int32)[None, :]
    ).reshape(rows)
    my_seq = place // chunks
    weight = jnp.where(row_at % length < seq_lengths[my_seq], seq_weight[my_seq], 0.0)
    all_labels = ids_all[seqs:].reshape(-1)
    label = (all_labels[row_at] - 2 * shard * vrows).reshape(1, rows)

    p_low, tops, stats = vocab_logits(label, table_all, final_rows, vrows)
    stats = stats.reshape(8, nt, own)
    merged = (stats[0], stats[1], stats[2], stats[3])
    others = [swap(stats, "tensor", off) for off in range(1, nt)]
    best = stats[0]
    for off in range(1, nt):
        best = jnp.maximum(best, jnp.stack([others[off - 1][0, o ^ off] for o in range(nt)]))
    summed = stats[1] * jnp.exp(stats[0] - best)
    target = stats[2]
    plain = stats[3]
    for off in range(1, nt):
        them = jnp.stack([others[off - 1][:, o ^ off] for o in range(nt)], axis=1)
        summed = summed + them[1] * jnp.exp(them[0] - best)
        target = target + them[2]
        plain = plain + them[3]
    log_total = best + jnp.log(summed)
    token_loss = (
        log_total
        - (1.0 - SMOOTHING) * target
        - SMOOTHING / V * plain
        + ZLOSS_WEIGHT * log_total * log_total
    )
    loss_here = jnp.sum(weight[:own] * token_loss[0])
    seq_part = jnp.where(jnp.arange(seqs) == my_seq, loss_here, 0.0)
    soft = (weight.reshape(nt, own) * (1.0 + 2.0 * ZLOSS_WEIGHT * log_total)).reshape(1, 1, rows)
    scale = soft * jnp.exp(tops - log_total.reshape(1, 1, rows))
    result = vocab_rows(label, scale, weight.reshape(1, rows), p_low, table_all, vrows, nt)
    q_low = result[0]
    sent = returned(result[1:])
    table_grad = vocab_table_grad(q_low, final_rows)
    sent, table_grad = lax.optimization_barrier((sent, table_grad))
    table_share = lax.psum_scatter(table_grad, "dp", scatter_dimension=1, tiled=True)
    grad_res, payload, grad_final_gain = back_rows(
        sent, [], residual, final_gain, None, (saved[L - 1][9], saved[L - 1][8])
    )

    block_pieces = [None] * (2 * L)
    side_pieces = [None] * L
    channel_pieces = [None] * L
    head_pieces = [None] * L
    shared_pieces = [None] * L
    for layer_index in reversed(range(L)):
        wzx, wout, wside, gain, bcp, chan, head = mats[layer_index]
        residual_in, normed, zx, side, c_out, cum, y, s_in, factor, branch = saved[layer_index]
        grads, u_low, dy, dz, dstate, gain_grad = gate_back(
            scal_shard, spread(payload), wout, y, zx, c_out, cum, chan
        )
        states = [hop(dstate, -k) for k in hops]
        grad_out_w = tn(u_low, grads)
        result = mixer_back(
            scal_shard, states, s_in, zx, side, dy, dz, y, wzx, wside, chan, bcp, head, nt
        )
        dzx, dside, chan_grad, bcp_grad, head_grad, rim_grad = result[:6]
        rims = [
            lax.ppermute(rim_grad, both, [(b, a) for a, b in rim_pairs(to)]) for to in range(nt)
        ]
        below = (saved[layer_index - 1][9], saved[layer_index - 1][8]) if layer_index else None
        grad_res, payload, grad_gain_in = back_rows(
            returned(result[6:]), rims, residual_in, gains[layer_index], grad_res, below
        )
        grad_zx_w = tn(normed, dzx)
        grad_side_w = tn(normed, dside)
        block_pieces[2 * layer_index] = to_blocks(grad_zx_w.astype(BF))
        block_pieces[2 * layer_index + 1] = to_blocks(grad_out_w.astype(BF))
        spaced = lax.dynamic_update_slice(
            jnp.zeros((D, LANES), F32),
            grad_side_w[:, 2 * N : 2 * N + heads],
            (jnp.zeros((), jnp.int32), shard * heads),
        )
        side_pieces[layer_index] = jnp.concatenate([grad_side_w[:, : 2 * N], spaced], axis=1)
        channel_pieces[layer_index] = jnp.concatenate([chan_grad[:5], gain_grad], axis=0)
        head_pieces[layer_index] = head_grad[:3, :heads]
        shared_pieces[layer_index] = jnp.concatenate(
            [grad_gain_in[0], bcp_grad[:4].reshape(-1), bcp_grad[4]]
        )

    embed = cut_parts(scal, spread(payload), nd)
    embed = [embed[0]] + [swap(embed[off], "dp", off) for off in range(1, nd)]

    inverse = jnp.zeros((tiles,), jnp.int32).at[block_slot[0]].set(jnp.arange(tiles, dtype=jnp.int32))
    ordered_grads = jnp.concatenate(block_pieces, axis=0)
    slot_grads = ordered_grads[inverse].reshape(nd, own_tiles * BLK, BLK)
    side_grads = (
        jnp.stack(side_pieces)
        .astype(BF)
        .reshape(L, nd, nt, side_rows, 2 * N + LANES)
        .transpose(1, 2, 0, 3, 4)
        .reshape(nd, nt, side_part, LANES)
    )
    shared_grads = jnp.concatenate(shared_pieces + [grad_final_gain[0]]).astype(BF)
    shared_grads = jnp.pad(
        shared_grads.reshape(nd, nt, share_size), ((0, 0), (0, 0), (0, share_pad - share_size))
    ).reshape(nd, nt, share_pad // LANES, LANES)
    small_grads = jnp.concatenate([side_grads, shared_grads], axis=2).reshape(nd, -1, LANES)
    tile_grads = jnp.concatenate([slot_grads, small_grads], axis=1)
    tile_grads, table_share = lax.optimization_barrier((tile_grads, table_share))
    block_share = lax.psum_scatter(tile_grads, "dp", scatter_dimension=0, tiled=True)[0]
    block_grads = block_share[: own_tiles * BLK].astype(F32)
    small_share = block_share[own_tiles * BLK :].reshape(nt, piece_rows, LANES)
    mine = jnp.zeros((piece_rows, LANES), F32)
    for off in range(nt):
        sent = lax.dynamic_index_in_dim(small_share, shard ^ off, 0, False)
        mine = mine + (sent if off == 0 else swap(sent, "tensor", off)).astype(F32)
    side_share = mine[:side_part].reshape(L, side_rows, 2 * N + LANES)[:, :, : 2 * N + H]
    shared_share = mine[side_part:].reshape(-1)[:share_size]
    lines = jnp.concatenate(
        [
            jnp.stack(channel_pieces).reshape(-1, LANES),
            jnp.pad(jnp.stack(head_pieces).reshape(-1), (0, LANES - L * 3 * heads)).reshape(1, LANES),
        ],
        axis=0,
    )
    lines = total_over(lines, "dp")
    channel_sum = lines[:-1].reshape(channel_params.shape)
    head_sum = lines[-1, : L * 3 * heads].reshape(head_params.shape)

    grad_table, table_square = add_rows(
        scal, jnp.maximum(code, 0), listed, count, table_share, embed, vrows
    )
    rotated = soap_turn(block_grads.reshape(layer_blocks.shape), block_bases)
    first_copy = (place == 0).astype(F32)
    square_part = (
        jnp.sum(block_grads * block_grads)
        + jnp.sum(table_square)
        + jnp.sum(side_share * side_share)
        + jnp.sum(shared_share * shared_share)
        + first_copy * (jnp.sum(channel_sum * channel_sum) + jnp.sum(head_sum * head_sum))
    )
    packed = jnp.pad(jnp.concatenate([seq_part, square_part[None]]), (0, 8 * LANES - seqs - 1))
    packed, rotated = lax.optimization_barrier((packed, rotated))
    packed = sum_everywhere(packed.reshape(8, LANES), nd, nt)[0]
    seq_loss = packed[:seqs]
    clip_norm = jnp.sqrt(packed[seqs])
    factor = jnp.minimum(1.0, CLIP_LIMIT / (clip_norm + 1e-06))
    steps_done = step_count[0].astype(F32)
    fix_one = 1.0 - jnp.power(BETA_FIRST, steps_done)
    fix_two = 1.0 - jnp.power(BETA_SECOND, steps_done)
    table_out = adam_update(
        vocab_table, grad_table, vocab_first, vocab_second, factor, fix_one, fix_two, WEIGHT_DECAY
    )
    block_out = soap_update(
        layer_blocks,
        rotated,
        block_bases,
        block_first,
        block_second,
        factor,
        fix_one,
        fix_two,
    )
    side_next = adam_update(
        side_proj, side_share, side_first, side_second, factor, fix_one, fix_two, WEIGHT_DECAY
    )
    shared_next = adam_update(
        shared_params, shared_share, shared_first, shared_second, factor, fix_one, fix_two, 0.0
    )
    channel_next = adam_update(
        channel_params, channel_sum, channel_first, channel_second, factor, fix_one, fix_two, 0.0
    )
    head_next = adam_update(
        head_params, head_sum, head_first, head_second, factor, fix_one, fix_two, 0.0
    )
    return (
        seq_loss,
        clip_norm,
        table_out[0],
        table_out[1],
        table_out[2],
        block_out[0],
        block_out[1],
        block_out[2],
        block_out[3],
        side_next[0],
        side_next[1],
        side_next[2],
        shared_next[0] - shared_params,
        shared_next[1],
        shared_next[2],
        channel_next[0] - channel_params,
        channel_next[1],
        channel_next[2],
        head_next[0] - head_params,
        head_next[1],
        head_next[2],
    )


def solution(mesh):
    table = P("tensor", "dp")
    block = P("dp", "tensor", None, None, None)
    side = P(None, ("dp", "tensor"), None)
    shared = P(("dp", "tensor"))
    channel = P(None, None, "tensor")
    in_specs = (
        P(None, "dp"),
        P(None, "dp"),
        P(),
        P(),
        P(),
        P("tensor", None),
        *[table] * 3,
        block,
        P("dp", "tensor", None, None, None, None),
        block,
        block,
        *[side] * 3,
        *[shared] * 3,
        *[channel] * 6,
    )
    out_specs = (
        P(),
        P(),
        *[table] * 3,
        *[block] * 4,
        *[side] * 3,
        *[shared] * 3,
        *[channel] * 6,
    )
    return jax.shard_map(shards, mesh=mesh, in_specs=in_specs, out_specs=out_specs, check_vma=False)
```

```python
import functools

import jax
import jax.numpy as jnp
from jax import lax
from jax.experimental import pallas as pl
from jax.experimental.pallas import tpu as pltpu
from jax.sharding import PartitionSpec as P

D = 1024
DI = 2048
H = 32
P_SIZE = 64
N = 128
V = 50288
SPAN = 256
L = 2
MB = 2
BLK = 128
RIM = 16
PAIRS = 1280
PART = 320
LANES = 128

HIGHEST = lax.Precision.HIGHEST
NORM_EPS = 1e-05
SMOOTHING = 0.1
ZLOSS_WEIGHT = 0.005
CLIP_LIMIT = 0.02
BETA_FIRST = 0.9
BETA_SECOND = 0.95
ADAM_EPS = 1e-08
LEARN_RATE = 0.03
WEIGHT_DECAY = 0.01

BF = jnp.bfloat16
F32 = jnp.float32
MIB = 1 << 20


def nn(a, b, precision=None):
    return lax.dot_general(
        a, b, (((1,), (0,)), ((), ())), precision=precision, preferred_element_type=F32
    )


def nt_dot(a, b, precision=None):
    return lax.dot_general(
        a, b, (((1,), (1,)), ((), ())), precision=precision, preferred_element_type=F32
    )


def tn(a, b, precision=None):
    return lax.dot_general(
        a, b, (((0,), (0,)), ((), ())), precision=precision, preferred_element_type=F32
    )


def iota(shape, dim):
    return lax.broadcasted_iota(jnp.int32, shape, dim)


def head_map(inner):
    return (iota((LANES, inner), 0) == iota((LANES, inner), 1) // P_SIZE).astype(F32).astype(BF)


def swap(x, axis, offset):
    size = lax.axis_size(axis)
    return lax.ppermute(x, axis, [(i, i ^ offset) for i in range(size)])


def halves(x):
    high = x.astype(BF)
    return high, (x - high.astype(F32)).astype(BF)


def thirds(x):
    high = x.astype(BF)
    rest = x - high.astype(F32)
    mid = rest.astype(BF)
    return high, mid, (rest - mid.astype(F32)).astype(BF)


def widen(x, expand):
    high, low = halves(x)
    twice = jnp.concatenate([expand, expand], axis=0)
    return nn(jnp.concatenate([high, low], axis=1), twice)


def narrow(x, expand):
    high, low = halves(x)
    return nt_dot(high, expand) + nt_dot(low, expand)


def tri_sum(tri, x):
    wide = nn(tri, jnp.concatenate(thirds(x), axis=1))
    size = x.shape[1]
    return wide[:, :size] + wide[:, size : 2 * size] + wide[:, 2 * size :]


def lanes3(column):
    high, mid, low = thirds(column)
    lane = iota((column.shape[0], LANES), 1)
    zero = jnp.zeros((column.shape[0], LANES), F32)
    wide = jnp.where(lane == 0, high.astype(F32), zero)
    wide = jnp.where(lane == 1, mid.astype(F32), wide)
    return jnp.where(lane == 2, low.astype(F32), wide).astype(BF)


def column3(wide):
    return wide[:, 0:1] + wide[:, 1:2] + wide[:, 2:3]


def rows3(line, inner):
    high, mid, low = thirds(line)
    at = iota((RIM, LANES), 0)
    wide = jnp.where(at == 0, high.astype(F32), 0.0)
    wide = jnp.where(at == 1, mid.astype(F32), wide)
    wide = jnp.where(at == 2, low.astype(F32), wide)
    if inner > LANES:
        wide = jnp.concatenate([wide, jnp.zeros((RIM, inner - LANES), F32)], axis=1)
    return wide.astype(BF)


def sigmoid(x):
    return 1.0 / (1.0 + jnp.exp(-x))


def softplus(x):
    return jnp.maximum(x, 0.0) + jnp.log1p(jnp.exp(-jnp.abs(x)))


def call(kernel, name, out_shape, args, smem=(), scratch=(), mib=60, flops=0, moved=0, **extra):
    specs = [
        pl.BlockSpec(memory_space=pltpu.SMEM if i in smem else pltpu.VMEM)
        for i in range(len(args))
    ]
    return pl.pallas_call(
        kernel,
        out_shape=out_shape,
        in_specs=specs,
        out_specs=jax.tree.map(lambda _: pl.BlockSpec(memory_space=pltpu.VMEM), out_shape),
        scratch_shapes=list(scratch),
        compiler_params=pltpu.CompilerParams(vmem_limit_bytes=mib * MIB),
        cost_estimate=pl.CostEstimate(flops=flops, bytes_accessed=moved, transcendentals=0),
        name=name,
        **extra,
    )(*args)


def sds(shape, dtype):
    return jax.ShapeDtypeStruct(shape, dtype)


def list_held(held, total):
    runs = held.reshape(-1, LANES)
    upper = iota((LANES, LANES), 0) <= iota((LANES, LANES), 1)
    rank = nn(runs.astype(BF), upper.astype(BF)).astype(jnp.int32) - 1
    here = (rank[:, :, None] == iota((1, 1, LANES), 2)) & runs[:, :, None]
    at = jnp.sum(jnp.where(here, iota((1, LANES, 1), 1), 0), axis=1)
    counts = rank[:, -1] + 1
    first = iota(at.shape, 0) * LANES
    listed = jnp.where(iota(at.shape, 1) < counts[:, None], at + first, total)
    return listed.reshape(-1), counts


def over_listed(listed, count, body):
    def run(at_run, carry):
        def turn(step, inner_carry):
            for lane in range(8):
                body(listed[at_run * LANES + step * 8 + lane])
            return inner_carry

        lax.fori_loop(0, (count[at_run] + 7) // 8, turn, 0)
        return carry

    lax.fori_loop(0, count.shape[0], run, 0)


def look_kernel(groups, rows, scal, code, listed, count, table, *rest):
    outs, work = rest[:groups], rest[groups]
    place = scal[0]

    def fill(step, carry):
        work[pl.ds(pl.multiple_of(step * rows, rows), rows), :] = jnp.zeros((rows, table.shape[1]), F32)
        return carry

    lax.fori_loop(0, groups, fill, 0)

    def take(at):
        work[pl.ds(at, 1), :] = table[pl.ds(code[at], 1), :]

    over_listed(listed, count, take)
    for off in range(groups):
        base = pl.multiple_of((place ^ off) * rows, rows)
        outs[off][...] = work[pl.ds(base, rows), :].astype(BF)


def gather_rows(scal, code, listed, count, table, groups, rows):
    cols = table.shape[1]
    return call(
        functools.partial(look_kernel, groups, rows),
        "look",
        [sds((rows, cols), BF)] * groups,
        (scal, code, listed, count, table),
        smem=(0, 1, 2, 3),
        scratch=[pltpu.VMEM((groups * rows + 8, cols), F32)],
        moved=30 * MIB,
    )


def join_kernel(groups, shards, own, scal, *rest):
    parts, outs, work = rest[:groups], rest[groups : groups + shards], rest[-1]
    place, shard = scal[0], scal[1]
    half = groups // 2
    cols = parts[0].shape[1]
    for off in range(half):
        at = ((place ^ off) % half) * cols
        work[:, pl.ds(pl.multiple_of(at, cols), cols)] = parts[off][...] + parts[off + half][...]
    for off in range(shards):
        at = pl.multiple_of((shard ^ off) * own, own)
        outs[off][...] = work[pl.ds(at, own), :]


def join_parts(scal, parts, shards, own):
    rows = parts[0].shape[0]
    return call(
        functools.partial(join_kernel, len(parts), shards, own),
        "join",
        [sds((own, D), BF)] * shards,
        (scal, *parts),
        smem=(0,),
        scratch=[pltpu.VMEM((rows, D), BF)],
        moved=4 * MIB,
    )


def add_kernel(groups, rows, vrows, scal, code, listed, count, share, parts, *rest):
    out, square, work, bins = rest
    place = scal[0]
    bins[...] = share[0:vrows, :].astype(F32)
    for off in range(groups):
        base = pl.multiple_of((place ^ off) * rows, rows)
        work[pl.ds(base, rows), :] = parts[off].astype(F32)
    work[groups * rows :, :] = jnp.zeros((8, work.shape[1]), F32)

    def add(at):
        to = pl.ds(code[at], 1)
        bins[to, :] = bins[to, :] + work[pl.ds(at, 1), :]

    over_listed(listed, count, add)
    total = bins[...]
    out[...] = total.astype(BF)
    square[...] = jnp.sqrt(jnp.sum(total * total, axis=0, keepdims=True))


def add_rows(scal, code, listed, count, share, parts, vrows):
    cols = share.shape[1]
    groups, rows, _ = parts.shape
    return call(
        functools.partial(add_kernel, groups, rows, vrows),
        "addrows",
        [sds((vrows, cols), BF), sds((1, cols), F32)],
        (scal, code, listed, count, share, parts),
        smem=(0, 1, 2, 3),
        scratch=[pltpu.VMEM((rows * groups + 8, cols), F32), pltpu.VMEM((vrows, cols), F32)],
        moved=30 * MIB,
    )


def tiles_kernel(slots_each, zx_count, per_layer, layers, slot, tiles, *outs):
    for layer in range(layers):
        for at in range(per_layer):
            where = slot[0, layer * per_layer + at]
            owner = where // slots_each
            first = pl.multiple_of((where % slots_each) * BLK, BLK)
            tile = tiles[owner, pl.ds(first, BLK), :]
            if at < zx_count:
                wide = outs[2 * layer].shape[1] // BLK
                row, col = at // wide, at % wide
                out = outs[2 * layer]
            else:
                wide = D // BLK
                row, col = (at - zx_count) // wide, (at - zx_count) % wide
                out = outs[2 * layer + 1]
            out[row * BLK : (row + 1) * BLK, col * BLK : (col + 1) * BLK] = tile


def place_tiles(slot, tiles, slots_each, inner, zx_count, per_layer):
    return call(
        functools.partial(tiles_kernel, slots_each, zx_count, per_layer, L),
        "placetiles",
        [sds((D, 2 * inner), BF), sds((inner, D), BF)] * L,
        (slot, tiles),
        smem=(0,),
        moved=14 * MIB,
    )


def pack_kernel(slots_each, per_layer, layers, shards, heads, scal, slot, *refs):
    mats, sides, refs = refs[: 2 * layers], refs[2 * layers : 3 * layers], refs[3 * layers :]
    shared, lines, out, work = refs
    for layer in range(layers):
        zx, wout = mats[2 * layer], mats[2 * layer + 1]
        zx_wide, out_wide = zx.shape[1] // BLK, wout.shape[1] // BLK
        zx_count = zx.shape[0] // BLK * zx_wide
        for at in range(per_layer):
            where = slot[0, layer * per_layer + at]
            if at < zx_count:
                source, row, col = zx, at // zx_wide, at % zx_wide
            else:
                source = wout
                row, col = (at - zx_count) // out_wide, (at - zx_count) % out_wide
            first = pl.multiple_of((where % slots_each) * BLK, BLK)
            out[where // slots_each, pl.ds(first, BLK), :] = source[
                row * BLK : (row + 1) * BLK, col * BLK : (col + 1) * BLK
            ]
        work[layer, :, : 2 * N] = sides[layer][:, : 2 * N]
        work[layer, :, 2 * N :] = pltpu.roll(sides[layer][:, 2 * N :], scal[0] * heads, 1)
    groups = out.shape[0]
    each = work.shape[1] // (groups * shards)
    piece = layers * each * work.shape[2] // LANES
    base = slots_each * BLK
    for group in range(groups):
        for shard in range(shards):
            first = (group * shards + shard) * each
            blocks = [
                work[layer, first : first + each, col : col + LANES]
                for layer in range(layers)
                for col in range(0, work.shape[2], LANES)
            ]
            at = base + shard * piece
            out[group, at : at + piece, :] = jnp.concatenate(blocks, axis=0).astype(BF)
    base += shards * piece
    out[:, base : base + shared.shape[1], :] = shared[...]
    for group in range(groups):
        out[group, base + shared.shape[1] :, :] = lines[...]


def pack_tiles(scal, slot, mats, sides, shared, lines, slots_each, per_layer, shards, heads):
    groups = shared.shape[0]
    layers = len(sides)
    depth, width = sides[0].shape
    extra = layers * depth * width // (groups * LANES) + shared.shape[1] + lines.shape[0]
    return call(
        functools.partial(pack_kernel, slots_each, per_layer, layers, shards, heads),
        "packtiles",
        sds((groups, slots_each * BLK + extra, LANES), BF),
        (scal, slot, *mats, *sides, shared, lines),
        smem=(0, 1),
        scratch=[pltpu.VMEM((layers, depth, width), F32)],
        moved=14 * MIB,
    )


def norm_rows(values, gain):
    return values * lax.rsqrt(jnp.mean(values * values, axis=-1, keepdims=True) + NORM_EPS) * gain


def total_of(parts):
    total = parts[0][...].astype(F32)
    for part in parts[1:]:
        total = total + part[...].astype(F32)
    return total


def enter_kernel(count, *refs):
    parts, (gain, residual, normed) = refs[:count], refs[count:]
    total = total_of(parts)
    residual[...] = total
    normed[...] = norm_rows(total, gain[...]).astype(BF)


def enter(parts, gain):
    own = parts[0].shape[0]
    return call(
        functools.partial(enter_kernel, len(parts)),
        "enter",
        [sds((own, D), F32), sds((own, D), BF)],
        (*parts, gain),
        moved=2 * MIB,
    )


def join_residual_kernel(count, *refs):
    parts, (before, gain, residual, branch, factor, normed) = refs[:count], refs[count:]
    total = total_of(parts)
    scale = lax.rsqrt(column3(total[:, D:]) / DI + NORM_EPS)
    branch[...] = total[:, :D]
    factor[...] = scale
    after = before[...] + scale * total[:, :D]
    residual[...] = after
    normed[...] = norm_rows(after, gain[...]).astype(BF)


def join_residual(parts, before, gain):
    own = before.shape[0]
    return call(
        functools.partial(join_residual_kernel, len(parts)),
        "residual",
        [sds((own, D), F32), sds((own, D), F32), sds((own, 1), F32), sds((own, D), BF)],
        (*parts, before, gain),
        moved=3 * MIB,
    )


def back_rows_kernel(count, rim_count, last, *refs):
    parts, refs = refs[:count], refs[count:]
    rims, refs = refs[:rim_count], refs[rim_count:]
    residual, gain, refs = refs[0], refs[1], refs[2:]
    grad_in = None
    if rim_count:
        grad_in, refs = refs[0], refs[1:]
    if not last:
        branch, factor, refs = refs[0], refs[1], refs[2:]
    if rim_count:
        grad_out, payload, gain_grad, work = refs
    else:
        grad_out, payload, gain_grad = refs
    grad = total_of(parts)
    if rim_count:
        work[...] = grad
        own = work.shape[0]
        work[own - RIM :, :] += total_of(rims)
        grad = work[...]
    values = residual[...]
    inv = lax.rsqrt(jnp.mean(values * values, axis=-1, keepdims=True) + NORM_EPS)
    gain_grad[...] = jnp.sum(grad * values * inv, axis=0, keepdims=True)
    scaled = grad * gain[...]
    result = inv * scaled - values * (inv * inv * inv) * jnp.mean(
        scaled * values, axis=-1, keepdims=True
    )
    if grad_in is not None:
        result = grad_in[...] + result
    grad_out[...] = result
    if last:
        payload[...] = result.astype(BF)
    else:
        scale = factor[...]
        payload[:, :D] = (scale * result).astype(BF)
        inner_rows = jnp.sum(result * branch[...], axis=-1, keepdims=True)
        payload[:, D:] = lanes3(scale * scale * scale * inner_rows / DI)


def back_rows(parts, rims, residual, gain, grad_in, below):
    own = residual.shape[0]
    last = below is None
    args = (*parts, *rims, residual, gain)
    if rims:
        args = (*args, grad_in)
    if not last:
        args = (*args, *below)
    return call(
        functools.partial(back_rows_kernel, len(parts), len(rims), last),
        "backrows",
        [
            sds((own, D), F32),
            sds((own, D if last else D + LANES), BF),
            sds((1, D), F32),
        ],
        args,
        scratch=[pltpu.VMEM((own, D), F32)] if rims else [],
        moved=4 * MIB,
    )


def send(source, target, send_sem, recv_sem, device):
    copy = pltpu.make_async_remote_copy(
        src_ref=source,
        dst_ref=target,
        send_sem=send_sem,
        recv_sem=recv_sem,
        device_id=device,
        device_id_type=pl.DeviceIdType.MESH,
    )
    copy.start()
    return copy


def finish_kernel(groups, shards, chunks, own, *refs):
    parts, rim, residual, gain, grad_in, out = refs[:shards], *refs[shards : shards + 5]
    (from_shards, from_rims, payload, full, work, term_sems, rim_sems, row_sems, out_sems) = refs[
        shards + 5 :
    ]
    place, shard = lax.axis_index("dp"), lax.axis_index("tensor")
    half = groups // 2
    cols = out.shape[2]
    chunk = lax.rem(place, chunks)
    last = shard == shards - 1
    shard_peers = [(place, shard ^ off) for off in range(1, shards)]
    group_peers = [(place ^ off, shard) for off in range(1, groups)]
    barrier = pltpu.get_barrier_semaphore()

    def greet(device):
        pl.semaphore_signal(barrier, inc=1, device_id=device, device_id_type=pl.DeviceIdType.MESH)

    for peer in shard_peers + group_peers:
        greet(peer)

    @pl.when(jnp.logical_not(last))
    def _():
        greet((lax.rem(place + groups - 1, groups), shards - 1))

    @pl.when(last)
    def _():
        for other in range(shards - 1):
            greet((lax.rem(place + 1, groups), other))

    pl.semaphore_wait(barrier, shards + groups - 2 + jnp.where(last, shards - 1, 1))

    def rim_copy():
        return pltpu.make_async_remote_copy(
            src_ref=rim,
            dst_ref=from_rims.at[shard],
            send_sem=rim_sems.at[0, shard],
            recv_sem=rim_sems.at[1, shard],
            device_id=(place - 1, shards - 1),
            device_id_type=pl.DeviceIdType.MESH,
        )

    @pl.when(chunk > 0)
    def _():
        rim_copy().start()

    terms = [
        send(
            parts[off],
            from_shards.at[off - 1],
            term_sems.at[0, off],
            term_sems.at[1, off],
            shard_peers[off - 1],
        )
        for off in range(1, shards)
    ]
    values = residual[...]
    inv = lax.rsqrt(jnp.mean(values * values, axis=-1, keepdims=True) + NORM_EPS)
    for term in terms:
        term.wait()
    total = parts[0][...].astype(F32)
    for off in range(1, shards):
        total = total + from_shards[off - 1].astype(F32)
    work[...] = total

    @pl.when(jnp.logical_and(chunk + 1 < chunks, last))
    def _():
        for other in range(shards):
            pltpu.make_async_remote_copy(
                src_ref=rim,
                dst_ref=from_rims.at[other],
                send_sem=rim_sems.at[0, other],
                recv_sem=rim_sems.at[1, other],
                device_id=(place + 1, other),
                device_id_type=pl.DeviceIdType.MESH,
            ).wait_recv()
        edge = from_rims[0].astype(F32)
        for other in range(1, shards):
            edge = edge + from_rims[other].astype(F32)
        work[own - RIM :, :] += edge

    @pl.when(chunk > 0)
    def _():
        rim_copy().wait_send()

    scaled = work[...] * gain[...]
    result = (
        grad_in[...]
        + inv * scaled
        - values * (inv * inv * inv) * jnp.mean(scaled * values, axis=-1, keepdims=True)
    ).astype(BF)
    payload[...] = result
    rows_out = [
        send(
            payload,
            full.at[off],
            row_sems.at[0, off],
            row_sems.at[1, off],
            shard_peers[off - 1],
        )
        for off in range(1, shards)
    ]
    full[0] = result

    def first_col(group):
        return pl.multiple_of(lax.rem(group, half) * cols, cols)

    cuts = []
    for off in range(shards):
        if off > 0:
            rows_out[off - 1].wait()
        at = pl.ds(pl.multiple_of((shard ^ off) * own, own), own)
        for other in range(1, groups):
            cuts.append(
                send(
                    full.at[off, :, pl.ds(first_col(place ^ other), cols)],
                    out.at[other, at, :],
                    out_sems.at[0, off, other],
                    out_sems.at[1, off, other],
                    group_peers[other - 1],
                )
            )
        out[0, at, :] = full[off, :, pl.ds(first_col(place), cols)]
    for cut in cuts:
        cut.wait()


def finish_rows(parts, rim, residual, gain, grad_in, groups, chunks):
    shards = len(parts)
    own = parts[0].shape[0]
    vmem = pl.BlockSpec(memory_space=pltpu.VMEM)
    args = (*parts, rim, residual, gain, grad_in)
    return pl.pallas_call(
        functools.partial(finish_kernel, groups, shards, chunks, own),
        out_shape=sds((groups, own * shards, 2 * D // groups), BF),
        in_specs=[vmem] * len(args),
        out_specs=vmem,
        scratch_shapes=[
            pltpu.VMEM((shards - 1, own, D), BF),
            pltpu.VMEM((shards, RIM, D), BF),
            pltpu.VMEM((own, D), BF),
            pltpu.VMEM((shards, own, D), BF),
            pltpu.VMEM((own, D), F32),
            pltpu.SemaphoreType.DMA((2, shards)),
            pltpu.SemaphoreType.DMA((2, shards)),
            pltpu.SemaphoreType.DMA((2, shards)),
            pltpu.SemaphoreType.DMA((2, shards, groups)),
        ],
        compiler_params=pltpu.CompilerParams(
            collective_id=3, has_side_effects=True, vmem_limit_bytes=32 * MIB
        ),
        name="finish",
    )(*args)


def open_kernel(groups, shards, ids, piece, ids_out, pieces_out, send, recv):
    place, shard = lax.axis_index("dp"), lax.axis_index("tensor")
    peers = [(place, shard ^ off) for off in range(1, shards)]
    peers += [(place ^ off, shard) for off in range(1, groups)]
    barrier = pltpu.get_barrier_semaphore()
    for peer in peers:
        pl.semaphore_signal(barrier, inc=1, device_id=peer, device_id_type=pl.DeviceIdType.MESH)
    pl.semaphore_wait(barrier, len(peers))
    copies = []
    for i, peer in enumerate(peers):
        copy = pltpu.make_async_remote_copy(
            src_ref=piece if i < shards - 1 else ids,
            dst_ref=pieces_out.at[shard] if i < shards - 1 else ids_out.at[place],
            send_sem=send.at[i],
            recv_sem=recv.at[i],
            device_id=peer,
            device_id_type=pl.DeviceIdType.MESH,
        )
        copy.start()
        copies.append(copy)
    ids_out[place] = ids[...]
    pieces_out[shard] = piece[...]
    for copy in copies:
        copy.wait()


def open_exchange(ids, piece, groups, shards):
    count = groups + shards - 2
    vmem = pl.BlockSpec(memory_space=pltpu.VMEM)
    return pl.pallas_call(
        functools.partial(open_kernel, groups, shards),
        out_shape=[sds((groups, *ids.shape), jnp.int32), sds((shards, *piece.shape), BF)],
        in_specs=[vmem, vmem],
        out_specs=[vmem, vmem],
        scratch_shapes=[pltpu.SemaphoreType.DMA((count,)), pltpu.SemaphoreType.DMA((count,))],
        compiler_params=pltpu.CompilerParams(
            collective_id=2, has_side_effects=True, vmem_limit_bytes=8 * MIB
        ),
        name="open",
    )(ids, piece)


def sum_kernel(groups, shards, once, split, *refs):
    loss = refs[0]
    refs = refs[1:]
    count = once + split
    ones, many, refs = refs[:once], refs[once:count], refs[count:]
    o_ref, start, mid, from_shards, from_groups, send, recv = refs
    place, shard = lax.axis_index("dp"), lax.axis_index("tensor")
    peers = [(place, shard ^ off) for off in range(1, shards)]
    peers += [(place ^ off, shard) for off in range(1, groups)]
    barrier = pltpu.get_barrier_semaphore()
    for peer in peers:
        pl.semaphore_signal(barrier, inc=1, device_id=peer, device_id_type=pl.DeviceIdType.MESH)

    def square(refs):
        total = jnp.zeros((1, 1), F32)
        for ref in refs:
            flat = jnp.sum(ref[...] * ref[...], axis=0, keepdims=True)
            total = total + jnp.sum(flat, axis=1, keepdims=True)
        return total

    first = (place == 0).astype(F32)
    part = square(many) + first * square(ones)
    start[...] = loss[...] + jnp.where(iota((8, LANES), 1) == LANES - 1, part, 0.0)
    pl.semaphore_wait(barrier, len(peers))

    def exchange(source, slots, first, some):
        copies = []
        for i, peer in enumerate(some):
            copy = pltpu.make_async_remote_copy(
                src_ref=source,
                dst_ref=slots.at[i],
                send_sem=send.at[first + i],
                recv_sem=recv.at[first + i],
                device_id=peer,
                device_id_type=pl.DeviceIdType.MESH,
            )
            copy.start()
            copies.append(copy)
        for copy in copies:
            copy.wait()
        total = source[...]
        for i in range(len(some)):
            total = total + slots[i]
        return total

    mid[...] = exchange(start, from_shards, 0, peers[: shards - 1])
    total = exchange(mid, from_groups, shards - 1, peers[shards - 1 :])
    norm = jnp.sqrt(total[0:1, LANES - 1 : LANES])
    factor = jnp.minimum(1.0, CLIP_LIMIT / (norm + 1e-06))
    row = iota((8, LANES), 0)
    o_ref[...] = jnp.where(row == 0, total, jnp.where(row == 1, norm, factor))


def sum_everywhere(loss, ones, many, groups, shards):
    count = groups + shards - 2
    args = (loss, *ones, *many)
    vmem = pl.BlockSpec(memory_space=pltpu.VMEM)
    return pl.pallas_call(
        functools.partial(sum_kernel, groups, shards, len(ones), len(many)),
        out_shape=sds((8, LANES), F32),
        in_specs=[vmem] * len(args),
        out_specs=vmem,
        scratch_shapes=[
            pltpu.VMEM((8, LANES), F32),
            pltpu.VMEM((8, LANES), F32),
            pltpu.VMEM((shards - 1, 8, LANES), F32),
            pltpu.VMEM((groups - 1, 8, LANES), F32),
            pltpu.SemaphoreType.DMA((count,)),
            pltpu.SemaphoreType.DMA((count,)),
        ],
        compiler_params=pltpu.CompilerParams(
            collective_id=1, has_side_effects=True, vmem_limit_bytes=8 * MIB
        ),
        name="sumall",
    )(*args)


def conv_sum(raw, params, rows, lanes):
    total = params[4:5, :] + params[0:1, :] * raw[pl.ds(RIM - 3, rows), lanes]
    for k in range(1, 4):
        total = total + params[k : k + 1, :] * raw[pl.ds(RIM - 3 + k, rows), lanes]
    return total


def front_kernel(shards, own, scal, *rest):
    blocks, rest = rest[:shards], rest[shards:]
    rims, rest = rest[:shards], rest[shards:]
    wzx, wside, chan, bcp, head = rest[:5]
    normed, zx, side, yloc, final, c_out, cum_out, xs_scr = rest[5:]
    shard = scal[0]
    rows = own * shards
    inner = chan.shape[1]
    rim = rims[0][...]
    for other in rims[1:]:
        rim = rim + other[...]
    normed[0:RIM, :] = rim
    for off in range(shards):
        at = pl.multiple_of(RIM + (shard ^ off) * own, RIM)
        normed[pl.ds(at, own), :] = blocks[off][...]
    zx[...] = nn(normed[...], wzx[...])
    side[...] = nn(normed[...], wside[...])
    pre = conv_sum(zx, chan, rows, pl.ds(inner, inner))
    xs_scr[...] = pre * sigmoid(pre)
    pre = conv_sum(side, bcp, rows, pl.ds(0, 2 * N))
    bc = (pre * sigmoid(pre)).astype(BF)
    c_out[...] = bc[:, N:]
    dt = softplus(side[RIM:, 2 * N :] + head[0:1, :])
    rate = -dt * jnp.exp(head[1:2, :])
    expand = head_map(inner)
    skip = widen(head[...], expand)[2:3, :]
    lower = (iota((SPAN, SPAN), 0) >= iota((SPAN, SPAN), 1)).astype(F32)
    lower_low = lower.astype(BF)
    first_half = iota((SPAN, LANES), 1) < P_SIZE
    state = None
    base = jnp.zeros((1, LANES), F32)
    for span in range(rows // SPAN):
        here = slice(span * SPAN, (span + 1) * SPAN)
        cum = tri_sum(lower_low, rate[here])
        cum_t = cum.T
        tot = cum[SPAN - 1 : SPAN, :]
        keys = bc[here, :N]
        queries = bc[here, N:]
        scores = nt_dot(queries, keys)
        xs = xs_scr[here, :]
        scaled = xs * widen(dt[here], expand)
        scaled_low = scaled.astype(BF)
        pieces = []
        for pair in range(inner // LANES):
            values = scaled_low[:, pair * LANES : (pair + 1) * LANES]
            both = []
            for h in (2 * pair, 2 * pair + 1):
                gap = cum[:, h : h + 1] - cum_t[h : h + 1, :]
                decay = jnp.exp(jnp.minimum(gap, 0.0)) * lower
                both.append(nn((scores * decay).astype(BF), values))
            pieces.append(jnp.where(first_half, both[0], both[1]))
        y = jnp.concatenate(pieces, axis=1) + skip * xs
        if state is not None:
            y = y + widen(jnp.exp(cum), expand) * nn(queries, state.astype(BF))
        yloc[here, :] = y
        tail = widen(jnp.exp(tot - cum), expand)
        fresh = tn(keys, (scaled * tail).astype(BF))
        if state is not None:
            fresh = fresh + widen(jnp.exp(tot), expand) * state
        state = fresh
        cum_out[here, :] = cum + base
        base = base + tot
    final[0:N, :] = state.astype(BF)
    final[N:, :] = rows3(base, inner)


def mixer_front(scal, blocks, rims, wzx, wside, chan, bcp, head):
    shards = len(blocks)
    own = blocks[0].shape[0]
    rows = own * shards
    inner = chan.shape[1]
    return call(
        functools.partial(front_kernel, shards, own),
        "front",
        [
            sds((rows + RIM, D), BF),
            sds((rows + RIM, 2 * inner), F32),
            sds((rows + RIM, 2 * N + LANES), F32),
            sds((rows, inner), F32),
            sds((N + RIM, inner), BF),
            sds((rows, N), BF),
            sds((rows, LANES), F32),
        ],
        (scal, *blocks, *rims, wzx, wside, chan, bcp, head),
        smem=(0,),
        scratch=[pltpu.VMEM((rows, inner), F32)],
        flops=8 * rows * D * inner,
        moved=12 * MIB,
    )


def chain(parts, expand):
    total = None
    past = jnp.zeros((1, LANES), F32)
    for part in parts:
        term = widen(jnp.exp(past), expand) * part[0:N, :].astype(F32)
        total = term if total is None else total + term
        past = past + jnp.sum(part[N:, :LANES].astype(F32), axis=0, keepdims=True)
    return total


def middle_kernel(shards, own, hops, scal, *rest):
    states, rest = rest[:hops], rest[hops:]
    yloc, zx, c_in, cum, wout, chan = rest[:6]
    y_out, s_out = rest[6:8]
    parts, work = rest[8 : 8 + shards], rest[-1]
    shard = scal[0]
    rows, inner = yloc.shape
    expand = head_map(inner)
    state = chain(states, expand)
    s_out[...] = state
    y = yloc[...] + widen(jnp.exp(cum[...]), expand) * nn(c_in[...], state.astype(BF))
    y_out[...] = y
    z = zx[RIM:, :inner]
    gated = y * (z * sigmoid(z))
    work[:, :D] = nn((gated * chan[5:6, :]).astype(BF), wout[...]).astype(BF)
    work[:, D:] = lanes3(jnp.sum(gated * gated, axis=1, keepdims=True))
    for off in range(shards):
        at = pl.multiple_of((shard ^ off) * own, own)
        parts[off][...] = work[pl.ds(at, own), :]


def mixer_middle(scal, states, yloc, zx, c_in, cum, wout, chan, shards):
    rows, inner = yloc.shape
    own = rows // shards
    return call(
        functools.partial(middle_kernel, shards, own, len(states)),
        "middle",
        [sds((rows, inner), F32), sds((N, inner), F32)]
        + [sds((own, D + LANES), BF)] * shards,
        (scal, *states, yloc, zx, c_in, cum, wout, chan),
        smem=(0,),
        scratch=[pltpu.VMEM((rows, D + LANES), BF)],
        flops=2 * rows * D * inner,
        moved=8 * MIB,
    )


def gate_back_kernel(shards, own, scal, *rest):
    blocks, rest = rest[:shards], rest[shards:]
    wout, y_in, zx, c_in, cum, chan = rest[:6]
    grads, u_out, dy_out, dz_out, state_out, gain_out, coef = rest[6:]
    shard = scal[0]
    inner = chan.shape[1]
    for off in range(shards):
        at = pl.multiple_of((shard ^ off) * own, own)
        grads[pl.ds(at, own), :] = blocks[off][:, :D]
        coef[pl.ds(at, own), :] = column3(blocks[off][:, D:].astype(F32))
    du = nt_dot(grads[...], wout[...])
    z = zx[RIM:, :inner]
    y = y_in[...]
    sig = sigmoid(z)
    silu = z * sig
    gated = y * silu
    gain_out[...] = jnp.sum(du * gated, axis=0, keepdims=True)
    gain = chan[5:6, :]
    u_out[...] = (gated * gain).astype(BF)
    dgated = du * gain - gated * coef[...]
    dy = dgated * silu
    dy_out[...] = dy
    dz_out[...] = (dgated * y * (sig * (1.0 + z * (1.0 - sig)))).astype(BF)
    grown = widen(jnp.exp(cum[...]), head_map(inner))
    state_out[0:N, :] = tn(c_in[...], (dy * grown).astype(BF)).astype(BF)
    rows = dy.shape[0]
    state_out[N:, :] = rows3(cum[rows - 1 : rows, :], inner)


def gate_back(scal, blocks, wout, y, zx, c_in, cum, chan):
    shards = len(blocks)
    own = blocks[0].shape[0]
    rows, inner = y.shape
    return call(
        functools.partial(gate_back_kernel, shards, own),
        "gateback",
        [
            sds((rows, D), BF),
            sds((rows, inner), BF),
            sds((rows, inner), F32),
            sds((rows, inner), BF),
            sds((N + RIM, inner), BF),
            sds((1, inner), F32),
        ],
        (scal, *blocks, wout, y, zx, c_in, cum, chan),
        smem=(0,),
        scratch=[pltpu.VMEM((rows, 1), F32)],
        flops=2 * rows * D * inner,
        moved=10 * MIB,
    )


def silu_slope(pre):
    sig = sigmoid(pre)
    return sig * (1.0 + pre * (1.0 - sig))


def conv_back(ds_scr, raw, params, rows, lanes, width, low_out, out_lanes):
    ext = rows + RIM
    total = params[0:1, :] * ds_scr[pl.ds(3, ext), :]
    for k in range(1, 4):
        total = total + params[k : k + 1, :] * ds_scr[pl.ds(3 - k, ext), :]
    low_out[:, out_lanes] = total.astype(BF)
    ds = ds_scr[pl.ds(RIM, rows), :]
    grads = [
        jnp.sum(ds * raw[pl.ds(RIM - 3 + k, rows), lanes], axis=0, keepdims=True) for k in range(4)
    ]
    grads.append(jnp.sum(ds, axis=0, keepdims=True))
    grads.append(jnp.zeros((3, width), F32))
    return jnp.concatenate(grads, axis=0)


def within_kernel(s_in, zx, side, dy_in, chan, bcp, head, *outs):
    xs_out, bc_out, cum_out, starts_out, dscaled_out, dbc_out = outs
    rows, inner = dy_in.shape
    expand = head_map(inner)
    pre_x = conv_sum(zx, chan, rows, pl.ds(inner, inner))
    xs_out[...] = pre_x * sigmoid(pre_x)
    pre_bc = conv_sum(side, bcp, rows, pl.ds(0, 2 * N))
    bc = (pre_bc * sigmoid(pre_bc)).astype(BF)
    bc_out[...] = bc
    dt = softplus(side[RIM:, 2 * N :] + head[0:1, :])
    rate = -dt * jnp.exp(head[1:2, :])
    lower_low = (iota((SPAN, SPAN), 0) >= iota((SPAN, SPAN), 1)).astype(F32).astype(BF)
    upper = (iota((SPAN, SPAN), 0) <= iota((SPAN, SPAN), 1)).astype(F32)
    first_half = iota((SPAN, LANES), 1) < P_SIZE
    spans = rows // SPAN
    start = s_in[...]
    for span in range(spans):
        here = slice(span * SPAN, (span + 1) * SPAN)
        cum = tri_sum(lower_low, rate[here])
        cum_out[here, :] = cum
        cum_t = cum.T
        keys = bc[here, :N]
        queries = bc[here, N:]
        xs = xs_out[here, :]
        starts_out[span] = start
        start_low = start.astype(BF)
        if span + 1 < spans:
            tot = cum[SPAN - 1 : SPAN, :]
            scale = widen(dt[here] * jnp.exp(tot - cum), expand)
            fresh = tn(keys, (xs * scale).astype(BF))
            start = widen(jnp.exp(tot), expand) * start + fresh
        scores_t = nt_dot(keys, queries)
        dy = dy_in[here, :]
        dy_low = dy.astype(BF)
        scaled_low = (xs * widen(dt[here], expand)).astype(BF)
        dscores_t = jnp.zeros((SPAN, SPAN), F32)
        for pair in range(inner // LANES):
            lanes = slice(pair * LANES, (pair + 1) * LANES)
            values = scaled_low[:, lanes]
            dpair = dy_low[:, lanes]
            both = []
            for h in (2 * pair, 2 * pair + 1):
                gap = cum_t[h : h + 1, :] - cum[:, h : h + 1]
                decay = jnp.exp(jnp.minimum(gap, 0.0)) * upper
                mine = first_half if h % 2 == 0 else jnp.logical_not(first_half)
                outer = nt_dot(jnp.where(mine, values, jnp.zeros_like(values)), dpair)
                dscores_t = dscores_t + outer * decay
                both.append(nn((scores_t * decay).astype(BF), dpair))
            dscaled_out[here, lanes] = jnp.where(first_half, both[0], both[1])
        dscores_low = dscores_t.astype(BF)
        dy_grown = (dy * widen(jnp.exp(cum), expand)).astype(BF)
        dbc_out[here, :N] = nn(dscores_low, queries)
        dbc_out[here, N:] = tn(dscores_low, keys) + nt_dot(dy_grown, start_low)


def mixer_within(s_in, zx, side, dy, chan, bcp, head):
    rows, inner = dy.shape
    return call(
        within_kernel,
        "within",
        [
            sds((rows, inner), F32),
            sds((rows, 2 * N), BF),
            sds((rows, LANES), F32),
            sds((rows // SPAN, N, inner), F32),
            sds((rows, inner), F32),
            sds((rows, 2 * N), F32),
        ],
        (s_in, zx, side, dy, chan, bcp, head),
        flops=8 * rows * D * inner,
        moved=16 * MIB,
    )


def back_kernel(shards, own, hops, scal, *rest):
    states, rest = rest[:hops], rest[hops:]
    xs_in, bc_in, cum_in, starts, dscaled_in, dbc_in, rest = *rest[:6], rest[6:]
    zx, side, dy_in, dz_in, y_in, wzx, wside, chan, bcp, head = rest[:10]
    normed, gain = rest[10:12]
    dzx, dside, chan_out, bcp_out, head_out, rim_out, gain_out = rest[12:19]
    parts, rest = rest[19 : 19 + shards], rest[19 + shards :]
    dsx, dsbc, work = rest
    shard = scal[0]
    rows, inner = dy_in.shape
    expand = head_map(inner)
    raw_dt = side[RIM:, 2 * N :] + head[0:1, :]
    dt = softplus(raw_dt)
    grow = jnp.exp(head[1:2, :])
    rate = -dt * grow
    skip = widen(head[...], expand)[2:3, :]
    upper_low = (iota((SPAN, SPAN), 0) <= iota((SPAN, SPAN), 1)).astype(F32).astype(BF)
    spans = rows // SPAN
    dstate = chain(states, expand)
    dsx[0:RIM, :] = jnp.zeros((RIM, inner), F32)
    dsx[RIM + rows :, :] = jnp.zeros((RIM, inner), F32)
    dsbc[0:RIM, :] = jnp.zeros((RIM, 2 * N), F32)
    dsbc[RIM + rows :, :] = jnp.zeros((RIM, 2 * N), F32)
    dside[0:RIM, 2 * N :] = jnp.zeros((RIM, LANES), BF)
    dzx[0:RIM, :inner] = jnp.zeros((RIM, inner), BF)
    dzx[RIM:, :inner] = dz_in[...]
    dbias = jnp.zeros((1, LANES), F32)
    dgrow = jnp.zeros((1, LANES), F32)
    dskip = jnp.zeros((1, LANES), F32)
    for span in reversed(range(spans)):
        here = slice(span * SPAN, (span + 1) * SPAN)
        there = slice(RIM + span * SPAN, RIM + (span + 1) * SPAN)
        cum = cum_in[here, :]
        tot = cum[SPAN - 1 : SPAN, :]
        keys = bc_in[here, :N]
        queries = bc_in[here, N:]
        xs = xs_in[here, :]
        dy = dy_in[here, :]
        dy_low = dy.astype(BF)
        dt_wide = widen(dt[here], expand)
        scaled = xs * dt_wide
        scaled_low = scaled.astype(BF)
        tail = widen(jnp.exp(tot - cum), expand)
        dstate_low = dstate.astype(BF)
        through = tail * nn(keys, dstate_low)
        dscaled = dscaled_in[here, :] + through
        plain = y_in[here, :] - skip * xs
        held = scaled_low.astype(F32)
        dcum = narrow(dy_low.astype(F32) * plain - held * dscaled, expand)
        tot_wide = widen(jnp.exp(tot), expand)
        over = jnp.sum(held * through, axis=0, keepdims=True) + jnp.sum(
            tot_wide * dstate * starts[span], axis=0, keepdims=True
        )
        dtot = narrow(jnp.broadcast_to(over, (8, inner)), expand)[0:1, :]
        drate = tri_sum(upper_low, dcum) + dtot
        ddt = narrow(dscaled * xs, expand) - drate * grow
        dgrow = dgrow + jnp.sum(drate * rate[here], axis=0, keepdims=True)
        draw = ddt * sigmoid(raw_dt[here])
        dbias = dbias + jnp.sum(draw, axis=0, keepdims=True)
        dside[there, 2 * N :] = draw.astype(BF)
        over = jnp.sum(dy * xs, axis=0, keepdims=True)
        dskip = dskip + narrow(jnp.broadcast_to(over, (8, inner)), expand)[0:1, :]
        dsx[there, :] = dscaled * dt_wide + skip * dy
        dsbc[there, :N] = dbc_in[here, :N] + nt_dot((scaled * tail).astype(BF), dstate_low)
        dsbc[there, N:] = dbc_in[here, N:]
        if span > 0:
            grown = widen(jnp.exp(cum), expand)
            dstate = tot_wide * dstate + tn(queries, (dy * grown).astype(BF))
    body = pl.ds(RIM, rows)
    pre_x = conv_sum(zx, chan, rows, pl.ds(inner, inner))
    dsx[body, :] = dsx[body, :] * silu_slope(pre_x)
    pre_bc = conv_sum(side, bcp, rows, pl.ds(0, 2 * N))
    dsbc[body, :] = dsbc[body, :] * silu_slope(pre_bc)
    chan_out[...] = conv_back(
        dsx, zx, chan, rows, pl.ds(inner, inner), inner, dzx, pl.ds(inner, inner)
    )
    bcp_out[...] = conv_back(dsbc, side, bcp, rows, pl.ds(0, 2 * N), 2 * N, dside, pl.ds(0, 2 * N))
    head_out[...] = jnp.concatenate([dbias, dgrow, dskip, jnp.zeros((5, LANES), F32)], axis=0)
    dnormed = nt_dot(dzx[...], wzx[...]) + nt_dot(dside[...], wside[...])
    work[...] = dnormed.astype(BF)
    gain_out[...] = jnp.sum(dnormed * normed[...].astype(F32), axis=0, keepdims=True) / gain[...]
    rim_out[...] = work[0:RIM, :]
    for off in range(shards):
        at = pl.multiple_of(RIM + (shard ^ off) * own, RIM)
        parts[off][...] = work[pl.ds(at, own), :]


def mixer_back(
    scal, states, inside, zx, side, dy, dz, y, wzx, wside, chan, bcp, head, normed, gain, shards
):
    rows, inner = dy.shape
    own = rows // shards
    ext = rows + RIM
    return call(
        functools.partial(back_kernel, shards, own, len(states)),
        "back",
        [
            sds((ext, 2 * inner), BF),
            sds((ext, 2 * N + LANES), BF),
            sds((8, inner), F32),
            sds((8, 2 * N), F32),
            sds((8, LANES), F32),
            sds((RIM, D), BF),
            sds((1, D), F32),
        ]
        + [sds((own, D), BF)] * shards,
        (scal, *states, *inside, zx, side, dy, dz, y, wzx, wside, chan, bcp, head, normed, gain),
        smem=(0,),
        scratch=[
            pltpu.VMEM((ext + RIM, inner), F32),
            pltpu.VMEM((ext + RIM, 2 * N), F32),
            pltpu.VMEM((ext, D), BF),
        ],
        flops=8 * rows * D * inner,
        moved=16 * MIB,
    )


def logits_kernel(shards, own, vrows, label, table, *rest):
    blocks, rest = rest[:shards], rest[shards:]
    p_out, tops, stats, rows_scr, top, total, target, plain = rest
    step = pl.program_id(0)
    rows = own * shards

    @pl.when(step == 0)
    def _():
        for off in range(shards):
            rows_scr[:, off * own : (off + 1) * own] = blocks[off][...].T
        top[...] = jnp.full((1, rows), -1e30, F32)
        total[...] = jnp.zeros((1, rows), F32)
        target[...] = jnp.zeros((1, rows), F32)
        plain[...] = jnp.zeros((1, rows), F32)

    highest, summed, hit, whole = top[...], total[...], target[...], plain[...]
    line = 2 * iota((PART, rows), 0)
    for half in range(2):
        for part_at in range(PAIRS // PART):
            first = step * PAIRS + part_at * PART
            here = slice(part_at * PART, (part_at + 1) * PART)
            padding = jnp.where(first + iota((PART, LANES), 0) < vrows, 0.0, -1e30)
            padding = jnp.concatenate([padding] * (rows // LANES), axis=1)
            raw = nn(table[here, half * D : (half + 1) * D], rows_scr[...])
            shown = raw + padding
            before = highest
            highest = jnp.maximum(before, jnp.max(shown, axis=0, keepdims=True))
            part = jnp.exp(shown - highest)
            summed = summed * jnp.exp(before - highest) + jnp.sum(part, axis=0, keepdims=True)
            wanted = label[...] - 2 * first - half
            hit = hit + jnp.sum(jnp.where(line == wanted, raw, 0.0), axis=0, keepdims=True)
            whole = whole + jnp.sum(raw, axis=0, keepdims=True)
            p_out[half, here, :] = part.astype(BF)
            at = 8 * (half * (PAIRS // PART) + part_at)
            tops[0, at : at + 8, :] = jnp.broadcast_to(highest, (8, rows))
    top[...] = highest
    total[...] = summed
    target[...] = hit
    plain[...] = whole
    stats[...] = jnp.concatenate([highest, summed, hit, whole, jnp.zeros((4, rows), F32)], axis=0)


def vocab_logits(label, table, blocks, vrows):
    shards = len(blocks)
    own = blocks[0].shape[0]
    rows = own * shards
    padded = table.shape[0]
    steps = padded // PAIRS
    whole = lambda i: (0, 0)
    return pl.pallas_call(
        functools.partial(logits_kernel, shards, own, vrows),
        grid=(steps,),
        out_shape=[
            sds((2, padded, rows), BF),
            sds((steps, 16 * (PAIRS // PART), rows), F32),
            sds((8, rows), F32),
        ],
        in_specs=[
            pl.BlockSpec((1, rows), whole),
            pl.BlockSpec((PAIRS, 2 * D), lambda i: (i, 0)),
        ]
        + [pl.BlockSpec((own, D), whole)] * shards,
        out_specs=[
            pl.BlockSpec((2, PAIRS, rows), lambda i: (0, i, 0)),
            pl.BlockSpec((1, 16 * (PAIRS // PART), rows), lambda i: (i, 0, 0)),
            pl.BlockSpec((8, rows), whole),
        ],
        scratch_shapes=[pltpu.VMEM((D, rows), BF)] + [pltpu.VMEM((1, rows), F32)] * 4,
        compiler_params=pltpu.CompilerParams(
            dimension_semantics=("arbitrary",), vmem_limit_bytes=56 * MIB
        ),
        cost_estimate=pl.CostEstimate(
            flops=4 * rows * D * padded, bytes_accessed=40 * MIB, transcendentals=2 * rows * padded
        ),
        name="logits",
    )(label, table, *blocks)


def logit_grads(step, label, scale, weight, p_in):
    pairs, rows = p_in.shape[1:]
    line = 2 * iota((PART, rows), 0)
    usual = (SMOOTHING / V) * weight[...]
    special = (1.0 - SMOOTHING + SMOOTHING / V) * weight[...]
    for half in range(2):
        pieces = []
        for part_at in range(pairs // PART):
            wanted = label[...] - 2 * (step * pairs + part_at * PART) - half
            share = jnp.where(line == wanted, special, usual)
            at = 8 * (half * (pairs // PART) + part_at)
            grown = p_in[half, part_at * PART : (part_at + 1) * PART, :].astype(F32)
            pieces.append((grown * scale[0, at : at + 1, :] - share).astype(BF))
        yield half, jnp.concatenate(pieces, axis=0)


def rows_kernel(shards, own, label, scale, weight, p_in, table, *rest):
    parts, acc = rest[:shards], rest[-1]
    step = pl.program_id(0)

    @pl.when(step == 0)
    def _():
        acc[...] = jnp.zeros_like(acc)

    for half, q in logit_grads(step, label, scale, weight, p_in):
        acc[...] += tn(q, table[:, half * D : (half + 1) * D])

    @pl.when(step == pl.num_programs(0) - 1)
    def _():
        for off in range(shards):
            parts[off][...] = acc[off * own : (off + 1) * own, :].astype(BF)


def vocab_specs(rows):
    whole = lambda i: (0, 0)
    return [
        pl.BlockSpec((1, rows), whole),
        pl.BlockSpec((1, 16 * (PAIRS // PART), rows), lambda i: (i, 0, 0)),
        pl.BlockSpec((1, rows), whole),
        pl.BlockSpec((2, PAIRS, rows), lambda i: (0, i, 0)),
    ]


def vocab_rows(label, scale, weight, p_in, table, shards):
    _, padded, rows = p_in.shape
    own = rows // shards
    whole = lambda i: (0, 0)
    return pl.pallas_call(
        functools.partial(rows_kernel, shards, own),
        grid=(padded // PAIRS,),
        out_shape=[sds((own, D), BF)] * shards,
        in_specs=vocab_specs(rows) + [pl.BlockSpec((PAIRS, 2 * D), lambda i: (i, 0))],
        out_specs=[pl.BlockSpec((own, D), whole)] * shards,
        scratch_shapes=[pltpu.VMEM((rows, D), F32)],
        compiler_params=pltpu.CompilerParams(
            dimension_semantics=("arbitrary",), vmem_limit_bytes=56 * MIB
        ),
        cost_estimate=pl.CostEstimate(
            flops=4 * rows * D * padded, bytes_accessed=40 * MIB, transcendentals=0
        ),
        name="rowgrads",
    )(label, scale, weight, p_in, table)


def table_kernel(shards, own, label, scale, weight, p_in, *rest):
    blocks, out, rows_scr = rest[:shards], rest[shards], rest[-1]
    step = pl.program_id(0)

    @pl.when(step == 0)
    def _():
        for off in range(shards):
            rows_scr[off * own : (off + 1) * own, :] = blocks[off][...]

    for half, q in logit_grads(step, label, scale, weight, p_in):
        out[:, half * D : (half + 1) * D] = nn(q, rows_scr[...]).astype(BF)


def vocab_table_grad(label, scale, weight, p_in, blocks):
    _, padded, rows = p_in.shape
    shards = len(blocks)
    own = blocks[0].shape[0]
    whole = lambda i: (0, 0)
    return pl.pallas_call(
        functools.partial(table_kernel, shards, own),
        grid=(padded // PAIRS,),
        out_shape=sds((padded, 2 * D), BF),
        in_specs=vocab_specs(rows) + [pl.BlockSpec((own, D), whole)] * shards,
        out_specs=pl.BlockSpec((PAIRS, 2 * D), lambda i: (i, 0)),
        scratch_shapes=[pltpu.VMEM((rows, D), BF)],
        compiler_params=pltpu.CompilerParams(
            dimension_semantics=("arbitrary",), vmem_limit_bytes=56 * MIB
        ),
        cost_estimate=pl.CostEstimate(
            flops=4 * rows * D * padded, bytes_accessed=40 * MIB, transcendentals=0
        ),
        name="tablegrads",
    )(label, scale, weight, p_in, *blocks)


def adam_update(weight_in, gradient, moment_one, moment_two, factor, fix_one, fix_two, decay_rate):
    gradient = gradient * factor
    one_next = BETA_FIRST * moment_one + (1.0 - BETA_FIRST) * gradient
    two_next = BETA_SECOND * moment_two + (1.0 - BETA_SECOND) * gradient * gradient
    direction = one_next / fix_one / (jnp.sqrt(two_next / fix_two) + ADAM_EPS)
    return (weight_in - LEARN_RATE * (direction + decay_rate * weight_in), one_next, two_next)


def turn_kernel(share, bases, turned, root):
    count = bases.shape[0]
    total = jnp.zeros((1, BLK), F32)

    def turn(at, total):
        grad = share[pl.ds(pl.multiple_of(at * BLK, BLK), BLK), :].astype(F32)
        half_turn = tn(bases[at, 0], grad, HIGHEST)
        turned[at] = nn(half_turn, bases[at, 1], HIGHEST)
        return total + jnp.sum(grad * grad, axis=0, keepdims=True)

    for at in range(count):
        total = turn(at, total)
    root[...] = jnp.sqrt(total)


def turn_tiles(share, bases):
    count = bases.shape[0]
    return call(
        turn_kernel,
        "turn",
        [sds((count, BLK, BLK), F32), sds((1, BLK), F32)],
        (share, bases),
        moved=6 * MIB,
    )


def last_kernel(small, fixes, sums, *refs):
    tiles, turned, bases, tile_one, tile_two = refs[:5]
    little, refs = refs[5 : 5 + 4 * small], refs[5 + 4 * small :]
    tiles_out, copy_out, tile_one_out, tile_two_out = refs[:4]
    little_out = refs[4:]
    factor, fix_one, fix_two = sums[2:3, 0:1], fixes[0], fixes[1]
    for at in range(tiles.shape[0]):
        rotated = turned[at] * factor
        one_next = BETA_FIRST * tile_one[at] + (1.0 - BETA_FIRST) * rotated
        two_next = BETA_SECOND * tile_two[at] + (1.0 - BETA_SECOND) * rotated * rotated
        direction = one_next / fix_one / (jnp.sqrt(two_next / fix_two) + ADAM_EPS)
        back_half = nn(bases[at, 0], direction, HIGHEST)
        back = nt_dot(back_half, bases[at, 1], HIGHEST)
        after = tiles[at] - LEARN_RATE * (back + WEIGHT_DECAY * tiles[at])
        tiles_out[at] = after
        copy_out[at] = after.astype(BF)
        tile_one_out[at] = one_next
        tile_two_out[at] = two_next

    @pl.when(pl.program_id(0) == 0)
    def _():
        for which in range(small):
            before, gradient, first, second = (ref[...] for ref in little[4 * which : 4 * which + 4])
            results = adam_update(
                before,
                gradient,
                first,
                second,
                factor,
                fix_one,
                fix_two,
                WEIGHT_DECAY if which == 0 else 0.0,
            )
            outs = little_out[3 * which : 3 * which + 3]
            outs[0][...] = results[0] if which == 0 else results[0] - before
            outs[1][...], outs[2][...] = results[1], results[2]


def last_update(fixes, sums, tiles, turned, bases, tile_one, tile_two, little):
    count = tiles.shape[0]
    each = 4 if count % 4 == 0 else 2
    tile_spec = pl.BlockSpec((each, BLK, BLK), lambda i: (i, 0, 0))
    base_spec = pl.BlockSpec((each, 2, BLK, BLK), lambda i: (i, 0, 0, 0))
    whole = [pl.BlockSpec(x.shape, lambda i: (0, 0)) for group in little for x in group]
    return pl.pallas_call(
        functools.partial(last_kernel, len(little)),
        grid=(count // each,),
        out_shape=[sds(tiles.shape, F32), sds(tiles.shape, BF), sds(tiles.shape, F32), sds(tiles.shape, F32)]
        + [sds(group[0].shape, F32) for group in little for _ in range(3)],
        in_specs=[
            pl.BlockSpec(memory_space=pltpu.SMEM),
            pl.BlockSpec(sums.shape, lambda i: (0, 0)),
        ]
        + [tile_spec, tile_spec, base_spec, tile_spec, tile_spec]
        + whole,
        out_specs=[tile_spec] * 4
        + [spec for which in range(len(little)) for spec in whole[4 * which : 4 * which + 3]],
        compiler_params=pltpu.CompilerParams(
            dimension_semantics=("arbitrary",), vmem_limit_bytes=48 * MIB
        ),
        cost_estimate=pl.CostEstimate(
            flops=24 * count * BLK * BLK * BLK, bytes_accessed=16 * MIB, transcendentals=0
        ),
        name="update",
    )(
        fixes,
        sums,
        tiles,
        turned,
        bases,
        tile_one,
        tile_two,
        *[x for group in little for x in group],
    )


def total_over(x, axis):
    out = x
    for off in range(1, lax.axis_size(axis)):
        out = out + swap(x, axis, off)
    return out


def shards(
    token_ids,
    labels,
    seq_lengths,
    micro_batch,
    step_count,
    block_slot,
    vocab_table,
    vocab_first,
    vocab_second,
    layer_blocks,
    block_bases,
    block_first,
    block_second,
    side_proj,
    side_first,
    side_second,
    shared_params,
    shared_first,
    shared_second,
    channel_params,
    channel_first,
    channel_second,
    head_params,
    head_first,
    head_second,
):
    nt = lax.axis_size("tensor")
    nd = lax.axis_size("dp")
    shard = lax.axis_index("tensor")
    place = lax.axis_index("dp")
    seqs = token_ids.shape[0]
    length = token_ids.shape[1] * nd
    chunks = nd // seqs
    rows = seqs * length // nd
    own = rows // nt
    vrows = vocab_table.shape[0]
    padded = -(-vrows // PAIRS) * PAIRS
    half = nd // 2
    inner = channel_params.shape[2]
    heads = head_params.shape[2]
    tiles = block_slot.shape[1]
    zx_count = D * 2 * inner // (BLK * BLK)
    per_layer = 3 * D * inner // (BLK * BLK)
    stride = D + 10 * N
    both = ("dp", "tensor")
    side_rows = side_proj.shape[1]
    share_size = shared_params.shape[0]
    share_pad = -(-share_size // 2048) * 2048

    piece = jnp.concatenate(
        [
            jnp.pad(side_proj.astype(BF), ((0, 0), (0, 0), (0, LANES - H))).reshape(-1, LANES),
            jnp.pad(shared_params.astype(BF), (0, share_pad - share_size)).reshape(-1, LANES),
        ],
        axis=0,
    )
    piece_rows = piece.shape[0]
    side_part = piece_rows - share_pad // LANES
    ids = jnp.pad(jnp.concatenate([token_ids, labels], axis=0), ((0, 8 - 2 * seqs), (0, 0)))
    ids_all, pieces = open_exchange(ids, piece, nd, nt)
    ids_all = ids_all.transpose(1, 0, 2).reshape(8, length)
    all_ids = ids_all[:seqs].reshape(-1)
    local_row = all_ids // 2 - shard * vrows
    held = (local_row >= 0) & (local_row < vrows) & (all_ids % 2 == place // half)
    scal = jnp.stack([place, shard]).astype(jnp.int32)
    scal_shard = shard.astype(jnp.int32).reshape(1)
    code = jnp.concatenate([jnp.where(held, local_row, 0), jnp.zeros((8,), jnp.int32)])
    listed, count = list_held(held, nd * rows)
    own_tiles = layer_blocks.shape[2]
    gathered = lax.all_gather(
        jnp.concatenate(
            [layer_blocks.astype(BF).reshape(own_tiles * BLK, BLK), pieces.reshape(-1, LANES)], axis=0
        ),
        "dp",
        axis=0,
        tiled=False,
    )
    parts = gather_rows(scal, code, listed, count, vocab_table, nd, rows)
    table_now, parts = lax.optimization_barrier((vocab_table, parts))
    parts = [parts[0]] + [swap(parts[off], "dp", off) for off in range(1, nd)]
    table_low = jnp.pad(table_now.astype(BF), ((0, padded - vrows), (0, 0)))
    placed = place_tiles(block_slot, gathered, own_tiles, inner, zx_count, per_layer)
    small = gathered[:, own_tiles * BLK :].reshape(nd, nt, piece_rows, LANES)
    side_full = (
        small[:, :, :side_part]
        .reshape(nd, nt, L, side_rows, 2 * N + LANES)
        .transpose(2, 0, 1, 3, 4)
        .reshape(L, D, 2 * N + LANES)
    )
    shared_full = small[:, :, side_part:].reshape(nd * nt, share_pad)[:, :share_size].reshape(-1)
    shared_full = shared_full.astype(F32)

    parts = join_parts(scal, parts, nt, own)
    table_all = lax.all_gather(table_low, "dp", axis=1, tiled=True)

    def layer_mats(layer_index):
        zx_part, out_part = placed[2 * layer_index], placed[2 * layer_index + 1]
        dt_part = lax.dynamic_slice_in_dim(
            side_full[layer_index], 2 * N + shard * heads, heads, 1
        )
        side_here = jnp.concatenate(
            [
                side_full[layer_index][:, : 2 * N],
                jnp.pad(dt_part, ((0, 0), (0, LANES - heads))),
            ],
            axis=1,
        )
        base = layer_index * stride
        gain = shared_full[base : base + D]
        taps = shared_full[base + D : base + D + 8 * N].reshape(4, 2 * N)
        bias = shared_full[base + D + 8 * N : base + stride].reshape(1, 2 * N)
        bcp = jnp.concatenate([taps, bias, jnp.zeros((3, 2 * N), F32)], axis=0)
        chan = jnp.pad(channel_params[layer_index], ((0, 2), (0, 0)))
        head = jnp.pad(head_params[layer_index], ((0, 5), (0, LANES - heads)))
        return (zx_part, out_part, side_here, gain, bcp, chan, head)

    def spread(x):
        return [x] + [swap(x, "tensor", off) for off in range(1, nt)]

    def rim_pairs(to):
        return [
            (k * nt + nt - 1, (k + 1) * nt + to) for k in range(nd) if k % chunks + 1 < chunks
        ]

    def hop(x, distance):
        pairs = [
            (k, k + distance)
            for k in range(nd)
            if 0 <= k % chunks + distance < chunks
        ]
        return lax.ppermute(x, "dp", pairs)

    def returned(parts):
        return [parts[0]] + [swap(parts[off], "tensor", off) for off in range(1, nt)]

    hops = range(1, chunks)
    mats = [layer_mats(layer_index) for layer_index in range(L)]
    final_gain = shared_full[L * stride :][None, :]
    gains = [mats[layer_index][3][None, :] for layer_index in range(L)] + [final_gain]
    saved = []
    residual, normed_own = enter(returned(parts), gains[0])
    for layer_index in range(L):
        wzx, wout, wside, gain, bcp, chan, head = mats[layer_index]
        edge = normed_own[own - RIM :]
        rims = [lax.ppermute(edge, both, rim_pairs(to)) for to in range(nt)]
        normed, zx, side, yloc, final, c_out, cum = mixer_front(
            scal_shard, spread(normed_own), rims, wzx, wside, chan, bcp, head
        )
        states = [hop(final, k) for k in hops]
        result = mixer_middle(scal_shard, states, yloc, zx, c_out, cum, wout, chan, nt)
        y, s_in = result[:2]
        before = residual
        residual, branch, factor, normed_own = join_residual(
            returned(result[2:]), before, gains[layer_index + 1]
        )
        saved.append((before, normed, zx, side, c_out, cum, y, s_in, factor, branch))
    final_rows = spread(normed_own)

    member = micro_batch[:, None] == jnp.arange(MB, dtype=jnp.int32)[None, :]
    batch_tokens = jnp.sum(jnp.where(member, seq_lengths[:, None], 0), axis=0).astype(F32)
    seq_weight = 1.0 / (MB * jnp.sum(jnp.where(member, batch_tokens[None, :], 0.0), axis=1))
    block_order = shard ^ jnp.arange(nt, dtype=jnp.int32)
    row_at = (
        place * rows + block_order[:, None] * own + jnp.arange(own, dtype=jnp.int32)[None, :]
    ).reshape(rows)
    my_seq = place // chunks
    weight = jnp.where(row_at % length < seq_lengths[my_seq], seq_weight[my_seq], 0.0)
    all_labels = ids_all[seqs : 2 * seqs].reshape(-1)
    label = (all_labels[row_at] - 2 * shard * vrows).reshape(1, rows)

    p_low, tops, stats = vocab_logits(label, table_all, final_rows, vrows)
    stats = stats.reshape(8, nt, own)
    merged = (stats[0], stats[1], stats[2], stats[3])
    others = [swap(stats, "tensor", off) for off in range(1, nt)]
    best = stats[0]
    for off in range(1, nt):
        best = jnp.maximum(best, jnp.stack([others[off - 1][0, o ^ off] for o in range(nt)]))
    summed = stats[1] * jnp.exp(stats[0] - best)
    target = stats[2]
    plain = stats[3]
    for off in range(1, nt):
        them = jnp.stack([others[off - 1][:, o ^ off] for o in range(nt)], axis=1)
        summed = summed + them[1] * jnp.exp(them[0] - best)
        target = target + them[2]
        plain = plain + them[3]
    log_total = best + jnp.log(summed)
    token_loss = (
        log_total
        - (1.0 - SMOOTHING) * target
        - SMOOTHING / V * plain
        + ZLOSS_WEIGHT * log_total * log_total
    )
    loss_here = jnp.sum(weight[:own] * token_loss[0])
    seq_part = jnp.where(
        (iota((8, LANES), 0) == 0) & (iota((8, LANES), 1) == my_seq), loss_here, 0.0
    )
    soft = (weight.reshape(nt, own) * (1.0 + 2.0 * ZLOSS_WEIGHT * log_total)).reshape(1, 1, rows)
    scale = soft * jnp.exp(tops - log_total.reshape(1, 1, rows))
    row_weight = weight.reshape(1, rows)
    sent = returned(vocab_rows(label, scale, row_weight, p_low, table_all, nt))
    table_grad = vocab_table_grad(label, scale, row_weight, p_low, final_rows)
    sent, table_grad = lax.optimization_barrier((sent, table_grad))
    table_share = lax.psum_scatter(table_grad, "dp", scatter_dimension=1, tiled=True)
    grad_res, payload, grad_final_gain = back_rows(
        sent, [], residual, final_gain, None, (saved[L - 1][9], saved[L - 1][8])
    )

    block_pieces = [None] * (2 * L)
    side_pieces = [None] * L
    channel_pieces = [None] * L
    head_pieces = [None] * L
    shared_pieces = [None] * L
    for layer_index in reversed(range(L)):
        wzx, wout, wside, gain, bcp, chan, head = mats[layer_index]
        residual_in, normed, zx, side, c_out, cum, y, s_in, factor, branch = saved[layer_index]
        grads, u_low, dy, dz, dstate, gain_grad = gate_back(
            scal_shard, spread(payload), wout, y, zx, c_out, cum, chan
        )
        states = [hop(dstate, -k) for k in hops]
        grad_out_w = tn(u_low, grads)
        inside = mixer_within(s_in, zx, side, dy, chan, bcp, head)
        result = mixer_back(
            scal_shard,
            states,
            inside,
            zx,
            side,
            dy,
            dz,
            y,
            wzx,
            wside,
            chan,
            bcp,
            head,
            normed,
            gains[layer_index],
            nt,
        )
        dzx, dside, chan_grad, bcp_grad, head_grad, rim_grad, grad_gain_in = result[:7]
        parts_out = result[7:]
        grad_zx_w = tn(normed, dzx)
        grad_side_w = tn(normed, dside)
        block_pieces[2 * layer_index] = grad_zx_w.astype(BF)
        block_pieces[2 * layer_index + 1] = grad_out_w.astype(BF)
        side_pieces[layer_index] = grad_side_w
        shared_pieces[layer_index] = jnp.concatenate(
            [grad_gain_in[0], bcp_grad[:4].reshape(-1), bcp_grad[4]]
        )
        channel_pieces[layer_index] = jnp.concatenate([chan_grad[:5], gain_grad], axis=0)
        head_pieces[layer_index] = head_grad[:3, :heads]
        if layer_index == 0:
            shared_grads = jnp.concatenate(shared_pieces + [grad_final_gain[0]]).astype(BF)
            shared_grads = jnp.pad(
                shared_grads.reshape(nd * nt, share_size), ((0, 0), (0, share_pad - share_size))
            ).reshape(nd, nt * share_pad // LANES, LANES)
            lines = jnp.concatenate(
                [
                    jnp.stack(channel_pieces).reshape(-1, LANES),
                    jnp.pad(jnp.stack(head_pieces).reshape(-1), (0, LANES - L * 3 * heads)).reshape(
                        1, LANES
                    ),
                ],
                axis=0,
            ).astype(BF)
            line_count = lines.shape[0]
            line_rows = -(-line_count // RIM) * RIM
            lines = jnp.pad(lines, ((0, line_rows - line_count), (0, 0)))
            tile_grads = pack_tiles(
                scal_shard,
                block_slot,
                block_pieces,
                side_pieces,
                shared_grads,
                lines,
                own_tiles,
                per_layer,
                nt,
                heads,
            )
            tile_grads, table_share, parts_out, rim_grad = lax.optimization_barrier(
                (tile_grads, table_share, parts_out, rim_grad)
            )
            block_share = lax.psum_scatter(tile_grads, "dp", scatter_dimension=0, tiled=True)[0]
        if layer_index:
            rims = [
                lax.ppermute(rim_grad, both, [(b, a) for a, b in rim_pairs(to)]) for to in range(nt)
            ]
            grad_res, payload, _ = back_rows(
                returned(parts_out),
                rims,
                residual_in,
                gains[layer_index],
                grad_res,
                (saved[layer_index - 1][9], saved[layer_index - 1][8]),
            )
        else:
            embed = finish_rows(
                parts_out, rim_grad, residual_in, gains[0], grad_res, nd, chunks
            )

    side_count = nt * side_part
    small_share = jnp.concatenate(
        [
            block_share[own_tiles * BLK : own_tiles * BLK + side_count].reshape(nt, side_part, LANES),
            block_share[own_tiles * BLK + side_count : own_tiles * BLK + nt * piece_rows].reshape(
                nt, piece_rows - side_part, LANES
            ),
        ],
        axis=1,
    )
    mine = jnp.zeros((piece_rows, LANES), F32)
    for off in range(nt):
        piece = lax.dynamic_index_in_dim(small_share, shard ^ off, 0, False)
        mine = mine + (piece if off == 0 else swap(piece, "tensor", off)).astype(F32)
    side_share = (
        mine[:side_part]
        .reshape(L, 2 * N // LANES + 1, side_rows, LANES)
        .transpose(0, 2, 1, 3)
        .reshape(L * side_rows, 2 * N + LANES)[:, : 2 * N + H]
    )
    shared_share = mine[side_part:].reshape(1, -1)[:, :share_size]
    lines = block_share[own_tiles * BLK + nt * piece_rows :].astype(F32)
    channel_sum = lines[: line_count - 1].reshape(L * 6, inner)
    head_sum = lines[line_count - 1, : L * 3 * heads].reshape(L * 3, heads)
    rotated, tile_root = turn_tiles(block_share, block_bases.reshape(own_tiles, 2, BLK, BLK))
    grad_table, table_root = add_rows(scal, code, listed, count, table_share, embed, vrows)
    sums = sum_everywhere(
        seq_part,
        [channel_sum, head_sum],
        [table_root, tile_root, side_share, shared_share],
        nd,
        nt,
    )
    seq_loss = sums[0, :seqs]
    clip_norm = sums[1, 0]
    steps_done = step_count[0].astype(F32)
    fix_one = 1.0 - jnp.power(BETA_FIRST, steps_done)
    fix_two = 1.0 - jnp.power(BETA_SECOND, steps_done)
    tile_shape = layer_blocks.shape[2:]
    flat = lambda x: x.reshape((-1, x.shape[-1]))
    little = [
        [flat(side_proj), side_share, flat(side_first), flat(side_second)],
        [flat(shared_params), shared_share, flat(shared_first), flat(shared_second)],
        [flat(channel_params), channel_sum, flat(channel_first), flat(channel_second)],
        [flat(head_params), head_sum, flat(head_first), flat(head_second)],
    ]
    updated = last_update(
        jnp.stack([fix_one, fix_two]),
        sums,
        layer_blocks.reshape(tile_shape),
        rotated,
        block_bases.reshape((own_tiles, 2, BLK, BLK)),
        block_first.reshape(tile_shape),
        block_second.reshape(tile_shape),
        little,
    )
    table_out = adam_update(
        vocab_table,
        grad_table.astype(F32),
        vocab_first,
        vocab_second,
        sums[2, 0],
        fix_one,
        fix_two,
        WEIGHT_DECAY,
    )
    block_out = [x.reshape(layer_blocks.shape) for x in updated[:4]]
    like = [side_proj] * 3 + [shared_params] * 3 + [channel_params] * 3 + [head_params] * 3
    small_out = [x.reshape(y.shape) for x, y in zip(updated[4:], like)]
    return (
        seq_loss,
        clip_norm,
        table_out[0],
        table_out[1],
        table_out[2],
        block_out[0],
        block_out[1],
        block_out[2],
        block_out[3],
        *small_out,
    )


def solution(mesh):
    table = P("tensor", "dp")
    block = P("dp", "tensor", None, None, None)
    side = P(None, ("dp", "tensor"), None)
    shared = P(("dp", "tensor"))
    channel = P(None, None, "tensor")
    in_specs = (
        P(None, "dp"),
        P(None, "dp"),
        P(),
        P(),
        P(),
        P("tensor", None),
        *[table] * 3,
        block,
        P("dp", "tensor", None, None, None, None),
        block,
        block,
        *[side] * 3,
        *[shared] * 3,
        *[channel] * 6,
    )
    out_specs = (
        P(),
        P(),
        *[table] * 3,
        *[block] * 4,
        *[side] * 3,
        *[shared] * 3,
        *[channel] * 6,
    )
    return jax.shard_map(shards, mesh=mesh, in_specs=in_specs, out_specs=out_specs, check_vma=False)
```

```python
import functools

import jax
import jax.numpy as jnp
from jax import lax
from jax.experimental import pallas as pl
from jax.experimental.pallas import tpu as pltpu
from jax.sharding import PartitionSpec as P

D = 1024
DI = 2048
H = 32
P_SIZE = 64
N = 128
V = 50288
SPAN = 256
L = 2
MB = 2
BLK = 128
RIM = 16
PAIRS = 1280
PART = 320
LANES = 128

HIGHEST = lax.Precision.HIGHEST
NORM_EPS = 1e-05
SMOOTHING = 0.1
ZLOSS_WEIGHT = 0.005
CLIP_LIMIT = 0.02
BETA_FIRST = 0.9
BETA_SECOND = 0.95
ADAM_EPS = 1e-08
LEARN_RATE = 0.03
WEIGHT_DECAY = 0.01

BF = jnp.bfloat16
F32 = jnp.float32
MIB = 1 << 20


def nn(a, b, precision=None):
    return lax.dot_general(
        a, b, (((1,), (0,)), ((), ())), precision=precision, preferred_element_type=F32
    )


def nt_dot(a, b, precision=None):
    return lax.dot_general(
        a, b, (((1,), (1,)), ((), ())), precision=precision, preferred_element_type=F32
    )


def tn(a, b, precision=None):
    return lax.dot_general(
        a, b, (((0,), (0,)), ((), ())), precision=precision, preferred_element_type=F32
    )


def iota(shape, dim):
    return lax.broadcasted_iota(jnp.int32, shape, dim)


def head_map(inner):
    return (iota((LANES, inner), 0) == iota((LANES, inner), 1) // P_SIZE).astype(F32).astype(BF)


def swap(x, axis, offset):
    size = lax.axis_size(axis)
    return lax.ppermute(x, axis, [(i, i ^ offset) for i in range(size)])


def halves(x):
    high = x.astype(BF)
    return high, (x - high.astype(F32)).astype(BF)


def thirds(x):
    high = x.astype(BF)
    rest = x - high.astype(F32)
    mid = rest.astype(BF)
    return high, mid, (rest - mid.astype(F32)).astype(BF)


def widen(x, expand):
    high, low = halves(x)
    twice = jnp.concatenate([expand, expand], axis=0)
    return nn(jnp.concatenate([high, low], axis=1), twice)


def narrow(x, expand):
    high, low = halves(x)
    return nt_dot(high, expand) + nt_dot(low, expand)


def tri_sum(tri, x):
    wide = nn(tri, jnp.concatenate(thirds(x), axis=1))
    size = x.shape[1]
    return wide[:, :size] + wide[:, size : 2 * size] + wide[:, 2 * size :]


def lanes3(column):
    high, mid, low = thirds(column)
    lane = iota((column.shape[0], LANES), 1)
    zero = jnp.zeros((column.shape[0], LANES), F32)
    wide = jnp.where(lane == 0, high.astype(F32), zero)
    wide = jnp.where(lane == 1, mid.astype(F32), wide)
    return jnp.where(lane == 2, low.astype(F32), wide).astype(BF)


def column3(wide):
    return wide[:, 0:1] + wide[:, 1:2] + wide[:, 2:3]


def rows3(line, inner):
    high, mid, low = thirds(line)
    at = iota((RIM, LANES), 0)
    wide = jnp.where(at == 0, high.astype(F32), 0.0)
    wide = jnp.where(at == 1, mid.astype(F32), wide)
    wide = jnp.where(at == 2, low.astype(F32), wide)
    if inner > LANES:
        wide = jnp.concatenate([wide, jnp.zeros((RIM, inner - LANES), F32)], axis=1)
    return wide.astype(BF)


def sigmoid(x):
    return 1.0 / (1.0 + jnp.exp(-x))


def softplus(x):
    return jnp.maximum(x, 0.0) + jnp.log1p(jnp.exp(-jnp.abs(x)))


def call(kernel, name, out_shape, args, smem=(), scratch=(), mib=60, flops=0, moved=0, **extra):
    specs = [
        pl.BlockSpec(memory_space=pltpu.SMEM if i in smem else pltpu.VMEM)
        for i in range(len(args))
    ]
    return pl.pallas_call(
        kernel,
        out_shape=out_shape,
        in_specs=specs,
        out_specs=jax.tree.map(lambda _: pl.BlockSpec(memory_space=pltpu.VMEM), out_shape),
        scratch_shapes=list(scratch),
        compiler_params=pltpu.CompilerParams(vmem_limit_bytes=mib * MIB),
        cost_estimate=pl.CostEstimate(flops=flops, bytes_accessed=moved, transcendentals=0),
        name=name,
        **extra,
    )(*args)


def sds(shape, dtype):
    return jax.ShapeDtypeStruct(shape, dtype)


def list_held(held, total):
    runs = held.reshape(-1, LANES)
    upper = iota((LANES, LANES), 0) <= iota((LANES, LANES), 1)
    rank = nn(runs.astype(BF), upper.astype(BF)).astype(jnp.int32) - 1
    here = (rank[:, :, None] == iota((1, 1, LANES), 2)) & runs[:, :, None]
    at = jnp.sum(jnp.where(here, iota((1, LANES, 1), 1), 0), axis=1)
    counts = rank[:, -1] + 1
    first = iota(at.shape, 0) * LANES
    listed = jnp.where(iota(at.shape, 1) < counts[:, None], at + first, total)
    return listed.reshape(-1), counts


def over_listed(listed, count, body):
    def run(at_run, carry):
        def turn(step, inner_carry):
            for lane in range(8):
                body(listed[at_run * LANES + step * 8 + lane])
            return inner_carry

        lax.fori_loop(0, (count[at_run] + 7) // 8, turn, 0)
        return carry

    lax.fori_loop(0, count.shape[0], run, 0)


def look_kernel(groups, rows, scal, code, listed, count, table, *rest):
    outs, work = rest[:groups], rest[groups]
    place = scal[0]

    def fill(step, carry):
        work[pl.ds(pl.multiple_of(step * rows, rows), rows), :] = jnp.zeros((rows, table.shape[1]), F32)
        return carry

    lax.fori_loop(0, groups, fill, 0)

    def take(at):
        work[pl.ds(at, 1), :] = table[pl.ds(code[at], 1), :]

    over_listed(listed, count, take)
    for off in range(groups):
        base = pl.multiple_of((place ^ off) * rows, rows)
        outs[off][...] = work[pl.ds(base, rows), :].astype(BF)


def gather_rows(scal, code, listed, count, table, groups, rows):
    cols = table.shape[1]
    return call(
        functools.partial(look_kernel, groups, rows),
        "look",
        [sds((rows, cols), BF)] * groups,
        (scal, code, listed, count, table),
        smem=(0, 1, 2, 3),
        scratch=[pltpu.VMEM((groups * rows + 8, cols), F32)],
        moved=30 * MIB,
    )


def join_kernel(groups, shards, own, scal, *rest):
    parts, outs, work = rest[:groups], rest[groups : groups + shards], rest[-1]
    place, shard = scal[0], scal[1]
    half = groups // 2
    cols = parts[0].shape[1]
    for off in range(half):
        at = ((place ^ off) % half) * cols
        work[:, pl.ds(pl.multiple_of(at, cols), cols)] = parts[off][...] + parts[off + half][...]
    for off in range(shards):
        at = pl.multiple_of((shard ^ off) * own, own)
        outs[off][...] = work[pl.ds(at, own), :]


def join_parts(scal, parts, shards, own):
    rows = parts[0].shape[0]
    return call(
        functools.partial(join_kernel, len(parts), shards, own),
        "join",
        [sds((own, D), BF)] * shards,
        (scal, *parts),
        smem=(0,),
        scratch=[pltpu.VMEM((rows, D), BF)],
        moved=4 * MIB,
    )


def add_kernel(groups, rows, vrows, scal, code, listed, count, share, parts, *rest):
    out, square, work, bins = rest
    place = scal[0]
    bins[...] = share[0:vrows, :].astype(F32)
    for off in range(groups):
        base = pl.multiple_of((place ^ off) * rows, rows)
        work[pl.ds(base, rows), :] = parts[off].astype(F32)
    work[groups * rows :, :] = jnp.zeros((8, work.shape[1]), F32)

    def add(at):
        to = pl.ds(code[at], 1)
        bins[to, :] = bins[to, :] + work[pl.ds(at, 1), :]

    over_listed(listed, count, add)
    total = bins[...]
    out[...] = total.astype(BF)
    square[...] = jnp.sqrt(jnp.sum(total * total, axis=0, keepdims=True))


def add_rows(scal, code, listed, count, share, parts, vrows):
    cols = share.shape[1]
    groups, rows, _ = parts.shape
    return call(
        functools.partial(add_kernel, groups, rows, vrows),
        "addrows",
        [sds((vrows, cols), BF), sds((1, cols), F32)],
        (scal, code, listed, count, share, parts),
        smem=(0, 1, 2, 3),
        scratch=[pltpu.VMEM((rows * groups + 8, cols), F32), pltpu.VMEM((vrows, cols), F32)],
        moved=30 * MIB,
    )


def tiles_kernel(slots_each, zx_count, per_layer, layers, slot, tiles, *outs):
    for layer in range(layers):
        for at in range(per_layer):
            where = slot[0, layer * per_layer + at]
            owner = where // slots_each
            first = pl.multiple_of((where % slots_each) * BLK, BLK)
            tile = tiles[owner, pl.ds(first, BLK), :]
            if at < zx_count:
                wide = outs[2 * layer].shape[1] // BLK
                row, col = at // wide, at % wide
                out = outs[2 * layer]
            else:
                wide = D // BLK
                row, col = (at - zx_count) // wide, (at - zx_count) % wide
                out = outs[2 * layer + 1]
            out[row * BLK : (row + 1) * BLK, col * BLK : (col + 1) * BLK] = tile


def place_tiles(slot, tiles, slots_each, inner, zx_count, per_layer):
    return call(
        functools.partial(tiles_kernel, slots_each, zx_count, per_layer, L),
        "placetiles",
        [sds((D, 2 * inner), BF), sds((inner, D), BF)] * L,
        (slot, tiles),
        smem=(0,),
        moved=14 * MIB,
    )


def pack_kernel(slots_each, per_layer, layers, shards, heads, scal, slot, *refs):
    mats, sides, refs = refs[: 2 * layers], refs[2 * layers : 3 * layers], refs[3 * layers :]
    shared, lines, out, work = refs
    for layer in range(layers):
        zx, wout = mats[2 * layer], mats[2 * layer + 1]
        zx_wide, out_wide = zx.shape[1] // BLK, D // BLK
        zx_count = zx.shape[0] // BLK * zx_wide
        for at in range(per_layer):
            where = slot[0, layer * per_layer + at]
            if at < zx_count:
                source, row, col = zx, at // zx_wide, at % zx_wide
            else:
                source = wout
                row, col = (at - zx_count) // out_wide, (at - zx_count) % out_wide
            first = pl.multiple_of((where % slots_each) * BLK, BLK)
            out[where // slots_each, pl.ds(first, BLK), :] = source[
                row * BLK : (row + 1) * BLK, col * BLK : (col + 1) * BLK
            ]
        work[layer, :, : 2 * N] = sides[layer][:, : 2 * N]
        work[layer, :, 2 * N :] = pltpu.roll(sides[layer][:, 2 * N :], scal[0] * heads, 1)
    groups = out.shape[0]
    each = work.shape[1] // (groups * shards)
    piece = layers * each * work.shape[2] // LANES
    base = slots_each * BLK
    for group in range(groups):
        for shard in range(shards):
            first = (group * shards + shard) * each
            blocks = [
                work[layer, first : first + each, col : col + LANES]
                for layer in range(layers)
                for col in range(0, work.shape[2], LANES)
            ]
            at = base + shard * piece
            out[group, at : at + piece, :] = jnp.concatenate(blocks, axis=0).astype(BF)
    base += shards * piece
    out[:, base : base + shared.shape[1], :] = shared[...]
    for group in range(groups):
        out[group, base + shared.shape[1] :, :] = lines[...]


def pack_tiles(scal, slot, mats, sides, shared, lines, slots_each, per_layer, shards, heads):
    groups = shared.shape[0]
    layers = len(sides)
    depth, width = sides[0].shape
    extra = layers * depth * width // (groups * LANES) + shared.shape[1] + lines.shape[0]
    return call(
        functools.partial(pack_kernel, slots_each, per_layer, layers, shards, heads),
        "packtiles",
        sds((groups, slots_each * BLK + extra, LANES), BF),
        (scal, slot, *mats, *sides, shared, lines),
        smem=(0, 1),
        scratch=[pltpu.VMEM((layers, depth, width), F32)],
        moved=14 * MIB,
    )


def norm_rows(values, gain):
    return values * lax.rsqrt(jnp.mean(values * values, axis=-1, keepdims=True) + NORM_EPS) * gain


def total_of(parts):
    total = parts[0][...].astype(F32)
    for part in parts[1:]:
        total = total + part[...].astype(F32)
    return total


def send(source, target, send_sem, recv_sem, device):
    copy = pltpu.make_async_remote_copy(
        src_ref=source,
        dst_ref=target,
        send_sem=send_sem,
        recv_sem=recv_sem,
        device_id=device,
        device_id_type=pl.DeviceIdType.MESH,
    )
    copy.start()
    return copy


def greet_shards(groups, shards, rims):
    place, shard = lax.axis_index("dp"), lax.axis_index("tensor")
    last = shard == shards - 1
    barrier = pltpu.get_barrier_semaphore()

    def greet(device):
        pl.semaphore_signal(barrier, inc=1, device_id=device, device_id_type=pl.DeviceIdType.MESH)

    for off in range(1, shards):
        greet((place, shard ^ off))
    if not rims:
        pl.semaphore_wait(barrier, shards - 1)
        return
    greet((lax.rem(place + groups - 1, groups), shards - 1))

    @pl.when(last)
    def _():
        for other in range(shards):
            greet((lax.rem(place + 1, groups), other))

    pl.semaphore_wait(barrier, shards - 1 + jnp.where(last, shards + 1, 1))


def pass_along(rows, own, base, shards, sems):
    place, shard = lax.axis_index("dp"), lax.axis_index("tensor")

    def copy(way, hop, source, to):
        at = pl.ds(pl.multiple_of(base + source * own, RIM), own)
        return pltpu.make_async_remote_copy(
            src_ref=rows.at[at, :],
            dst_ref=rows.at[at, :],
            send_sem=sems.at[0, way, hop],
            recv_sem=sems.at[1, way, hop],
            device_id=(place, to),
            device_id_type=pl.DeviceIdType.MESH,
        )

    def up(hop):
        return copy(0, hop, shard - hop, shard + 1)

    def down(hop):
        return copy(1, hop, shard + hop, shard - 1)

    can_up, can_down = shard + 1 < shards, shard > 0
    for hop in range(shards):
        if hop > 0:

            @pl.when(shard - hop >= 0)
            def _():
                copy(0, hop - 1, shard - hop, shard - 1).wait_recv()

        if hop < shards - 1:

            @pl.when(jnp.logical_and(shard - hop >= 0, can_up))
            def _():
                up(hop).start()

        if hop > 0:

            @pl.when(shard + hop < shards)
            def _():
                copy(1, hop - 1, shard + hop, shard + 1).wait_recv()

        if hop < shards - 1:

            @pl.when(jnp.logical_and(shard + hop < shards, can_down))
            def _():
                down(hop).start()

    for hop in range(shards - 1):

        @pl.when(jnp.logical_and(shard - hop >= 0, can_up))
        def _():
            up(hop).wait_send()

        @pl.when(jnp.logical_and(shard + hop < shards, can_down))
        def _():
            down(hop).wait_send()


def exchange_terms(parts, slots, work, sems):
    place, shard = lax.axis_index("dp"), lax.axis_index("tensor")
    shards = len(parts)

    def copy(off, source, to, slot):
        return pltpu.make_async_remote_copy(
            src_ref=source,
            dst_ref=slots.at[slot],
            send_sem=sems.at[0, off],
            recv_sem=sems.at[1, slot],
            device_id=(place, to),
            device_id_type=pl.DeviceIdType.MESH,
        )

    def direct(off):
        return copy(off, parts[off], shard ^ off, off)

    if shards != 4:
        for off in range(1, shards):
            direct(off).start()
        for off in range(1, shards):
            direct(off).wait()
        total = parts[0][...].astype(F32)
        for off in range(1, shards):
            total = total + slots[off].astype(F32)
        work[...] = total
        return
    relay, added = 0, 4
    outer = jnp.logical_or(shard == 0, shard == shards - 1)
    inner = jnp.logical_not(outer)

    @pl.when(outer)
    def _():
        copy(3, parts[3], shard ^ 1, relay).start()
        direct(2).start()
        direct(1).start()

    @pl.when(inner)
    def _():
        direct(3).start()
        direct(1).start()
        copy(0, parts[3], shard ^ 1, relay).wait_recv()
        slots[added] = (slots[relay].astype(F32) + parts[2][...].astype(F32)).astype(BF)
        copy(2, slots.at[added], shard ^ 2, 2).start()

    direct(1).wait_recv()
    total = parts[0][...].astype(F32) + slots[1].astype(F32)
    direct(2).wait_recv()
    work[...] = total + slots[2].astype(F32)

    @pl.when(inner)
    def _():
        direct(3).wait_recv()
        work[...] += slots[3].astype(F32)

    for off in range(1, shards):
        direct(off).wait_send()


def term_scratch(shards, own, width):
    return [
        pltpu.VMEM((shards + 1, own, width), BF),
        pltpu.VMEM((own, width), F32),
        pltpu.SemaphoreType.DMA((2, shards + 1)),
    ]


def forward_kernel(groups, shards, chunks, packed, rims, *refs):
    parts, refs = refs[:shards], refs[shards:]
    if packed:
        before, gain, residual, branch, factor, normed, *refs = refs
    else:
        gain, residual, normed, *refs = refs
    slots, work, term_sems, row_sems, rim_sems = refs
    own = parts[0].shape[0]
    rows = own * shards
    place, shard = lax.axis_index("dp"), lax.axis_index("tensor")
    chunk = lax.rem(place, chunks)
    greet_shards(groups, shards, rims)
    exchange_terms(parts, slots, work, term_sems)
    total = work[...]
    if packed:
        scale = lax.rsqrt(column3(total[:, D:]) / DI + NORM_EPS)
        branch[...] = total[:, :D]
        factor[...] = scale
        total = before[...] + scale * total[:, :D]
    residual[...] = total
    at = pl.ds(pl.multiple_of(RIM + shard * own, RIM), own)
    normed[at, :] = norm_rows(total, gain[...]).astype(BF)

    def rim_copy(to, device):
        return pltpu.make_async_remote_copy(
            src_ref=normed.at[rows : rows + RIM, :],
            dst_ref=normed.at[0:RIM, :],
            send_sem=rim_sems.at[0, to],
            recv_sem=rim_sems.at[1, 0],
            device_id=device,
            device_id_type=pl.DeviceIdType.MESH,
        )

    gives = jnp.logical_and(shard == shards - 1, chunk + 1 < chunks)
    if rims:

        @pl.when(gives)
        def _():
            for to in range(shards):
                rim_copy(to, (place + 1, to)).start()

        @pl.when(chunk == 0)
        def _():
            normed[0:RIM, :] = jnp.zeros((RIM, D), BF)

    else:
        normed[0:RIM, :] = jnp.zeros((RIM, D), BF)
    pass_along(normed, own, RIM, shards, row_sems)
    if rims:

        @pl.when(chunk > 0)
        def _():
            rim_copy(0, (place - 1, shards - 1)).wait_recv()

        @pl.when(gives)
        def _():
            for to in range(shards):
                rim_copy(to, (place + 1, to)).wait_send()


def forward_rows(parts, before, gain, groups, chunks, rims, cid):
    shards = len(parts)
    own, width = parts[0].shape
    packed = before is not None
    args = (*parts, before, gain) if packed else (*parts, gain)
    vmem = pl.BlockSpec(memory_space=pltpu.VMEM)
    outs = [sds((own, D), F32)]
    if packed:
        outs += [sds((own, D), F32), sds((own, 1), F32)]
    outs += [sds((RIM + own * shards, D), BF)]
    return pl.pallas_call(
        functools.partial(forward_kernel, groups, shards, chunks, packed, rims),
        out_shape=outs,
        in_specs=[vmem] * len(args),
        out_specs=[vmem] * len(outs),
        scratch_shapes=[
            *term_scratch(shards, own, width),
            pltpu.SemaphoreType.DMA((2, 2, shards)),
            pltpu.SemaphoreType.DMA((2, shards)),
        ],
        compiler_params=pltpu.CompilerParams(
            collective_id=cid, has_side_effects=True, vmem_limit_bytes=32 * MIB
        ),
        name="forward",
    )(*args)


def backward_kernel(groups, shards, chunks, exchanged, *refs):
    parts, refs = refs[:shards], refs[shards:]
    if exchanged:
        residual, gain, branch, factor, grad_out, rows_out, gain_grad, row_sems = refs
    else:
        rim, residual, gain, grad_in, branch, factor, grad_out, rows_out, refs = *refs[:8], refs[8:]
        slots, work, term_sems, from_rims, rim_sems, row_sems = refs
    own = parts[0].shape[0]
    place, shard = lax.axis_index("dp"), lax.axis_index("tensor")
    chunk = lax.rem(place, chunks)
    greet_shards(groups, shards, not exchanged)
    values = residual[...]
    inv = lax.rsqrt(jnp.mean(values * values, axis=-1, keepdims=True) + NORM_EPS)
    if exchanged:
        grad = total_of(parts)
        gain_grad[...] = jnp.sum(grad * values * inv, axis=0, keepdims=True)
    else:

        def rim_copy(slot, device):
            return pltpu.make_async_remote_copy(
                src_ref=rim,
                dst_ref=from_rims.at[slot],
                send_sem=rim_sems.at[0, slot],
                recv_sem=rim_sems.at[1, slot],
                device_id=device,
                device_id_type=pl.DeviceIdType.MESH,
            )

        @pl.when(chunk > 0)
        def _():
            rim_copy(shard, (place - 1, shards - 1)).start()

        exchange_terms(parts, slots, work, term_sems)

        @pl.when(jnp.logical_and(shard == shards - 1, chunk + 1 < chunks))
        def _():
            for other in range(shards):
                rim_copy(other, (place + 1, other)).wait_recv()
            edge = from_rims[0].astype(F32)
            for other in range(1, shards):
                edge = edge + from_rims[other].astype(F32)
            work[own - RIM :, :] += edge

        @pl.when(chunk > 0)
        def _():
            rim_copy(shard, (place - 1, shards - 1)).wait_send()

        grad = work[...]
    scaled = grad * gain[...]
    result = inv * scaled - values * (inv * inv * inv) * jnp.mean(
        scaled * values, axis=-1, keepdims=True
    )
    if not exchanged:
        result = grad_in[...] + result
    grad_out[...] = result
    scale = factor[...]
    at = pl.ds(pl.multiple_of(shard * own, RIM), own)
    rows_out[at, :D] = (scale * result).astype(BF)
    inner_rows = jnp.sum(result * branch[...], axis=-1, keepdims=True)
    rows_out[at, D:] = lanes3(scale * scale * scale * inner_rows / DI)
    pass_along(rows_out, own, 0, shards, row_sems)


def backward_rows(parts, rim, residual, gain, grad_in, branch, factor, groups, chunks, cid):
    shards = len(parts)
    own = residual.shape[0]
    exchanged = rim is None
    vmem = pl.BlockSpec(memory_space=pltpu.VMEM)
    outs = [sds((own, D), F32), sds((own * shards, D + LANES), BF)]
    row_sems = pltpu.SemaphoreType.DMA((2, 2, shards))
    if exchanged:
        args = (*parts, residual, gain, branch, factor)
        outs.append(sds((1, D), F32))
        scratch = [row_sems]
    else:
        args = (*parts, rim, residual, gain, grad_in, branch, factor)
        scratch = [
            *term_scratch(shards, own, D),
            pltpu.VMEM((shards, RIM, D), BF),
            pltpu.SemaphoreType.DMA((2, shards)),
            row_sems,
        ]
    return pl.pallas_call(
        functools.partial(backward_kernel, groups, shards, chunks, exchanged),
        out_shape=outs,
        in_specs=[vmem] * len(args),
        out_specs=[vmem] * len(outs),
        scratch_shapes=scratch,
        compiler_params=pltpu.CompilerParams(
            collective_id=cid, has_side_effects=True, vmem_limit_bytes=32 * MIB
        ),
        name="backward",
    )(*args)


def stats_kernel(shards, chunks, stats, tops, weight, scale_out, loss_out, slots, sems):
    place, shard = lax.axis_index("dp"), lax.axis_index("tensor")
    rows = weight.shape[1]
    own = rows // shards
    greet_shards(0, shards, False)
    copies = [
        send(stats, slots.at[off - 1], sems.at[0, off], sems.at[1, off], (place, shard ^ off))
        for off in range(1, shards)
    ]
    for copy in copies:
        copy.wait()
    others = [stats[...]] + [slots[off] for off in range(shards - 1)]
    best = others[0][0:1, :]
    for one in others[1:]:
        best = jnp.maximum(best, one[0:1, :])
    summed, target, plain = jnp.zeros((1, rows), F32), jnp.zeros((1, rows), F32), jnp.zeros((1, rows), F32)
    for one in others:
        summed = summed + one[1:2, :] * jnp.exp(one[0:1, :] - best)
        target = target + one[2:3, :]
        plain = plain + one[3:4, :]
    log_total = best + jnp.log(summed)
    token_loss = (
        log_total
        - (1.0 - SMOOTHING) * target
        - SMOOTHING / V * plain
        + ZLOSS_WEIGHT * log_total * log_total
    )
    lane = iota((1, rows), 1)
    mine = jnp.logical_and(lane >= shard * own, lane < (shard + 1) * own)
    loss = jnp.sum(jnp.where(mine, weight[...] * token_loss, 0.0), axis=1, keepdims=True)
    here = jnp.logical_and(iota((8, LANES), 0) == 0, iota((8, LANES), 1) == place // chunks)
    loss_out[...] = jnp.where(here, loss, 0.0)
    soft = weight[...] * (1.0 + 2.0 * ZLOSS_WEIGHT * log_total)
    for step in range(tops.shape[0]):
        scale_out[step] = soft * jnp.exp(tops[step] - log_total)


def merge_stats(stats, tops, weight, shards, chunks):
    vmem = pl.BlockSpec(memory_space=pltpu.VMEM)
    return pl.pallas_call(
        functools.partial(stats_kernel, shards, chunks),
        out_shape=[sds(tops.shape, F32), sds((8, LANES), F32)],
        in_specs=[vmem] * 3,
        out_specs=[vmem] * 2,
        scratch_shapes=[
            pltpu.VMEM((shards - 1, *stats.shape), F32),
            pltpu.SemaphoreType.DMA((2, shards)),
        ],
        compiler_params=pltpu.CompilerParams(
            collective_id=9, has_side_effects=True, vmem_limit_bytes=8 * MIB
        ),
        name="stats",
    )(stats, tops, weight)


def finish_kernel(groups, shards, chunks, own, *refs):
    parts, rim, residual, gain, grad_in, out = refs[:shards], *refs[shards : shards + 5]
    slots, work, term_sems, from_rims, payload, full, rim_sems, row_sems, out_sems = refs[shards + 5 :]
    place, shard = lax.axis_index("dp"), lax.axis_index("tensor")
    half = groups // 2
    cols = out.shape[2]
    chunk = lax.rem(place, chunks)
    last = shard == shards - 1
    shard_peers = [(place, shard ^ off) for off in range(1, shards)]
    group_peers = [(place ^ off, shard) for off in range(1, groups)]
    barrier = pltpu.get_barrier_semaphore()

    def greet(device):
        pl.semaphore_signal(barrier, inc=1, device_id=device, device_id_type=pl.DeviceIdType.MESH)

    for peer in shard_peers + group_peers:
        greet(peer)

    @pl.when(jnp.logical_not(last))
    def _():
        greet((lax.rem(place + groups - 1, groups), shards - 1))

    @pl.when(last)
    def _():
        for other in range(shards - 1):
            greet((lax.rem(place + 1, groups), other))

    pl.semaphore_wait(barrier, shards + groups - 2 + jnp.where(last, shards - 1, 1))

    def rim_copy():
        return pltpu.make_async_remote_copy(
            src_ref=rim,
            dst_ref=from_rims.at[shard],
            send_sem=rim_sems.at[0, shard],
            recv_sem=rim_sems.at[1, shard],
            device_id=(place - 1, shards - 1),
            device_id_type=pl.DeviceIdType.MESH,
        )

    @pl.when(chunk > 0)
    def _():
        rim_copy().start()

    values = residual[...]
    inv = lax.rsqrt(jnp.mean(values * values, axis=-1, keepdims=True) + NORM_EPS)
    exchange_terms(parts, slots, work, term_sems)

    @pl.when(jnp.logical_and(chunk + 1 < chunks, last))
    def _():
        for other in range(shards):
            pltpu.make_async_remote_copy(
                src_ref=rim,
                dst_ref=from_rims.at[other],
                send_sem=rim_sems.at[0, other],
                recv_sem=rim_sems.at[1, other],
                device_id=(place + 1, other),
                device_id_type=pl.DeviceIdType.MESH,
            ).wait_recv()
        edge = from_rims[0].astype(F32)
        for other in range(1, shards):
            edge = edge + from_rims[other].astype(F32)
        work[own - RIM :, :] += edge

    @pl.when(chunk > 0)
    def _():
        rim_copy().wait_send()

    scaled = work[...] * gain[...]
    result = (
        grad_in[...]
        + inv * scaled
        - values * (inv * inv * inv) * jnp.mean(scaled * values, axis=-1, keepdims=True)
    ).astype(BF)
    payload[...] = result
    rows_out = [
        send(
            payload,
            full.at[off],
            row_sems.at[0, off],
            row_sems.at[1, off],
            shard_peers[off - 1],
        )
        for off in range(1, shards)
    ]
    full[0] = result

    def first_col(group):
        return pl.multiple_of(lax.rem(group, half) * cols, cols)

    cuts = []
    for off in range(shards):
        if off > 0:
            rows_out[off - 1].wait()
        at = pl.ds(pl.multiple_of((shard ^ off) * own, own), own)
        for other in range(1, groups):
            cuts.append(
                send(
                    full.at[off, :, pl.ds(first_col(place ^ other), cols)],
                    out.at[other, at, :],
                    out_sems.at[0, off, other],
                    out_sems.at[1, off, other],
                    group_peers[other - 1],
                )
            )
        out[0, at, :] = full[off, :, pl.ds(first_col(place), cols)]
    for cut in cuts:
        cut.wait()


def finish_rows(parts, rim, residual, gain, grad_in, groups, chunks):
    shards = len(parts)
    own = parts[0].shape[0]
    vmem = pl.BlockSpec(memory_space=pltpu.VMEM)
    args = (*parts, rim, residual, gain, grad_in)
    return pl.pallas_call(
        functools.partial(finish_kernel, groups, shards, chunks, own),
        out_shape=sds((groups, own * shards, 2 * D // groups), BF),
        in_specs=[vmem] * len(args),
        out_specs=vmem,
        scratch_shapes=[
            *term_scratch(shards, own, D),
            pltpu.VMEM((shards, RIM, D), BF),
            pltpu.VMEM((own, D), BF),
            pltpu.VMEM((shards, own, D), BF),
            pltpu.SemaphoreType.DMA((2, shards)),
            pltpu.SemaphoreType.DMA((2, shards)),
            pltpu.SemaphoreType.DMA((2, shards, groups)),
        ],
        compiler_params=pltpu.CompilerParams(
            collective_id=3, has_side_effects=True, vmem_limit_bytes=32 * MIB
        ),
        name="finish",
    )(*args)


def open_kernel(groups, shards, ids, piece, share, ids_out, pieces_out, share_out, middle, sends, gets):
    place, shard = lax.axis_index("dp"), lax.axis_index("tensor")
    near = [(place, shard ^ off) for off in range(1, shards)]
    far = [(place ^ off, shard) for off in range(1, groups)]
    barrier = pltpu.get_barrier_semaphore()
    for peer in near + far:
        pl.semaphore_signal(barrier, inc=1, device_id=peer, device_id_type=pl.DeviceIdType.MESH)
    pl.semaphore_wait(barrier, len(near) + len(far))
    shares, others = [], []
    for i, peer in enumerate(near):
        shares.append(send(share, middle.at[shard], sends.at[0, i], gets.at[0, i], peer))
    for i, peer in enumerate(far):
        others.append(send(ids, ids_out.at[place], sends.at[1, i], gets.at[1, i], peer))
    for i, peer in enumerate(near):
        others.append(send(piece, pieces_out.at[shard], sends.at[2, i], gets.at[2, i], peer))
    middle[shard] = share[...]
    ids_out[place] = ids[...]
    pieces_out[shard] = piece[...]
    for copy in shares:
        copy.wait()
    for i, peer in enumerate(far):
        others.append(send(middle, share_out.at[place], sends.at[3, i], gets.at[3, i], peer))
    share_out[place] = middle[...]
    for copy in others:
        copy.wait()


def open_exchange(ids, piece, share, groups, shards):
    count = max(groups, shards)
    vmem = pl.BlockSpec(memory_space=pltpu.VMEM)
    return pl.pallas_call(
        functools.partial(open_kernel, groups, shards),
        out_shape=[
            sds((groups, *ids.shape), jnp.int32),
            sds((shards, *piece.shape), BF),
            sds((groups, shards, *share.shape), BF),
        ],
        in_specs=[vmem] * 3,
        out_specs=[vmem] * 3,
        scratch_shapes=[
            pltpu.VMEM((shards, *share.shape), BF),
            pltpu.SemaphoreType.DMA((4, count)),
            pltpu.SemaphoreType.DMA((4, count)),
        ],
        compiler_params=pltpu.CompilerParams(
            collective_id=2, has_side_effects=True, vmem_limit_bytes=8 * MIB
        ),
        name="open",
    )(ids, piece, share)


def sum_kernel(groups, shards, once, split, *refs):
    loss = refs[0]
    refs = refs[1:]
    count = once + split
    ones, many, refs = refs[:once], refs[once:count], refs[count:]
    o_ref, start, mid, from_shards, from_groups, send, recv = refs
    place, shard = lax.axis_index("dp"), lax.axis_index("tensor")
    peers = [(place, shard ^ off) for off in range(1, shards)]
    peers += [(place ^ off, shard) for off in range(1, groups)]
    barrier = pltpu.get_barrier_semaphore()
    for peer in peers:
        pl.semaphore_signal(barrier, inc=1, device_id=peer, device_id_type=pl.DeviceIdType.MESH)

    def square(refs):
        total = jnp.zeros((1, 1), F32)
        for ref in refs:
            flat = jnp.sum(ref[...] * ref[...], axis=0, keepdims=True)
            total = total + jnp.sum(flat, axis=1, keepdims=True)
        return total

    first = (place == 0).astype(F32)
    part = square(many) + first * square(ones)
    start[...] = loss[...] + jnp.where(iota((8, LANES), 1) == LANES - 1, part, 0.0)
    pl.semaphore_wait(barrier, len(peers))

    def exchange(source, slots, first, some):
        copies = []
        for i, peer in enumerate(some):
            copy = pltpu.make_async_remote_copy(
                src_ref=source,
                dst_ref=slots.at[i],
                send_sem=send.at[first + i],
                recv_sem=recv.at[first + i],
                device_id=peer,
                device_id_type=pl.DeviceIdType.MESH,
            )
            copy.start()
            copies.append(copy)
        for copy in copies:
            copy.wait()
        total = source[...]
        for i in range(len(some)):
            total = total + slots[i]
        return total

    mid[...] = exchange(start, from_shards, 0, peers[: shards - 1])
    total = exchange(mid, from_groups, shards - 1, peers[shards - 1 :])
    norm = jnp.sqrt(total[0:1, LANES - 1 : LANES])
    factor = jnp.minimum(1.0, CLIP_LIMIT / (norm + 1e-06))
    row = iota((8, LANES), 0)
    o_ref[...] = jnp.where(row == 0, total, jnp.where(row == 1, norm, factor))


def sum_everywhere(loss, ones, many, groups, shards):
    count = groups + shards - 2
    args = (loss, *ones, *many)
    vmem = pl.BlockSpec(memory_space=pltpu.VMEM)
    return pl.pallas_call(
        functools.partial(sum_kernel, groups, shards, len(ones), len(many)),
        out_shape=sds((8, LANES), F32),
        in_specs=[vmem] * len(args),
        out_specs=vmem,
        scratch_shapes=[
            pltpu.VMEM((8, LANES), F32),
            pltpu.VMEM((8, LANES), F32),
            pltpu.VMEM((shards - 1, 8, LANES), F32),
            pltpu.VMEM((groups - 1, 8, LANES), F32),
            pltpu.SemaphoreType.DMA((count,)),
            pltpu.SemaphoreType.DMA((count,)),
        ],
        compiler_params=pltpu.CompilerParams(
            collective_id=1, has_side_effects=True, vmem_limit_bytes=8 * MIB
        ),
        name="sumall",
    )(*args)


def conv_sum(raw, params, rows, lanes):
    total = params[4:5, :] + params[0:1, :] * raw[pl.ds(RIM - 3, rows), lanes]
    for k in range(1, 4):
        total = total + params[k : k + 1, :] * raw[pl.ds(RIM - 3 + k, rows), lanes]
    return total


def front_kernel(normed, wzx, wside, chan, bcp, head, *rest):
    zx, side, yloc, final, c_out, cum_out, xs_scr = rest
    rows = normed.shape[0] - RIM
    inner = chan.shape[1]
    zx[...] = nn(normed[...], wzx[...])
    side[...] = nn(normed[...], wside[...])
    pre = conv_sum(zx, chan, rows, pl.ds(inner, inner))
    xs_scr[...] = pre * sigmoid(pre)
    pre = conv_sum(side, bcp, rows, pl.ds(0, 2 * N))
    bc = (pre * sigmoid(pre)).astype(BF)
    c_out[...] = bc[:, N:]
    dt = softplus(side[RIM:, 2 * N :] + head[0:1, :])
    rate = -dt * jnp.exp(head[1:2, :])
    expand = head_map(inner)
    skip = widen(head[...], expand)[2:3, :]
    lower = (iota((SPAN, SPAN), 0) >= iota((SPAN, SPAN), 1)).astype(F32)
    lower_low = lower.astype(BF)
    first_half = iota((SPAN, LANES), 1) < P_SIZE
    state = None
    base = jnp.zeros((1, LANES), F32)
    for span in range(rows // SPAN):
        here = slice(span * SPAN, (span + 1) * SPAN)
        cum = tri_sum(lower_low, rate[here])
        cum_t = cum.T
        tot = cum[SPAN - 1 : SPAN, :]
        keys = bc[here, :N]
        queries = bc[here, N:]
        scores = nt_dot(queries, keys)
        xs = xs_scr[here, :]
        scaled = xs * widen(dt[here], expand)
        scaled_low = scaled.astype(BF)
        pieces = []
        for pair in range(inner // LANES):
            values = scaled_low[:, pair * LANES : (pair + 1) * LANES]
            both = []
            for h in (2 * pair, 2 * pair + 1):
                gap = cum[:, h : h + 1] - cum_t[h : h + 1, :]
                decay = jnp.exp(jnp.minimum(gap, 0.0)) * lower
                both.append(nn((scores * decay).astype(BF), values))
            pieces.append(jnp.where(first_half, both[0], both[1]))
        y = jnp.concatenate(pieces, axis=1) + skip * xs
        if state is not None:
            y = y + widen(jnp.exp(cum), expand) * nn(queries, state.astype(BF))
        yloc[here, :] = y
        tail = widen(jnp.exp(tot - cum), expand)
        fresh = tn(keys, (scaled * tail).astype(BF))
        if state is not None:
            fresh = fresh + widen(jnp.exp(tot), expand) * state
        state = fresh
        cum_out[here, :] = cum + base
        base = base + tot
    final[0:N, :] = state.astype(BF)
    final[N:, :] = rows3(base, inner)


def mixer_front(normed, wzx, wside, chan, bcp, head):
    rows = normed.shape[0] - RIM
    inner = chan.shape[1]
    return call(
        front_kernel,
        "front",
        [
            sds((rows + RIM, 2 * inner), F32),
            sds((rows + RIM, 2 * N + LANES), F32),
            sds((rows, inner), F32),
            sds((N + RIM, inner), BF),
            sds((rows, N), BF),
            sds((rows, LANES), F32),
        ],
        (normed, wzx, wside, chan, bcp, head),
        scratch=[pltpu.VMEM((rows, inner), F32)],
        flops=8 * rows * D * inner,
        moved=12 * MIB,
    )


def chain(parts, expand):
    total = None
    past = jnp.zeros((1, LANES), F32)
    for part in parts:
        term = widen(jnp.exp(past), expand) * part[0:N, :].astype(F32)
        total = term if total is None else total + term
        past = past + jnp.sum(part[N:, :LANES].astype(F32), axis=0, keepdims=True)
    return total


def middle_kernel(shards, own, hops, scal, *rest):
    states, rest = rest[:hops], rest[hops:]
    yloc, zx, c_in, cum, wout, chan = rest[:6]
    y_out, s_out = rest[6:8]
    parts, work = rest[8 : 8 + shards], rest[-1]
    shard = scal[0]
    rows, inner = yloc.shape
    expand = head_map(inner)
    state = chain(states, expand)
    s_out[...] = state
    y = yloc[...] + widen(jnp.exp(cum[...]), expand) * nn(c_in[...], state.astype(BF))
    y_out[...] = y
    z = zx[RIM:, :inner]
    gated = y * (z * sigmoid(z))
    work[:, :D] = nn((gated * chan[5:6, :]).astype(BF), wout[...]).astype(BF)
    work[:, D:] = lanes3(jnp.sum(gated * gated, axis=1, keepdims=True))
    for off in range(shards):
        at = pl.multiple_of((shard ^ off) * own, own)
        parts[off][...] = work[pl.ds(at, own), :]


def mixer_middle(scal, states, yloc, zx, c_in, cum, wout, chan, shards):
    rows, inner = yloc.shape
    own = rows // shards
    return call(
        functools.partial(middle_kernel, shards, own, len(states)),
        "middle",
        [sds((rows, inner), F32), sds((N, inner), F32)]
        + [sds((own, D + LANES), BF)] * shards,
        (scal, *states, yloc, zx, c_in, cum, wout, chan),
        smem=(0,),
        scratch=[pltpu.VMEM((rows, D + LANES), BF)],
        flops=2 * rows * D * inner,
        moved=8 * MIB,
    )


def gate_back_kernel(grads, wout, y_in, zx, c_in, cum, chan, *rest):
    u_out, dy_out, dz_out, state_out, gain_out = rest
    inner = chan.shape[1]
    du = nt_dot(grads[:, :D], wout[...])
    coef = column3(grads[:, D:].astype(F32))
    z = zx[RIM:, :inner]
    y = y_in[...]
    sig = sigmoid(z)
    silu = z * sig
    gated = y * silu
    gain_out[...] = jnp.sum(du * gated, axis=0, keepdims=True)
    gain = chan[5:6, :]
    u_out[...] = (gated * gain).astype(BF)
    dgated = du * gain - gated * coef
    dy = dgated * silu
    dy_out[...] = dy
    dz_out[...] = (dgated * y * (sig * (1.0 + z * (1.0 - sig)))).astype(BF)
    grown = widen(jnp.exp(cum[...]), head_map(inner))
    state_out[0:N, :] = tn(c_in[...], (dy * grown).astype(BF)).astype(BF)
    rows = dy.shape[0]
    state_out[N:, :] = rows3(cum[rows - 1 : rows, :], inner)


def gate_back(grads, wout, y, zx, c_in, cum, chan):
    rows, inner = y.shape
    return call(
        gate_back_kernel,
        "gateback",
        [
            sds((rows, inner), BF),
            sds((rows, inner), F32),
            sds((rows, inner), BF),
            sds((N + RIM, inner), BF),
            sds((1, inner), F32),
        ],
        (grads, wout, y, zx, c_in, cum, chan),
        flops=2 * rows * D * inner,
        moved=10 * MIB,
    )


def silu_slope(pre):
    sig = sigmoid(pre)
    return sig * (1.0 + pre * (1.0 - sig))


def conv_back(ds_scr, raw, params, rows, lanes, width, low_out, out_lanes):
    ext = rows + RIM
    total = params[0:1, :] * ds_scr[pl.ds(3, ext), :]
    for k in range(1, 4):
        total = total + params[k : k + 1, :] * ds_scr[pl.ds(3 - k, ext), :]
    low_out[:, out_lanes] = total.astype(BF)
    ds = ds_scr[pl.ds(RIM, rows), :]
    grads = [
        jnp.sum(ds * raw[pl.ds(RIM - 3 + k, rows), lanes], axis=0, keepdims=True) for k in range(4)
    ]
    grads.append(jnp.sum(ds, axis=0, keepdims=True))
    grads.append(jnp.zeros((3, width), F32))
    return jnp.concatenate(grads, axis=0)


def within_kernel(s_in, zx, side, dy_in, chan, bcp, head, *outs):
    xs_out, bc_out, cum_out, starts_out, dscaled_out, dbc_out = outs
    rows, inner = dy_in.shape
    expand = head_map(inner)
    pre_x = conv_sum(zx, chan, rows, pl.ds(inner, inner))
    xs_out[...] = pre_x * sigmoid(pre_x)
    pre_bc = conv_sum(side, bcp, rows, pl.ds(0, 2 * N))
    bc = (pre_bc * sigmoid(pre_bc)).astype(BF)
    bc_out[...] = bc
    dt = softplus(side[RIM:, 2 * N :] + head[0:1, :])
    rate = -dt * jnp.exp(head[1:2, :])
    lower_low = (iota((SPAN, SPAN), 0) >= iota((SPAN, SPAN), 1)).astype(F32).astype(BF)
    upper = (iota((SPAN, SPAN), 0) <= iota((SPAN, SPAN), 1)).astype(F32)
    first_half = iota((SPAN, LANES), 1) < P_SIZE
    spans = rows // SPAN
    start = s_in[...]
    for span in range(spans):
        here = slice(span * SPAN, (span + 1) * SPAN)
        cum = tri_sum(lower_low, rate[here])
        cum_out[here, :] = cum
        cum_t = cum.T
        keys = bc[here, :N]
        queries = bc[here, N:]
        xs = xs_out[here, :]
        starts_out[span] = start
        start_low = start.astype(BF)
        if span + 1 < spans:
            tot = cum[SPAN - 1 : SPAN, :]
            scale = widen(dt[here] * jnp.exp(tot - cum), expand)
            fresh = tn(keys, (xs * scale).astype(BF))
            start = widen(jnp.exp(tot), expand) * start + fresh
        scores_t = nt_dot(keys, queries)
        dy = dy_in[here, :]
        dy_low = dy.astype(BF)
        scaled_low = (xs * widen(dt[here], expand)).astype(BF)
        dscores_t = jnp.zeros((SPAN, SPAN), F32)
        for pair in range(inner // LANES):
            lanes = slice(pair * LANES, (pair + 1) * LANES)
            values = scaled_low[:, lanes]
            dpair = dy_low[:, lanes]
            both = []
            for h in (2 * pair, 2 * pair + 1):
                gap = cum_t[h : h + 1, :] - cum[:, h : h + 1]
                decay = jnp.exp(jnp.minimum(gap, 0.0)) * upper
                mine = first_half if h % 2 == 0 else jnp.logical_not(first_half)
                outer = nt_dot(jnp.where(mine, values, jnp.zeros_like(values)), dpair)
                dscores_t = dscores_t + outer * decay
                both.append(nn((scores_t * decay).astype(BF), dpair))
            dscaled_out[here, lanes] = jnp.where(first_half, both[0], both[1])
        dscores_low = dscores_t.astype(BF)
        dy_grown = (dy * widen(jnp.exp(cum), expand)).astype(BF)
        dbc_out[here, :N] = nn(dscores_low, queries)
        dbc_out[here, N:] = tn(dscores_low, keys) + nt_dot(dy_grown, start_low)


def mixer_within(s_in, zx, side, dy, chan, bcp, head):
    rows, inner = dy.shape
    return call(
        within_kernel,
        "within",
        [
            sds((rows, inner), F32),
            sds((rows, 2 * N), BF),
            sds((rows, LANES), F32),
            sds((rows // SPAN, N, inner), F32),
            sds((rows, inner), F32),
            sds((rows, 2 * N), F32),
        ],
        (s_in, zx, side, dy, chan, bcp, head),
        flops=8 * rows * D * inner,
        moved=16 * MIB,
    )


def back_kernel(shards, own, hops, scal, *rest):
    states, rest = rest[:hops], rest[hops:]
    xs_in, bc_in, cum_in, starts, dscaled_in, dbc_in, rest = *rest[:6], rest[6:]
    zx, side, dy_in, dz_in, y_in, wzx, wside, chan, bcp, head = rest[:10]
    normed, gain = rest[10:12]
    dzx, dside, chan_out, bcp_out, head_out, rim_out, gain_out = rest[12:19]
    parts, rest = rest[19 : 19 + shards], rest[19 + shards :]
    dsx, dsbc, work = rest
    shard = scal[0]
    rows, inner = dy_in.shape
    expand = head_map(inner)
    raw_dt = side[RIM:, 2 * N :] + head[0:1, :]
    dt = softplus(raw_dt)
    grow = jnp.exp(head[1:2, :])
    rate = -dt * grow
    skip = widen(head[...], expand)[2:3, :]
    upper_low = (iota((SPAN, SPAN), 0) <= iota((SPAN, SPAN), 1)).astype(F32).astype(BF)
    spans = rows // SPAN
    dstate = chain(states, expand)
    dsx[0:RIM, :] = jnp.zeros((RIM, inner), F32)
    dsx[RIM + rows :, :] = jnp.zeros((RIM, inner), F32)
    dsbc[0:RIM, :] = jnp.zeros((RIM, 2 * N), F32)
    dsbc[RIM + rows :, :] = jnp.zeros((RIM, 2 * N), F32)
    dside[0:RIM, 2 * N :] = jnp.zeros((RIM, LANES), BF)
    dzx[0:RIM, :inner] = jnp.zeros((RIM, inner), BF)
    dzx[RIM:, :inner] = dz_in[...]
    dbias = jnp.zeros((1, LANES), F32)
    dgrow = jnp.zeros((1, LANES), F32)
    dskip = jnp.zeros((1, LANES), F32)
    for span in reversed(range(spans)):
        here = slice(span * SPAN, (span + 1) * SPAN)
        there = slice(RIM + span * SPAN, RIM + (span + 1) * SPAN)
        cum = cum_in[here, :]
        tot = cum[SPAN - 1 : SPAN, :]
        keys = bc_in[here, :N]
        queries = bc_in[here, N:]
        xs = xs_in[here, :]
        dy = dy_in[here, :]
        dy_low = dy.astype(BF)
        dt_wide = widen(dt[here], expand)
        scaled = xs * dt_wide
        scaled_low = scaled.astype(BF)
        tail = widen(jnp.exp(tot - cum), expand)
        dstate_low = dstate.astype(BF)
        through = tail * nn(keys, dstate_low)
        dscaled = dscaled_in[here, :] + through
        plain = y_in[here, :] - skip * xs
        held = scaled_low.astype(F32)
        dcum = narrow(dy_low.astype(F32) * plain - held * dscaled, expand)
        tot_wide = widen(jnp.exp(tot), expand)
        over = jnp.sum(held * through, axis=0, keepdims=True) + jnp.sum(
            tot_wide * dstate * starts[span], axis=0, keepdims=True
        )
        dtot = narrow(jnp.broadcast_to(over, (8, inner)), expand)[0:1, :]
        drate = tri_sum(upper_low, dcum) + dtot
        ddt = narrow(dscaled * xs, expand) - drate * grow
        dgrow = dgrow + jnp.sum(drate * rate[here], axis=0, keepdims=True)
        draw = ddt * sigmoid(raw_dt[here])
        dbias = dbias + jnp.sum(draw, axis=0, keepdims=True)
        dside[there, 2 * N :] = draw.astype(BF)
        over = jnp.sum(dy * xs, axis=0, keepdims=True)
        dskip = dskip + narrow(jnp.broadcast_to(over, (8, inner)), expand)[0:1, :]
        dsx[there, :] = dscaled * dt_wide + skip * dy
        dsbc[there, :N] = dbc_in[here, :N] + nt_dot((scaled * tail).astype(BF), dstate_low)
        dsbc[there, N:] = dbc_in[here, N:]
        if span > 0:
            grown = widen(jnp.exp(cum), expand)
            dstate = tot_wide * dstate + tn(queries, (dy * grown).astype(BF))
    body = pl.ds(RIM, rows)
    pre_x = conv_sum(zx, chan, rows, pl.ds(inner, inner))
    dsx[body, :] = dsx[body, :] * silu_slope(pre_x)
    pre_bc = conv_sum(side, bcp, rows, pl.ds(0, 2 * N))
    dsbc[body, :] = dsbc[body, :] * silu_slope(pre_bc)
    chan_out[...] = conv_back(
        dsx, zx, chan, rows, pl.ds(inner, inner), inner, dzx, pl.ds(inner, inner)
    )
    bcp_out[...] = conv_back(dsbc, side, bcp, rows, pl.ds(0, 2 * N), 2 * N, dside, pl.ds(0, 2 * N))
    head_out[...] = jnp.concatenate([dbias, dgrow, dskip, jnp.zeros((5, LANES), F32)], axis=0)
    dnormed = nt_dot(dzx[...], wzx[...]) + nt_dot(dside[...], wside[...])
    work[...] = dnormed.astype(BF)
    gain_out[...] = jnp.sum(dnormed * normed[...].astype(F32), axis=0, keepdims=True) / gain[...]
    rim_out[...] = work[0:RIM, :]
    for off in range(shards):
        at = pl.multiple_of(RIM + (shard ^ off) * own, RIM)
        parts[off][...] = work[pl.ds(at, own), :]


def mixer_back(
    scal, states, inside, zx, side, dy, dz, y, wzx, wside, chan, bcp, head, normed, gain, shards
):
    rows, inner = dy.shape
    own = rows // shards
    ext = rows + RIM
    return call(
        functools.partial(back_kernel, shards, own, len(states)),
        "back",
        [
            sds((ext, 2 * inner), BF),
            sds((ext, 2 * N + LANES), BF),
            sds((8, inner), F32),
            sds((8, 2 * N), F32),
            sds((8, LANES), F32),
            sds((RIM, D), BF),
            sds((1, D), F32),
        ]
        + [sds((own, D), BF)] * shards,
        (scal, *states, *inside, zx, side, dy, dz, y, wzx, wside, chan, bcp, head, normed, gain),
        smem=(0,),
        scratch=[
            pltpu.VMEM((ext + RIM, inner), F32),
            pltpu.VMEM((ext + RIM, 2 * N), F32),
            pltpu.VMEM((ext, D), BF),
        ],
        flops=8 * rows * D * inner,
        moved=16 * MIB,
    )


def logits_kernel(vrows, label, table, normed, *rest):
    p_out, tops, stats, rows_scr, top, total, target, plain = rest
    step = pl.program_id(0)
    rows = normed.shape[0] - RIM

    @pl.when(step == 0)
    def _():
        rows_scr[...] = normed[RIM:, :].T
        top[...] = jnp.full((1, rows), -1e30, F32)
        total[...] = jnp.zeros((1, rows), F32)
        target[...] = jnp.zeros((1, rows), F32)
        plain[...] = jnp.zeros((1, rows), F32)

    highest, summed, hit, whole = top[...], total[...], target[...], plain[...]
    line = 2 * iota((PART, rows), 0)
    for half in range(2):
        for part_at in range(PAIRS // PART):
            first = step * PAIRS + part_at * PART
            here = slice(part_at * PART, (part_at + 1) * PART)
            padding = jnp.where(first + iota((PART, LANES), 0) < vrows, 0.0, -1e30)
            padding = jnp.concatenate([padding] * (rows // LANES), axis=1)
            raw = nn(table[here, half * D : (half + 1) * D], rows_scr[...])
            shown = raw + padding
            before = highest
            highest = jnp.maximum(before, jnp.max(shown, axis=0, keepdims=True))
            part = jnp.exp(shown - highest)
            summed = summed * jnp.exp(before - highest) + jnp.sum(part, axis=0, keepdims=True)
            wanted = label[...] - 2 * first - half
            hit = hit + jnp.sum(jnp.where(line == wanted, raw, 0.0), axis=0, keepdims=True)
            whole = whole + jnp.sum(raw, axis=0, keepdims=True)
            p_out[half, here, :] = part.astype(BF)
            at = 8 * (half * (PAIRS // PART) + part_at)
            tops[0, at : at + 8, :] = jnp.broadcast_to(highest, (8, rows))
    top[...] = highest
    total[...] = summed
    target[...] = hit
    plain[...] = whole
    stats[...] = jnp.concatenate([highest, summed, hit, whole, jnp.zeros((4, rows), F32)], axis=0)


def vocab_logits(label, table, normed, vrows):
    rows = normed.shape[0] - RIM
    padded = table.shape[0]
    steps = padded // PAIRS
    whole = lambda i: (0, 0)
    return pl.pallas_call(
        functools.partial(logits_kernel, vrows),
        grid=(steps,),
        out_shape=[
            sds((2, padded, rows), BF),
            sds((steps, 16 * (PAIRS // PART), rows), F32),
            sds((8, rows), F32),
        ],
        in_specs=[
            pl.BlockSpec((1, rows), whole),
            pl.BlockSpec((PAIRS, 2 * D), lambda i: (i, 0)),
            pl.BlockSpec(normed.shape, whole),
        ],
        out_specs=[
            pl.BlockSpec((2, PAIRS, rows), lambda i: (0, i, 0)),
            pl.BlockSpec((1, 16 * (PAIRS // PART), rows), lambda i: (i, 0, 0)),
            pl.BlockSpec((8, rows), whole),
        ],
        scratch_shapes=[pltpu.VMEM((D, rows), BF)] + [pltpu.VMEM((1, rows), F32)] * 4,
        compiler_params=pltpu.CompilerParams(
            dimension_semantics=("arbitrary",), vmem_limit_bytes=56 * MIB
        ),
        cost_estimate=pl.CostEstimate(
            flops=4 * rows * D * padded, bytes_accessed=40 * MIB, transcendentals=2 * rows * padded
        ),
        name="logits",
    )(label, table, normed)


def logit_grads(step, label, scale, weight, p_in):
    pairs, rows = p_in.shape[1:]
    line = 2 * iota((PART, rows), 0)
    usual = (SMOOTHING / V) * weight[...]
    special = (1.0 - SMOOTHING + SMOOTHING / V) * weight[...]
    for half in range(2):
        pieces = []
        for part_at in range(pairs // PART):
            wanted = label[...] - 2 * (step * pairs + part_at * PART) - half
            share = jnp.where(line == wanted, special, usual)
            at = 8 * (half * (pairs // PART) + part_at)
            grown = p_in[half, part_at * PART : (part_at + 1) * PART, :].astype(F32)
            pieces.append((grown * scale[0, at : at + 1, :] - share).astype(BF))
        yield half, jnp.concatenate(pieces, axis=0)


def rows_kernel(shards, own, scal, label, scale, weight, p_in, table, *rest):
    parts, acc = rest[:shards], rest[-1]
    step = pl.program_id(0)

    @pl.when(step == 0)
    def _():
        acc[...] = jnp.zeros_like(acc)

    for half, q in logit_grads(step, label, scale, weight, p_in):
        acc[...] += tn(q, table[:, half * D : (half + 1) * D])

    @pl.when(step == pl.num_programs(0) - 1)
    def _():
        for off in range(shards):
            at = pl.ds(pl.multiple_of((scal[0] ^ off) * own, own), own)
            parts[off][...] = acc[at, :].astype(BF)


def vocab_specs(rows):
    whole = lambda i: (0, 0)
    return [
        pl.BlockSpec((1, rows), whole),
        pl.BlockSpec((1, 16 * (PAIRS // PART), rows), lambda i: (i, 0, 0)),
        pl.BlockSpec((1, rows), whole),
        pl.BlockSpec((2, PAIRS, rows), lambda i: (0, i, 0)),
    ]


def vocab_rows(scal, label, scale, weight, p_in, table, shards):
    _, padded, rows = p_in.shape
    own = rows // shards
    whole = lambda i: (0, 0)
    return pl.pallas_call(
        functools.partial(rows_kernel, shards, own),
        grid=(padded // PAIRS,),
        out_shape=[sds((own, D), BF)] * shards,
        in_specs=[pl.BlockSpec(memory_space=pltpu.SMEM)]
        + vocab_specs(rows)
        + [pl.BlockSpec((PAIRS, 2 * D), lambda i: (i, 0))],
        out_specs=[pl.BlockSpec((own, D), whole)] * shards,
        scratch_shapes=[pltpu.VMEM((rows, D), F32)],
        compiler_params=pltpu.CompilerParams(
            dimension_semantics=("arbitrary",), vmem_limit_bytes=56 * MIB
        ),
        cost_estimate=pl.CostEstimate(
            flops=4 * rows * D * padded, bytes_accessed=40 * MIB, transcendentals=0
        ),
        name="rowgrads",
    )(scal, label, scale, weight, p_in, table)


def table_kernel(label, scale, weight, p_in, normed, out, rows_scr):
    step = pl.program_id(0)

    @pl.when(step == 0)
    def _():
        rows_scr[...] = normed[RIM:, :]

    for half, q in logit_grads(step, label, scale, weight, p_in):
        out[:, half * D : (half + 1) * D] = nn(q, rows_scr[...]).astype(BF)


def vocab_table_grad(label, scale, weight, p_in, normed):
    _, padded, rows = p_in.shape
    whole = lambda i: (0, 0)
    return pl.pallas_call(
        table_kernel,
        grid=(padded // PAIRS,),
        out_shape=sds((padded, 2 * D), BF),
        in_specs=vocab_specs(rows) + [pl.BlockSpec(normed.shape, whole)],
        out_specs=pl.BlockSpec((PAIRS, 2 * D), lambda i: (i, 0)),
        scratch_shapes=[pltpu.VMEM((rows, D), BF)],
        compiler_params=pltpu.CompilerParams(
            dimension_semantics=("arbitrary",), vmem_limit_bytes=56 * MIB
        ),
        cost_estimate=pl.CostEstimate(
            flops=4 * rows * D * padded, bytes_accessed=40 * MIB, transcendentals=0
        ),
        name="tablegrads",
    )(label, scale, weight, p_in, normed)


def adam_update(weight_in, gradient, moment_one, moment_two, factor, fix_one, fix_two, decay_rate):
    gradient = gradient * factor
    one_next = BETA_FIRST * moment_one + (1.0 - BETA_FIRST) * gradient
    two_next = BETA_SECOND * moment_two + (1.0 - BETA_SECOND) * gradient * gradient
    direction = one_next / fix_one / (jnp.sqrt(two_next / fix_two) + ADAM_EPS)
    return (weight_in - LEARN_RATE * (direction + decay_rate * weight_in), one_next, two_next)


def turn_kernel(share, bases, turned, root):
    count = bases.shape[0]
    total = jnp.zeros((1, BLK), F32)

    def turn(at, total):
        grad = share[pl.ds(pl.multiple_of(at * BLK, BLK), BLK), :].astype(F32)
        half_turn = tn(bases[at, 0], grad, HIGHEST)
        turned[at] = nn(half_turn, bases[at, 1], HIGHEST)
        return total + jnp.sum(grad * grad, axis=0, keepdims=True)

    for at in range(count):
        total = turn(at, total)
    root[...] = jnp.sqrt(total)


def turn_tiles(share, bases):
    count = bases.shape[0]
    return call(
        turn_kernel,
        "turn",
        [sds((count, BLK, BLK), F32), sds((1, BLK), F32)],
        (share, bases),
        moved=6 * MIB,
    )


def last_kernel(small, fixes, sums, *refs):
    tiles, turned, bases, tile_one, tile_two = refs[:5]
    little, refs = refs[5 : 5 + 4 * small], refs[5 + 4 * small :]
    tiles_out, copy_out, tile_one_out, tile_two_out = refs[:4]
    little_out = refs[4:]
    factor, fix_one, fix_two = sums[2:3, 0:1], fixes[0], fixes[1]
    for at in range(tiles.shape[0]):
        rotated = turned[at] * factor
        one_next = BETA_FIRST * tile_one[at] + (1.0 - BETA_FIRST) * rotated
        two_next = BETA_SECOND * tile_two[at] + (1.0 - BETA_SECOND) * rotated * rotated
        direction = one_next / fix_one / (jnp.sqrt(two_next / fix_two) + ADAM_EPS)
        back_half = nn(bases[at, 0], direction, HIGHEST)
        back = nt_dot(back_half, bases[at, 1], HIGHEST)
        after = tiles[at] - LEARN_RATE * (back + WEIGHT_DECAY * tiles[at])
        tiles_out[at] = after
        copy_out[at] = after.astype(BF)
        tile_one_out[at] = one_next
        tile_two_out[at] = two_next

    @pl.when(pl.program_id(0) == 0)
    def _():
        for which in range(small):
            before, gradient, first, second = (ref[...] for ref in little[4 * which : 4 * which + 4])
            results = adam_update(
                before,
                gradient,
                first,
                second,
                factor,
                fix_one,
                fix_two,
                WEIGHT_DECAY if which == 0 else 0.0,
            )
            outs = little_out[3 * which : 3 * which + 3]
            outs[0][...] = results[0] if which == 0 else results[0] - before
            outs[1][...], outs[2][...] = results[1], results[2]


def last_update(fixes, sums, tiles, turned, bases, tile_one, tile_two, little):
    count = tiles.shape[0]
    each = 4 if count % 4 == 0 else 2
    tile_spec = pl.BlockSpec((each, BLK, BLK), lambda i: (i, 0, 0))
    base_spec = pl.BlockSpec((each, 2, BLK, BLK), lambda i: (i, 0, 0, 0))
    whole = [pl.BlockSpec(x.shape, lambda i: (0, 0)) for group in little for x in group]
    return pl.pallas_call(
        functools.partial(last_kernel, len(little)),
        grid=(count // each,),
        out_shape=[sds(tiles.shape, F32), sds(tiles.shape, BF), sds(tiles.shape, F32), sds(tiles.shape, F32)]
        + [sds(group[0].shape, F32) for group in little for _ in range(3)],
        in_specs=[
            pl.BlockSpec(memory_space=pltpu.SMEM),
            pl.BlockSpec(sums.shape, lambda i: (0, 0)),
        ]
        + [tile_spec, tile_spec, base_spec, tile_spec, tile_spec]
        + whole,
        out_specs=[tile_spec] * 4
        + [spec for which in range(len(little)) for spec in whole[4 * which : 4 * which + 3]],
        compiler_params=pltpu.CompilerParams(
            dimension_semantics=("arbitrary",), vmem_limit_bytes=48 * MIB
        ),
        cost_estimate=pl.CostEstimate(
            flops=24 * count * BLK * BLK * BLK, bytes_accessed=16 * MIB, transcendentals=0
        ),
        name="update",
    )(
        fixes,
        sums,
        tiles,
        turned,
        bases,
        tile_one,
        tile_two,
        *[x for group in little for x in group],
    )


def total_over(x, axis):
    out = x
    for off in range(1, lax.axis_size(axis)):
        out = out + swap(x, axis, off)
    return out


def shards(
    token_ids,
    labels,
    seq_lengths,
    micro_batch,
    step_count,
    block_slot,
    vocab_table,
    vocab_first,
    vocab_second,
    layer_blocks,
    block_bases,
    block_first,
    block_second,
    side_proj,
    side_first,
    side_second,
    shared_params,
    shared_first,
    shared_second,
    channel_params,
    channel_first,
    channel_second,
    head_params,
    head_first,
    head_second,
):
    nt = lax.axis_size("tensor")
    nd = lax.axis_size("dp")
    shard = lax.axis_index("tensor")
    place = lax.axis_index("dp")
    seqs = token_ids.shape[0]
    length = token_ids.shape[1] * nd
    chunks = nd // seqs
    rows = seqs * length // nd
    own = rows // nt
    vrows = vocab_table.shape[0]
    padded = -(-vrows // PAIRS) * PAIRS
    half = nd // 2
    inner = channel_params.shape[2]
    heads = head_params.shape[2]
    tiles = block_slot.shape[1]
    zx_count = D * 2 * inner // (BLK * BLK)
    per_layer = 3 * D * inner // (BLK * BLK)
    stride = D + 10 * N
    both = ("dp", "tensor")
    side_rows = side_proj.shape[1]
    share_size = shared_params.shape[0]
    share_pad = -(-share_size // 2048) * 2048

    piece = jnp.pad(side_proj.astype(BF), ((0, 0), (0, 0), (0, LANES - H))).reshape(-1, LANES)
    share = jnp.pad(shared_params.astype(BF), (0, share_pad - share_size)).reshape(-1, LANES)
    side_part = piece.shape[0]
    piece_rows = side_part + share.shape[0]
    ids = jnp.pad(jnp.concatenate([token_ids, labels], axis=0), ((0, 8 - 2 * seqs), (0, 0)))
    ids_all, pieces, shared_all = open_exchange(ids, piece, share, nd, nt)
    shared_full = shared_all.reshape(nd * nt, share_pad)[:, :share_size].reshape(-1).astype(F32)
    ids_all = ids_all.transpose(1, 0, 2).reshape(8, length)
    all_ids = ids_all[:seqs].reshape(-1)
    local_row = all_ids // 2 - shard * vrows
    held = (local_row >= 0) & (local_row < vrows) & (all_ids % 2 == place // half)
    scal = jnp.stack([place, shard]).astype(jnp.int32)
    scal_shard = shard.astype(jnp.int32).reshape(1)
    code = jnp.concatenate([jnp.where(held, local_row, 0), jnp.zeros((8,), jnp.int32)])
    listed, count = list_held(held, nd * rows)
    own_tiles = layer_blocks.shape[2]
    gathered = lax.all_gather(
        jnp.concatenate(
            [layer_blocks.astype(BF).reshape(own_tiles * BLK, BLK), pieces.reshape(-1, LANES)], axis=0
        ),
        "dp",
        axis=0,
        tiled=False,
    )
    parts = gather_rows(scal, code, listed, count, vocab_table, nd, rows)
    table_now, parts = lax.optimization_barrier((vocab_table, parts))
    parts = [parts[0]] + [swap(parts[off], "dp", off) for off in range(1, nd)]
    table_low = jnp.pad(table_now.astype(BF), ((0, padded - vrows), (0, 0)))
    parts = join_parts(scal, parts, nt, own)
    residual, normed = forward_rows(
        parts, None, shared_full[None, :D], nd, chunks, True, 4
    )
    gathered, normed = lax.optimization_barrier((gathered, normed))
    placed = place_tiles(block_slot, gathered, own_tiles, inner, zx_count, per_layer)
    side_full = (
        gathered[:, own_tiles * BLK :]
        .reshape(nd, nt, L, side_rows, 2 * N + LANES)
        .transpose(2, 0, 1, 3, 4)
        .reshape(L, D, 2 * N + LANES)
    )
    table_all = lax.all_gather(table_low, "dp", axis=1, tiled=True)

    def layer_mats(layer_index):
        zx_part, out_part = placed[2 * layer_index], placed[2 * layer_index + 1]
        dt_part = lax.dynamic_slice_in_dim(
            side_full[layer_index], 2 * N + shard * heads, heads, 1
        )
        side_here = jnp.concatenate(
            [
                side_full[layer_index][:, : 2 * N],
                jnp.pad(dt_part, ((0, 0), (0, LANES - heads))),
            ],
            axis=1,
        )
        base = layer_index * stride
        gain = shared_full[base : base + D]
        taps = shared_full[base + D : base + D + 8 * N].reshape(4, 2 * N)
        bias = shared_full[base + D + 8 * N : base + stride].reshape(1, 2 * N)
        bcp = jnp.concatenate([taps, bias, jnp.zeros((3, 2 * N), F32)], axis=0)
        chan = jnp.pad(channel_params[layer_index], ((0, 2), (0, 0)))
        head = jnp.pad(head_params[layer_index], ((0, 5), (0, LANES - heads)))
        return (zx_part, out_part, side_here, gain, bcp, chan, head)

    def hop(x, distance):
        pairs = [
            (k, k + distance)
            for k in range(nd)
            if 0 <= k % chunks + distance < chunks
        ]
        return lax.ppermute(x, "dp", pairs)

    def returned(parts):
        return [parts[0]] + [swap(parts[off], "tensor", off) for off in range(1, nt)]

    hops = range(1, chunks)
    mats = [layer_mats(layer_index) for layer_index in range(L)]
    final_gain = shared_full[L * stride :][None, :]
    gains = [mats[layer_index][3][None, :] for layer_index in range(L)] + [final_gain]
    saved = []
    for layer_index in range(L):
        wzx, wout, wside, gain, bcp, chan, head = mats[layer_index]
        zx, side, yloc, final, c_out, cum = mixer_front(normed, wzx, wside, chan, bcp, head)
        states = [hop(final, k) for k in hops]
        result = mixer_middle(scal_shard, states, yloc, zx, c_out, cum, wout, chan, nt)
        y, s_in = result[:2]
        below = normed
        before = residual
        inside = layer_index + 1 < L
        residual, branch, factor, normed = forward_rows(
            result[2:], before, gains[layer_index + 1], nd, chunks, inside, 5 + layer_index
        )
        saved.append((before, below, zx, side, c_out, cum, y, s_in, factor, branch))

    member = micro_batch[:, None] == jnp.arange(MB, dtype=jnp.int32)[None, :]
    batch_tokens = jnp.sum(jnp.where(member, seq_lengths[:, None], 0), axis=0).astype(F32)
    seq_weight = 1.0 / (MB * jnp.sum(jnp.where(member, batch_tokens[None, :], 0.0), axis=1))
    row_at = place * rows + jnp.arange(rows, dtype=jnp.int32)
    my_seq = place // chunks
    weight = jnp.where(row_at % length < seq_lengths[my_seq], seq_weight[my_seq], 0.0)
    all_labels = ids_all[seqs : 2 * seqs].reshape(-1)
    label = (lax.dynamic_slice_in_dim(all_labels, place * rows, rows) - 2 * shard * vrows).reshape(
        1, rows
    )
    row_weight = weight.reshape(1, rows)
    p_low, tops, stats = vocab_logits(label, table_all, normed, vrows)
    scale, seq_part = merge_stats(stats, tops, row_weight, nt, chunks)
    sent = returned(vocab_rows(scal_shard, label, scale, row_weight, p_low, table_all, nt))
    table_grad = vocab_table_grad(label, scale, row_weight, p_low, normed)
    sent, table_grad = lax.optimization_barrier((sent, table_grad))
    table_share = lax.psum_scatter(table_grad, "dp", scatter_dimension=1, tiled=True)
    grad_res, payload, grad_final_gain = backward_rows(
        sent, None, residual, final_gain, None, saved[L - 1][9], saved[L - 1][8], nd, chunks, 10
    )

    block_pieces = [None] * (2 * L)
    side_pieces = [None] * L
    channel_pieces = [None] * L
    head_pieces = [None] * L
    shared_pieces = [None] * L
    for layer_index in reversed(range(L)):
        wzx, wout, wside, gain, bcp, chan, head = mats[layer_index]
        residual_in, normed, zx, side, c_out, cum, y, s_in, factor, branch = saved[layer_index]
        u_low, dy, dz, dstate, gain_grad = gate_back(payload, wout, y, zx, c_out, cum, chan)
        states = [hop(dstate, -k) for k in hops]
        grad_out_w = tn(u_low, payload)
        inside = mixer_within(s_in, zx, side, dy, chan, bcp, head)
        result = mixer_back(
            scal_shard,
            states,
            inside,
            zx,
            side,
            dy,
            dz,
            y,
            wzx,
            wside,
            chan,
            bcp,
            head,
            normed,
            gains[layer_index],
            nt,
        )
        dzx, dside, chan_grad, bcp_grad, head_grad, rim_grad, grad_gain_in = result[:7]
        parts_out = result[7:]
        grad_zx_w = tn(normed, dzx)
        grad_side_w = tn(normed, dside)
        block_pieces[2 * layer_index] = grad_zx_w.astype(BF)
        block_pieces[2 * layer_index + 1] = grad_out_w.astype(BF)
        side_pieces[layer_index] = grad_side_w
        shared_pieces[layer_index] = jnp.concatenate(
            [grad_gain_in[0], bcp_grad[:4].reshape(-1), bcp_grad[4]]
        )
        channel_pieces[layer_index] = jnp.concatenate([chan_grad[:5], gain_grad], axis=0)
        head_pieces[layer_index] = head_grad[:3, :heads]
        if layer_index == 0:
            shared_grads = jnp.concatenate(shared_pieces + [grad_final_gain[0]]).astype(BF)
            shared_grads = jnp.pad(
                shared_grads.reshape(nd * nt, share_size), ((0, 0), (0, share_pad - share_size))
            ).reshape(nd, nt * share_pad // LANES, LANES)
            lines = jnp.concatenate(
                [
                    jnp.stack(channel_pieces).reshape(-1, LANES),
                    jnp.pad(jnp.stack(head_pieces).reshape(-1), (0, LANES - L * 3 * heads)).reshape(
                        1, LANES
                    ),
                ],
                axis=0,
            ).astype(BF)
            line_count = lines.shape[0]
            line_rows = -(-line_count // RIM) * RIM
            lines = jnp.pad(lines, ((0, line_rows - line_count), (0, 0)))
            tile_grads = pack_tiles(
                scal_shard,
                block_slot,
                block_pieces,
                side_pieces,
                shared_grads,
                lines,
                own_tiles,
                per_layer,
                nt,
                heads,
            )
            tile_grads, table_share, parts_out, rim_grad = lax.optimization_barrier(
                (tile_grads, table_share, parts_out, rim_grad)
            )
            block_share = lax.psum_scatter(tile_grads, "dp", scatter_dimension=0, tiled=True)[0]
        if layer_index:
            grad_res, payload = backward_rows(
                parts_out,
                rim_grad,
                residual_in,
                gains[layer_index],
                grad_res,
                saved[layer_index - 1][9],
                saved[layer_index - 1][8],
                nd,
                chunks,
                10 + layer_index,
            )
        else:
            embed = finish_rows(
                parts_out, rim_grad, residual_in, gains[0], grad_res, nd, chunks
            )

    side_count = nt * side_part
    small_share = jnp.concatenate(
        [
            block_share[own_tiles * BLK : own_tiles * BLK + side_count].reshape(nt, side_part, LANES),
            block_share[own_tiles * BLK + side_count : own_tiles * BLK + nt * piece_rows].reshape(
                nt, piece_rows - side_part, LANES
            ),
        ],
        axis=1,
    )
    mine = jnp.zeros((piece_rows, LANES), F32)
    for off in range(nt):
        piece = lax.dynamic_index_in_dim(small_share, shard ^ off, 0, False)
        mine = mine + (piece if off == 0 else swap(piece, "tensor", off)).astype(F32)
    side_share = (
        mine[:side_part]
        .reshape(L, 2 * N // LANES + 1, side_rows, LANES)
        .transpose(0, 2, 1, 3)
        .reshape(L * side_rows, 2 * N + LANES)[:, : 2 * N + H]
    )
    shared_share = mine[side_part:].reshape(1, -1)[:, :share_size]
    lines = block_share[own_tiles * BLK + nt * piece_rows :].astype(F32)
    channel_sum = lines[: line_count - 1].reshape(L * 6, inner)
    head_sum = lines[line_count - 1, : L * 3 * heads].reshape(L * 3, heads)
    rotated, tile_root = turn_tiles(block_share, block_bases.reshape(own_tiles, 2, BLK, BLK))
    grad_table, table_root = add_rows(scal, code, listed, count, table_share, embed, vrows)
    sums = sum_everywhere(
        seq_part,
        [channel_sum, head_sum],
        [table_root, tile_root, side_share, shared_share],
        nd,
        nt,
    )
    seq_loss = sums[0, :seqs]
    clip_norm = sums[1, 0]
    steps_done = step_count[0].astype(F32)
    fix_one = 1.0 - jnp.power(BETA_FIRST, steps_done)
    fix_two = 1.0 - jnp.power(BETA_SECOND, steps_done)
    tile_shape = layer_blocks.shape[2:]
    flat = lambda x: x.reshape((-1, x.shape[-1]))
    little = [
        [flat(side_proj), side_share, flat(side_first), flat(side_second)],
        [flat(shared_params), shared_share, flat(shared_first), flat(shared_second)],
        [flat(channel_params), channel_sum, flat(channel_first), flat(channel_second)],
        [flat(head_params), head_sum, flat(head_first), flat(head_second)],
    ]
    updated = last_update(
        jnp.stack([fix_one, fix_two]),
        sums,
        layer_blocks.reshape(tile_shape),
        rotated,
        block_bases.reshape((own_tiles, 2, BLK, BLK)),
        block_first.reshape(tile_shape),
        block_second.reshape(tile_shape),
        little,
    )
    table_out = adam_update(
        vocab_table,
        grad_table.astype(F32),
        vocab_first,
        vocab_second,
        sums[2, 0],
        fix_one,
        fix_two,
        WEIGHT_DECAY,
    )
    block_out = [x.reshape(layer_blocks.shape) for x in updated[:4]]
    like = [side_proj] * 3 + [shared_params] * 3 + [channel_params] * 3 + [head_params] * 3
    small_out = [x.reshape(y.shape) for x, y in zip(updated[4:], like)]
    return (
        seq_loss,
        clip_norm,
        table_out[0],
        table_out[1],
        table_out[2],
        block_out[0],
        block_out[1],
        block_out[2],
        block_out[3],
        *small_out,
    )


def solution(mesh):
    table = P("tensor", "dp")
    block = P("dp", "tensor", None, None, None)
    side = P(None, ("dp", "tensor"), None)
    shared = P(("dp", "tensor"))
    channel = P(None, None, "tensor")
    in_specs = (
        P(None, "dp"),
        P(None, "dp"),
        P(),
        P(),
        P(),
        P("tensor", None),
        *[table] * 3,
        block,
        P("dp", "tensor", None, None, None, None),
        block,
        block,
        *[side] * 3,
        *[shared] * 3,
        *[channel] * 6,
    )
    out_specs = (
        P(),
        P(),
        *[table] * 3,
        *[block] * 4,
        *[side] * 3,
        *[shared] * 3,
        *[channel] * 6,
    )
    return jax.shard_map(shards, mesh=mesh, in_specs=in_specs, out_specs=out_specs, check_vma=False)
```

```python
import functools

import jax
import jax.numpy as jnp
from jax import lax
from jax.experimental import pallas as pl
from jax.experimental.pallas import tpu as pltpu
from jax.sharding import PartitionSpec as P

D = 1024
DI = 2048
H = 32
P_SIZE = 64
N = 128
V = 50288
SPAN = 256
L = 2
MB = 2
BLK = 128
RIM = 16
PAIRS = 1280
PART = 320
LANES = 128

HIGHEST = lax.Precision.HIGHEST
NORM_EPS = 1e-05
SMOOTHING = 0.1
ZLOSS_WEIGHT = 0.005
CLIP_LIMIT = 0.02
BETA_FIRST = 0.9
BETA_SECOND = 0.95
ADAM_EPS = 1e-08
LEARN_RATE = 0.03
WEIGHT_DECAY = 0.01

BF = jnp.bfloat16
F32 = jnp.float32
MIB = 1 << 20


def nn(a, b, precision=None):
    return lax.dot_general(
        a, b, (((1,), (0,)), ((), ())), precision=precision, preferred_element_type=F32
    )


def nt_dot(a, b, precision=None):
    return lax.dot_general(
        a, b, (((1,), (1,)), ((), ())), precision=precision, preferred_element_type=F32
    )


def tn(a, b, precision=None):
    return lax.dot_general(
        a, b, (((0,), (0,)), ((), ())), precision=precision, preferred_element_type=F32
    )


def iota(shape, dim):
    return lax.broadcasted_iota(jnp.int32, shape, dim)


def head_map(inner):
    return (iota((LANES, inner), 0) == iota((LANES, inner), 1) // P_SIZE).astype(F32).astype(BF)


def swap(x, axis, offset):
    size = lax.axis_size(axis)
    return lax.ppermute(x, axis, [(i, i ^ offset) for i in range(size)])


def halves(x):
    high = x.astype(BF)
    return high, (x - high.astype(F32)).astype(BF)


def thirds(x):
    high = x.astype(BF)
    rest = x - high.astype(F32)
    mid = rest.astype(BF)
    return high, mid, (rest - mid.astype(F32)).astype(BF)


def widen(x, expand):
    high, low = halves(x)
    twice = jnp.concatenate([expand, expand], axis=0)
    return nn(jnp.concatenate([high, low], axis=1), twice)


def narrow(x, expand):
    high, low = halves(x)
    return nt_dot(high, expand) + nt_dot(low, expand)


def tri_sum(tri, x):
    wide = nn(tri, jnp.concatenate(thirds(x), axis=1))
    size = x.shape[1]
    return wide[:, :size] + wide[:, size : 2 * size] + wide[:, 2 * size :]


def lanes3(column):
    high, mid, low = thirds(column)
    lane = iota((column.shape[0], LANES), 1)
    zero = jnp.zeros((column.shape[0], LANES), F32)
    wide = jnp.where(lane == 0, high.astype(F32), zero)
    wide = jnp.where(lane == 1, mid.astype(F32), wide)
    return jnp.where(lane == 2, low.astype(F32), wide).astype(BF)


def column3(wide):
    return wide[:, 0:1] + wide[:, 1:2] + wide[:, 2:3]


def rows3(line, inner):
    high, mid, low = thirds(line)
    at = iota((RIM, LANES), 0)
    wide = jnp.where(at == 0, high.astype(F32), 0.0)
    wide = jnp.where(at == 1, mid.astype(F32), wide)
    wide = jnp.where(at == 2, low.astype(F32), wide)
    if inner > LANES:
        wide = jnp.concatenate([wide, jnp.zeros((RIM, inner - LANES), F32)], axis=1)
    return wide.astype(BF)


def sigmoid(x):
    return 1.0 / (1.0 + jnp.exp(-x))


def softplus(x):
    return jnp.maximum(x, 0.0) + jnp.log1p(jnp.exp(-jnp.abs(x)))


def call(kernel, name, out_shape, args, smem=(), scratch=(), mib=60, flops=0, moved=0, **extra):
    specs = [
        pl.BlockSpec(memory_space=pltpu.SMEM if i in smem else pltpu.VMEM)
        for i in range(len(args))
    ]
    return pl.pallas_call(
        kernel,
        out_shape=out_shape,
        in_specs=specs,
        out_specs=jax.tree.map(lambda _: pl.BlockSpec(memory_space=pltpu.VMEM), out_shape),
        scratch_shapes=list(scratch),
        compiler_params=pltpu.CompilerParams(vmem_limit_bytes=mib * MIB),
        cost_estimate=pl.CostEstimate(flops=flops, bytes_accessed=moved, transcendentals=0),
        name=name,
        **extra,
    )(*args)


def sds(shape, dtype):
    return jax.ShapeDtypeStruct(shape, dtype)


def list_held(held, total):
    runs = held.reshape(-1, LANES)
    upper = iota((LANES, LANES), 0) <= iota((LANES, LANES), 1)
    rank = nn(runs.astype(BF), upper.astype(BF)).astype(jnp.int32) - 1
    here = (rank[:, :, None] == iota((1, 1, LANES), 2)) & runs[:, :, None]
    at = jnp.sum(jnp.where(here, iota((1, LANES, 1), 1), 0), axis=1)
    counts = rank[:, -1] + 1
    first = iota(at.shape, 0) * LANES
    listed = jnp.where(iota(at.shape, 1) < counts[:, None], at + first, total)
    return listed.reshape(-1), counts


def over_listed(listed, count, body):
    def run(at_run, carry):
        def turn(step, inner_carry):
            for lane in range(8):
                body(listed[at_run * LANES + step * 8 + lane])
            return inner_carry

        lax.fori_loop(0, (count[at_run] + 7) // 8, turn, 0)
        return carry

    lax.fori_loop(0, count.shape[0], run, 0)


def look_kernel(groups, rows, scal, code, listed, count, table, *rest):
    outs, low, work = rest[:groups], rest[groups], rest[groups + 1]
    place = scal[0]
    vrows = table.shape[0]
    edge = vrows // RIM * RIM
    low[edge:, :] = jnp.zeros((low.shape[0] - edge, low.shape[1]), BF)
    low[0:vrows, :] = table[...].astype(BF)

    def fill(step, carry):
        work[pl.ds(pl.multiple_of(step * rows, rows), rows), :] = jnp.zeros((rows, table.shape[1]), F32)
        return carry

    lax.fori_loop(0, groups, fill, 0)

    def take(at):
        work[pl.ds(at, 1), :] = table[pl.ds(code[at], 1), :]

    over_listed(listed, count, take)
    for off in range(groups):
        base = pl.multiple_of((place ^ off) * rows, rows)
        outs[off][...] = work[pl.ds(base, rows), :].astype(BF)


def gather_rows(scal, code, listed, count, table, groups, rows, padded):
    cols = table.shape[1]
    return call(
        functools.partial(look_kernel, groups, rows),
        "look",
        [sds((rows, cols), BF)] * groups + [sds((padded, cols), BF)],
        (scal, code, listed, count, table),
        smem=(0, 1, 2, 3),
        scratch=[pltpu.VMEM((groups * rows + 8, cols), F32)],
        moved=30 * MIB,
    )


def add_kernel(groups, rows, vrows, scal, code, listed, count, share, parts, *rest):
    out, square, work, bins = rest
    place = scal[0]
    bins[...] = share[0:vrows, :].astype(F32)
    for off in range(groups):
        base = pl.multiple_of((place ^ off) * rows, rows)
        work[pl.ds(base, rows), :] = parts[off].astype(F32)
    work[groups * rows :, :] = jnp.zeros((8, work.shape[1]), F32)

    def add(at):
        to = pl.ds(code[at], 1)
        bins[to, :] = bins[to, :] + work[pl.ds(at, 1), :]

    over_listed(listed, count, add)
    total = bins[...]
    out[...] = total.astype(BF)
    square[...] = jnp.sqrt(jnp.sum(total * total, axis=0, keepdims=True))


def add_rows(scal, code, listed, count, share, parts, vrows):
    cols = share.shape[1]
    groups, rows, _ = parts.shape
    return call(
        functools.partial(add_kernel, groups, rows, vrows),
        "addrows",
        [sds((vrows, cols), BF), sds((1, cols), F32)],
        (scal, code, listed, count, share, parts),
        smem=(0, 1, 2, 3),
        scratch=[pltpu.VMEM((rows * groups + 8, cols), F32), pltpu.VMEM((vrows, cols), F32)],
        moved=30 * MIB,
    )


def tiles_kernel(slots_each, zx_count, per_layer, layers, slot, tiles, *outs):
    for layer in range(layers):
        for at in range(per_layer):
            where = slot[0, layer * per_layer + at]
            owner = where // slots_each
            first = pl.multiple_of((where % slots_each) * BLK, BLK)
            tile = tiles[owner, pl.ds(first, BLK), :]
            if at < zx_count:
                wide = outs[2 * layer].shape[1] // BLK
                row, col = at // wide, at % wide
                out = outs[2 * layer]
            else:
                wide = D // BLK
                row, col = (at - zx_count) // wide, (at - zx_count) % wide
                out = outs[2 * layer + 1]
            out[row * BLK : (row + 1) * BLK, col * BLK : (col + 1) * BLK] = tile


def place_tiles(slot, tiles, slots_each, inner, zx_count, per_layer):
    return call(
        functools.partial(tiles_kernel, slots_each, zx_count, per_layer, L),
        "placetiles",
        [sds((D, 2 * inner), BF), sds((inner, D), BF)] * L,
        (slot, tiles),
        smem=(0,),
        moved=14 * MIB,
    )


def pack_kernel(slots_each, per_layer, layers, shards, heads, scal, slot, *refs):
    mats, sides, refs = refs[: 2 * layers], refs[2 * layers : 3 * layers], refs[3 * layers :]
    shared, lines, out, work = refs
    for layer in range(layers):
        zx, wout = mats[2 * layer], mats[2 * layer + 1]
        zx_wide, out_wide = zx.shape[1] // BLK, D // BLK
        zx_count = zx.shape[0] // BLK * zx_wide
        for at in range(per_layer):
            where = slot[0, layer * per_layer + at]
            if at < zx_count:
                source, row, col = zx, at // zx_wide, at % zx_wide
            else:
                source = wout
                row, col = (at - zx_count) // out_wide, (at - zx_count) % out_wide
            first = pl.multiple_of((where % slots_each) * BLK, BLK)
            out[where // slots_each, pl.ds(first, BLK), :] = source[
                row * BLK : (row + 1) * BLK, col * BLK : (col + 1) * BLK
            ]
        work[layer, :, : 2 * N] = sides[layer][:, : 2 * N]
        work[layer, :, 2 * N :] = pltpu.roll(sides[layer][:, 2 * N :], scal[0] * heads, 1)
    groups = out.shape[0]
    each = work.shape[1] // (groups * shards)
    piece = layers * each * work.shape[2] // LANES
    base = slots_each * BLK
    for group in range(groups):
        for shard in range(shards):
            first = (group * shards + shard) * each
            blocks = [
                work[layer, first : first + each, col : col + LANES]
                for layer in range(layers)
                for col in range(0, work.shape[2], LANES)
            ]
            at = base + shard * piece
            out[group, at : at + piece, :] = jnp.concatenate(blocks, axis=0).astype(BF)
    base += shards * piece
    out[:, base : base + shared.shape[1], :] = shared[...]
    for group in range(groups):
        out[group, base + shared.shape[1] :, :] = lines[...]


def pack_tiles(scal, slot, mats, sides, shared, lines, slots_each, per_layer, shards, heads):
    groups = shared.shape[0]
    layers = len(sides)
    depth, width = sides[0].shape
    extra = layers * depth * width // (groups * LANES) + shared.shape[1] + lines.shape[0]
    return call(
        functools.partial(pack_kernel, slots_each, per_layer, layers, shards, heads),
        "packtiles",
        sds((groups, slots_each * BLK + extra, LANES), BF),
        (scal, slot, *mats, *sides, shared, lines),
        smem=(0, 1),
        scratch=[pltpu.VMEM((layers, depth, width), F32)],
        moved=14 * MIB,
    )


def norm_rows(values, gain):
    return values * lax.rsqrt(jnp.mean(values * values, axis=-1, keepdims=True) + NORM_EPS) * gain


def total_of(parts):
    total = parts[0][...].astype(F32)
    for part in parts[1:]:
        total = total + part[...].astype(F32)
    return total


def send(source, target, send_sem, recv_sem, device):
    copy = pltpu.make_async_remote_copy(
        src_ref=source,
        dst_ref=target,
        send_sem=send_sem,
        recv_sem=recv_sem,
        device_id=device,
        device_id_type=pl.DeviceIdType.MESH,
    )
    copy.start()
    return copy


def greet_shards(groups, shards, rims, wide=False):
    place, shard = lax.axis_index("dp"), lax.axis_index("tensor")
    last = shard == shards - 1
    barrier = pltpu.get_barrier_semaphore()

    def greet(device):
        pl.semaphore_signal(barrier, inc=1, device_id=device, device_id_type=pl.DeviceIdType.MESH)

    for off in range(1, shards):
        greet((place, shard ^ off))
    if not rims:
        pl.semaphore_wait(barrier, shards - 1)
        return
    if wide:
        for off in range(1, groups):
            greet((place ^ off, shard))

        @pl.when(jnp.logical_not(last))
        def _():
            greet((lax.rem(place + groups - 1, groups), shards - 1))

        @pl.when(last)
        def _():
            for other in range(shards - 1):
                greet((lax.rem(place + 1, groups), other))

        pl.semaphore_wait(barrier, shards + groups - 2 + jnp.where(last, shards - 1, 1))
        return
    greet((lax.rem(place + groups - 1, groups), shards - 1))

    @pl.when(last)
    def _():
        for other in range(shards):
            greet((lax.rem(place + 1, groups), other))

    pl.semaphore_wait(barrier, shards - 1 + jnp.where(last, shards + 1, 1))


def pass_along(rows, own, base, shards, sems):
    place, shard = lax.axis_index("dp"), lax.axis_index("tensor")

    def copy(way, hop, source, to):
        at = pl.ds(pl.multiple_of(base + source * own, RIM), own)
        return pltpu.make_async_remote_copy(
            src_ref=rows.at[at, :],
            dst_ref=rows.at[at, :],
            send_sem=sems.at[0, way, hop],
            recv_sem=sems.at[1, way, hop],
            device_id=(place, to),
            device_id_type=pl.DeviceIdType.MESH,
        )

    def up(hop):
        return copy(0, hop, shard - hop, shard + 1)

    def down(hop):
        return copy(1, hop, shard + hop, shard - 1)

    can_up, can_down = shard + 1 < shards, shard > 0
    for hop in range(shards):
        if hop > 0:

            @pl.when(shard - hop >= 0)
            def _():
                copy(0, hop - 1, shard - hop, shard - 1).wait_recv()

        if hop < shards - 1:

            @pl.when(jnp.logical_and(shard - hop >= 0, can_up))
            def _():
                up(hop).start()

        if hop > 0:

            @pl.when(shard + hop < shards)
            def _():
                copy(1, hop - 1, shard + hop, shard + 1).wait_recv()

        if hop < shards - 1:

            @pl.when(jnp.logical_and(shard + hop < shards, can_down))
            def _():
                down(hop).start()

    for hop in range(shards - 1):

        @pl.when(jnp.logical_and(shard - hop >= 0, can_up))
        def _():
            up(hop).wait_send()

        @pl.when(jnp.logical_and(shard + hop < shards, can_down))
        def _():
            down(hop).wait_send()


def exchange_terms(parts, slots, work, sems, ready=None):
    place, shard = lax.axis_index("dp"), lax.axis_index("tensor")
    shards = len(parts)

    def copy(off, source, to, slot):
        return pltpu.make_async_remote_copy(
            src_ref=source,
            dst_ref=slots.at[slot],
            send_sem=sems.at[0, off],
            recv_sem=sems.at[1, slot],
            device_id=(place, to),
            device_id_type=pl.DeviceIdType.MESH,
        )

    def direct(off):
        return copy(off, parts[off], shard ^ off, off)

    if shards != 4:
        for off in reversed(range(1, shards)):
            if ready:
                ready(off)
            direct(off).start()
        if ready:
            ready(0)
        for off in range(1, shards):
            direct(off).wait()
        total = parts[0][...].astype(F32)
        for off in range(1, shards):
            total = total + slots[off].astype(F32)
        work[...] = total
        return
    relay, added = 0, 4
    outer = jnp.logical_or(shard == 0, shard == shards - 1)
    inner = jnp.logical_not(outer)

    def pass_relayed():
        copy(0, parts[3], shard ^ 1, relay).wait_recv()
        slots[added] = (slots[relay].astype(F32) + parts[2][...].astype(F32)).astype(BF)
        copy(2, slots.at[added], shard ^ 2, 2).start()

    if ready:
        ready(3)

        @pl.when(outer)
        def _():
            copy(3, parts[3], shard ^ 1, relay).start()

        @pl.when(inner)
        def _():
            direct(3).start()

        ready(2)

        @pl.when(outer)
        def _():
            direct(2).start()

        @pl.when(inner)
        def _():
            pass_relayed()

        ready(1)
        direct(1).start()
        ready(0)
    else:

        @pl.when(outer)
        def _():
            copy(3, parts[3], shard ^ 1, relay).start()
            direct(2).start()
            direct(1).start()

        @pl.when(inner)
        def _():
            direct(3).start()
            direct(1).start()
            pass_relayed()

    direct(1).wait_recv()
    total = parts[0][...].astype(F32) + slots[1].astype(F32)
    direct(2).wait_recv()
    work[...] = total + slots[2].astype(F32)

    @pl.when(inner)
    def _():
        direct(3).wait_recv()
        work[...] += slots[3].astype(F32)

    for off in range(1, shards):
        direct(off).wait_send()


def term_scratch(shards, own, width):
    return [
        pltpu.VMEM((shards + 1, own, width), BF),
        pltpu.VMEM((own, width), F32),
        pltpu.SemaphoreType.DMA((2, shards + 1)),
    ]


def forward_kernel(groups, shards, chunks, packed, rims, *refs):
    ready = None
    place, shard = lax.axis_index("dp"), lax.axis_index("tensor")
    if packed:
        parts, refs = refs[:shards], refs[shards:]
        before, gain, residual, branch, factor, normed, *refs = refs
        slots, work, term_sems, row_sems, rim_sems = refs
        own = parts[0].shape[0]
        greet_shards(groups, shards, rims)
    else:
        looked, refs = refs[:groups], refs[groups:]
        gain, residual, normed, *refs = refs
        slots, work, term_sems, row_sems, rim_sems, arrived, terms, look_sems = refs
        own = terms.shape[1]
        half, cols = groups // 2, looked[0].shape[1]
        parts = [terms.at[off] for off in range(shards)]
        greet_shards(groups, shards, rims, True)

        def block(off):
            return pl.ds(pl.multiple_of((shard ^ off) * own, own), own)

        copies = {
            (off, other): send(
                looked[other].at[block(off), :],
                arrived.at[off, other],
                look_sems.at[0, off, other],
                look_sems.at[1, off, other],
                (place ^ other, shard),
            )
            for off in reversed(range(shards))
            for other in range(1, groups)
        }

        def ready(off):
            for other in range(1, groups):
                copies[off, other].wait()
            arrived[off, 0] = looked[0][block(off), :]
            for other in range(half):
                at = pl.multiple_of(lax.rem(place ^ other, half) * cols, cols)
                terms[off, :, pl.ds(at, cols)] = arrived[off, other] + arrived[off, other + half]

    rows = own * shards
    chunk = lax.rem(place, chunks)
    exchange_terms(parts, slots, work, term_sems, ready)
    total = work[...]
    if packed:
        scale = lax.rsqrt(column3(total[:, D:]) / DI + NORM_EPS)
        branch[...] = total[:, :D]
        factor[...] = scale
        total = before[...] + scale * total[:, :D]
    residual[...] = total
    at = pl.ds(pl.multiple_of(RIM + shard * own, RIM), own)
    normed[at, :] = norm_rows(total, gain[...]).astype(BF)

    def rim_copy(to, device):
        return pltpu.make_async_remote_copy(
            src_ref=normed.at[rows : rows + RIM, :],
            dst_ref=normed.at[0:RIM, :],
            send_sem=rim_sems.at[0, to],
            recv_sem=rim_sems.at[1, 0],
            device_id=device,
            device_id_type=pl.DeviceIdType.MESH,
        )

    gives = jnp.logical_and(shard == shards - 1, chunk + 1 < chunks)
    if rims:

        @pl.when(gives)
        def _():
            for to in range(shards):
                rim_copy(to, (place + 1, to)).start()

        @pl.when(chunk == 0)
        def _():
            normed[0:RIM, :] = jnp.zeros((RIM, D), BF)

    else:
        normed[0:RIM, :] = jnp.zeros((RIM, D), BF)
    pass_along(normed, own, RIM, shards, row_sems)
    if rims:

        @pl.when(chunk > 0)
        def _():
            rim_copy(0, (place - 1, shards - 1)).wait_recv()

        @pl.when(gives)
        def _():
            for to in range(shards):
                rim_copy(to, (place + 1, to)).wait_send()


def forward_rows(parts, before, gain, groups, chunks, rims, cid, entry=0):
    packed = before is not None
    if packed:
        shards = len(parts)
        own, width = parts[0].shape
        args = (*parts, before, gain)
        extra = []
    else:
        shards = entry
        own, width = parts[0].shape[0] // shards, D
        args = (*parts, gain)
        extra = [
            pltpu.VMEM((shards, groups, own, parts[0].shape[1]), BF),
            pltpu.VMEM((shards, own, D), BF),
            pltpu.SemaphoreType.DMA((2, shards, groups)),
        ]
    vmem = pl.BlockSpec(memory_space=pltpu.VMEM)
    outs = [sds((own, D), F32)]
    if packed:
        outs += [sds((own, D), F32), sds((own, 1), F32)]
    outs += [sds((RIM + own * shards, D), BF)]
    return pl.pallas_call(
        functools.partial(forward_kernel, groups, shards, chunks, packed, rims),
        out_shape=outs,
        in_specs=[vmem] * len(args),
        out_specs=[vmem] * len(outs),
        scratch_shapes=[
            *term_scratch(shards, own, width),
            pltpu.SemaphoreType.DMA((2, 2, shards)),
            pltpu.SemaphoreType.DMA((2, shards)),
            *extra,
        ],
        compiler_params=pltpu.CompilerParams(
            collective_id=cid, has_side_effects=True, vmem_limit_bytes=60 * MIB
        ),
        name="forward" if packed else "enter",
    )(*args)


def backward_kernel(groups, shards, chunks, exchanged, *refs):
    parts, refs = refs[:shards], refs[shards:]
    if exchanged:
        residual, gain, branch, factor, grad_out, rows_out, gain_grad, row_sems = refs
    else:
        rim, residual, gain, grad_in, branch, factor, grad_out, rows_out, refs = *refs[:8], refs[8:]
        slots, work, term_sems, from_rims, rim_sems, row_sems = refs
    own = parts[0].shape[0]
    place, shard = lax.axis_index("dp"), lax.axis_index("tensor")
    chunk = lax.rem(place, chunks)
    greet_shards(groups, shards, not exchanged)
    values = residual[...]
    inv = lax.rsqrt(jnp.mean(values * values, axis=-1, keepdims=True) + NORM_EPS)
    if exchanged:
        grad = total_of(parts)
        gain_grad[...] = jnp.sum(grad * values * inv, axis=0, keepdims=True)
    else:

        def rim_copy(slot, device):
            return pltpu.make_async_remote_copy(
                src_ref=rim,
                dst_ref=from_rims.at[slot],
                send_sem=rim_sems.at[0, slot],
                recv_sem=rim_sems.at[1, slot],
                device_id=device,
                device_id_type=pl.DeviceIdType.MESH,
            )

        @pl.when(chunk > 0)
        def _():
            rim_copy(shard, (place - 1, shards - 1)).start()

        exchange_terms(parts, slots, work, term_sems)

        @pl.when(jnp.logical_and(shard == shards - 1, chunk + 1 < chunks))
        def _():
            for other in range(shards):
                rim_copy(other, (place + 1, other)).wait_recv()
            edge = from_rims[0].astype(F32)
            for other in range(1, shards):
                edge = edge + from_rims[other].astype(F32)
            work[own - RIM :, :] += edge

        @pl.when(chunk > 0)
        def _():
            rim_copy(shard, (place - 1, shards - 1)).wait_send()

        grad = work[...]
    scaled = grad * gain[...]
    result = inv * scaled - values * (inv * inv * inv) * jnp.mean(
        scaled * values, axis=-1, keepdims=True
    )
    if not exchanged:
        result = grad_in[...] + result
    grad_out[...] = result
    scale = factor[...]
    at = pl.ds(pl.multiple_of(shard * own, RIM), own)
    rows_out[at, :D] = (scale * result).astype(BF)
    inner_rows = jnp.sum(result * branch[...], axis=-1, keepdims=True)
    rows_out[at, D:] = lanes3(scale * scale * scale * inner_rows / DI)
    pass_along(rows_out, own, 0, shards, row_sems)


def backward_rows(parts, rim, residual, gain, grad_in, branch, factor, groups, chunks, cid):
    shards = len(parts)
    own = residual.shape[0]
    exchanged = rim is None
    vmem = pl.BlockSpec(memory_space=pltpu.VMEM)
    outs = [sds((own, D), F32), sds((own * shards, D + LANES), BF)]
    row_sems = pltpu.SemaphoreType.DMA((2, 2, shards))
    if exchanged:
        args = (*parts, residual, gain, branch, factor)
        outs.append(sds((1, D), F32))
        scratch = [row_sems]
    else:
        args = (*parts, rim, residual, gain, grad_in, branch, factor)
        scratch = [
            *term_scratch(shards, own, D),
            pltpu.VMEM((shards, RIM, D), BF),
            pltpu.SemaphoreType.DMA((2, shards)),
            row_sems,
        ]
    return pl.pallas_call(
        functools.partial(backward_kernel, groups, shards, chunks, exchanged),
        out_shape=outs,
        in_specs=[vmem] * len(args),
        out_specs=[vmem] * len(outs),
        scratch_shapes=scratch,
        compiler_params=pltpu.CompilerParams(
            collective_id=cid, has_side_effects=True, vmem_limit_bytes=60 * MIB
        ),
        name="backward",
    )(*args)


def stats_kernel(shards, chunks, stats, tops, weight, scale_out, loss_out, slots, sems):
    place, shard = lax.axis_index("dp"), lax.axis_index("tensor")
    rows = weight.shape[1]
    own = rows // shards
    greet_shards(0, shards, False)
    copies = [
        send(stats, slots.at[off - 1], sems.at[0, off], sems.at[1, off], (place, shard ^ off))
        for off in range(1, shards)
    ]
    for copy in copies:
        copy.wait()
    others = [stats[...]] + [slots[off] for off in range(shards - 1)]
    best = others[0][0:1, :]
    for one in others[1:]:
        best = jnp.maximum(best, one[0:1, :])
    summed, target, plain = jnp.zeros((1, rows), F32), jnp.zeros((1, rows), F32), jnp.zeros((1, rows), F32)
    for one in others:
        summed = summed + one[1:2, :] * jnp.exp(one[0:1, :] - best)
        target = target + one[2:3, :]
        plain = plain + one[3:4, :]
    log_total = best + jnp.log(summed)
    token_loss = (
        log_total
        - (1.0 - SMOOTHING) * target
        - SMOOTHING / V * plain
        + ZLOSS_WEIGHT * log_total * log_total
    )
    lane = iota((1, rows), 1)
    mine = jnp.logical_and(lane >= shard * own, lane < (shard + 1) * own)
    loss = jnp.sum(jnp.where(mine, weight[...] * token_loss, 0.0), axis=1, keepdims=True)
    here = jnp.logical_and(iota((8, LANES), 0) == 0, iota((8, LANES), 1) == place // chunks)
    loss_out[...] = jnp.where(here, loss, 0.0)
    soft = weight[...] * (1.0 + 2.0 * ZLOSS_WEIGHT * log_total)
    for step in range(tops.shape[0]):
        scale_out[step] = soft * jnp.exp(tops[step] - log_total)


def merge_stats(stats, tops, weight, shards, chunks):
    vmem = pl.BlockSpec(memory_space=pltpu.VMEM)
    return pl.pallas_call(
        functools.partial(stats_kernel, shards, chunks),
        out_shape=[sds(tops.shape, F32), sds((8, LANES), F32)],
        in_specs=[vmem] * 3,
        out_specs=[vmem] * 2,
        scratch_shapes=[
            pltpu.VMEM((shards - 1, *stats.shape), F32),
            pltpu.SemaphoreType.DMA((2, shards)),
        ],
        compiler_params=pltpu.CompilerParams(
            collective_id=9, has_side_effects=True, vmem_limit_bytes=8 * MIB
        ),
        name="stats",
    )(stats, tops, weight)


def finish_kernel(groups, shards, chunks, own, *refs):
    parts, rim, residual, gain, grad_in, out = refs[:shards], *refs[shards : shards + 5]
    slots, work, term_sems, from_rims, payload, full, rim_sems, row_sems, out_sems = refs[shards + 5 :]
    place, shard = lax.axis_index("dp"), lax.axis_index("tensor")
    half = groups // 2
    cols = out.shape[2]
    chunk = lax.rem(place, chunks)
    last = shard == shards - 1
    shard_peers = [(place, shard ^ off) for off in range(1, shards)]
    group_peers = [(place ^ off, shard) for off in range(1, groups)]
    barrier = pltpu.get_barrier_semaphore()

    def greet(device):
        pl.semaphore_signal(barrier, inc=1, device_id=device, device_id_type=pl.DeviceIdType.MESH)

    for peer in shard_peers + group_peers:
        greet(peer)

    @pl.when(jnp.logical_not(last))
    def _():
        greet((lax.rem(place + groups - 1, groups), shards - 1))

    @pl.when(last)
    def _():
        for other in range(shards - 1):
            greet((lax.rem(place + 1, groups), other))

    pl.semaphore_wait(barrier, shards + groups - 2 + jnp.where(last, shards - 1, 1))

    def rim_copy():
        return pltpu.make_async_remote_copy(
            src_ref=rim,
            dst_ref=from_rims.at[shard],
            send_sem=rim_sems.at[0, shard],
            recv_sem=rim_sems.at[1, shard],
            device_id=(place - 1, shards - 1),
            device_id_type=pl.DeviceIdType.MESH,
        )

    @pl.when(chunk > 0)
    def _():
        rim_copy().start()

    values = residual[...]
    inv = lax.rsqrt(jnp.mean(values * values, axis=-1, keepdims=True) + NORM_EPS)
    exchange_terms(parts, slots, work, term_sems)

    @pl.when(jnp.logical_and(chunk + 1 < chunks, last))
    def _():
        for other in range(shards):
            pltpu.make_async_remote_copy(
                src_ref=rim,
                dst_ref=from_rims.at[other],
                send_sem=rim_sems.at[0, other],
                recv_sem=rim_sems.at[1, other],
                device_id=(place + 1, other),
                device_id_type=pl.DeviceIdType.MESH,
            ).wait_recv()
        edge = from_rims[0].astype(F32)
        for other in range(1, shards):
            edge = edge + from_rims[other].astype(F32)
        work[own - RIM :, :] += edge

    @pl.when(chunk > 0)
    def _():
        rim_copy().wait_send()

    scaled = work[...] * gain[...]
    result = (
        grad_in[...]
        + inv * scaled
        - values * (inv * inv * inv) * jnp.mean(scaled * values, axis=-1, keepdims=True)
    ).astype(BF)
    payload[...] = result
    rows_out = [
        send(
            payload,
            full.at[off],
            row_sems.at[0, off],
            row_sems.at[1, off],
            shard_peers[off - 1],
        )
        for off in range(1, shards)
    ]
    full[0] = result

    def first_col(group):
        return pl.multiple_of(lax.rem(group, half) * cols, cols)

    cuts = []
    for off in range(shards):
        if off > 0:
            rows_out[off - 1].wait()
        at = pl.ds(pl.multiple_of((shard ^ off) * own, own), own)
        for other in range(1, groups):
            cuts.append(
                send(
                    full.at[off, :, pl.ds(first_col(place ^ other), cols)],
                    out.at[other, at, :],
                    out_sems.at[0, off, other],
                    out_sems.at[1, off, other],
                    group_peers[other - 1],
                )
            )
        out[0, at, :] = full[off, :, pl.ds(first_col(place), cols)]
    for cut in cuts:
        cut.wait()


def finish_rows(parts, rim, residual, gain, grad_in, groups, chunks):
    shards = len(parts)
    own = parts[0].shape[0]
    vmem = pl.BlockSpec(memory_space=pltpu.VMEM)
    args = (*parts, rim, residual, gain, grad_in)
    return pl.pallas_call(
        functools.partial(finish_kernel, groups, shards, chunks, own),
        out_shape=sds((groups, own * shards, 2 * D // groups), BF),
        in_specs=[vmem] * len(args),
        out_specs=vmem,
        scratch_shapes=[
            *term_scratch(shards, own, D),
            pltpu.VMEM((shards, RIM, D), BF),
            pltpu.VMEM((own, D), BF),
            pltpu.VMEM((shards, own, D), BF),
            pltpu.SemaphoreType.DMA((2, shards)),
            pltpu.SemaphoreType.DMA((2, shards)),
            pltpu.SemaphoreType.DMA((2, shards, groups)),
        ],
        compiler_params=pltpu.CompilerParams(
            collective_id=3, has_side_effects=True, vmem_limit_bytes=60 * MIB
        ),
        name="finish",
    )(*args)


def open_kernel(groups, shards, ids, piece, share, ids_out, pieces_out, share_out, middle, sends, gets):
    place, shard = lax.axis_index("dp"), lax.axis_index("tensor")
    near = [(place, shard ^ off) for off in range(1, shards)]
    far = [(place ^ off, shard) for off in range(1, groups)]
    barrier = pltpu.get_barrier_semaphore()
    for peer in near + far:
        pl.semaphore_signal(barrier, inc=1, device_id=peer, device_id_type=pl.DeviceIdType.MESH)
    pl.semaphore_wait(barrier, len(near) + len(far))
    shares, others = [], []
    for i, peer in enumerate(near):
        shares.append(send(share, middle.at[shard], sends.at[0, i], gets.at[0, i], peer))
    for i, peer in enumerate(far):
        others.append(send(ids, ids_out.at[place], sends.at[1, i], gets.at[1, i], peer))
    for i, peer in enumerate(near):
        others.append(send(piece, pieces_out.at[shard], sends.at[2, i], gets.at[2, i], peer))
    middle[shard] = share[...]
    ids_out[place] = ids[...]
    pieces_out[shard] = piece[...]
    for copy in shares:
        copy.wait()
    for i, peer in enumerate(far):
        others.append(send(middle, share_out.at[place], sends.at[3, i], gets.at[3, i], peer))
    share_out[place] = middle[...]
    for copy in others:
        copy.wait()


def open_exchange(ids, piece, share, groups, shards):
    count = max(groups, shards)
    vmem = pl.BlockSpec(memory_space=pltpu.VMEM)
    return pl.pallas_call(
        functools.partial(open_kernel, groups, shards),
        out_shape=[
            sds((groups, *ids.shape), jnp.int32),
            sds((shards, *piece.shape), BF),
            sds((groups, shards, *share.shape), BF),
        ],
        in_specs=[vmem] * 3,
        out_specs=[vmem] * 3,
        scratch_shapes=[
            pltpu.VMEM((shards, *share.shape), BF),
            pltpu.SemaphoreType.DMA((4, count)),
            pltpu.SemaphoreType.DMA((4, count)),
        ],
        compiler_params=pltpu.CompilerParams(
            collective_id=2, has_side_effects=True, vmem_limit_bytes=8 * MIB
        ),
        name="open",
    )(ids, piece, share)


def sum_kernel(groups, shards, once, split, *refs):
    loss = refs[0]
    refs = refs[1:]
    count = once + split
    ones, many, refs = refs[:once], refs[once:count], refs[count:]
    o_ref, start, mid, from_shards, from_groups, send, recv = refs
    place, shard = lax.axis_index("dp"), lax.axis_index("tensor")
    peers = [(place, shard ^ off) for off in range(1, shards)]
    peers += [(place ^ off, shard) for off in range(1, groups)]
    barrier = pltpu.get_barrier_semaphore()
    for peer in peers:
        pl.semaphore_signal(barrier, inc=1, device_id=peer, device_id_type=pl.DeviceIdType.MESH)

    def square(refs):
        total = jnp.zeros((1, 1), F32)
        for ref in refs:
            flat = jnp.sum(ref[...] * ref[...], axis=0, keepdims=True)
            total = total + jnp.sum(flat, axis=1, keepdims=True)
        return total

    first = (place == 0).astype(F32)
    part = square(many) + first * square(ones)
    start[...] = loss[...] + jnp.where(iota((8, LANES), 1) == LANES - 1, part, 0.0)
    pl.semaphore_wait(barrier, len(peers))

    def exchange(source, slots, first, some):
        copies = []
        for i, peer in enumerate(some):
            copy = pltpu.make_async_remote_copy(
                src_ref=source,
                dst_ref=slots.at[i],
                send_sem=send.at[first + i],
                recv_sem=recv.at[first + i],
                device_id=peer,
                device_id_type=pl.DeviceIdType.MESH,
            )
            copy.start()
            copies.append(copy)
        for copy in copies:
            copy.wait()
        total = source[...]
        for i in range(len(some)):
            total = total + slots[i]
        return total

    mid[...] = exchange(start, from_shards, 0, peers[: shards - 1])
    total = exchange(mid, from_groups, shards - 1, peers[shards - 1 :])
    norm = jnp.sqrt(total[0:1, LANES - 1 : LANES])
    factor = jnp.minimum(1.0, CLIP_LIMIT / (norm + 1e-06))
    row = iota((8, LANES), 0)
    o_ref[...] = jnp.where(row == 0, total, jnp.where(row == 1, norm, factor))


def sum_everywhere(loss, ones, many, groups, shards):
    count = groups + shards - 2
    args = (loss, *ones, *many)
    vmem = pl.BlockSpec(memory_space=pltpu.VMEM)
    return pl.pallas_call(
        functools.partial(sum_kernel, groups, shards, len(ones), len(many)),
        out_shape=sds((8, LANES), F32),
        in_specs=[vmem] * len(args),
        out_specs=vmem,
        scratch_shapes=[
            pltpu.VMEM((8, LANES), F32),
            pltpu.VMEM((8, LANES), F32),
            pltpu.VMEM((shards - 1, 8, LANES), F32),
            pltpu.VMEM((groups - 1, 8, LANES), F32),
            pltpu.SemaphoreType.DMA((count,)),
            pltpu.SemaphoreType.DMA((count,)),
        ],
        compiler_params=pltpu.CompilerParams(
            collective_id=1, has_side_effects=True, vmem_limit_bytes=8 * MIB
        ),
        name="sumall",
    )(*args)


def conv_sum(raw, params, rows, lanes):
    total = params[4:5, :] + params[0:1, :] * raw[pl.ds(RIM - 3, rows), lanes]
    for k in range(1, 4):
        total = total + params[k : k + 1, :] * raw[pl.ds(RIM - 3 + k, rows), lanes]
    return total


def front_kernel(normed, wzx, wside, chan, bcp, head, *rest):
    zx, side, yloc, final, c_out, cum_out, xs_scr = rest
    rows = normed.shape[0] - RIM
    inner = chan.shape[1]
    zx[...] = nn(normed[...], wzx[...])
    side[...] = nn(normed[...], wside[...])
    pre = conv_sum(zx, chan, rows, pl.ds(inner, inner))
    xs_scr[...] = pre * sigmoid(pre)
    pre = conv_sum(side, bcp, rows, pl.ds(0, 2 * N))
    bc = (pre * sigmoid(pre)).astype(BF)
    c_out[...] = bc[:, N:]
    dt = softplus(side[RIM:, 2 * N :] + head[0:1, :])
    rate = -dt * jnp.exp(head[1:2, :])
    expand = head_map(inner)
    skip = widen(head[...], expand)[2:3, :]
    lower = (iota((SPAN, SPAN), 0) >= iota((SPAN, SPAN), 1)).astype(F32)
    lower_low = lower.astype(BF)
    first_half = iota((SPAN, LANES), 1) < P_SIZE
    state = None
    base = jnp.zeros((1, LANES), F32)
    for span in range(rows // SPAN):
        here = slice(span * SPAN, (span + 1) * SPAN)
        cum = tri_sum(lower_low, rate[here])
        cum_t = cum.T
        tot = cum[SPAN - 1 : SPAN, :]
        keys = bc[here, :N]
        queries = bc[here, N:]
        scores = nt_dot(queries, keys)
        xs = xs_scr[here, :]
        scaled = xs * widen(dt[here], expand)
        scaled_low = scaled.astype(BF)
        pieces = []
        for pair in range(inner // LANES):
            values = scaled_low[:, pair * LANES : (pair + 1) * LANES]
            both = []
            for h in (2 * pair, 2 * pair + 1):
                gap = cum[:, h : h + 1] - cum_t[h : h + 1, :]
                decay = jnp.exp(jnp.minimum(gap, 0.0)) * lower
                both.append(nn((scores * decay).astype(BF), values))
            pieces.append(jnp.where(first_half, both[0], both[1]))
        y = jnp.concatenate(pieces, axis=1) + skip * xs
        if state is not None:
            y = y + widen(jnp.exp(cum), expand) * nn(queries, state.astype(BF))
        yloc[here, :] = y
        tail = widen(jnp.exp(tot - cum), expand)
        fresh = tn(keys, (scaled * tail).astype(BF))
        if state is not None:
            fresh = fresh + widen(jnp.exp(tot), expand) * state
        state = fresh
        cum_out[here, :] = cum + base
        base = base + tot
    final[0:N, :] = state.astype(BF)
    final[N:, :] = rows3(base, inner)


def mixer_front(normed, wzx, wside, chan, bcp, head):
    rows = normed.shape[0] - RIM
    inner = chan.shape[1]
    return call(
        front_kernel,
        "front",
        [
            sds((rows + RIM, 2 * inner), F32),
            sds((rows + RIM, 2 * N + LANES), F32),
            sds((rows, inner), F32),
            sds((N + RIM, inner), BF),
            sds((rows, N), BF),
            sds((rows, LANES), F32),
        ],
        (normed, wzx, wside, chan, bcp, head),
        scratch=[pltpu.VMEM((rows, inner), F32)],
        flops=8 * rows * D * inner,
        moved=12 * MIB,
    )


def chain(parts, expand):
    total = None
    past = jnp.zeros((1, LANES), F32)
    for part in parts:
        term = widen(jnp.exp(past), expand) * part[0:N, :].astype(F32)
        total = term if total is None else total + term
        past = past + jnp.sum(part[N:, :LANES].astype(F32), axis=0, keepdims=True)
    return total


def middle_kernel(shards, own, hops, scal, *rest):
    states, rest = rest[:hops], rest[hops:]
    yloc, zx, c_in, cum, wout, chan = rest[:6]
    y_out, s_out = rest[6:8]
    parts, work = rest[8 : 8 + shards], rest[-1]
    shard = scal[0]
    rows, inner = yloc.shape
    expand = head_map(inner)
    state = chain(states, expand)
    s_out[...] = state
    y = yloc[...] + widen(jnp.exp(cum[...]), expand) * nn(c_in[...], state.astype(BF))
    y_out[...] = y
    z = zx[RIM:, :inner]
    gated = y * (z * sigmoid(z))
    work[:, :D] = nn((gated * chan[5:6, :]).astype(BF), wout[...]).astype(BF)
    work[:, D:] = lanes3(jnp.sum(gated * gated, axis=1, keepdims=True))
    for off in range(shards):
        at = pl.multiple_of((shard ^ off) * own, own)
        parts[off][...] = work[pl.ds(at, own), :]


def mixer_middle(scal, states, yloc, zx, c_in, cum, wout, chan, shards):
    rows, inner = yloc.shape
    own = rows // shards
    return call(
        functools.partial(middle_kernel, shards, own, len(states)),
        "middle",
        [sds((rows, inner), F32), sds((N, inner), F32)]
        + [sds((own, D + LANES), BF)] * shards,
        (scal, *states, yloc, zx, c_in, cum, wout, chan),
        smem=(0,),
        scratch=[pltpu.VMEM((rows, D + LANES), BF)],
        flops=2 * rows * D * inner,
        moved=8 * MIB,
    )


def gate_back_kernel(grads, wout, y_in, zx, c_in, cum, chan, *rest):
    u_out, dy_out, dz_out, state_out, gain_out = rest
    inner = chan.shape[1]
    du = nt_dot(grads[:, :D], wout[...])
    coef = column3(grads[:, D:].astype(F32))
    z = zx[RIM:, :inner]
    y = y_in[...]
    sig = sigmoid(z)
    silu = z * sig
    gated = y * silu
    gain_out[...] = jnp.sum(du * gated, axis=0, keepdims=True)
    gain = chan[5:6, :]
    u_out[...] = (gated * gain).astype(BF)
    dgated = du * gain - gated * coef
    dy = dgated * silu
    dy_out[...] = dy
    dz_out[...] = (dgated * y * (sig * (1.0 + z * (1.0 - sig)))).astype(BF)
    grown = widen(jnp.exp(cum[...]), head_map(inner))
    state_out[0:N, :] = tn(c_in[...], (dy * grown).astype(BF)).astype(BF)
    rows = dy.shape[0]
    state_out[N:, :] = rows3(cum[rows - 1 : rows, :], inner)


def gate_back(grads, wout, y, zx, c_in, cum, chan):
    rows, inner = y.shape
    return call(
        gate_back_kernel,
        "gateback",
        [
            sds((rows, inner), BF),
            sds((rows, inner), F32),
            sds((rows, inner), BF),
            sds((N + RIM, inner), BF),
            sds((1, inner), F32),
        ],
        (grads, wout, y, zx, c_in, cum, chan),
        flops=2 * rows * D * inner,
        moved=10 * MIB,
    )


def silu_slope(pre):
    sig = sigmoid(pre)
    return sig * (1.0 + pre * (1.0 - sig))


def conv_back(ds_scr, raw, params, rows, lanes, width, low_out, out_lanes):
    ext = rows + RIM
    total = params[0:1, :] * ds_scr[pl.ds(3, ext), :]
    for k in range(1, 4):
        total = total + params[k : k + 1, :] * ds_scr[pl.ds(3 - k, ext), :]
    low_out[:, out_lanes] = total.astype(BF)
    ds = ds_scr[pl.ds(RIM, rows), :]
    grads = [
        jnp.sum(ds * raw[pl.ds(RIM - 3 + k, rows), lanes], axis=0, keepdims=True) for k in range(4)
    ]
    grads.append(jnp.sum(ds, axis=0, keepdims=True))
    grads.append(jnp.zeros((3, width), F32))
    return jnp.concatenate(grads, axis=0)


def within_kernel(s_in, zx, side, dy_in, chan, bcp, head, *outs):
    xs_out, bc_out, cum_out, starts_out, dscaled_out, dbc_out = outs
    rows, inner = dy_in.shape
    expand = head_map(inner)
    pre_x = conv_sum(zx, chan, rows, pl.ds(inner, inner))
    xs_out[...] = pre_x * sigmoid(pre_x)
    pre_bc = conv_sum(side, bcp, rows, pl.ds(0, 2 * N))
    bc = (pre_bc * sigmoid(pre_bc)).astype(BF)
    bc_out[...] = bc
    dt = softplus(side[RIM:, 2 * N :] + head[0:1, :])
    rate = -dt * jnp.exp(head[1:2, :])
    lower_low = (iota((SPAN, SPAN), 0) >= iota((SPAN, SPAN), 1)).astype(F32).astype(BF)
    upper = (iota((SPAN, SPAN), 0) <= iota((SPAN, SPAN), 1)).astype(F32)
    first_half = iota((SPAN, LANES), 1) < P_SIZE
    spans = rows // SPAN
    start = s_in[...]
    for span in range(spans):
        here = slice(span * SPAN, (span + 1) * SPAN)
        cum = tri_sum(lower_low, rate[here])
        cum_out[here, :] = cum
        cum_t = cum.T
        keys = bc[here, :N]
        queries = bc[here, N:]
        xs = xs_out[here, :]
        starts_out[span] = start
        start_low = start.astype(BF)
        if span + 1 < spans:
            tot = cum[SPAN - 1 : SPAN, :]
            scale = widen(dt[here] * jnp.exp(tot - cum), expand)
            fresh = tn(keys, (xs * scale).astype(BF))
            start = widen(jnp.exp(tot), expand) * start + fresh
        scores_t = nt_dot(keys, queries)
        dy = dy_in[here, :]
        dy_low = dy.astype(BF)
        scaled_low = (xs * widen(dt[here], expand)).astype(BF)
        dscores_t = jnp.zeros((SPAN, SPAN), F32)
        for pair in range(inner // LANES):
            lanes = slice(pair * LANES, (pair + 1) * LANES)
            values = scaled_low[:, lanes]
            dpair = dy_low[:, lanes]
            both = []
            for h in (2 * pair, 2 * pair + 1):
                gap = cum_t[h : h + 1, :] - cum[:, h : h + 1]
                decay = jnp.exp(jnp.minimum(gap, 0.0)) * upper
                mine = first_half if h % 2 == 0 else jnp.logical_not(first_half)
                outer = nt_dot(jnp.where(mine, values, jnp.zeros_like(values)), dpair)
                dscores_t = dscores_t + outer * decay
                both.append(nn((scores_t * decay).astype(BF), dpair))
            dscaled_out[here, lanes] = jnp.where(first_half, both[0], both[1])
        dscores_low = dscores_t.astype(BF)
        dy_grown = (dy * widen(jnp.exp(cum), expand)).astype(BF)
        dbc_out[here, :N] = nn(dscores_low, queries)
        dbc_out[here, N:] = tn(dscores_low, keys) + nt_dot(dy_grown, start_low)


def mixer_within(s_in, zx, side, dy, chan, bcp, head):
    rows, inner = dy.shape
    return call(
        within_kernel,
        "within",
        [
            sds((rows, inner), F32),
            sds((rows, 2 * N), BF),
            sds((rows, LANES), F32),
            sds((rows // SPAN, N, inner), F32),
            sds((rows, inner), F32),
            sds((rows, 2 * N), F32),
        ],
        (s_in, zx, side, dy, chan, bcp, head),
        flops=8 * rows * D * inner,
        moved=16 * MIB,
    )


def back_kernel(shards, own, hops, scal, *rest):
    states, rest = rest[:hops], rest[hops:]
    xs_in, bc_in, cum_in, starts, dscaled_in, dbc_in, rest = *rest[:6], rest[6:]
    zx, side, dy_in, dz_in, y_in, wzx, wside, chan, bcp, head = rest[:10]
    normed, gain = rest[10:12]
    dzx, dside, chan_out, bcp_out, head_out, rim_out, gain_out = rest[12:19]
    parts, rest = rest[19 : 19 + shards], rest[19 + shards :]
    dsx, dsbc, work = rest
    shard = scal[0]
    rows, inner = dy_in.shape
    expand = head_map(inner)
    raw_dt = side[RIM:, 2 * N :] + head[0:1, :]
    dt = softplus(raw_dt)
    grow = jnp.exp(head[1:2, :])
    rate = -dt * grow
    skip = widen(head[...], expand)[2:3, :]
    upper_low = (iota((SPAN, SPAN), 0) <= iota((SPAN, SPAN), 1)).astype(F32).astype(BF)
    spans = rows // SPAN
    dstate = chain(states, expand)
    dsx[0:RIM, :] = jnp.zeros((RIM, inner), F32)
    dsx[RIM + rows :, :] = jnp.zeros((RIM, inner), F32)
    dsbc[0:RIM, :] = jnp.zeros((RIM, 2 * N), F32)
    dsbc[RIM + rows :, :] = jnp.zeros((RIM, 2 * N), F32)
    dside[0:RIM, 2 * N :] = jnp.zeros((RIM, LANES), BF)
    dzx[0:RIM, :inner] = jnp.zeros((RIM, inner), BF)
    dzx[RIM:, :inner] = dz_in[...]
    dbias = jnp.zeros((1, LANES), F32)
    dgrow = jnp.zeros((1, LANES), F32)
    dskip = jnp.zeros((1, LANES), F32)
    for span in reversed(range(spans)):
        here = slice(span * SPAN, (span + 1) * SPAN)
        there = slice(RIM + span * SPAN, RIM + (span + 1) * SPAN)
        cum = cum_in[here, :]
        tot = cum[SPAN - 1 : SPAN, :]
        keys = bc_in[here, :N]
        queries = bc_in[here, N:]
        xs = xs_in[here, :]
        dy = dy_in[here, :]
        dy_low = dy.astype(BF)
        dt_wide = widen(dt[here], expand)
        scaled = xs * dt_wide
        scaled_low = scaled.astype(BF)
        tail = widen(jnp.exp(tot - cum), expand)
        dstate_low = dstate.astype(BF)
        through = tail * nn(keys, dstate_low)
        dscaled = dscaled_in[here, :] + through
        plain = y_in[here, :] - skip * xs
        held = scaled_low.astype(F32)
        dcum = narrow(dy_low.astype(F32) * plain - held * dscaled, expand)
        tot_wide = widen(jnp.exp(tot), expand)
        over = jnp.sum(held * through, axis=0, keepdims=True) + jnp.sum(
            tot_wide * dstate * starts[span], axis=0, keepdims=True
        )
        dtot = narrow(jnp.broadcast_to(over, (8, inner)), expand)[0:1, :]
        drate = tri_sum(upper_low, dcum) + dtot
        ddt = narrow(dscaled * xs, expand) - drate * grow
        dgrow = dgrow + jnp.sum(drate * rate[here], axis=0, keepdims=True)
        draw = ddt * sigmoid(raw_dt[here])
        dbias = dbias + jnp.sum(draw, axis=0, keepdims=True)
        dside[there, 2 * N :] = draw.astype(BF)
        over = jnp.sum(dy * xs, axis=0, keepdims=True)
        dskip = dskip + narrow(jnp.broadcast_to(over, (8, inner)), expand)[0:1, :]
        dsx[there, :] = dscaled * dt_wide + skip * dy
        dsbc[there, :N] = dbc_in[here, :N] + nt_dot((scaled * tail).astype(BF), dstate_low)
        dsbc[there, N:] = dbc_in[here, N:]
        if span > 0:
            grown = widen(jnp.exp(cum), expand)
            dstate = tot_wide * dstate + tn(queries, (dy * grown).astype(BF))
    body = pl.ds(RIM, rows)
    pre_x = conv_sum(zx, chan, rows, pl.ds(inner, inner))
    dsx[body, :] = dsx[body, :] * silu_slope(pre_x)
    pre_bc = conv_sum(side, bcp, rows, pl.ds(0, 2 * N))
    dsbc[body, :] = dsbc[body, :] * silu_slope(pre_bc)
    chan_out[...] = conv_back(
        dsx, zx, chan, rows, pl.ds(inner, inner), inner, dzx, pl.ds(inner, inner)
    )
    bcp_out[...] = conv_back(dsbc, side, bcp, rows, pl.ds(0, 2 * N), 2 * N, dside, pl.ds(0, 2 * N))
    head_out[...] = jnp.concatenate([dbias, dgrow, dskip, jnp.zeros((5, LANES), F32)], axis=0)
    dnormed = nt_dot(dzx[...], wzx[...]) + nt_dot(dside[...], wside[...])
    work[...] = dnormed.astype(BF)
    gain_out[...] = jnp.sum(dnormed * normed[...].astype(F32), axis=0, keepdims=True) / gain[...]
    rim_out[...] = work[0:RIM, :]
    for off in range(shards):
        at = pl.multiple_of(RIM + (shard ^ off) * own, RIM)
        parts[off][...] = work[pl.ds(at, own), :]


def mixer_back(
    scal, states, inside, zx, side, dy, dz, y, wzx, wside, chan, bcp, head, normed, gain, shards
):
    rows, inner = dy.shape
    own = rows // shards
    ext = rows + RIM
    return call(
        functools.partial(back_kernel, shards, own, len(states)),
        "back",
        [
            sds((ext, 2 * inner), BF),
            sds((ext, 2 * N + LANES), BF),
            sds((8, inner), F32),
            sds((8, 2 * N), F32),
            sds((8, LANES), F32),
            sds((RIM, D), BF),
            sds((1, D), F32),
        ]
        + [sds((own, D), BF)] * shards,
        (scal, *states, *inside, zx, side, dy, dz, y, wzx, wside, chan, bcp, head, normed, gain),
        smem=(0,),
        scratch=[
            pltpu.VMEM((ext + RIM, inner), F32),
            pltpu.VMEM((ext + RIM, 2 * N), F32),
            pltpu.VMEM((ext, D), BF),
        ],
        flops=8 * rows * D * inner,
        moved=16 * MIB,
    )


def logits_kernel(vrows, label, table, normed, *rest):
    p_out, tops, stats, rows_scr, top, total, target, plain = rest
    step = pl.program_id(0)
    rows = normed.shape[0] - RIM

    @pl.when(step == 0)
    def _():
        rows_scr[...] = normed[RIM:, :].T
        top[...] = jnp.full((1, rows), -1e30, F32)
        total[...] = jnp.zeros((1, rows), F32)
        target[...] = jnp.zeros((1, rows), F32)
        plain[...] = jnp.zeros((1, rows), F32)

    highest, summed, hit, whole = top[...], total[...], target[...], plain[...]
    line = 2 * iota((PART, rows), 0)
    for half in range(2):
        for part_at in range(PAIRS // PART):
            first = step * PAIRS + part_at * PART
            here = slice(part_at * PART, (part_at + 1) * PART)
            padding = jnp.where(first + iota((PART, LANES), 0) < vrows, 0.0, -1e30)
            padding = jnp.concatenate([padding] * (rows // LANES), axis=1)
            raw = nn(table[here, half * D : (half + 1) * D], rows_scr[...])
            shown = raw + padding
            before = highest
            highest = jnp.maximum(before, jnp.max(shown, axis=0, keepdims=True))
            part = jnp.exp(shown - highest)
            summed = summed * jnp.exp(before - highest) + jnp.sum(part, axis=0, keepdims=True)
            wanted = label[...] - 2 * first - half
            hit = hit + jnp.sum(jnp.where(line == wanted, raw, 0.0), axis=0, keepdims=True)
            whole = whole + jnp.sum(raw, axis=0, keepdims=True)
            p_out[half, here, :] = part.astype(BF)
            at = 8 * (half * (PAIRS // PART) + part_at)
            tops[0, at : at + 8, :] = jnp.broadcast_to(highest, (8, rows))
    top[...] = highest
    total[...] = summed
    target[...] = hit
    plain[...] = whole
    stats[...] = jnp.concatenate([highest, summed, hit, whole, jnp.zeros((4, rows), F32)], axis=0)


def vocab_logits(label, table, normed, vrows):
    rows = normed.shape[0] - RIM
    padded = table.shape[0]
    steps = padded // PAIRS
    whole = lambda i: (0, 0)
    return pl.pallas_call(
        functools.partial(logits_kernel, vrows),
        grid=(steps,),
        out_shape=[
            sds((2, padded, rows), BF),
            sds((steps, 16 * (PAIRS // PART), rows), F32),
            sds((8, rows), F32),
        ],
        in_specs=[
            pl.BlockSpec((1, rows), whole),
            pl.BlockSpec((PAIRS, 2 * D), lambda i: (i, 0)),
            pl.BlockSpec(normed.shape, whole),
        ],
        out_specs=[
            pl.BlockSpec((2, PAIRS, rows), lambda i: (0, i, 0)),
            pl.BlockSpec((1, 16 * (PAIRS // PART), rows), lambda i: (i, 0, 0)),
            pl.BlockSpec((8, rows), whole),
        ],
        scratch_shapes=[pltpu.VMEM((D, rows), BF)] + [pltpu.VMEM((1, rows), F32)] * 4,
        compiler_params=pltpu.CompilerParams(
            dimension_semantics=("arbitrary",), vmem_limit_bytes=56 * MIB
        ),
        cost_estimate=pl.CostEstimate(
            flops=4 * rows * D * padded, bytes_accessed=40 * MIB, transcendentals=2 * rows * padded
        ),
        name="logits",
    )(label, table, normed)


def logit_grads(step, label, scale, weight, p_in):
    pairs, rows = p_in.shape[1:]
    line = 2 * iota((PART, rows), 0)
    usual = (SMOOTHING / V) * weight[...]
    special = (1.0 - SMOOTHING + SMOOTHING / V) * weight[...]
    for half in range(2):
        pieces = []
        for part_at in range(pairs // PART):
            wanted = label[...] - 2 * (step * pairs + part_at * PART) - half
            share = jnp.where(line == wanted, special, usual)
            at = 8 * (half * (pairs // PART) + part_at)
            grown = p_in[half, part_at * PART : (part_at + 1) * PART, :].astype(F32)
            pieces.append((grown * scale[0, at : at + 1, :] - share).astype(BF))
        yield half, jnp.concatenate(pieces, axis=0)


def rows_kernel(shards, own, scal, label, scale, weight, p_in, table, *rest):
    parts, acc = rest[:shards], rest[-1]
    step = pl.program_id(0)

    @pl.when(step == 0)
    def _():
        acc[...] = jnp.zeros_like(acc)

    for half, q in logit_grads(step, label, scale, weight, p_in):
        acc[...] += tn(q, table[:, half * D : (half + 1) * D])

    @pl.when(step == pl.num_programs(0) - 1)
    def _():
        for off in range(shards):
            at = pl.ds(pl.multiple_of((scal[0] ^ off) * own, own), own)
            parts[off][...] = acc[at, :].astype(BF)


def vocab_specs(rows):
    whole = lambda i: (0, 0)
    return [
        pl.BlockSpec((1, rows), whole),
        pl.BlockSpec((1, 16 * (PAIRS // PART), rows), lambda i: (i, 0, 0)),
        pl.BlockSpec((1, rows), whole),
        pl.BlockSpec((2, PAIRS, rows), lambda i: (0, i, 0)),
    ]


def vocab_rows(scal, label, scale, weight, p_in, table, shards):
    _, padded, rows = p_in.shape
    own = rows // shards
    whole = lambda i: (0, 0)
    return pl.pallas_call(
        functools.partial(rows_kernel, shards, own),
        grid=(padded // PAIRS,),
        out_shape=[sds((own, D), BF)] * shards,
        in_specs=[pl.BlockSpec(memory_space=pltpu.SMEM)]
        + vocab_specs(rows)
        + [pl.BlockSpec((PAIRS, 2 * D), lambda i: (i, 0))],
        out_specs=[pl.BlockSpec((own, D), whole)] * shards,
        scratch_shapes=[pltpu.VMEM((rows, D), F32)],
        compiler_params=pltpu.CompilerParams(
            dimension_semantics=("arbitrary",), vmem_limit_bytes=56 * MIB
        ),
        cost_estimate=pl.CostEstimate(
            flops=4 * rows * D * padded, bytes_accessed=40 * MIB, transcendentals=0
        ),
        name="rowgrads",
    )(scal, label, scale, weight, p_in, table)


def table_kernel(label, scale, weight, p_in, normed, out, rows_scr):
    step = pl.program_id(0)

    @pl.when(step == 0)
    def _():
        rows_scr[...] = normed[RIM:, :]

    for half, q in logit_grads(step, label, scale, weight, p_in):
        out[:, half * D : (half + 1) * D] = nn(q, rows_scr[...]).astype(BF)


def vocab_table_grad(label, scale, weight, p_in, normed):
    _, padded, rows = p_in.shape
    whole = lambda i: (0, 0)
    return pl.pallas_call(
        table_kernel,
        grid=(padded // PAIRS,),
        out_shape=sds((padded, 2 * D), BF),
        in_specs=vocab_specs(rows) + [pl.BlockSpec(normed.shape, whole)],
        out_specs=pl.BlockSpec((PAIRS, 2 * D), lambda i: (i, 0)),
        scratch_shapes=[pltpu.VMEM((rows, D), BF)],
        compiler_params=pltpu.CompilerParams(
            dimension_semantics=("arbitrary",), vmem_limit_bytes=56 * MIB
        ),
        cost_estimate=pl.CostEstimate(
            flops=4 * rows * D * padded, bytes_accessed=40 * MIB, transcendentals=0
        ),
        name="tablegrads",
    )(label, scale, weight, p_in, normed)


def adam_update(weight_in, gradient, moment_one, moment_two, factor, fix_one, fix_two, decay_rate):
    gradient = gradient * factor
    one_next = BETA_FIRST * moment_one + (1.0 - BETA_FIRST) * gradient
    two_next = BETA_SECOND * moment_two + (1.0 - BETA_SECOND) * gradient * gradient
    direction = one_next / fix_one / (jnp.sqrt(two_next / fix_two) + ADAM_EPS)
    return (weight_in - LEARN_RATE * (direction + decay_rate * weight_in), one_next, two_next)


def turn_kernel(share, bases, turned, root):
    count = bases.shape[0]
    total = jnp.zeros((1, BLK), F32)

    def turn(at, total):
        grad = share[pl.ds(pl.multiple_of(at * BLK, BLK), BLK), :].astype(F32)
        half_turn = tn(bases[at, 0], grad, HIGHEST)
        turned[at] = nn(half_turn, bases[at, 1], HIGHEST)
        return total + jnp.sum(grad * grad, axis=0, keepdims=True)

    for at in range(count):
        total = turn(at, total)
    root[...] = jnp.sqrt(total)


def turn_tiles(share, bases):
    count = bases.shape[0]
    return call(
        turn_kernel,
        "turn",
        [sds((count, BLK, BLK), F32), sds((1, BLK), F32)],
        (share, bases),
        moved=6 * MIB,
    )


def last_kernel(small, fixes, sums, *refs):
    tiles, turned, bases, tile_one, tile_two = refs[:5]
    little, refs = refs[5 : 5 + 4 * small], refs[5 + 4 * small :]
    tiles_out, copy_out, tile_one_out, tile_two_out = refs[:4]
    little_out = refs[4:]
    factor, fix_one, fix_two = sums[2:3, 0:1], fixes[0], fixes[1]
    for at in range(tiles.shape[0]):
        rotated = turned[at] * factor
        one_next = BETA_FIRST * tile_one[at] + (1.0 - BETA_FIRST) * rotated
        two_next = BETA_SECOND * tile_two[at] + (1.0 - BETA_SECOND) * rotated * rotated
        direction = one_next / fix_one / (jnp.sqrt(two_next / fix_two) + ADAM_EPS)
        back_half = nn(bases[at, 0], direction, HIGHEST)
        back = nt_dot(back_half, bases[at, 1], HIGHEST)
        after = tiles[at] - LEARN_RATE * (back + WEIGHT_DECAY * tiles[at])
        tiles_out[at] = after
        copy_out[at] = after.astype(BF)
        tile_one_out[at] = one_next
        tile_two_out[at] = two_next

    @pl.when(pl.program_id(0) == 0)
    def _():
        for which in range(small):
            before, gradient, first, second = (ref[...] for ref in little[4 * which : 4 * which + 4])
            results = adam_update(
                before,
                gradient,
                first,
                second,
                factor,
                fix_one,
                fix_two,
                WEIGHT_DECAY if which == 0 else 0.0,
            )
            outs = little_out[3 * which : 3 * which + 3]
            outs[0][...] = results[0] if which == 0 else results[0] - before
            outs[1][...], outs[2][...] = results[1], results[2]


def last_update(fixes, sums, tiles, turned, bases, tile_one, tile_two, little):
    count = tiles.shape[0]
    each = 4 if count % 4 == 0 else 2
    tile_spec = pl.BlockSpec((each, BLK, BLK), lambda i: (i, 0, 0))
    base_spec = pl.BlockSpec((each, 2, BLK, BLK), lambda i: (i, 0, 0, 0))
    whole = [
        pl.BlockSpec(x.shape, lambda i, rank=x.ndim: (0,) * rank) for group in little for x in group
    ]
    return pl.pallas_call(
        functools.partial(last_kernel, len(little)),
        grid=(count // each,),
        out_shape=[sds(tiles.shape, F32), sds(tiles.shape, BF), sds(tiles.shape, F32), sds(tiles.shape, F32)]
        + [sds(group[0].shape, F32) for group in little for _ in range(3)],
        in_specs=[
            pl.BlockSpec(memory_space=pltpu.SMEM),
            pl.BlockSpec(sums.shape, lambda i: (0, 0)),
        ]
        + [tile_spec, tile_spec, base_spec, tile_spec, tile_spec]
        + whole,
        out_specs=[tile_spec] * 4
        + [spec for which in range(len(little)) for spec in whole[4 * which : 4 * which + 3]],
        compiler_params=pltpu.CompilerParams(
            dimension_semantics=("arbitrary",), vmem_limit_bytes=48 * MIB
        ),
        cost_estimate=pl.CostEstimate(
            flops=24 * count * BLK * BLK * BLK, bytes_accessed=16 * MIB, transcendentals=0
        ),
        name="update",
    )(
        fixes,
        sums,
        tiles,
        turned,
        bases,
        tile_one,
        tile_two,
        *[x for group in little for x in group],
    )


def total_over(x, axis):
    out = x
    for off in range(1, lax.axis_size(axis)):
        out = out + swap(x, axis, off)
    return out


def shards(
    token_ids,
    labels,
    seq_lengths,
    micro_batch,
    step_count,
    block_slot,
    vocab_table,
    vocab_first,
    vocab_second,
    layer_blocks,
    block_bases,
    block_first,
    block_second,
    side_proj,
    side_first,
    side_second,
    shared_params,
    shared_first,
    shared_second,
    channel_params,
    channel_first,
    channel_second,
    head_params,
    head_first,
    head_second,
):
    nt = lax.axis_size("tensor")
    nd = lax.axis_size("dp")
    shard = lax.axis_index("tensor")
    place = lax.axis_index("dp")
    seqs = token_ids.shape[0]
    length = token_ids.shape[1] * nd
    chunks = nd // seqs
    rows = seqs * length // nd
    own = rows // nt
    vrows = vocab_table.shape[0]
    padded = -(-vrows // PAIRS) * PAIRS
    half = nd // 2
    inner = channel_params.shape[2]
    heads = head_params.shape[2]
    tiles = block_slot.shape[1]
    zx_count = D * 2 * inner // (BLK * BLK)
    per_layer = 3 * D * inner // (BLK * BLK)
    stride = D + 10 * N
    both = ("dp", "tensor")
    side_rows = side_proj.shape[1]
    share_size = shared_params.shape[0]
    share_pad = -(-share_size // 2048) * 2048

    piece = jnp.pad(side_proj.astype(BF), ((0, 0), (0, 0), (0, LANES - H))).reshape(-1, LANES)
    share = jnp.pad(shared_params.astype(BF), (0, share_pad - share_size)).reshape(-1, LANES)
    side_part = piece.shape[0]
    piece_rows = side_part + share.shape[0]
    ids = jnp.pad(jnp.concatenate([token_ids, labels], axis=0), ((0, 8 - 2 * seqs), (0, 0)))
    ids_all, pieces, shared_all = open_exchange(ids, piece, share, nd, nt)
    shared_full = shared_all.reshape(nd * nt, share_pad)[:, :share_size].reshape(-1).astype(F32)
    ids_all = ids_all.transpose(1, 0, 2).reshape(8, length)
    all_ids = ids_all[:seqs].reshape(-1)
    local_row = all_ids // 2 - shard * vrows
    held = (local_row >= 0) & (local_row < vrows) & (all_ids % 2 == place // half)
    scal = jnp.stack([place, shard]).astype(jnp.int32)
    scal_shard = shard.astype(jnp.int32).reshape(1)
    code = jnp.concatenate([jnp.where(held, local_row, 0), jnp.zeros((8,), jnp.int32)])
    listed, count = list_held(held, nd * rows)
    own_tiles = layer_blocks.shape[2]
    gathered = lax.all_gather(
        jnp.concatenate(
            [layer_blocks.astype(BF).reshape(own_tiles * BLK, BLK), pieces.reshape(-1, LANES)], axis=0
        ),
        "dp",
        axis=0,
        tiled=False,
    )
    *parts, table_low = gather_rows(
        scal, code, listed, count, vocab_table, nd, rows, padded
    )
    residual, normed = forward_rows(
        parts, None, shared_full[None, :D], nd, chunks, True, 4, nt
    )
    table_low, normed = lax.optimization_barrier((table_low, normed))
    gathered, normed = lax.optimization_barrier((gathered, normed))
    placed = place_tiles(block_slot, gathered, own_tiles, inner, zx_count, per_layer)
    side_full = (
        gathered[:, own_tiles * BLK :]
        .reshape(nd, nt, L, side_rows, 2 * N + LANES)
        .transpose(2, 0, 1, 3, 4)
        .reshape(L, D, 2 * N + LANES)
    )
    table_all = lax.all_gather(table_low, "dp", axis=1, tiled=True)

    def layer_mats(layer_index):
        zx_part, out_part = placed[2 * layer_index], placed[2 * layer_index + 1]
        dt_part = lax.dynamic_slice_in_dim(
            side_full[layer_index], 2 * N + shard * heads, heads, 1
        )
        side_here = jnp.concatenate(
            [
                side_full[layer_index][:, : 2 * N],
                jnp.pad(dt_part, ((0, 0), (0, LANES - heads))),
            ],
            axis=1,
        )
        base = layer_index * stride
        gain = shared_full[base : base + D]
        taps = shared_full[base + D : base + D + 8 * N].reshape(4, 2 * N)
        bias = shared_full[base + D + 8 * N : base + stride].reshape(1, 2 * N)
        bcp = jnp.concatenate([taps, bias, jnp.zeros((3, 2 * N), F32)], axis=0)
        chan = jnp.pad(channel_params[layer_index], ((0, 2), (0, 0)))
        head = jnp.pad(head_params[layer_index], ((0, 5), (0, LANES - heads)))
        return (zx_part, out_part, side_here, gain, bcp, chan, head)

    def hop(x, distance):
        pairs = [
            (k, k + distance)
            for k in range(nd)
            if 0 <= k % chunks + distance < chunks
        ]
        return lax.ppermute(x, "dp", pairs)

    def returned(parts):
        return [parts[0]] + [swap(parts[off], "tensor", off) for off in range(1, nt)]

    hops = range(1, chunks)
    mats = [layer_mats(layer_index) for layer_index in range(L)]
    final_gain = shared_full[L * stride :][None, :]
    gains = [mats[layer_index][3][None, :] for layer_index in range(L)] + [final_gain]
    saved = []
    for layer_index in range(L):
        wzx, wout, wside, gain, bcp, chan, head = mats[layer_index]
        zx, side, yloc, final, c_out, cum = mixer_front(normed, wzx, wside, chan, bcp, head)
        states = [hop(final, k) for k in hops]
        result = mixer_middle(scal_shard, states, yloc, zx, c_out, cum, wout, chan, nt)
        y, s_in = result[:2]
        below = normed
        before = residual
        inside = layer_index + 1 < L
        residual, branch, factor, normed = forward_rows(
            result[2:], before, gains[layer_index + 1], nd, chunks, inside, 5 + layer_index
        )
        saved.append((before, below, zx, side, c_out, cum, y, s_in, factor, branch))

    member = micro_batch[:, None] == jnp.arange(MB, dtype=jnp.int32)[None, :]
    batch_tokens = jnp.sum(jnp.where(member, seq_lengths[:, None], 0), axis=0).astype(F32)
    seq_weight = 1.0 / (MB * jnp.sum(jnp.where(member, batch_tokens[None, :], 0.0), axis=1))
    row_at = place * rows + jnp.arange(rows, dtype=jnp.int32)
    my_seq = place // chunks
    weight = jnp.where(row_at % length < seq_lengths[my_seq], seq_weight[my_seq], 0.0)
    all_labels = ids_all[seqs : 2 * seqs].reshape(-1)
    label = (lax.dynamic_slice_in_dim(all_labels, place * rows, rows) - 2 * shard * vrows).reshape(
        1, rows
    )
    row_weight = weight.reshape(1, rows)
    p_low, tops, stats = vocab_logits(label, table_all, normed, vrows)
    scale, seq_part = merge_stats(stats, tops, row_weight, nt, chunks)
    sent = returned(vocab_rows(scal_shard, label, scale, row_weight, p_low, table_all, nt))
    table_grad = vocab_table_grad(label, scale, row_weight, p_low, normed)
    sent, table_grad = lax.optimization_barrier((sent, table_grad))
    table_share = lax.psum_scatter(table_grad, "dp", scatter_dimension=1, tiled=True)
    grad_res, payload, grad_final_gain = backward_rows(
        sent, None, residual, final_gain, None, saved[L - 1][9], saved[L - 1][8], nd, chunks, 10
    )

    block_pieces = [None] * (2 * L)
    side_pieces = [None] * L
    channel_pieces = [None] * L
    head_pieces = [None] * L
    shared_pieces = [None] * L
    for layer_index in reversed(range(L)):
        wzx, wout, wside, gain, bcp, chan, head = mats[layer_index]
        residual_in, normed, zx, side, c_out, cum, y, s_in, factor, branch = saved[layer_index]
        u_low, dy, dz, dstate, gain_grad = gate_back(payload, wout, y, zx, c_out, cum, chan)
        states = [hop(dstate, -k) for k in hops]
        grad_out_w = tn(u_low, payload)
        inside = mixer_within(s_in, zx, side, dy, chan, bcp, head)
        result = mixer_back(
            scal_shard,
            states,
            inside,
            zx,
            side,
            dy,
            dz,
            y,
            wzx,
            wside,
            chan,
            bcp,
            head,
            normed,
            gains[layer_index],
            nt,
        )
        dzx, dside, chan_grad, bcp_grad, head_grad, rim_grad, grad_gain_in = result[:7]
        parts_out = result[7:]
        grad_zx_w = tn(normed, dzx)
        grad_side_w = tn(normed, dside)
        block_pieces[2 * layer_index] = grad_zx_w.astype(BF)
        block_pieces[2 * layer_index + 1] = grad_out_w.astype(BF)
        side_pieces[layer_index] = grad_side_w
        shared_pieces[layer_index] = jnp.concatenate(
            [grad_gain_in[0], bcp_grad[:4].reshape(-1), bcp_grad[4]]
        )
        channel_pieces[layer_index] = jnp.concatenate([chan_grad[:5], gain_grad], axis=0)
        head_pieces[layer_index] = head_grad[:3, :heads]
        if layer_index == 0:
            shared_grads = jnp.concatenate(shared_pieces + [grad_final_gain[0]]).astype(BF)
            shared_grads = jnp.pad(
                shared_grads.reshape(nd * nt, share_size), ((0, 0), (0, share_pad - share_size))
            ).reshape(nd, nt * share_pad // LANES, LANES)
            lines = jnp.concatenate(
                [
                    jnp.stack(channel_pieces).reshape(-1, LANES),
                    jnp.pad(jnp.stack(head_pieces).reshape(-1), (0, LANES - L * 3 * heads)).reshape(
                        1, LANES
                    ),
                ],
                axis=0,
            ).astype(BF)
            line_count = lines.shape[0]
            line_rows = -(-line_count // RIM) * RIM
            lines = jnp.pad(lines, ((0, line_rows - line_count), (0, 0)))
            tile_grads = pack_tiles(
                scal_shard,
                block_slot,
                block_pieces,
                side_pieces,
                shared_grads,
                lines,
                own_tiles,
                per_layer,
                nt,
                heads,
            )
            tile_grads, table_share, parts_out, rim_grad = lax.optimization_barrier(
                (tile_grads, table_share, parts_out, rim_grad)
            )
            block_share = lax.psum_scatter(tile_grads, "dp", scatter_dimension=0, tiled=True)[0]
        if layer_index:
            grad_res, payload = backward_rows(
                parts_out,
                rim_grad,
                residual_in,
                gains[layer_index],
                grad_res,
                saved[layer_index - 1][9],
                saved[layer_index - 1][8],
                nd,
                chunks,
                10 + layer_index,
            )
        else:
            embed = finish_rows(
                parts_out, rim_grad, residual_in, gains[0], grad_res, nd, chunks
            )

    side_count = nt * side_part
    small_share = jnp.concatenate(
        [
            block_share[own_tiles * BLK : own_tiles * BLK + side_count].reshape(nt, side_part, LANES),
            block_share[own_tiles * BLK + side_count : own_tiles * BLK + nt * piece_rows].reshape(
                nt, piece_rows - side_part, LANES
            ),
        ],
        axis=1,
    )
    mine = jnp.zeros((piece_rows, LANES), F32)
    for off in range(nt):
        piece = lax.dynamic_index_in_dim(small_share, shard ^ off, 0, False)
        mine = mine + (piece if off == 0 else swap(piece, "tensor", off)).astype(F32)
    side_share = (
        mine[:side_part]
        .reshape(L, 2 * N // LANES + 1, side_rows, LANES)
        .transpose(0, 2, 1, 3)
        .reshape(L * side_rows, 2 * N + LANES)[:, : 2 * N + H]
    )
    shared_share = mine[side_part:].reshape(1, -1)[:, :share_size]
    lines = block_share[own_tiles * BLK + nt * piece_rows :].astype(F32)
    channel_sum = lines[: line_count - 1].reshape(L * 6, inner)
    head_sum = lines[line_count - 1, : L * 3 * heads].reshape(L * 3, heads)
    rotated, tile_root = turn_tiles(block_share, block_bases.reshape(own_tiles, 2, BLK, BLK))
    grad_table, table_root = add_rows(scal, code, listed, count, table_share, embed, vrows)
    sums = sum_everywhere(
        seq_part,
        [channel_sum, head_sum],
        [table_root, tile_root, side_share, shared_share],
        nd,
        nt,
    )
    seq_loss = sums[0, :seqs]
    clip_norm = sums[1, 0]
    steps_done = step_count[0].astype(F32)
    fix_one = 1.0 - jnp.power(BETA_FIRST, steps_done)
    fix_two = 1.0 - jnp.power(BETA_SECOND, steps_done)
    tile_shape = layer_blocks.shape[2:]
    flat = lambda x: x.reshape((-1, x.shape[-1]))
    little = [
        [flat(side_proj), side_share, flat(side_first), flat(side_second)],
        [flat(shared_params), shared_share, flat(shared_first), flat(shared_second)],
        [channel_params, channel_sum.reshape(channel_params.shape), channel_first, channel_second],
        [head_params, head_sum.reshape(head_params.shape), head_first, head_second],
    ]
    updated = last_update(
        jnp.stack([fix_one, fix_two]),
        sums,
        layer_blocks.reshape(tile_shape),
        rotated,
        block_bases.reshape((own_tiles, 2, BLK, BLK)),
        block_first.reshape(tile_shape),
        block_second.reshape(tile_shape),
        little,
    )
    table_out = adam_update(
        vocab_table,
        grad_table.astype(F32),
        vocab_first,
        vocab_second,
        sums[2, 0],
        fix_one,
        fix_two,
        WEIGHT_DECAY,
    )
    block_out = [x.reshape(layer_blocks.shape) for x in updated[:4]]
    like = [side_proj] * 3 + [shared_params] * 3 + [channel_params] * 3 + [head_params] * 3
    small_out = [x.reshape(y.shape) for x, y in zip(updated[4:], like)]
    return (
        seq_loss,
        clip_norm,
        table_out[0],
        table_out[1],
        table_out[2],
        block_out[0],
        block_out[1],
        block_out[2],
        block_out[3],
        *small_out,
    )


def solution(mesh):
    table = P("tensor", "dp")
    block = P("dp", "tensor", None, None, None)
    side = P(None, ("dp", "tensor"), None)
    shared = P(("dp", "tensor"))
    channel = P(None, None, "tensor")
    in_specs = (
        P(None, "dp"),
        P(None, "dp"),
        P(),
        P(),
        P(),
        P("tensor", None),
        *[table] * 3,
        block,
        P("dp", "tensor", None, None, None, None),
        block,
        block,
        *[side] * 3,
        *[shared] * 3,
        *[channel] * 6,
    )
    out_specs = (
        P(),
        P(),
        *[table] * 3,
        *[block] * 4,
        *[side] * 3,
        *[shared] * 3,
        *[channel] * 6,
    )
    return jax.shard_map(shards, mesh=mesh, in_specs=in_specs, out_specs=out_specs, check_vma=False)
```

```python
import functools

import jax
import jax.numpy as jnp
from jax import lax
from jax.experimental import pallas as pl
from jax.experimental.pallas import tpu as pltpu
from jax.sharding import PartitionSpec as P

D = 1024
DI = 2048
H = 32
P_SIZE = 64
N = 128
V = 50288
SPAN = 256
L = 2
MB = 2
BLK = 128
RIM = 16
PAIRS = 1280
PART = 320
LANES = 128

HIGHEST = lax.Precision.HIGHEST
NORM_EPS = 1e-05
SMOOTHING = 0.1
ZLOSS_WEIGHT = 0.005
CLIP_LIMIT = 0.02
BETA_FIRST = 0.9
BETA_SECOND = 0.95
ADAM_EPS = 1e-08
LEARN_RATE = 0.03
WEIGHT_DECAY = 0.01

BF = jnp.bfloat16
F32 = jnp.float32
MIB = 1 << 20


def nn(a, b, precision=None):
    return lax.dot_general(
        a, b, (((1,), (0,)), ((), ())), precision=precision, preferred_element_type=F32
    )


def nt_dot(a, b, precision=None):
    return lax.dot_general(
        a, b, (((1,), (1,)), ((), ())), precision=precision, preferred_element_type=F32
    )


def tn(a, b, precision=None):
    return lax.dot_general(
        a, b, (((0,), (0,)), ((), ())), precision=precision, preferred_element_type=F32
    )


def iota(shape, dim):
    return lax.broadcasted_iota(jnp.int32, shape, dim)


def head_map(inner):
    return (iota((LANES, inner), 0) == iota((LANES, inner), 1) // P_SIZE).astype(F32).astype(BF)


def swap(x, axis, offset):
    size = lax.axis_size(axis)
    return lax.ppermute(x, axis, [(i, i ^ offset) for i in range(size)])


def halves(x):
    high = x.astype(BF)
    return high, (x - high.astype(F32)).astype(BF)


def thirds(x):
    high = x.astype(BF)
    rest = x - high.astype(F32)
    mid = rest.astype(BF)
    return high, mid, (rest - mid.astype(F32)).astype(BF)


def widen(x, expand):
    high, low = halves(x)
    twice = jnp.concatenate([expand, expand], axis=0)
    return nn(jnp.concatenate([high, low], axis=1), twice)


def narrow(x, expand):
    high, low = halves(x)
    return nt_dot(high, expand) + nt_dot(low, expand)


def tri_sum(tri, x):
    wide = nn(tri, jnp.concatenate(thirds(x), axis=1))
    size = x.shape[1]
    return wide[:, :size] + wide[:, size : 2 * size] + wide[:, 2 * size :]


def lanes3(column):
    high, mid, low = thirds(column)
    lane = iota((column.shape[0], LANES), 1)
    zero = jnp.zeros((column.shape[0], LANES), F32)
    wide = jnp.where(lane == 0, high.astype(F32), zero)
    wide = jnp.where(lane == 1, mid.astype(F32), wide)
    return jnp.where(lane == 2, low.astype(F32), wide).astype(BF)


def column3(wide):
    return wide[:, 0:1] + wide[:, 1:2] + wide[:, 2:3]


def rows3(line, inner):
    high, mid, low = thirds(line)
    at = iota((RIM, LANES), 0)
    wide = jnp.where(at == 0, high.astype(F32), 0.0)
    wide = jnp.where(at == 1, mid.astype(F32), wide)
    wide = jnp.where(at == 2, low.astype(F32), wide)
    if inner > LANES:
        wide = jnp.concatenate([wide, jnp.zeros((RIM, inner - LANES), F32)], axis=1)
    return wide.astype(BF)


def sigmoid(x):
    return 1.0 / (1.0 + jnp.exp(-x))


def softplus(x):
    return jnp.maximum(x, 0.0) + jnp.log1p(jnp.exp(-jnp.abs(x)))


def call(kernel, name, out_shape, args, smem=(), scratch=(), mib=60, flops=0, moved=0, **extra):
    specs = [
        pl.BlockSpec(memory_space=pltpu.SMEM if i in smem else pltpu.VMEM)
        for i in range(len(args))
    ]
    return pl.pallas_call(
        kernel,
        out_shape=out_shape,
        in_specs=specs,
        out_specs=jax.tree.map(lambda _: pl.BlockSpec(memory_space=pltpu.VMEM), out_shape),
        scratch_shapes=list(scratch),
        compiler_params=pltpu.CompilerParams(vmem_limit_bytes=mib * MIB),
        cost_estimate=pl.CostEstimate(flops=flops, bytes_accessed=moved, transcendentals=0),
        name=name,
        **extra,
    )(*args)


def sds(shape, dtype):
    return jax.ShapeDtypeStruct(shape, dtype)


def list_held(held, total):
    runs = held.reshape(-1, LANES)
    upper = iota((LANES, LANES), 0) <= iota((LANES, LANES), 1)
    rank = nn(runs.astype(BF), upper.astype(BF)).astype(jnp.int32) - 1
    here = (rank[:, :, None] == iota((1, 1, LANES), 2)) & runs[:, :, None]
    at = jnp.sum(jnp.where(here, iota((1, LANES, 1), 1), 0), axis=1)
    counts = rank[:, -1] + 1
    first = iota(at.shape, 0) * LANES
    listed = jnp.where(iota(at.shape, 1) < counts[:, None], at + first, total)
    return listed.reshape(-1), counts


def over_listed(listed, count, body):
    def run(at_run, carry):
        def turn(step, inner_carry):
            for lane in range(8):
                body(listed[at_run * LANES + step * 8 + lane])
            return inner_carry

        lax.fori_loop(0, (count[at_run] + 7) // 8, turn, 0)
        return carry

    lax.fori_loop(0, count.shape[0], run, 0)


def look_kernel(groups, rows, scal, code, listed, count, table, *rest):
    outs, low, work = rest[:groups], rest[groups], rest[groups + 1]
    place = scal[0]
    vrows = table.shape[0]
    edge = vrows // RIM * RIM
    low[edge:, :] = jnp.zeros((low.shape[0] - edge, low.shape[1]), BF)
    low[0:vrows, :] = table[...].astype(BF)

    def fill(step, carry):
        work[pl.ds(pl.multiple_of(step * rows, rows), rows), :] = jnp.zeros((rows, table.shape[1]), F32)
        return carry

    lax.fori_loop(0, groups, fill, 0)

    def take(at):
        work[pl.ds(at, 1), :] = table[pl.ds(code[at], 1), :]

    over_listed(listed, count, take)
    for off in range(groups):
        base = pl.multiple_of((place ^ off) * rows, rows)
        outs[off][...] = work[pl.ds(base, rows), :].astype(BF)


def gather_rows(scal, code, listed, count, table, groups, rows, padded):
    cols = table.shape[1]
    return call(
        functools.partial(look_kernel, groups, rows),
        "look",
        [sds((rows, cols), BF)] * groups + [sds((padded, cols), BF)],
        (scal, code, listed, count, table),
        smem=(0, 1, 2, 3),
        scratch=[pltpu.VMEM((groups * rows + 8, cols), F32)],
        moved=30 * MIB,
    )


def add_kernel(groups, rows, vrows, scal, code, listed, count, share, parts, *rest):
    out, square, work, bins = rest
    place = scal[0]
    bins[...] = share[0:vrows, :].astype(F32)
    for off in range(groups):
        base = pl.multiple_of((place ^ off) * rows, rows)
        work[pl.ds(base, rows), :] = parts[off].astype(F32)
    work[groups * rows :, :] = jnp.zeros((8, work.shape[1]), F32)

    def add(at):
        to = pl.ds(code[at], 1)
        bins[to, :] = bins[to, :] + work[pl.ds(at, 1), :]

    over_listed(listed, count, add)
    total = bins[...]
    out[...] = total.astype(BF)
    square[...] = jnp.sqrt(jnp.sum(total * total, axis=0, keepdims=True))


def add_rows(scal, code, listed, count, share, parts, vrows):
    cols = share.shape[1]
    groups, rows, _ = parts.shape
    return call(
        functools.partial(add_kernel, groups, rows, vrows),
        "addrows",
        [sds((vrows, cols), BF), sds((1, cols), F32)],
        (scal, code, listed, count, share, parts),
        smem=(0, 1, 2, 3),
        scratch=[pltpu.VMEM((rows * groups + 8, cols), F32), pltpu.VMEM((vrows, cols), F32)],
        moved=30 * MIB,
    )


def tiles_kernel(slots_each, zx_count, per_layer, first_layer, slot, tiles, *outs):
    for layer in (first_layer,):
        for at in range(per_layer):
            where = slot[0, layer * per_layer + at]
            owner = where // slots_each
            first = pl.multiple_of((where % slots_each) * BLK, BLK)
            tile = tiles[owner, pl.ds(first, BLK), :]
            if at < zx_count:
                wide = outs[0].shape[1] // BLK
                row, col = at // wide, at % wide
                out = outs[0]
            else:
                wide = D // BLK
                row, col = (at - zx_count) // wide, (at - zx_count) % wide
                out = outs[1]
            out[row * BLK : (row + 1) * BLK, col * BLK : (col + 1) * BLK] = tile


def place_tiles(slot, tiles, slots_each, inner, zx_count, per_layer, layer):
    return call(
        functools.partial(tiles_kernel, slots_each, zx_count, per_layer, layer),
        "placetiles",
        [sds((D, 2 * inner), BF), sds((inner, D), BF)],
        (slot, tiles),
        smem=(0,),
        moved=14 * MIB,
    )


def pack_kernel(slots_each, per_layer, layers, shards, heads, scal, slot, *refs):
    mats, sides, refs = refs[: 2 * layers], refs[2 * layers : 3 * layers], refs[3 * layers :]
    shared, lines, out, work = refs
    for layer in range(layers):
        zx, wout = mats[2 * layer], mats[2 * layer + 1]
        zx_wide, out_wide = zx.shape[1] // BLK, D // BLK
        zx_count = zx.shape[0] // BLK * zx_wide
        for at in range(per_layer):
            where = slot[0, layer * per_layer + at]
            if at < zx_count:
                source, row, col = zx, at // zx_wide, at % zx_wide
            else:
                source = wout
                row, col = (at - zx_count) // out_wide, (at - zx_count) % out_wide
            first = pl.multiple_of((where % slots_each) * BLK, BLK)
            out[where // slots_each, pl.ds(first, BLK), :] = source[
                row * BLK : (row + 1) * BLK, col * BLK : (col + 1) * BLK
            ]
        work[layer, :, : 2 * N] = sides[layer][:, : 2 * N]
        work[layer, :, 2 * N :] = pltpu.roll(sides[layer][:, 2 * N :], scal[0] * heads, 1)
    groups = out.shape[0]
    each = work.shape[1] // (groups * shards)
    piece = layers * each * work.shape[2] // LANES
    base = slots_each * BLK
    for group in range(groups):
        for shard in range(shards):
            first = (group * shards + shard) * each
            blocks = [
                work[layer, first : first + each, col : col + LANES]
                for layer in range(layers)
                for col in range(0, work.shape[2], LANES)
            ]
            at = base + shard * piece
            out[group, at : at + piece, :] = jnp.concatenate(blocks, axis=0).astype(BF)
    base += shards * piece
    out[:, base : base + shared.shape[1], :] = shared[...]
    for group in range(groups):
        out[group, base + shared.shape[1] :, :] = lines[...]


def pack_tiles(scal, slot, mats, sides, shared, lines, slots_each, per_layer, shards, heads):
    groups = shared.shape[0]
    layers = len(sides)
    depth, width = sides[0].shape
    extra = layers * depth * width // (groups * LANES) + shared.shape[1] + lines.shape[0]
    return call(
        functools.partial(pack_kernel, slots_each, per_layer, layers, shards, heads),
        "packtiles",
        sds((groups, slots_each * BLK + extra, LANES), BF),
        (scal, slot, *mats, *sides, shared, lines),
        smem=(0, 1),
        scratch=[pltpu.VMEM((layers, depth, width), F32)],
        moved=14 * MIB,
    )


def norm_rows(values, gain):
    return values * lax.rsqrt(jnp.mean(values * values, axis=-1, keepdims=True) + NORM_EPS) * gain


def total_of(parts):
    total = parts[0][...].astype(F32)
    for part in parts[1:]:
        total = total + part[...].astype(F32)
    return total


def send(source, target, send_sem, recv_sem, device):
    copy = pltpu.make_async_remote_copy(
        src_ref=source,
        dst_ref=target,
        send_sem=send_sem,
        recv_sem=recv_sem,
        device_id=device,
        device_id_type=pl.DeviceIdType.MESH,
    )
    copy.start()
    return copy


def greet_shards(groups, shards, rims, wide=False):
    place, shard = lax.axis_index("dp"), lax.axis_index("tensor")
    last = shard == shards - 1
    barrier = pltpu.get_barrier_semaphore()

    def greet(device):
        pl.semaphore_signal(barrier, inc=1, device_id=device, device_id_type=pl.DeviceIdType.MESH)

    for off in range(1, shards):
        greet((place, shard ^ off))
    if not rims:
        pl.semaphore_wait(barrier, shards - 1)
        return
    if wide:
        for off in range(1, groups):
            greet((place ^ off, shard))

        @pl.when(jnp.logical_not(last))
        def _():
            greet((lax.rem(place + groups - 1, groups), shards - 1))

        @pl.when(last)
        def _():
            for other in range(shards - 1):
                greet((lax.rem(place + 1, groups), other))

        pl.semaphore_wait(barrier, shards + groups - 2 + jnp.where(last, shards - 1, 1))
        return
    greet((lax.rem(place + groups - 1, groups), shards - 1))

    @pl.when(last)
    def _():
        for other in range(shards):
            greet((lax.rem(place + 1, groups), other))

    pl.semaphore_wait(barrier, shards - 1 + jnp.where(last, shards + 1, 1))


def pass_along(rows, own, base, shards, sems):
    place, shard = lax.axis_index("dp"), lax.axis_index("tensor")

    def copy(way, hop, source, to):
        at = pl.ds(pl.multiple_of(base + source * own, RIM), own)
        return pltpu.make_async_remote_copy(
            src_ref=rows.at[at, :],
            dst_ref=rows.at[at, :],
            send_sem=sems.at[0, way, hop],
            recv_sem=sems.at[1, way, hop],
            device_id=(place, to),
            device_id_type=pl.DeviceIdType.MESH,
        )

    def up(hop):
        return copy(0, hop, shard - hop, shard + 1)

    def down(hop):
        return copy(1, hop, shard + hop, shard - 1)

    can_up, can_down = shard + 1 < shards, shard > 0
    for hop in range(shards):
        if hop > 0:

            @pl.when(shard - hop >= 0)
            def _():
                copy(0, hop - 1, shard - hop, shard - 1).wait_recv()

        if hop < shards - 1:

            @pl.when(jnp.logical_and(shard - hop >= 0, can_up))
            def _():
                up(hop).start()

        if hop > 0:

            @pl.when(shard + hop < shards)
            def _():
                copy(1, hop - 1, shard + hop, shard + 1).wait_recv()

        if hop < shards - 1:

            @pl.when(jnp.logical_and(shard + hop < shards, can_down))
            def _():
                down(hop).start()

    for hop in range(shards - 1):

        @pl.when(jnp.logical_and(shard - hop >= 0, can_up))
        def _():
            up(hop).wait_send()

        @pl.when(jnp.logical_and(shard + hop < shards, can_down))
        def _():
            down(hop).wait_send()


def exchange_terms(parts, slots, work, sems, ready=None):
    place, shard = lax.axis_index("dp"), lax.axis_index("tensor")
    shards = len(parts)

    def copy(off, source, to, slot):
        return pltpu.make_async_remote_copy(
            src_ref=source,
            dst_ref=slots.at[slot],
            send_sem=sems.at[0, off],
            recv_sem=sems.at[1, slot],
            device_id=(place, to),
            device_id_type=pl.DeviceIdType.MESH,
        )

    def direct(off):
        return copy(off, parts[off], shard ^ off, off)

    if shards != 4:
        for off in reversed(range(1, shards)):
            if ready:
                ready(off)
            direct(off).start()
        if ready:
            ready(0)
        for off in range(1, shards):
            direct(off).wait()
        total = parts[0][...].astype(F32)
        for off in range(1, shards):
            total = total + slots[off].astype(F32)
        work[...] = total
        return
    relay, added = 0, 4
    outer = jnp.logical_or(shard == 0, shard == shards - 1)
    inner = jnp.logical_not(outer)

    def pass_relayed():
        copy(0, parts[3], shard ^ 1, relay).wait_recv()
        slots[added] = (slots[relay].astype(F32) + parts[2][...].astype(F32)).astype(BF)
        copy(2, slots.at[added], shard ^ 2, 2).start()

    if ready:
        ready(3)

        @pl.when(outer)
        def _():
            copy(3, parts[3], shard ^ 1, relay).start()

        @pl.when(inner)
        def _():
            direct(3).start()

        ready(2)

        @pl.when(outer)
        def _():
            direct(2).start()

        @pl.when(inner)
        def _():
            pass_relayed()

        ready(1)
        direct(1).start()
        ready(0)
    else:

        @pl.when(outer)
        def _():
            copy(3, parts[3], shard ^ 1, relay).start()
            direct(2).start()
            direct(1).start()

        @pl.when(inner)
        def _():
            direct(3).start()
            direct(1).start()
            pass_relayed()

    direct(1).wait_recv()
    total = parts[0][...].astype(F32) + slots[1].astype(F32)
    direct(2).wait_recv()
    work[...] = total + slots[2].astype(F32)

    @pl.when(inner)
    def _():
        direct(3).wait_recv()
        work[...] += slots[3].astype(F32)

    for off in range(1, shards):
        direct(off).wait_send()


def term_scratch(shards, own, width):
    return [
        pltpu.VMEM((shards + 1, own, width), BF),
        pltpu.VMEM((own, width), F32),
        pltpu.SemaphoreType.DMA((2, shards + 1)),
    ]


def forward_kernel(groups, shards, chunks, packed, rims, *refs):
    ready = None
    place, shard = lax.axis_index("dp"), lax.axis_index("tensor")
    if packed:
        parts, refs = refs[:shards], refs[shards:]
        before, gain, residual, branch, factor, normed, *refs = refs
        slots, work, term_sems, row_sems, rim_sems = refs
        own = parts[0].shape[0]
        greet_shards(groups, shards, rims)
    else:
        looked, refs = refs[:groups], refs[groups:]
        gain, residual, normed, *refs = refs
        slots, work, term_sems, row_sems, rim_sems, arrived, terms, look_sems = refs
        own = terms.shape[1]
        half, cols = groups // 2, looked[0].shape[1]
        parts = [terms.at[off] for off in range(shards)]
        greet_shards(groups, shards, rims, True)

        def block(off):
            return pl.ds(pl.multiple_of((shard ^ off) * own, own), own)

        copies = {
            (off, other): send(
                looked[other].at[block(off), :],
                arrived.at[off, other],
                look_sems.at[0, off, other],
                look_sems.at[1, off, other],
                (place ^ other, shard),
            )
            for off in reversed(range(shards))
            for other in range(1, groups)
        }

        def ready(off):
            for other in range(1, groups):
                copies[off, other].wait()
            arrived[off, 0] = looked[0][block(off), :]
            for other in range(half):
                at = pl.multiple_of(lax.rem(place ^ other, half) * cols, cols)
                terms[off, :, pl.ds(at, cols)] = arrived[off, other] + arrived[off, other + half]

    rows = own * shards
    chunk = lax.rem(place, chunks)
    exchange_terms(parts, slots, work, term_sems, ready)
    total = work[...]
    if packed:
        scale = lax.rsqrt(column3(total[:, D:]) / DI + NORM_EPS)
        branch[...] = total[:, :D]
        factor[...] = scale
        total = before[...] + scale * total[:, :D]
    residual[...] = total
    at = pl.ds(pl.multiple_of(RIM + shard * own, RIM), own)
    normed[at, :] = norm_rows(total, gain[...]).astype(BF)

    def rim_copy(to, device):
        return pltpu.make_async_remote_copy(
            src_ref=normed.at[rows : rows + RIM, :],
            dst_ref=normed.at[0:RIM, :],
            send_sem=rim_sems.at[0, to],
            recv_sem=rim_sems.at[1, 0],
            device_id=device,
            device_id_type=pl.DeviceIdType.MESH,
        )

    gives = jnp.logical_and(shard == shards - 1, chunk + 1 < chunks)
    if rims:

        @pl.when(gives)
        def _():
            for to in range(shards):
                rim_copy(to, (place + 1, to)).start()

        @pl.when(chunk == 0)
        def _():
            normed[0:RIM, :] = jnp.zeros((RIM, D), BF)

    else:
        normed[0:RIM, :] = jnp.zeros((RIM, D), BF)
    pass_along(normed, own, RIM, shards, row_sems)
    if rims:

        @pl.when(chunk > 0)
        def _():
            rim_copy(0, (place - 1, shards - 1)).wait_recv()

        @pl.when(gives)
        def _():
            for to in range(shards):
                rim_copy(to, (place + 1, to)).wait_send()


def forward_rows(parts, before, gain, groups, chunks, rims, cid, entry=0):
    packed = before is not None
    if packed:
        shards = len(parts)
        own, width = parts[0].shape
        args = (*parts, before, gain)
        extra = []
    else:
        shards = entry
        own, width = parts[0].shape[0] // shards, D
        args = (*parts, gain)
        extra = [
            pltpu.VMEM((shards, groups, own, parts[0].shape[1]), BF),
            pltpu.VMEM((shards, own, D), BF),
            pltpu.SemaphoreType.DMA((2, shards, groups)),
        ]
    vmem = pl.BlockSpec(memory_space=pltpu.VMEM)
    outs = [sds((own, D), F32)]
    if packed:
        outs += [sds((own, D), F32), sds((own, 1), F32)]
    outs += [sds((RIM + own * shards, D), BF)]
    return pl.pallas_call(
        functools.partial(forward_kernel, groups, shards, chunks, packed, rims),
        out_shape=outs,
        in_specs=[vmem] * len(args),
        out_specs=[vmem] * len(outs),
        scratch_shapes=[
            *term_scratch(shards, own, width),
            pltpu.SemaphoreType.DMA((2, 2, shards)),
            pltpu.SemaphoreType.DMA((2, shards)),
            *extra,
        ],
        compiler_params=pltpu.CompilerParams(
            collective_id=cid, has_side_effects=True, vmem_limit_bytes=60 * MIB
        ),
        name="forward" if packed else "enter",
    )(*args)


def backward_kernel(groups, shards, chunks, exchanged, *refs):
    parts, refs = refs[:shards], refs[shards:]
    if exchanged:
        residual, gain, branch, factor, grad_out, rows_out, gain_grad, row_sems = refs
    else:
        rim, residual, gain, grad_in, branch, factor, grad_out, rows_out, refs = *refs[:8], refs[8:]
        slots, work, term_sems, from_rims, rim_sems, row_sems = refs
    own = parts[0].shape[0]
    place, shard = lax.axis_index("dp"), lax.axis_index("tensor")
    chunk = lax.rem(place, chunks)
    greet_shards(groups, shards, not exchanged)
    values = residual[...]
    inv = lax.rsqrt(jnp.mean(values * values, axis=-1, keepdims=True) + NORM_EPS)
    if exchanged:
        grad = total_of(parts)
        gain_grad[...] = jnp.sum(grad * values * inv, axis=0, keepdims=True)
    else:

        def rim_copy(slot, device):
            return pltpu.make_async_remote_copy(
                src_ref=rim,
                dst_ref=from_rims.at[slot],
                send_sem=rim_sems.at[0, slot],
                recv_sem=rim_sems.at[1, slot],
                device_id=device,
                device_id_type=pl.DeviceIdType.MESH,
            )

        @pl.when(chunk > 0)
        def _():
            rim_copy(shard, (place - 1, shards - 1)).start()

        exchange_terms(parts, slots, work, term_sems)

        @pl.when(jnp.logical_and(shard == shards - 1, chunk + 1 < chunks))
        def _():
            for other in range(shards):
                rim_copy(other, (place + 1, other)).wait_recv()
            edge = from_rims[0].astype(F32)
            for other in range(1, shards):
                edge = edge + from_rims[other].astype(F32)
            work[own - RIM :, :] += edge

        @pl.when(chunk > 0)
        def _():
            rim_copy(shard, (place - 1, shards - 1)).wait_send()

        grad = work[...]
    scaled = grad * gain[...]
    result = inv * scaled - values * (inv * inv * inv) * jnp.mean(
        scaled * values, axis=-1, keepdims=True
    )
    if not exchanged:
        result = grad_in[...] + result
    grad_out[...] = result
    scale = factor[...]
    at = pl.ds(pl.multiple_of(shard * own, RIM), own)
    rows_out[at, :D] = (scale * result).astype(BF)
    inner_rows = jnp.sum(result * branch[...], axis=-1, keepdims=True)
    rows_out[at, D:] = lanes3(scale * scale * scale * inner_rows / DI)
    pass_along(rows_out, own, 0, shards, row_sems)


def backward_rows(parts, rim, residual, gain, grad_in, branch, factor, groups, chunks, cid):
    shards = len(parts)
    own = residual.shape[0]
    exchanged = rim is None
    vmem = pl.BlockSpec(memory_space=pltpu.VMEM)
    outs = [sds((own, D), F32), sds((own * shards, D + LANES), BF)]
    row_sems = pltpu.SemaphoreType.DMA((2, 2, shards))
    if exchanged:
        args = (*parts, residual, gain, branch, factor)
        outs.append(sds((1, D), F32))
        scratch = [row_sems]
    else:
        args = (*parts, rim, residual, gain, grad_in, branch, factor)
        scratch = [
            *term_scratch(shards, own, D),
            pltpu.VMEM((shards, RIM, D), BF),
            pltpu.SemaphoreType.DMA((2, shards)),
            row_sems,
        ]
    return pl.pallas_call(
        functools.partial(backward_kernel, groups, shards, chunks, exchanged),
        out_shape=outs,
        in_specs=[vmem] * len(args),
        out_specs=[vmem] * len(outs),
        scratch_shapes=scratch,
        compiler_params=pltpu.CompilerParams(
            collective_id=cid, has_side_effects=True, vmem_limit_bytes=60 * MIB
        ),
        name="backward",
    )(*args)


def stats_kernel(shards, chunks, stats, tops, weight, scale_out, loss_out, slots, sems):
    place, shard = lax.axis_index("dp"), lax.axis_index("tensor")
    rows = weight.shape[1]
    own = rows // shards
    greet_shards(0, shards, False)
    copies = [
        send(stats, slots.at[off - 1], sems.at[0, off], sems.at[1, off], (place, shard ^ off))
        for off in range(1, shards)
    ]
    for copy in copies:
        copy.wait()
    others = [stats[...]] + [slots[off] for off in range(shards - 1)]
    best = others[0][0:1, :]
    for one in others[1:]:
        best = jnp.maximum(best, one[0:1, :])
    summed, target, plain = jnp.zeros((1, rows), F32), jnp.zeros((1, rows), F32), jnp.zeros((1, rows), F32)
    for one in others:
        summed = summed + one[1:2, :] * jnp.exp(one[0:1, :] - best)
        target = target + one[2:3, :]
        plain = plain + one[3:4, :]
    log_total = best + jnp.log(summed)
    token_loss = (
        log_total
        - (1.0 - SMOOTHING) * target
        - SMOOTHING / V * plain
        + ZLOSS_WEIGHT * log_total * log_total
    )
    lane = iota((1, rows), 1)
    mine = jnp.logical_and(lane >= shard * own, lane < (shard + 1) * own)
    loss = jnp.sum(jnp.where(mine, weight[...] * token_loss, 0.0), axis=1, keepdims=True)
    here = jnp.logical_and(iota((8, LANES), 0) == 0, iota((8, LANES), 1) == place // chunks)
    loss_out[...] = jnp.where(here, loss, 0.0)
    soft = weight[...] * (1.0 + 2.0 * ZLOSS_WEIGHT * log_total)
    for step in range(tops.shape[0]):
        scale_out[step] = soft * jnp.exp(tops[step] - log_total)


def merge_stats(stats, tops, weight, shards, chunks):
    vmem = pl.BlockSpec(memory_space=pltpu.VMEM)
    return pl.pallas_call(
        functools.partial(stats_kernel, shards, chunks),
        out_shape=[sds(tops.shape, F32), sds((8, LANES), F32)],
        in_specs=[vmem] * 3,
        out_specs=[vmem] * 2,
        scratch_shapes=[
            pltpu.VMEM((shards - 1, *stats.shape), F32),
            pltpu.SemaphoreType.DMA((2, shards)),
        ],
        compiler_params=pltpu.CompilerParams(
            collective_id=9, has_side_effects=True, vmem_limit_bytes=60 * MIB
        ),
        name="stats",
    )(stats, tops, weight)


def finish_kernel(groups, shards, chunks, own, *refs):
    parts, rim, residual, gain, grad_in, out = refs[:shards], *refs[shards : shards + 5]
    slots, work, term_sems, from_rims, payload, full, rim_sems, row_sems, out_sems = refs[shards + 5 :]
    place, shard = lax.axis_index("dp"), lax.axis_index("tensor")
    half = groups // 2
    cols = out.shape[2]
    chunk = lax.rem(place, chunks)
    last = shard == shards - 1
    shard_peers = [(place, shard ^ off) for off in range(1, shards)]
    group_peers = [(place ^ off, shard) for off in range(1, groups)]
    barrier = pltpu.get_barrier_semaphore()

    def greet(device):
        pl.semaphore_signal(barrier, inc=1, device_id=device, device_id_type=pl.DeviceIdType.MESH)

    for peer in shard_peers + group_peers:
        greet(peer)

    @pl.when(jnp.logical_not(last))
    def _():
        greet((lax.rem(place + groups - 1, groups), shards - 1))

    @pl.when(last)
    def _():
        for other in range(shards - 1):
            greet((lax.rem(place + 1, groups), other))

    pl.semaphore_wait(barrier, shards + groups - 2 + jnp.where(last, shards - 1, 1))

    def rim_copy():
        return pltpu.make_async_remote_copy(
            src_ref=rim,
            dst_ref=from_rims.at[shard],
            send_sem=rim_sems.at[0, shard],
            recv_sem=rim_sems.at[1, shard],
            device_id=(place - 1, shards - 1),
            device_id_type=pl.DeviceIdType.MESH,
        )

    @pl.when(chunk > 0)
    def _():
        rim_copy().start()

    values = residual[...]
    inv = lax.rsqrt(jnp.mean(values * values, axis=-1, keepdims=True) + NORM_EPS)
    exchange_terms(parts, slots, work, term_sems)

    @pl.when(jnp.logical_and(chunk + 1 < chunks, last))
    def _():
        for other in range(shards):
            pltpu.make_async_remote_copy(
                src_ref=rim,
                dst_ref=from_rims.at[other],
                send_sem=rim_sems.at[0, other],
                recv_sem=rim_sems.at[1, other],
                device_id=(place + 1, other),
                device_id_type=pl.DeviceIdType.MESH,
            ).wait_recv()
        edge = from_rims[0].astype(F32)
        for other in range(1, shards):
            edge = edge + from_rims[other].astype(F32)
        work[own - RIM :, :] += edge

    @pl.when(chunk > 0)
    def _():
        rim_copy().wait_send()

    scaled = work[...] * gain[...]
    result = (
        grad_in[...]
        + inv * scaled
        - values * (inv * inv * inv) * jnp.mean(scaled * values, axis=-1, keepdims=True)
    ).astype(BF)
    payload[...] = result
    rows_out = [
        send(
            payload,
            full.at[off],
            row_sems.at[0, off],
            row_sems.at[1, off],
            shard_peers[off - 1],
        )
        for off in range(1, shards)
    ]
    full[0] = result

    def first_col(group):
        return pl.multiple_of(lax.rem(group, half) * cols, cols)

    cuts = []
    for off in range(shards):
        if off > 0:
            rows_out[off - 1].wait()
        at = pl.ds(pl.multiple_of((shard ^ off) * own, own), own)
        for other in range(1, groups):
            cuts.append(
                send(
                    full.at[off, :, pl.ds(first_col(place ^ other), cols)],
                    out.at[other, at, :],
                    out_sems.at[0, off, other],
                    out_sems.at[1, off, other],
                    group_peers[other - 1],
                )
            )
        out[0, at, :] = full[off, :, pl.ds(first_col(place), cols)]
    for cut in cuts:
        cut.wait()


def finish_rows(parts, rim, residual, gain, grad_in, groups, chunks):
    shards = len(parts)
    own = parts[0].shape[0]
    vmem = pl.BlockSpec(memory_space=pltpu.VMEM)
    args = (*parts, rim, residual, gain, grad_in)
    return pl.pallas_call(
        functools.partial(finish_kernel, groups, shards, chunks, own),
        out_shape=sds((groups, own * shards, 2 * D // groups), BF),
        in_specs=[vmem] * len(args),
        out_specs=vmem,
        scratch_shapes=[
            *term_scratch(shards, own, D),
            pltpu.VMEM((shards, RIM, D), BF),
            pltpu.VMEM((own, D), BF),
            pltpu.VMEM((shards, own, D), BF),
            pltpu.SemaphoreType.DMA((2, shards)),
            pltpu.SemaphoreType.DMA((2, shards)),
            pltpu.SemaphoreType.DMA((2, shards, groups)),
        ],
        compiler_params=pltpu.CompilerParams(
            collective_id=3, has_side_effects=True, vmem_limit_bytes=60 * MIB
        ),
        name="finish",
    )(*args)


def open_kernel(groups, shards, ids, piece, share, ids_out, pieces_out, share_out, middle, sends, gets):
    place, shard = lax.axis_index("dp"), lax.axis_index("tensor")
    near = [(place, shard ^ off) for off in range(1, shards)]
    far = [(place ^ off, shard) for off in range(1, groups)]
    barrier = pltpu.get_barrier_semaphore()
    for peer in near + far:
        pl.semaphore_signal(barrier, inc=1, device_id=peer, device_id_type=pl.DeviceIdType.MESH)
    pl.semaphore_wait(barrier, len(near) + len(far))
    shares, others = [], []
    for i, peer in enumerate(near):
        shares.append(send(share, middle.at[shard], sends.at[0, i], gets.at[0, i], peer))
    for i, peer in enumerate(far):
        others.append(send(ids, ids_out.at[place], sends.at[1, i], gets.at[1, i], peer))
    for i, peer in enumerate(near):
        others.append(send(piece, pieces_out.at[shard], sends.at[2, i], gets.at[2, i], peer))
    middle[shard] = share[...]
    ids_out[place] = ids[...]
    pieces_out[shard] = piece[...]
    for copy in shares:
        copy.wait()
    for i, peer in enumerate(far):
        others.append(send(middle, share_out.at[place], sends.at[3, i], gets.at[3, i], peer))
    share_out[place] = middle[...]
    for copy in others:
        copy.wait()


def open_exchange(ids, piece, share, groups, shards):
    count = max(groups, shards)
    vmem = pl.BlockSpec(memory_space=pltpu.VMEM)
    return pl.pallas_call(
        functools.partial(open_kernel, groups, shards),
        out_shape=[
            sds((groups, *ids.shape), jnp.int32),
            sds((shards, *piece.shape), BF),
            sds((groups, shards, *share.shape), BF),
        ],
        in_specs=[vmem] * 3,
        out_specs=[vmem] * 3,
        scratch_shapes=[
            pltpu.VMEM((shards, *share.shape), BF),
            pltpu.SemaphoreType.DMA((4, count)),
            pltpu.SemaphoreType.DMA((4, count)),
        ],
        compiler_params=pltpu.CompilerParams(
            collective_id=2, has_side_effects=True, vmem_limit_bytes=60 * MIB
        ),
        name="open",
    )(ids, piece, share)


def sum_kernel(groups, shards, once, split, *refs):
    loss = refs[0]
    refs = refs[1:]
    count = once + split
    ones, many, refs = refs[:once], refs[once:count], refs[count:]
    o_ref, start, mid, from_shards, from_groups, send, recv = refs
    place, shard = lax.axis_index("dp"), lax.axis_index("tensor")
    peers = [(place, shard ^ off) for off in range(1, shards)]
    peers += [(place ^ off, shard) for off in range(1, groups)]
    barrier = pltpu.get_barrier_semaphore()
    for peer in peers:
        pl.semaphore_signal(barrier, inc=1, device_id=peer, device_id_type=pl.DeviceIdType.MESH)

    def square(refs):
        total = jnp.zeros((1, 1), F32)
        for ref in refs:
            flat = jnp.sum(ref[...] * ref[...], axis=0, keepdims=True)
            total = total + jnp.sum(flat, axis=1, keepdims=True)
        return total

    first = (place == 0).astype(F32)
    part = square(many) + first * square(ones)
    start[...] = loss[...] + jnp.where(iota((8, LANES), 1) == LANES - 1, part, 0.0)
    pl.semaphore_wait(barrier, len(peers))

    def exchange(source, slots, first, some):
        copies = []
        for i, peer in enumerate(some):
            copy = pltpu.make_async_remote_copy(
                src_ref=source,
                dst_ref=slots.at[i],
                send_sem=send.at[first + i],
                recv_sem=recv.at[first + i],
                device_id=peer,
                device_id_type=pl.DeviceIdType.MESH,
            )
            copy.start()
            copies.append(copy)
        for copy in copies:
            copy.wait()
        total = source[...]
        for i in range(len(some)):
            total = total + slots[i]
        return total

    mid[...] = exchange(start, from_shards, 0, peers[: shards - 1])
    total = exchange(mid, from_groups, shards - 1, peers[shards - 1 :])
    norm = jnp.sqrt(total[0:1, LANES - 1 : LANES])
    factor = jnp.minimum(1.0, CLIP_LIMIT / (norm + 1e-06))
    row = iota((8, LANES), 0)
    o_ref[...] = jnp.where(row == 0, total, jnp.where(row == 1, norm, factor))


def sum_everywhere(loss, ones, many, groups, shards):
    count = groups + shards - 2
    args = (loss, *ones, *many)
    vmem = pl.BlockSpec(memory_space=pltpu.VMEM)
    return pl.pallas_call(
        functools.partial(sum_kernel, groups, shards, len(ones), len(many)),
        out_shape=sds((8, LANES), F32),
        in_specs=[vmem] * len(args),
        out_specs=vmem,
        scratch_shapes=[
            pltpu.VMEM((8, LANES), F32),
            pltpu.VMEM((8, LANES), F32),
            pltpu.VMEM((shards - 1, 8, LANES), F32),
            pltpu.VMEM((groups - 1, 8, LANES), F32),
            pltpu.SemaphoreType.DMA((count,)),
            pltpu.SemaphoreType.DMA((count,)),
        ],
        compiler_params=pltpu.CompilerParams(
            collective_id=1, has_side_effects=True, vmem_limit_bytes=60 * MIB
        ),
        name="sumall",
    )(*args)


def conv_sum(raw, params, rows, lanes):
    total = params[4:5, :] + params[0:1, :] * raw[pl.ds(RIM - 3, rows), lanes]
    for k in range(1, 4):
        total = total + params[k : k + 1, :] * raw[pl.ds(RIM - 3 + k, rows), lanes]
    return total


def front_kernel(normed, wzx, wside, chan, bcp, head, *rest):
    z_out, xr, side, yloc, final, c_out, cum_out, xs_scr = rest
    rows = normed.shape[0] - RIM
    inner = chan.shape[1]
    z_out[...] = nn(normed[RIM:, :], wzx[:, :inner])
    xr[...] = nn(normed[...], wzx[:, inner:])
    side[...] = nn(normed[...], wside[...])
    pre = conv_sum(xr, chan, rows, pl.ds(0, inner))
    xs_scr[...] = pre * sigmoid(pre)
    pre = conv_sum(side, bcp, rows, pl.ds(0, 2 * N))
    bc = (pre * sigmoid(pre)).astype(BF)
    c_out[...] = bc[:, N:]
    dt = softplus(side[RIM:, 2 * N :] + head[0:1, :])
    rate = -dt * jnp.exp(head[1:2, :])
    expand = head_map(inner)
    skip = widen(head[...], expand)[2:3, :]
    lower = (iota((SPAN, SPAN), 0) >= iota((SPAN, SPAN), 1)).astype(F32)
    lower_low = lower.astype(BF)
    first_half = iota((SPAN, LANES), 1) < P_SIZE
    state = None
    base = jnp.zeros((1, LANES), F32)
    for span in range(rows // SPAN):
        here = slice(span * SPAN, (span + 1) * SPAN)
        cum = tri_sum(lower_low, rate[here])
        cum_t = cum.T
        tot = cum[SPAN - 1 : SPAN, :]
        keys = bc[here, :N]
        queries = bc[here, N:]
        scores = nt_dot(queries, keys)
        xs = xs_scr[here, :]
        scaled = xs * widen(dt[here], expand)
        scaled_low = scaled.astype(BF)
        pieces = []
        for pair in range(inner // LANES):
            values = scaled_low[:, pair * LANES : (pair + 1) * LANES]
            both = []
            for h in (2 * pair, 2 * pair + 1):
                gap = cum[:, h : h + 1] - cum_t[h : h + 1, :]
                decay = jnp.exp(jnp.minimum(gap, 0.0)) * lower
                both.append(nn((scores * decay).astype(BF), values))
            pieces.append(jnp.where(first_half, both[0], both[1]))
        y = jnp.concatenate(pieces, axis=1) + skip * xs
        if state is not None:
            y = y + widen(jnp.exp(cum), expand) * nn(queries, state.astype(BF))
        yloc[here, :] = y
        tail = widen(jnp.exp(tot - cum), expand)
        fresh = tn(keys, (scaled * tail).astype(BF))
        if state is not None:
            fresh = fresh + widen(jnp.exp(tot), expand) * state
        state = fresh
        cum_out[here, :] = cum + base
        base = base + tot
    final[0:N, :] = state.astype(BF)
    final[N:, :] = rows3(base, inner)


def mixer_front(normed, wzx, wside, chan, bcp, head):
    rows = normed.shape[0] - RIM
    inner = chan.shape[1]
    return call(
        front_kernel,
        "front",
        [
            sds((rows, inner), F32),
            sds((rows + RIM, inner), F32),
            sds((rows + RIM, 2 * N + LANES), F32),
            sds((rows, inner), F32),
            sds((N + RIM, inner), BF),
            sds((rows, N), BF),
            sds((rows, LANES), F32),
        ],
        (normed, wzx, wside, chan, bcp, head),
        scratch=[pltpu.VMEM((rows, inner), F32)],
        flops=8 * rows * D * inner,
        moved=12 * MIB,
    )


def chain(parts, expand):
    total = None
    past = jnp.zeros((1, LANES), F32)
    for part in parts:
        term = widen(jnp.exp(past), expand) * part[0:N, :].astype(F32)
        total = term if total is None else total + term
        past = past + jnp.sum(part[N:, :LANES].astype(F32), axis=0, keepdims=True)
    return total


def middle_kernel(shards, own, hops, scal, *rest):
    states, rest = rest[:hops], rest[hops:]
    yloc, z_in, c_in, cum, wout, chan = rest[:6]
    y_out, s_out = rest[6:8]
    parts, work = rest[8 : 8 + shards], rest[-1]
    shard = scal[0]
    rows, inner = yloc.shape
    expand = head_map(inner)
    state = chain(states, expand)
    s_out[...] = state
    y = yloc[...] + widen(jnp.exp(cum[...]), expand) * nn(c_in[...], state.astype(BF))
    y_out[...] = y
    z = z_in[...]
    gated = y * (z * sigmoid(z))
    work[:, :D] = nn((gated * chan[5:6, :]).astype(BF), wout[...]).astype(BF)
    work[:, D:] = lanes3(jnp.sum(gated * gated, axis=1, keepdims=True))
    for off in range(shards):
        at = pl.multiple_of((shard ^ off) * own, own)
        parts[off][...] = work[pl.ds(at, own), :]


def mixer_middle(scal, states, yloc, z_in, c_in, cum, wout, chan, shards):
    rows, inner = yloc.shape
    own = rows // shards
    return call(
        functools.partial(middle_kernel, shards, own, len(states)),
        "middle",
        [sds((rows, inner), F32), sds((N, inner), F32)]
        + [sds((own, D + LANES), BF)] * shards,
        (scal, *states, yloc, z_in, c_in, cum, wout, chan),
        smem=(0,),
        scratch=[pltpu.VMEM((rows, D + LANES), BF)],
        flops=2 * rows * D * inner,
        moved=8 * MIB,
    )


def gate_back_kernel(grads, wout, y_in, z_in, c_in, cum, chan, *rest):
    u_out, dy_out, dz_out, state_out, gain_out = rest
    inner = chan.shape[1]
    du = nt_dot(grads[:, :D], wout[...])
    coef = column3(grads[:, D:].astype(F32))
    z = z_in[...]
    y = y_in[...]
    sig = sigmoid(z)
    silu = z * sig
    gated = y * silu
    gain_out[...] = jnp.sum(du * gated, axis=0, keepdims=True)
    gain = chan[5:6, :]
    u_out[...] = (gated * gain).astype(BF)
    dgated = du * gain - gated * coef
    dy = dgated * silu
    dy_out[...] = dy
    dz_out[...] = (dgated * y * (sig * (1.0 + z * (1.0 - sig)))).astype(BF)
    grown = widen(jnp.exp(cum[...]), head_map(inner))
    state_out[0:N, :] = tn(c_in[...], (dy * grown).astype(BF)).astype(BF)
    rows = dy.shape[0]
    state_out[N:, :] = rows3(cum[rows - 1 : rows, :], inner)


def gate_back(grads, wout, y, z_in, c_in, cum, chan):
    rows, inner = y.shape
    return call(
        gate_back_kernel,
        "gateback",
        [
            sds((rows, inner), BF),
            sds((rows, inner), F32),
            sds((rows, inner), BF),
            sds((N + RIM, inner), BF),
            sds((1, inner), F32),
        ],
        (grads, wout, y, z_in, c_in, cum, chan),
        flops=2 * rows * D * inner,
        moved=10 * MIB,
    )


def silu_slope(pre):
    sig = sigmoid(pre)
    return sig * (1.0 + pre * (1.0 - sig))


def conv_back(ds_scr, raw, params, rows, lanes, width, low_out, out_lanes):
    ext = rows + RIM
    total = params[0:1, :] * ds_scr[pl.ds(3, ext), :]
    for k in range(1, 4):
        total = total + params[k : k + 1, :] * ds_scr[pl.ds(3 - k, ext), :]
    low_out[:, out_lanes] = total.astype(BF)
    ds = ds_scr[pl.ds(RIM, rows), :]
    grads = [
        jnp.sum(ds * raw[pl.ds(RIM - 3 + k, rows), lanes], axis=0, keepdims=True) for k in range(4)
    ]
    grads.append(jnp.sum(ds, axis=0, keepdims=True))
    grads.append(jnp.zeros((3, width), F32))
    return jnp.concatenate(grads, axis=0)


def within_kernel(s_in, xr, side, dy_in, chan, bcp, head, *outs):
    xs_out, bc_out, cum_out, starts_out, dscaled_out, dbc_out = outs
    rows, inner = dy_in.shape
    expand = head_map(inner)
    pre_x = conv_sum(xr, chan, rows, pl.ds(0, inner))
    xs_out[...] = pre_x * sigmoid(pre_x)
    pre_bc = conv_sum(side, bcp, rows, pl.ds(0, 2 * N))
    bc = (pre_bc * sigmoid(pre_bc)).astype(BF)
    bc_out[...] = bc
    dt = softplus(side[RIM:, 2 * N :] + head[0:1, :])
    rate = -dt * jnp.exp(head[1:2, :])
    lower_low = (iota((SPAN, SPAN), 0) >= iota((SPAN, SPAN), 1)).astype(F32).astype(BF)
    upper = (iota((SPAN, SPAN), 0) <= iota((SPAN, SPAN), 1)).astype(F32)
    first_half = iota((SPAN, LANES), 1) < P_SIZE
    spans = rows // SPAN
    start = s_in[...]
    for span in range(spans):
        here = slice(span * SPAN, (span + 1) * SPAN)
        cum = tri_sum(lower_low, rate[here])
        cum_out[here, :] = cum
        cum_t = cum.T
        keys = bc[here, :N]
        queries = bc[here, N:]
        xs = xs_out[here, :]
        starts_out[span] = start
        start_low = start.astype(BF)
        if span + 1 < spans:
            tot = cum[SPAN - 1 : SPAN, :]
            scale = widen(dt[here] * jnp.exp(tot - cum), expand)
            fresh = tn(keys, (xs * scale).astype(BF))
            start = widen(jnp.exp(tot), expand) * start + fresh
        scores_t = nt_dot(keys, queries)
        dy = dy_in[here, :]
        dy_low = dy.astype(BF)
        scaled_low = (xs * widen(dt[here], expand)).astype(BF)
        dscores_t = jnp.zeros((SPAN, SPAN), F32)
        for pair in range(inner // LANES):
            lanes = slice(pair * LANES, (pair + 1) * LANES)
            values = scaled_low[:, lanes]
            dpair = dy_low[:, lanes]
            both = []
            for h in (2 * pair, 2 * pair + 1):
                gap = cum_t[h : h + 1, :] - cum[:, h : h + 1]
                decay = jnp.exp(jnp.minimum(gap, 0.0)) * upper
                mine = first_half if h % 2 == 0 else jnp.logical_not(first_half)
                outer = nt_dot(jnp.where(mine, values, jnp.zeros_like(values)), dpair)
                dscores_t = dscores_t + outer * decay
                both.append(nn((scores_t * decay).astype(BF), dpair))
            dscaled_out[here, lanes] = jnp.where(first_half, both[0], both[1])
        dscores_low = dscores_t.astype(BF)
        dy_grown = (dy * widen(jnp.exp(cum), expand)).astype(BF)
        dbc_out[here, :N] = nn(dscores_low, queries)
        dbc_out[here, N:] = tn(dscores_low, keys) + nt_dot(dy_grown, start_low)


def mixer_within(s_in, xr, side, dy, chan, bcp, head):
    rows, inner = dy.shape
    return call(
        within_kernel,
        "within",
        [
            sds((rows, inner), F32),
            sds((rows, 2 * N), BF),
            sds((rows, LANES), F32),
            sds((rows // SPAN, N, inner), F32),
            sds((rows, inner), F32),
            sds((rows, 2 * N), F32),
        ],
        (s_in, xr, side, dy, chan, bcp, head),
        flops=8 * rows * D * inner,
        moved=16 * MIB,
    )


def back_kernel(shards, own, hops, scal, *rest):
    states, rest = rest[:hops], rest[hops:]
    xs_in, bc_in, cum_in, starts, dscaled_in, dbc_in, rest = *rest[:6], rest[6:]
    xr, side, dy_in, dz_in, y_in, wzx, wside, chan, bcp, head = rest[:10]
    normed, gain = rest[10:12]
    dzx, dside, chan_out, bcp_out, head_out, rim_out, gain_out = rest[12:19]
    parts, rest = rest[19 : 19 + shards], rest[19 + shards :]
    dsx, dsbc, work = rest
    shard = scal[0]
    rows, inner = dy_in.shape
    expand = head_map(inner)
    raw_dt = side[RIM:, 2 * N :] + head[0:1, :]
    dt = softplus(raw_dt)
    grow = jnp.exp(head[1:2, :])
    rate = -dt * grow
    skip = widen(head[...], expand)[2:3, :]
    upper_low = (iota((SPAN, SPAN), 0) <= iota((SPAN, SPAN), 1)).astype(F32).astype(BF)
    spans = rows // SPAN
    dstate = chain(states, expand)
    dsx[0:RIM, :] = jnp.zeros((RIM, inner), F32)
    dsx[RIM + rows :, :] = jnp.zeros((RIM, inner), F32)
    dsbc[0:RIM, :] = jnp.zeros((RIM, 2 * N), F32)
    dsbc[RIM + rows :, :] = jnp.zeros((RIM, 2 * N), F32)
    dside[0:RIM, 2 * N :] = jnp.zeros((RIM, LANES), BF)
    dzx[0:RIM, :inner] = jnp.zeros((RIM, inner), BF)
    dzx[RIM:, :inner] = dz_in[...]
    dbias = jnp.zeros((1, LANES), F32)
    dgrow = jnp.zeros((1, LANES), F32)
    dskip = jnp.zeros((1, LANES), F32)
    for span in reversed(range(spans)):
        here = slice(span * SPAN, (span + 1) * SPAN)
        there = slice(RIM + span * SPAN, RIM + (span + 1) * SPAN)
        cum = cum_in[here, :]
        tot = cum[SPAN - 1 : SPAN, :]
        keys = bc_in[here, :N]
        queries = bc_in[here, N:]
        xs = xs_in[here, :]
        dy = dy_in[here, :]
        dy_low = dy.astype(BF)
        dt_wide = widen(dt[here], expand)
        scaled = xs * dt_wide
        scaled_low = scaled.astype(BF)
        tail = widen(jnp.exp(tot - cum), expand)
        dstate_low = dstate.astype(BF)
        through = tail * nn(keys, dstate_low)
        dscaled = dscaled_in[here, :] + through
        plain = y_in[here, :] - skip * xs
        held = scaled_low.astype(F32)
        dcum = narrow(dy_low.astype(F32) * plain - held * dscaled, expand)
        tot_wide = widen(jnp.exp(tot), expand)
        over = jnp.sum(held * through, axis=0, keepdims=True) + jnp.sum(
            tot_wide * dstate * starts[span], axis=0, keepdims=True
        )
        dtot = narrow(jnp.broadcast_to(over, (8, inner)), expand)[0:1, :]
        drate = tri_sum(upper_low, dcum) + dtot
        ddt = narrow(dscaled * xs, expand) - drate * grow
        dgrow = dgrow + jnp.sum(drate * rate[here], axis=0, keepdims=True)
        draw = ddt * sigmoid(raw_dt[here])
        dbias = dbias + jnp.sum(draw, axis=0, keepdims=True)
        dside[there, 2 * N :] = draw.astype(BF)
        over = jnp.sum(dy * xs, axis=0, keepdims=True)
        dskip = dskip + narrow(jnp.broadcast_to(over, (8, inner)), expand)[0:1, :]
        dsx[there, :] = dscaled * dt_wide + skip * dy
        dsbc[there, :N] = dbc_in[here, :N] + nt_dot((scaled * tail).astype(BF), dstate_low)
        dsbc[there, N:] = dbc_in[here, N:]
        if span > 0:
            grown = widen(jnp.exp(cum), expand)
            dstate = tot_wide * dstate + tn(queries, (dy * grown).astype(BF))
    body = pl.ds(RIM, rows)
    pre_x = conv_sum(xr, chan, rows, pl.ds(0, inner))
    dsx[body, :] = dsx[body, :] * silu_slope(pre_x)
    pre_bc = conv_sum(side, bcp, rows, pl.ds(0, 2 * N))
    dsbc[body, :] = dsbc[body, :] * silu_slope(pre_bc)
    chan_out[...] = conv_back(
        dsx, xr, chan, rows, pl.ds(0, inner), inner, dzx, pl.ds(inner, inner)
    )
    bcp_out[...] = conv_back(dsbc, side, bcp, rows, pl.ds(0, 2 * N), 2 * N, dside, pl.ds(0, 2 * N))
    head_out[...] = jnp.concatenate([dbias, dgrow, dskip, jnp.zeros((5, LANES), F32)], axis=0)
    dnormed = nt_dot(dzx[...], wzx[...]) + nt_dot(dside[...], wside[...])
    work[...] = dnormed.astype(BF)
    gain_out[...] = jnp.sum(dnormed * normed[...].astype(F32), axis=0, keepdims=True) / gain[...]
    rim_out[...] = work[0:RIM, :]
    for off in range(shards):
        at = pl.multiple_of(RIM + (shard ^ off) * own, RIM)
        parts[off][...] = work[pl.ds(at, own), :]


def mixer_back(
    scal, states, inside, xr, side, dy, dz, y, wzx, wside, chan, bcp, head, normed, gain, shards
):
    rows, inner = dy.shape
    own = rows // shards
    ext = rows + RIM
    return call(
        functools.partial(back_kernel, shards, own, len(states)),
        "back",
        [
            sds((ext, 2 * inner), BF),
            sds((ext, 2 * N + LANES), BF),
            sds((8, inner), F32),
            sds((8, 2 * N), F32),
            sds((8, LANES), F32),
            sds((RIM, D), BF),
            sds((1, D), F32),
        ]
        + [sds((own, D), BF)] * shards,
        (scal, *states, *inside, xr, side, dy, dz, y, wzx, wside, chan, bcp, head, normed, gain),
        smem=(0,),
        scratch=[
            pltpu.VMEM((ext + RIM, inner), F32),
            pltpu.VMEM((ext + RIM, 2 * N), F32),
            pltpu.VMEM((ext, D), BF),
        ],
        flops=8 * rows * D * inner,
        moved=16 * MIB,
    )


def logits_kernel(vrows, label, table, normed, *rest):
    p_out, tops, stats, rows_scr, top, total, target, plain = rest
    step = pl.program_id(0)
    rows = normed.shape[0] - RIM

    @pl.when(step == 0)
    def _():
        rows_scr[...] = normed[RIM:, :].T
        top[...] = jnp.full((1, rows), -1e30, F32)
        total[...] = jnp.zeros((1, rows), F32)
        target[...] = jnp.zeros((1, rows), F32)
        plain[...] = jnp.zeros((1, rows), F32)

    highest, summed, hit, whole = top[...], total[...], target[...], plain[...]
    line = 2 * iota((PART, rows), 0)
    for half in range(2):
        for part_at in range(PAIRS // PART):
            first = step * PAIRS + part_at * PART
            here = slice(part_at * PART, (part_at + 1) * PART)
            padding = jnp.where(first + iota((PART, LANES), 0) < vrows, 0.0, -1e30)
            padding = jnp.concatenate([padding] * (rows // LANES), axis=1)
            raw = nn(table[here, half * D : (half + 1) * D], rows_scr[...])
            shown = raw + padding
            before = highest
            highest = jnp.maximum(before, jnp.max(shown, axis=0, keepdims=True))
            part = jnp.exp(shown - highest)
            summed = summed * jnp.exp(before - highest) + jnp.sum(part, axis=0, keepdims=True)
            wanted = label[...] - 2 * first - half
            hit = hit + jnp.sum(jnp.where(line == wanted, raw, 0.0), axis=0, keepdims=True)
            whole = whole + jnp.sum(raw, axis=0, keepdims=True)
            p_out[half, here, :] = part.astype(BF)
            at = 8 * (half * (PAIRS // PART) + part_at)
            tops[0, at : at + 8, :] = jnp.broadcast_to(highest, (8, rows))
    top[...] = highest
    total[...] = summed
    target[...] = hit
    plain[...] = whole
    stats[...] = jnp.concatenate([highest, summed, hit, whole, jnp.zeros((4, rows), F32)], axis=0)


def vocab_logits(label, table, normed, vrows):
    rows = normed.shape[0] - RIM
    padded = table.shape[0]
    steps = padded // PAIRS
    whole = lambda i: (0, 0)
    return pl.pallas_call(
        functools.partial(logits_kernel, vrows),
        grid=(steps,),
        out_shape=[
            sds((2, padded, rows), BF),
            sds((steps, 16 * (PAIRS // PART), rows), F32),
            sds((8, rows), F32),
        ],
        in_specs=[
            pl.BlockSpec((1, rows), whole),
            pl.BlockSpec((PAIRS, 2 * D), lambda i: (i, 0)),
            pl.BlockSpec(normed.shape, whole),
        ],
        out_specs=[
            pl.BlockSpec((2, PAIRS, rows), lambda i: (0, i, 0)),
            pl.BlockSpec((1, 16 * (PAIRS // PART), rows), lambda i: (i, 0, 0)),
            pl.BlockSpec((8, rows), whole),
        ],
        scratch_shapes=[pltpu.VMEM((D, rows), BF)] + [pltpu.VMEM((1, rows), F32)] * 4,
        compiler_params=pltpu.CompilerParams(
            dimension_semantics=("arbitrary",), vmem_limit_bytes=56 * MIB
        ),
        cost_estimate=pl.CostEstimate(
            flops=4 * rows * D * padded, bytes_accessed=40 * MIB, transcendentals=2 * rows * padded
        ),
        name="logits",
    )(label, table, normed)


def logit_grads(step, label, scale, weight, p_in):
    pairs, rows = p_in.shape[1:]
    line = 2 * iota((PART, rows), 0)
    usual = (SMOOTHING / V) * weight[...]
    special = (1.0 - SMOOTHING + SMOOTHING / V) * weight[...]
    for half in range(2):
        pieces = []
        for part_at in range(pairs // PART):
            wanted = label[...] - 2 * (step * pairs + part_at * PART) - half
            share = jnp.where(line == wanted, special, usual)
            at = 8 * (half * (pairs // PART) + part_at)
            grown = p_in[half, part_at * PART : (part_at + 1) * PART, :].astype(F32)
            pieces.append((grown * scale[0, at : at + 1, :] - share).astype(BF))
        yield half, jnp.concatenate(pieces, axis=0)


def rows_kernel(shards, own, scal, label, scale, weight, p_in, table, *rest):
    parts, acc = rest[:shards], rest[-1]
    step = pl.program_id(0)

    @pl.when(step == 0)
    def _():
        acc[...] = jnp.zeros_like(acc)

    for half, q in logit_grads(step, label, scale, weight, p_in):
        acc[...] += tn(q, table[:, half * D : (half + 1) * D])

    @pl.when(step == pl.num_programs(0) - 1)
    def _():
        for off in range(shards):
            at = pl.ds(pl.multiple_of((scal[0] ^ off) * own, own), own)
            parts[off][...] = acc[at, :].astype(BF)


def vocab_specs(rows):
    whole = lambda i: (0, 0)
    return [
        pl.BlockSpec((1, rows), whole),
        pl.BlockSpec((1, 16 * (PAIRS // PART), rows), lambda i: (i, 0, 0)),
        pl.BlockSpec((1, rows), whole),
        pl.BlockSpec((2, PAIRS, rows), lambda i: (0, i, 0)),
    ]


def vocab_rows(scal, label, scale, weight, p_in, table, shards):
    _, padded, rows = p_in.shape
    own = rows // shards
    whole = lambda i: (0, 0)
    return pl.pallas_call(
        functools.partial(rows_kernel, shards, own),
        grid=(padded // PAIRS,),
        out_shape=[sds((own, D), BF)] * shards,
        in_specs=[pl.BlockSpec(memory_space=pltpu.SMEM)]
        + vocab_specs(rows)
        + [pl.BlockSpec((PAIRS, 2 * D), lambda i: (i, 0))],
        out_specs=[pl.BlockSpec((own, D), whole)] * shards,
        scratch_shapes=[pltpu.VMEM((rows, D), F32)],
        compiler_params=pltpu.CompilerParams(
            dimension_semantics=("arbitrary",), vmem_limit_bytes=56 * MIB
        ),
        cost_estimate=pl.CostEstimate(
            flops=4 * rows * D * padded, bytes_accessed=40 * MIB, transcendentals=0
        ),
        name="rowgrads",
    )(scal, label, scale, weight, p_in, table)


def table_kernel(label, scale, weight, p_in, normed, out, rows_scr):
    step = pl.program_id(0)

    @pl.when(step == 0)
    def _():
        rows_scr[...] = normed[RIM:, :]

    for half, q in logit_grads(step, label, scale, weight, p_in):
        out[:, half * D : (half + 1) * D] = nn(q, rows_scr[...]).astype(BF)


def vocab_table_grad(label, scale, weight, p_in, normed):
    _, padded, rows = p_in.shape
    whole = lambda i: (0, 0)
    return pl.pallas_call(
        table_kernel,
        grid=(padded // PAIRS,),
        out_shape=sds((padded, 2 * D), BF),
        in_specs=vocab_specs(rows) + [pl.BlockSpec(normed.shape, whole)],
        out_specs=pl.BlockSpec((PAIRS, 2 * D), lambda i: (i, 0)),
        scratch_shapes=[pltpu.VMEM((rows, D), BF)],
        compiler_params=pltpu.CompilerParams(
            dimension_semantics=("arbitrary",), vmem_limit_bytes=56 * MIB
        ),
        cost_estimate=pl.CostEstimate(
            flops=4 * rows * D * padded, bytes_accessed=40 * MIB, transcendentals=0
        ),
        name="tablegrads",
    )(label, scale, weight, p_in, normed)


def adam_update(weight_in, gradient, moment_one, moment_two, factor, fix_one, fix_two, decay_rate):
    gradient = gradient * factor
    one_next = BETA_FIRST * moment_one + (1.0 - BETA_FIRST) * gradient
    two_next = BETA_SECOND * moment_two + (1.0 - BETA_SECOND) * gradient * gradient
    direction = one_next / fix_one / (jnp.sqrt(two_next / fix_two) + ADAM_EPS)
    return (weight_in - LEARN_RATE * (direction + decay_rate * weight_in), one_next, two_next)


def turn_kernel(share, bases, turned, root, total):
    step = pl.program_id(0)

    @pl.when(step == 0)
    def _():
        total[...] = jnp.zeros_like(total)

    for at in range(bases.shape[0]):
        grad = share[at * BLK : (at + 1) * BLK, :].astype(F32)
        half_turn = tn(bases[at, 0], grad, HIGHEST)
        turned[at] = nn(half_turn, bases[at, 1], HIGHEST)
        total[...] += jnp.sum(grad * grad, axis=0, keepdims=True)

    @pl.when(step == pl.num_programs(0) - 1)
    def _():
        root[...] = jnp.sqrt(total[...])


def turn_tiles(share, bases):
    count = bases.shape[0]
    each = 4 if count % 4 == 0 else 2
    return pl.pallas_call(
        turn_kernel,
        grid=(count // each,),
        out_shape=[sds((count, BLK, BLK), F32), sds((1, BLK), F32)],
        in_specs=[
            pl.BlockSpec((each * BLK, LANES), lambda i: (i, 0)),
            pl.BlockSpec((each, 2, BLK, BLK), lambda i: (i, 0, 0, 0)),
        ],
        out_specs=[
            pl.BlockSpec((each, BLK, BLK), lambda i: (i, 0, 0)),
            pl.BlockSpec((1, BLK), lambda i: (0, 0)),
        ],
        scratch_shapes=[pltpu.VMEM((1, BLK), F32)],
        compiler_params=pltpu.CompilerParams(
            dimension_semantics=("arbitrary",), vmem_limit_bytes=60 * MIB
        ),
        cost_estimate=pl.CostEstimate(
            flops=24 * count * BLK * BLK * BLK, bytes_accessed=6 * MIB, transcendentals=0
        ),
        name="turn",
    )(share, bases)


def last_kernel(small, fixes, sums, *refs):
    tiles, turned, bases, tile_one, tile_two = refs[:5]
    little, refs = refs[5 : 5 + 4 * small], refs[5 + 4 * small :]
    tiles_out, copy_out, tile_one_out, tile_two_out = refs[:4]
    little_out = refs[4:]
    factor, fix_one, fix_two = sums[2:3, 0:1], fixes[0], fixes[1]
    for at in range(tiles.shape[0]):
        rotated = turned[at] * factor
        one_next = BETA_FIRST * tile_one[at] + (1.0 - BETA_FIRST) * rotated
        two_next = BETA_SECOND * tile_two[at] + (1.0 - BETA_SECOND) * rotated * rotated
        direction = one_next / fix_one / (jnp.sqrt(two_next / fix_two) + ADAM_EPS)
        back_half = nn(bases[at, 0], direction, HIGHEST)
        back = nt_dot(back_half, bases[at, 1], HIGHEST)
        after = tiles[at] - LEARN_RATE * (back + WEIGHT_DECAY * tiles[at])
        tiles_out[at] = after
        copy_out[at] = after.astype(BF)
        tile_one_out[at] = one_next
        tile_two_out[at] = two_next

    @pl.when(pl.program_id(0) == 0)
    def _():
        for which in range(small):
            before, gradient, first, second = (ref[...] for ref in little[4 * which : 4 * which + 4])
            results = adam_update(
                before,
                gradient,
                first,
                second,
                factor,
                fix_one,
                fix_two,
                WEIGHT_DECAY if which == 0 else 0.0,
            )
            outs = little_out[3 * which : 3 * which + 3]
            outs[0][...] = results[0] if which == 0 else results[0] - before
            outs[1][...], outs[2][...] = results[1], results[2]


def last_update(fixes, sums, tiles, turned, bases, tile_one, tile_two, little):
    count = tiles.shape[0]
    each = 4 if count % 4 == 0 else 2
    tile_spec = pl.BlockSpec((each, BLK, BLK), lambda i: (i, 0, 0))
    base_spec = pl.BlockSpec((each, 2, BLK, BLK), lambda i: (i, 0, 0, 0))
    whole = [
        pl.BlockSpec(x.shape, lambda i, rank=x.ndim: (0,) * rank) for group in little for x in group
    ]
    return pl.pallas_call(
        functools.partial(last_kernel, len(little)),
        grid=(count // each,),
        out_shape=[sds(tiles.shape, F32), sds(tiles.shape, BF), sds(tiles.shape, F32), sds(tiles.shape, F32)]
        + [sds(group[0].shape, F32) for group in little for _ in range(3)],
        in_specs=[
            pl.BlockSpec(memory_space=pltpu.SMEM),
            pl.BlockSpec(sums.shape, lambda i: (0, 0)),
        ]
        + [tile_spec, tile_spec, base_spec, tile_spec, tile_spec]
        + whole,
        out_specs=[tile_spec] * 4
        + [spec for which in range(len(little)) for spec in whole[4 * which : 4 * which + 3]],
        compiler_params=pltpu.CompilerParams(
            dimension_semantics=("arbitrary",), vmem_limit_bytes=60 * MIB
        ),
        cost_estimate=pl.CostEstimate(
            flops=24 * count * BLK * BLK * BLK, bytes_accessed=16 * MIB, transcendentals=0
        ),
        name="update",
    )(
        fixes,
        sums,
        tiles,
        turned,
        bases,
        tile_one,
        tile_two,
        *[x for group in little for x in group],
    )


def total_over(x, axis):
    out = x
    for off in range(1, lax.axis_size(axis)):
        out = out + swap(x, axis, off)
    return out


def shards(
    token_ids,
    labels,
    seq_lengths,
    micro_batch,
    step_count,
    block_slot,
    vocab_table,
    vocab_first,
    vocab_second,
    layer_blocks,
    block_bases,
    block_first,
    block_second,
    side_proj,
    side_first,
    side_second,
    shared_params,
    shared_first,
    shared_second,
    channel_params,
    channel_first,
    channel_second,
    head_params,
    head_first,
    head_second,
):
    nt = lax.axis_size("tensor")
    nd = lax.axis_size("dp")
    shard = lax.axis_index("tensor")
    place = lax.axis_index("dp")
    seqs = token_ids.shape[0]
    length = token_ids.shape[1] * nd
    chunks = nd // seqs
    rows = seqs * length // nd
    own = rows // nt
    vrows = vocab_table.shape[0]
    padded = -(-vrows // PAIRS) * PAIRS
    half = nd // 2
    inner = channel_params.shape[2]
    heads = head_params.shape[2]
    tiles = block_slot.shape[1]
    zx_count = D * 2 * inner // (BLK * BLK)
    per_layer = 3 * D * inner // (BLK * BLK)
    stride = D + 10 * N
    both = ("dp", "tensor")
    side_rows = side_proj.shape[1]
    share_size = shared_params.shape[0]
    share_pad = -(-share_size // 2048) * 2048

    piece = jnp.pad(side_proj.astype(BF), ((0, 0), (0, 0), (0, LANES - H))).reshape(-1, LANES)
    share = jnp.pad(shared_params.astype(BF), (0, share_pad - share_size)).reshape(-1, LANES)
    side_part = piece.shape[0]
    piece_rows = side_part + share.shape[0]
    ids = jnp.pad(jnp.concatenate([token_ids, labels], axis=0), ((0, 8 - 2 * seqs), (0, 0)))
    ids_all, pieces, shared_all = open_exchange(ids, piece, share, nd, nt)
    shared_full = shared_all.reshape(nd * nt, share_pad)[:, :share_size].reshape(-1).astype(F32)
    ids_all = ids_all.transpose(1, 0, 2).reshape(8, length)
    all_ids = ids_all[:seqs].reshape(-1)
    local_row = all_ids // 2 - shard * vrows
    held = (local_row >= 0) & (local_row < vrows) & (all_ids % 2 == place // half)
    scal = jnp.stack([place, shard]).astype(jnp.int32)
    scal_shard = shard.astype(jnp.int32).reshape(1)
    code = jnp.concatenate([jnp.where(held, local_row, 0), jnp.zeros((8,), jnp.int32)])
    listed, count = list_held(held, nd * rows)
    own_tiles = layer_blocks.shape[2]
    gathered = lax.all_gather(
        jnp.concatenate(
            [layer_blocks.astype(BF).reshape(own_tiles * BLK, BLK), pieces.reshape(-1, LANES)], axis=0
        ),
        "dp",
        axis=0,
        tiled=False,
    )
    *parts, table_low = gather_rows(
        scal, code, listed, count, vocab_table, nd, rows, padded
    )
    residual, normed = forward_rows(
        parts, None, shared_full[None, :D], nd, chunks, True, 4, nt
    )
    table_low, normed = lax.optimization_barrier((table_low, normed))
    gathered, normed = lax.optimization_barrier((gathered, normed))
    side_full = (
        gathered[:, own_tiles * BLK :]
        .reshape(nd, nt, L, side_rows, 2 * N + LANES)
        .transpose(2, 0, 1, 3, 4)
        .reshape(L, D, 2 * N + LANES)
    )
    table_all = lax.all_gather(table_low, "dp", axis=1, tiled=True)

    def layer_mats(layer_index):
        dt_part = lax.dynamic_slice_in_dim(
            side_full[layer_index], 2 * N + shard * heads, heads, 1
        )
        side_here = jnp.concatenate(
            [
                side_full[layer_index][:, : 2 * N],
                jnp.pad(dt_part, ((0, 0), (0, LANES - heads))),
            ],
            axis=1,
        )
        base = layer_index * stride
        gain = shared_full[base : base + D]
        taps = shared_full[base + D : base + D + 8 * N].reshape(4, 2 * N)
        bias = shared_full[base + D + 8 * N : base + stride].reshape(1, 2 * N)
        bcp = jnp.concatenate([taps, bias, jnp.zeros((3, 2 * N), F32)], axis=0)
        chan = jnp.pad(channel_params[layer_index], ((0, 2), (0, 0)))
        head = jnp.pad(head_params[layer_index], ((0, 5), (0, LANES - heads)))
        return [None, None, side_here, gain, bcp, chan, head]

    def hop(x, distance):
        pairs = [
            (k, k + distance)
            for k in range(nd)
            if 0 <= k % chunks + distance < chunks
        ]
        return lax.ppermute(x, "dp", pairs)

    def returned(parts):
        return [parts[0]] + [swap(parts[off], "tensor", off) for off in range(1, nt)]

    hops = range(1, chunks)
    mats = [layer_mats(layer_index) for layer_index in range(L)]
    final_gain = shared_full[L * stride :][None, :]
    gains = [mats[layer_index][3][None, :] for layer_index in range(L)] + [final_gain]
    saved = []
    tiles_now = gathered
    for layer_index in range(L):
        mats[layer_index][:2] = place_tiles(
            block_slot, tiles_now, own_tiles, inner, zx_count, per_layer, layer_index
        )
        wzx, wout, wside, gain, bcp, chan, head = mats[layer_index]
        z, xr, side, yloc, final, c_out, cum = mixer_front(normed, wzx, wside, chan, bcp, head)
        final, tiles_now = lax.optimization_barrier((final, tiles_now))
        states = [hop(final, k) for k in hops]
        result = mixer_middle(scal_shard, states, yloc, z, c_out, cum, wout, chan, nt)
        y, s_in = result[:2]
        below = normed
        before = residual
        inside = layer_index + 1 < L
        residual, branch, factor, normed = forward_rows(
            result[2:], before, gains[layer_index + 1], nd, chunks, inside, 5 + layer_index
        )
        saved.append((before, below, z, xr, side, c_out, cum, y, s_in, factor, branch))

    member = micro_batch[:, None] == jnp.arange(MB, dtype=jnp.int32)[None, :]
    batch_tokens = jnp.sum(jnp.where(member, seq_lengths[:, None], 0), axis=0).astype(F32)
    seq_weight = 1.0 / (MB * jnp.sum(jnp.where(member, batch_tokens[None, :], 0.0), axis=1))
    row_at = place * rows + jnp.arange(rows, dtype=jnp.int32)
    my_seq = place // chunks
    weight = jnp.where(row_at % length < seq_lengths[my_seq], seq_weight[my_seq], 0.0)
    all_labels = ids_all[seqs : 2 * seqs].reshape(-1)
    label = (lax.dynamic_slice_in_dim(all_labels, place * rows, rows) - 2 * shard * vrows).reshape(
        1, rows
    )
    row_weight = weight.reshape(1, rows)
    p_low, tops, stats = vocab_logits(label, table_all, normed, vrows)
    scale, seq_part = merge_stats(stats, tops, row_weight, nt, chunks)
    sent = returned(vocab_rows(scal_shard, label, scale, row_weight, p_low, table_all, nt))
    table_grad = vocab_table_grad(label, scale, row_weight, p_low, normed)
    sent, table_grad = lax.optimization_barrier((sent, table_grad))
    table_share = lax.psum_scatter(table_grad, "dp", scatter_dimension=1, tiled=True)
    grad_res, payload, grad_final_gain = backward_rows(
        sent, None, residual, final_gain, None, saved[L - 1][10], saved[L - 1][9], nd, chunks, 10
    )

    block_pieces = [None] * (2 * L)
    side_pieces = [None] * L
    channel_pieces = [None] * L
    head_pieces = [None] * L
    shared_pieces = [None] * L
    for layer_index in reversed(range(L)):
        wzx, wout, wside, gain, bcp, chan, head = mats[layer_index]
        residual_in, normed, z, xr, side, c_out, cum, y, s_in, factor, branch = saved[layer_index]
        u_low, dy, dz, dstate, gain_grad = gate_back(payload, wout, y, z, c_out, cum, chan)
        states = [hop(dstate, -k) for k in hops]
        grad_out_w = tn(u_low, payload)
        inside = mixer_within(s_in, xr, side, dy, chan, bcp, head)
        result = mixer_back(
            scal_shard,
            states,
            inside,
            xr,
            side,
            dy,
            dz,
            y,
            wzx,
            wside,
            chan,
            bcp,
            head,
            normed,
            gains[layer_index],
            nt,
        )
        dzx, dside, chan_grad, bcp_grad, head_grad, rim_grad, grad_gain_in = result[:7]
        parts_out = result[7:]
        grad_zx_w = tn(normed, dzx)
        grad_side_w = tn(normed, dside)
        block_pieces[2 * layer_index] = grad_zx_w.astype(BF)
        block_pieces[2 * layer_index + 1] = grad_out_w.astype(BF)
        side_pieces[layer_index] = grad_side_w
        shared_pieces[layer_index] = jnp.concatenate(
            [grad_gain_in[0], bcp_grad[:4].reshape(-1), bcp_grad[4]]
        )
        channel_pieces[layer_index] = jnp.concatenate([chan_grad[:5], gain_grad], axis=0)
        head_pieces[layer_index] = head_grad[:3, :heads]
        if layer_index == 0:
            shared_grads = jnp.concatenate(shared_pieces + [grad_final_gain[0]]).astype(BF)
            shared_grads = jnp.pad(
                shared_grads.reshape(nd * nt, share_size), ((0, 0), (0, share_pad - share_size))
            ).reshape(nd, nt * share_pad // LANES, LANES)
            lines = jnp.concatenate(
                [
                    jnp.stack(channel_pieces).reshape(-1, LANES),
                    jnp.pad(jnp.stack(head_pieces).reshape(-1), (0, LANES - L * 3 * heads)).reshape(
                        1, LANES
                    ),
                ],
                axis=0,
            ).astype(BF)
            line_count = lines.shape[0]
            line_rows = -(-line_count // RIM) * RIM
            lines = jnp.pad(lines, ((0, line_rows - line_count), (0, 0)))
            tile_grads = pack_tiles(
                scal_shard,
                block_slot,
                block_pieces,
                side_pieces,
                shared_grads,
                lines,
                own_tiles,
                per_layer,
                nt,
                heads,
            )
            tile_grads, table_share, parts_out, rim_grad = lax.optimization_barrier(
                (tile_grads, table_share, parts_out, rim_grad)
            )
            block_share = lax.psum_scatter(tile_grads, "dp", scatter_dimension=0, tiled=True)[0]
        if layer_index:
            grad_res, payload = backward_rows(
                parts_out,
                rim_grad,
                residual_in,
                gains[layer_index],
                grad_res,
                saved[layer_index - 1][10],
                saved[layer_index - 1][9],
                nd,
                chunks,
                10 + layer_index,
            )
        else:
            embed = finish_rows(
                parts_out, rim_grad, residual_in, gains[0], grad_res, nd, chunks
            )

    side_count = nt * side_part
    small_share = jnp.concatenate(
        [
            block_share[own_tiles * BLK : own_tiles * BLK + side_count].reshape(nt, side_part, LANES),
            block_share[own_tiles * BLK + side_count : own_tiles * BLK + nt * piece_rows].reshape(
                nt, piece_rows - side_part, LANES
            ),
        ],
        axis=1,
    )
    mine = jnp.zeros((piece_rows, LANES), F32)
    for off in range(nt):
        piece = lax.dynamic_index_in_dim(small_share, shard ^ off, 0, False)
        mine = mine + (piece if off == 0 else swap(piece, "tensor", off)).astype(F32)
    side_share = (
        mine[:side_part]
        .reshape(L, 2 * N // LANES + 1, side_rows, LANES)
        .transpose(0, 2, 1, 3)
        .reshape(L * side_rows, 2 * N + LANES)[:, : 2 * N + H]
    )
    shared_share = mine[side_part:].reshape(1, -1)[:, :share_size]
    lines = block_share[own_tiles * BLK + nt * piece_rows :].astype(F32)
    channel_sum = lines[: line_count - 1].reshape(L * 6, inner)
    head_sum = lines[line_count - 1, : L * 3 * heads].reshape(L * 3, heads)
    rotated, tile_root = turn_tiles(block_share, block_bases.reshape(own_tiles, 2, BLK, BLK))
    grad_table, table_root = add_rows(scal, code, listed, count, table_share, embed, vrows)
    sums = sum_everywhere(
        seq_part,
        [channel_sum, head_sum],
        [table_root, tile_root, side_share, shared_share],
        nd,
        nt,
    )
    seq_loss = sums[0, :seqs]
    clip_norm = sums[1, 0]
    steps_done = step_count[0].astype(F32)
    fix_one = 1.0 - jnp.power(BETA_FIRST, steps_done)
    fix_two = 1.0 - jnp.power(BETA_SECOND, steps_done)
    tile_shape = layer_blocks.shape[2:]
    flat = lambda x: x.reshape((-1, x.shape[-1]))
    little = [
        [flat(side_proj), side_share, flat(side_first), flat(side_second)],
        [flat(shared_params), shared_share, flat(shared_first), flat(shared_second)],
        [channel_params, channel_sum.reshape(channel_params.shape), channel_first, channel_second],
        [head_params, head_sum.reshape(head_params.shape), head_first, head_second],
    ]
    updated = last_update(
        jnp.stack([fix_one, fix_two]),
        sums,
        layer_blocks.reshape(tile_shape),
        rotated,
        block_bases.reshape((own_tiles, 2, BLK, BLK)),
        block_first.reshape(tile_shape),
        block_second.reshape(tile_shape),
        little,
    )
    table_out = adam_update(
        vocab_table,
        grad_table.astype(F32),
        vocab_first,
        vocab_second,
        sums[2, 0],
        fix_one,
        fix_two,
        WEIGHT_DECAY,
    )
    block_out = [x.reshape(layer_blocks.shape) for x in updated[:4]]
    like = [side_proj] * 3 + [shared_params] * 3 + [channel_params] * 3 + [head_params] * 3
    small_out = [x.reshape(y.shape) for x, y in zip(updated[4:], like)]
    return (
        seq_loss,
        clip_norm,
        table_out[0],
        table_out[1],
        table_out[2],
        block_out[0],
        block_out[1],
        block_out[2],
        block_out[3],
        *small_out,
    )


def solution(mesh):
    table = P("tensor", "dp")
    block = P("dp", "tensor", None, None, None)
    side = P(None, ("dp", "tensor"), None)
    shared = P(("dp", "tensor"))
    channel = P(None, None, "tensor")
    in_specs = (
        P(None, "dp"),
        P(None, "dp"),
        P(),
        P(),
        P(),
        P("tensor", None),
        *[table] * 3,
        block,
        P("dp", "tensor", None, None, None, None),
        block,
        block,
        *[side] * 3,
        *[shared] * 3,
        *[channel] * 6,
    )
    out_specs = (
        P(),
        P(),
        *[table] * 3,
        *[block] * 4,
        *[side] * 3,
        *[shared] * 3,
        *[channel] * 6,
    )
    return jax.shard_map(shards, mesh=mesh, in_specs=in_specs, out_specs=out_specs, check_vma=False)
```

```python
import functools

import jax
import jax.numpy as jnp
from jax import lax
from jax.experimental import pallas as pl
from jax.experimental.pallas import tpu as pltpu
from jax.sharding import PartitionSpec as P

D = 1024
DI = 2048
H = 32
P_SIZE = 64
N = 128
V = 50288
SPAN = 256
L = 2
MB = 2
BLK = 128
RIM = 16
PAIRS = 1280
PART = 320
LANES = 128

HIGHEST = lax.Precision.HIGHEST
NORM_EPS = 1e-05
SMOOTHING = 0.1
ZLOSS_WEIGHT = 0.005
CLIP_LIMIT = 0.02
BETA_FIRST = 0.9
BETA_SECOND = 0.95
ADAM_EPS = 1e-08
LEARN_RATE = 0.03
WEIGHT_DECAY = 0.01

BF = jnp.bfloat16
F32 = jnp.float32
MIB = 1 << 20


def nn(a, b, precision=None):
    return lax.dot_general(
        a, b, (((1,), (0,)), ((), ())), precision=precision, preferred_element_type=F32
    )


def nt_dot(a, b, precision=None):
    return lax.dot_general(
        a, b, (((1,), (1,)), ((), ())), precision=precision, preferred_element_type=F32
    )


def tn(a, b, precision=None):
    return lax.dot_general(
        a, b, (((0,), (0,)), ((), ())), precision=precision, preferred_element_type=F32
    )


def iota(shape, dim):
    return lax.broadcasted_iota(jnp.int32, shape, dim)


def head_map(inner):
    return (iota((LANES, inner), 0) == iota((LANES, inner), 1) // P_SIZE).astype(F32).astype(BF)


def swap(x, axis, offset):
    size = lax.axis_size(axis)
    return lax.ppermute(x, axis, [(i, i ^ offset) for i in range(size)])


def halves(x):
    high = x.astype(BF)
    return high, (x - high.astype(F32)).astype(BF)


def thirds(x):
    high = x.astype(BF)
    rest = x - high.astype(F32)
    mid = rest.astype(BF)
    return high, mid, (rest - mid.astype(F32)).astype(BF)


def widen(x, expand):
    high, low = halves(x)
    twice = jnp.concatenate([expand, expand], axis=0)
    return nn(jnp.concatenate([high, low], axis=1), twice)


def narrow(x, expand):
    high, low = halves(x)
    return nt_dot(high, expand) + nt_dot(low, expand)


def tri_sum(tri, x):
    wide = nn(tri, jnp.concatenate(thirds(x), axis=1))
    size = x.shape[1]
    return wide[:, :size] + wide[:, size : 2 * size] + wide[:, 2 * size :]


def lanes3(column):
    high, mid, low = thirds(column)
    lane = iota((column.shape[0], LANES), 1)
    zero = jnp.zeros((column.shape[0], LANES), F32)
    wide = jnp.where(lane == 0, high.astype(F32), zero)
    wide = jnp.where(lane == 1, mid.astype(F32), wide)
    return jnp.where(lane == 2, low.astype(F32), wide).astype(BF)


def column3(wide):
    return wide[:, 0:1] + wide[:, 1:2] + wide[:, 2:3]


def rows3(line, inner):
    high, mid, low = thirds(line)
    at = iota((RIM, LANES), 0)
    wide = jnp.where(at == 0, high.astype(F32), 0.0)
    wide = jnp.where(at == 1, mid.astype(F32), wide)
    wide = jnp.where(at == 2, low.astype(F32), wide)
    if inner > LANES:
        wide = jnp.concatenate([wide, jnp.zeros((RIM, inner - LANES), F32)], axis=1)
    return wide.astype(BF)


def sigmoid(x):
    return 1.0 / (1.0 + jnp.exp(-x))


def softplus(x):
    return jnp.maximum(x, 0.0) + jnp.log1p(jnp.exp(-jnp.abs(x)))


def call(kernel, name, out_shape, args, smem=(), scratch=(), mib=60, flops=0, moved=0, **extra):
    specs = [
        pl.BlockSpec(memory_space=pltpu.SMEM if i in smem else pltpu.VMEM)
        for i in range(len(args))
    ]
    return pl.pallas_call(
        kernel,
        out_shape=out_shape,
        in_specs=specs,
        out_specs=jax.tree.map(lambda _: pl.BlockSpec(memory_space=pltpu.VMEM), out_shape),
        scratch_shapes=list(scratch),
        compiler_params=pltpu.CompilerParams(vmem_limit_bytes=mib * MIB),
        cost_estimate=pl.CostEstimate(flops=flops, bytes_accessed=moved, transcendentals=0),
        name=name,
        **extra,
    )(*args)


def sds(shape, dtype):
    return jax.ShapeDtypeStruct(shape, dtype)


def list_held(held, total):
    runs = held.reshape(-1, LANES)
    upper = iota((LANES, LANES), 0) <= iota((LANES, LANES), 1)
    rank = nn(runs.astype(BF), upper.astype(BF)).astype(jnp.int32) - 1
    here = (rank[:, :, None] == iota((1, 1, LANES), 2)) & runs[:, :, None]
    at = jnp.sum(jnp.where(here, iota((1, LANES, 1), 1), 0), axis=1)
    counts = rank[:, -1] + 1
    first = iota(at.shape, 0) * LANES
    listed = jnp.where(iota(at.shape, 1) < counts[:, None], at + first, total)
    return listed.reshape(-1), counts


def over_listed(listed, count, body):
    def run(at_run, carry):
        def turn(step, inner_carry):
            for lane in range(8):
                body(listed[at_run * LANES + step * 8 + lane])
            return inner_carry

        lax.fori_loop(0, (count[at_run] + 7) // 8, turn, 0)
        return carry

    lax.fori_loop(0, count.shape[0], run, 0)


def look_kernel(groups, rows, scal, code, listed, count, table, *rest):
    outs, low, work = rest[:groups], rest[groups], rest[groups + 1]
    place = scal[0]
    vrows = table.shape[0]
    edge = vrows // RIM * RIM
    low[edge:, :] = jnp.zeros((low.shape[0] - edge, low.shape[1]), BF)
    low[0:vrows, :] = table[...].astype(BF)

    def fill(step, carry):
        work[pl.ds(pl.multiple_of(step * rows, rows), rows), :] = jnp.zeros((rows, table.shape[1]), F32)
        return carry

    lax.fori_loop(0, groups, fill, 0)

    def take(at):
        work[pl.ds(at, 1), :] = table[pl.ds(code[at], 1), :]

    over_listed(listed, count, take)
    for off in range(groups):
        base = pl.multiple_of((place ^ off) * rows, rows)
        outs[off][...] = work[pl.ds(base, rows), :].astype(BF)


def gather_rows(scal, code, listed, count, table, groups, rows, padded):
    cols = table.shape[1]
    return call(
        functools.partial(look_kernel, groups, rows),
        "look",
        [sds((rows, cols), BF)] * groups + [sds((padded, cols), BF)],
        (scal, code, listed, count, table),
        smem=(0, 1, 2, 3),
        scratch=[pltpu.VMEM((groups * rows + 8, cols), F32)],
        moved=30 * MIB,
    )


def add_kernel(groups, rows, vrows, scal, code, listed, count, share, parts, *rest):
    out, square, work, bins = rest
    place = scal[0]
    bins[...] = share[0:vrows, :].astype(F32)
    for off in range(groups):
        base = pl.multiple_of((place ^ off) * rows, rows)
        work[pl.ds(base, rows), :] = parts[off].astype(F32)
    work[groups * rows :, :] = jnp.zeros((8, work.shape[1]), F32)

    def add(at):
        to = pl.ds(code[at], 1)
        bins[to, :] = bins[to, :] + work[pl.ds(at, 1), :]

    over_listed(listed, count, add)
    total = bins[...]
    out[...] = total.astype(BF)
    square[...] = jnp.sqrt(jnp.sum(total * total, axis=0, keepdims=True))


def add_rows(scal, code, listed, count, share, parts, vrows):
    cols = share.shape[1]
    groups, rows, _ = parts.shape
    return call(
        functools.partial(add_kernel, groups, rows, vrows),
        "addrows",
        [sds((vrows, cols), BF), sds((1, cols), F32)],
        (scal, code, listed, count, share, parts),
        smem=(0, 1, 2, 3),
        scratch=[pltpu.VMEM((rows * groups + 8, cols), F32), pltpu.VMEM((vrows, cols), F32)],
        moved=30 * MIB,
    )


def tiles_kernel(slots_each, zx_count, per_layer, first_layer, slot, tiles, *outs):
    for layer in (first_layer,):
        for at in range(per_layer):
            where = slot[0, layer * per_layer + at]
            owner = where // slots_each
            first = pl.multiple_of((where % slots_each) * BLK, BLK)
            tile = tiles[owner, pl.ds(first, BLK), :]
            if at < zx_count:
                wide = outs[0].shape[1] // BLK
                row, col = at // wide, at % wide
                out = outs[0]
            else:
                wide = D // BLK
                row, col = (at - zx_count) // wide, (at - zx_count) % wide
                out = outs[1]
            out[row * BLK : (row + 1) * BLK, col * BLK : (col + 1) * BLK] = tile


def place_tiles(slot, tiles, slots_each, inner, zx_count, per_layer, layer):
    return call(
        functools.partial(tiles_kernel, slots_each, zx_count, per_layer, layer),
        "placetiles",
        [sds((D, 2 * inner), BF), sds((inner, D), BF)],
        (slot, tiles),
        smem=(0,),
        moved=14 * MIB,
    )


def pack_kernel(slots_each, per_layer, layers, shards, heads, scal, slot, *refs):
    mats, sides, refs = refs[: 2 * layers], refs[2 * layers : 3 * layers], refs[3 * layers :]
    shared, lines, out, work = refs
    for layer in range(layers):
        zx, wout = mats[2 * layer], mats[2 * layer + 1]
        zx_wide, out_wide = zx.shape[1] // BLK, D // BLK
        zx_count = zx.shape[0] // BLK * zx_wide
        for at in range(per_layer):
            where = slot[0, layer * per_layer + at]
            if at < zx_count:
                source, row, col = zx, at // zx_wide, at % zx_wide
            else:
                source = wout
                row, col = (at - zx_count) // out_wide, (at - zx_count) % out_wide
            first = pl.multiple_of((where % slots_each) * BLK, BLK)
            out[where // slots_each, pl.ds(first, BLK), :] = source[
                row * BLK : (row + 1) * BLK, col * BLK : (col + 1) * BLK
            ]
        work[layer, :, : 2 * N] = sides[layer][:, : 2 * N]
        work[layer, :, 2 * N :] = pltpu.roll(sides[layer][:, 2 * N :], scal[0] * heads, 1)
    groups = out.shape[0]
    each = work.shape[1] // (groups * shards)
    piece = layers * each * work.shape[2] // LANES
    base = slots_each * BLK
    for group in range(groups):
        for shard in range(shards):
            first = (group * shards + shard) * each
            blocks = [
                work[layer, first : first + each, col : col + LANES]
                for layer in range(layers)
                for col in range(0, work.shape[2], LANES)
            ]
            at = base + shard * piece
            out[group, at : at + piece, :] = jnp.concatenate(blocks, axis=0).astype(BF)
    base += shards * piece
    out[:, base : base + shared.shape[1], :] = shared[...]
    for group in range(groups):
        out[group, base + shared.shape[1] :, :] = lines[...]


def pack_tiles(scal, slot, mats, sides, shared, lines, slots_each, per_layer, shards, heads):
    groups = shared.shape[0]
    layers = len(sides)
    depth, width = sides[0].shape
    extra = layers * depth * width // (groups * LANES) + shared.shape[1] + lines.shape[0]
    return call(
        functools.partial(pack_kernel, slots_each, per_layer, layers, shards, heads),
        "packtiles",
        sds((groups, slots_each * BLK + extra, LANES), BF),
        (scal, slot, *mats, *sides, shared, lines),
        smem=(0, 1),
        scratch=[pltpu.VMEM((layers, depth, width), F32)],
        moved=14 * MIB,
    )


def norm_rows(values, gain):
    return values * lax.rsqrt(jnp.mean(values * values, axis=-1, keepdims=True) + NORM_EPS) * gain


def total_of(parts):
    total = parts[0][...].astype(F32)
    for part in parts[1:]:
        total = total + part[...].astype(F32)
    return total


def send(source, target, send_sem, recv_sem, device):
    copy = pltpu.make_async_remote_copy(
        src_ref=source,
        dst_ref=target,
        send_sem=send_sem,
        recv_sem=recv_sem,
        device_id=device,
        device_id_type=pl.DeviceIdType.MESH,
    )
    copy.start()
    return copy


def greet_shards(groups, shards, rims, wide=False):
    place, shard = lax.axis_index("dp"), lax.axis_index("tensor")
    last = shard == shards - 1
    barrier = pltpu.get_barrier_semaphore()

    def greet(device):
        pl.semaphore_signal(barrier, inc=1, device_id=device, device_id_type=pl.DeviceIdType.MESH)

    for off in range(1, shards):
        greet((place, shard ^ off))
    if not rims:
        pl.semaphore_wait(barrier, shards - 1)
        return
    if wide:
        for off in range(1, groups):
            greet((place ^ off, shard))

        @pl.when(jnp.logical_not(last))
        def _():
            greet((lax.rem(place + groups - 1, groups), shards - 1))

        @pl.when(last)
        def _():
            for other in range(shards - 1):
                greet((lax.rem(place + 1, groups), other))

        pl.semaphore_wait(barrier, shards + groups - 2 + jnp.where(last, shards - 1, 1))
        return
    greet((lax.rem(place + groups - 1, groups), shards - 1))

    @pl.when(last)
    def _():
        for other in range(shards):
            greet((lax.rem(place + 1, groups), other))

    pl.semaphore_wait(barrier, shards - 1 + jnp.where(last, shards + 1, 1))


def pass_along(rows, own, base, shards, sems):
    place, shard = lax.axis_index("dp"), lax.axis_index("tensor")

    def copy(way, hop, source, to):
        at = pl.ds(pl.multiple_of(base + source * own, RIM), own)
        return pltpu.make_async_remote_copy(
            src_ref=rows.at[at, :],
            dst_ref=rows.at[at, :],
            send_sem=sems.at[0, way, hop],
            recv_sem=sems.at[1, way, hop],
            device_id=(place, to),
            device_id_type=pl.DeviceIdType.MESH,
        )

    def up(hop):
        return copy(0, hop, shard - hop, shard + 1)

    def down(hop):
        return copy(1, hop, shard + hop, shard - 1)

    can_up, can_down = shard + 1 < shards, shard > 0
    for hop in range(shards):
        if hop > 0:

            @pl.when(shard - hop >= 0)
            def _():
                copy(0, hop - 1, shard - hop, shard - 1).wait_recv()

        if hop < shards - 1:

            @pl.when(jnp.logical_and(shard - hop >= 0, can_up))
            def _():
                up(hop).start()

        if hop > 0:

            @pl.when(shard + hop < shards)
            def _():
                copy(1, hop - 1, shard + hop, shard + 1).wait_recv()

        if hop < shards - 1:

            @pl.when(jnp.logical_and(shard + hop < shards, can_down))
            def _():
                down(hop).start()

    for hop in range(shards - 1):

        @pl.when(jnp.logical_and(shard - hop >= 0, can_up))
        def _():
            up(hop).wait_send()

        @pl.when(jnp.logical_and(shard + hop < shards, can_down))
        def _():
            down(hop).wait_send()


def exchange_terms(parts, slots, work, sems, ready=None):
    place, shard = lax.axis_index("dp"), lax.axis_index("tensor")
    shards = len(parts)

    def copy(off, source, to, slot):
        return pltpu.make_async_remote_copy(
            src_ref=source,
            dst_ref=slots.at[slot],
            send_sem=sems.at[0, off],
            recv_sem=sems.at[1, slot],
            device_id=(place, to),
            device_id_type=pl.DeviceIdType.MESH,
        )

    def direct(off):
        return copy(off, parts[off], shard ^ off, off)

    if shards != 4:
        for off in reversed(range(1, shards)):
            if ready:
                ready(off)
            direct(off).start()
        if ready:
            ready(0)
        for off in range(1, shards):
            direct(off).wait()
        total = parts[0][...].astype(F32)
        for off in range(1, shards):
            total = total + slots[off].astype(F32)
        work[...] = total
        return
    relay, added = 0, 4
    outer = jnp.logical_or(shard == 0, shard == shards - 1)
    inner = jnp.logical_not(outer)

    def pass_relayed():
        copy(0, parts[3], shard ^ 1, relay).wait_recv()
        slots[added] = (slots[relay].astype(F32) + parts[2][...].astype(F32)).astype(BF)
        copy(2, slots.at[added], shard ^ 2, 2).start()

    if ready:
        ready(3)

        @pl.when(outer)
        def _():
            copy(3, parts[3], shard ^ 1, relay).start()

        @pl.when(inner)
        def _():
            direct(3).start()

        ready(2)

        @pl.when(outer)
        def _():
            direct(2).start()

        @pl.when(inner)
        def _():
            pass_relayed()

        ready(1)
        direct(1).start()
        ready(0)
    else:

        @pl.when(outer)
        def _():
            copy(3, parts[3], shard ^ 1, relay).start()
            direct(2).start()
            direct(1).start()

        @pl.when(inner)
        def _():
            direct(3).start()
            direct(1).start()
            pass_relayed()

    direct(1).wait_recv()
    total = parts[0][...].astype(F32) + slots[1].astype(F32)
    direct(2).wait_recv()
    work[...] = total + slots[2].astype(F32)

    @pl.when(inner)
    def _():
        direct(3).wait_recv()
        work[...] += slots[3].astype(F32)

    for off in range(1, shards):
        direct(off).wait_send()


def term_scratch(shards, own, width):
    return [
        pltpu.VMEM((shards + 1, own, width), BF),
        pltpu.VMEM((own, width), F32),
        pltpu.SemaphoreType.DMA((2, shards + 1)),
    ]


def forward_kernel(groups, shards, chunks, packed, rims, *refs):
    ready = None
    place, shard = lax.axis_index("dp"), lax.axis_index("tensor")
    if packed:
        parts, refs = refs[:shards], refs[shards:]
        before, gain, residual, branch, factor, normed, *refs = refs
        slots, work, term_sems, row_sems, rim_sems = refs
        own = parts[0].shape[0]
        greet_shards(groups, shards, rims)
    else:
        looked, refs = refs[:groups], refs[groups:]
        gain, residual, normed, *refs = refs
        slots, work, term_sems, row_sems, rim_sems, arrived, terms, look_sems = refs
        own = terms.shape[1]
        half, cols = groups // 2, looked[0].shape[1]
        parts = [terms.at[off] for off in range(shards)]
        greet_shards(groups, shards, rims, True)

        def block(off):
            return pl.ds(pl.multiple_of((shard ^ off) * own, own), own)

        copies = {
            (off, other): send(
                looked[other].at[block(off), :],
                arrived.at[off, other],
                look_sems.at[0, off, other],
                look_sems.at[1, off, other],
                (place ^ other, shard),
            )
            for off in reversed(range(shards))
            for other in range(1, groups)
        }

        def ready(off):
            for other in range(1, groups):
                copies[off, other].wait()
            arrived[off, 0] = looked[0][block(off), :]
            for other in range(half):
                at = pl.multiple_of(lax.rem(place ^ other, half) * cols, cols)
                terms[off, :, pl.ds(at, cols)] = arrived[off, other] + arrived[off, other + half]

    rows = own * shards
    chunk = lax.rem(place, chunks)
    exchange_terms(parts, slots, work, term_sems, ready)
    total = work[...]
    if packed:
        scale = lax.rsqrt(column3(total[:, D:]) / DI + NORM_EPS)
        branch[...] = total[:, :D]
        factor[...] = scale
        total = before[...] + scale * total[:, :D]
    residual[...] = total
    at = pl.ds(pl.multiple_of(RIM + shard * own, RIM), own)
    normed[at, :] = norm_rows(total, gain[...]).astype(BF)

    def rim_copy(to, device):
        return pltpu.make_async_remote_copy(
            src_ref=normed.at[rows : rows + RIM, :],
            dst_ref=normed.at[0:RIM, :],
            send_sem=rim_sems.at[0, to],
            recv_sem=rim_sems.at[1, 0],
            device_id=device,
            device_id_type=pl.DeviceIdType.MESH,
        )

    gives = jnp.logical_and(shard == shards - 1, chunk + 1 < chunks)
    if rims:

        @pl.when(gives)
        def _():
            for to in range(shards):
                rim_copy(to, (place + 1, to)).start()

        @pl.when(chunk == 0)
        def _():
            normed[0:RIM, :] = jnp.zeros((RIM, D), BF)

    else:
        normed[0:RIM, :] = jnp.zeros((RIM, D), BF)
    pass_along(normed, own, RIM, shards, row_sems)
    if rims:

        @pl.when(chunk > 0)
        def _():
            rim_copy(0, (place - 1, shards - 1)).wait_recv()

        @pl.when(gives)
        def _():
            for to in range(shards):
                rim_copy(to, (place + 1, to)).wait_send()


def forward_rows(parts, before, gain, groups, chunks, rims, cid, entry=0):
    packed = before is not None
    if packed:
        shards = len(parts)
        own, width = parts[0].shape
        args = (*parts, before, gain)
        extra = []
    else:
        shards = entry
        own, width = parts[0].shape[0] // shards, D
        args = (*parts, gain)
        extra = [
            pltpu.VMEM((shards, groups, own, parts[0].shape[1]), BF),
            pltpu.VMEM((shards, own, D), BF),
            pltpu.SemaphoreType.DMA((2, shards, groups)),
        ]
    vmem = pl.BlockSpec(memory_space=pltpu.VMEM)
    outs = [sds((own, D), F32)]
    if packed:
        outs += [sds((own, D), F32), sds((own, 1), F32)]
    outs += [sds((RIM + own * shards, D), BF)]
    return pl.pallas_call(
        functools.partial(forward_kernel, groups, shards, chunks, packed, rims),
        out_shape=outs,
        in_specs=[vmem] * len(args),
        out_specs=[vmem] * len(outs),
        scratch_shapes=[
            *term_scratch(shards, own, width),
            pltpu.SemaphoreType.DMA((2, 2, shards)),
            pltpu.SemaphoreType.DMA((2, shards)),
            *extra,
        ],
        compiler_params=pltpu.CompilerParams(
            collective_id=cid, has_side_effects=True, vmem_limit_bytes=60 * MIB
        ),
        name="forward" if packed else "enter",
    )(*args)


def backward_kernel(groups, shards, chunks, exchanged, *refs):
    parts, refs = refs[:shards], refs[shards:]
    if exchanged:
        residual, gain, branch, factor, grad_out, rows_out, gain_grad, row_sems = refs
    else:
        rim, residual, gain, grad_in, branch, factor, grad_out, rows_out, refs = *refs[:8], refs[8:]
        slots, work, term_sems, from_rims, rim_sems, row_sems = refs
    own = parts[0].shape[0]
    place, shard = lax.axis_index("dp"), lax.axis_index("tensor")
    chunk = lax.rem(place, chunks)
    greet_shards(groups, shards, not exchanged)
    values = residual[...]
    inv = lax.rsqrt(jnp.mean(values * values, axis=-1, keepdims=True) + NORM_EPS)
    if exchanged:
        grad = total_of(parts)
        gain_grad[...] = jnp.sum(grad * values * inv, axis=0, keepdims=True)
    else:

        def rim_copy(slot, device):
            return pltpu.make_async_remote_copy(
                src_ref=rim,
                dst_ref=from_rims.at[slot],
                send_sem=rim_sems.at[0, slot],
                recv_sem=rim_sems.at[1, slot],
                device_id=device,
                device_id_type=pl.DeviceIdType.MESH,
            )

        @pl.when(chunk > 0)
        def _():
            rim_copy(shard, (place - 1, shards - 1)).start()

        exchange_terms(parts, slots, work, term_sems)

        @pl.when(jnp.logical_and(shard == shards - 1, chunk + 1 < chunks))
        def _():
            for other in range(shards):
                rim_copy(other, (place + 1, other)).wait_recv()
            edge = from_rims[0].astype(F32)
            for other in range(1, shards):
                edge = edge + from_rims[other].astype(F32)
            work[own - RIM :, :] += edge

        @pl.when(chunk > 0)
        def _():
            rim_copy(shard, (place - 1, shards - 1)).wait_send()

        grad = work[...]
    scaled = grad * gain[...]
    result = inv * scaled - values * (inv * inv * inv) * jnp.mean(
        scaled * values, axis=-1, keepdims=True
    )
    if not exchanged:
        result = grad_in[...] + result
    grad_out[...] = result
    scale = factor[...]
    at = pl.ds(pl.multiple_of(shard * own, RIM), own)
    rows_out[at, :D] = (scale * result).astype(BF)
    inner_rows = jnp.sum(result * branch[...], axis=-1, keepdims=True)
    rows_out[at, D:] = lanes3(scale * scale * scale * inner_rows / DI)
    pass_along(rows_out, own, 0, shards, row_sems)


def backward_rows(parts, rim, residual, gain, grad_in, branch, factor, groups, chunks, cid):
    shards = len(parts)
    own = residual.shape[0]
    exchanged = rim is None
    vmem = pl.BlockSpec(memory_space=pltpu.VMEM)
    outs = [sds((own, D), F32), sds((own * shards, D + LANES), BF)]
    row_sems = pltpu.SemaphoreType.DMA((2, 2, shards))
    if exchanged:
        args = (*parts, residual, gain, branch, factor)
        outs.append(sds((1, D), F32))
        scratch = [row_sems]
    else:
        args = (*parts, rim, residual, gain, grad_in, branch, factor)
        scratch = [
            *term_scratch(shards, own, D),
            pltpu.VMEM((shards, RIM, D), BF),
            pltpu.SemaphoreType.DMA((2, shards)),
            row_sems,
        ]
    return pl.pallas_call(
        functools.partial(backward_kernel, groups, shards, chunks, exchanged),
        out_shape=outs,
        in_specs=[vmem] * len(args),
        out_specs=[vmem] * len(outs),
        scratch_shapes=scratch,
        compiler_params=pltpu.CompilerParams(
            collective_id=cid, has_side_effects=True, vmem_limit_bytes=60 * MIB
        ),
        name="backward",
    )(*args)


def stats_kernel(shards, chunks, stats, tops, weight, scale_out, loss_out, slots, sems):
    place, shard = lax.axis_index("dp"), lax.axis_index("tensor")
    rows = weight.shape[1]
    own = rows // shards
    greet_shards(0, shards, False)
    copies = [
        send(stats, slots.at[off - 1], sems.at[0, off], sems.at[1, off], (place, shard ^ off))
        for off in range(1, shards)
    ]
    for copy in copies:
        copy.wait()
    others = [stats[...]] + [slots[off] for off in range(shards - 1)]
    best = others[0][0:1, :]
    for one in others[1:]:
        best = jnp.maximum(best, one[0:1, :])
    summed, target, plain = jnp.zeros((1, rows), F32), jnp.zeros((1, rows), F32), jnp.zeros((1, rows), F32)
    for one in others:
        summed = summed + one[1:2, :] * jnp.exp(one[0:1, :] - best)
        target = target + one[2:3, :]
        plain = plain + one[3:4, :]
    log_total = best + jnp.log(summed)
    token_loss = (
        log_total
        - (1.0 - SMOOTHING) * target
        - SMOOTHING / V * plain
        + ZLOSS_WEIGHT * log_total * log_total
    )
    lane = iota((1, rows), 1)
    mine = jnp.logical_and(lane >= shard * own, lane < (shard + 1) * own)
    loss = jnp.sum(jnp.where(mine, weight[...] * token_loss, 0.0), axis=1, keepdims=True)
    here = jnp.logical_and(iota((8, LANES), 0) == 0, iota((8, LANES), 1) == place // chunks)
    loss_out[...] = jnp.where(here, loss, 0.0)
    soft = weight[...] * (1.0 + 2.0 * ZLOSS_WEIGHT * log_total)
    for step in range(tops.shape[0]):
        scale_out[step] = soft * jnp.exp(tops[step] - log_total)


def merge_stats(stats, tops, weight, shards, chunks):
    vmem = pl.BlockSpec(memory_space=pltpu.VMEM)
    return pl.pallas_call(
        functools.partial(stats_kernel, shards, chunks),
        out_shape=[sds(tops.shape, F32), sds((8, LANES), F32)],
        in_specs=[vmem] * 3,
        out_specs=[vmem] * 2,
        scratch_shapes=[
            pltpu.VMEM((shards - 1, *stats.shape), F32),
            pltpu.SemaphoreType.DMA((2, shards)),
        ],
        compiler_params=pltpu.CompilerParams(
            collective_id=9, has_side_effects=True, vmem_limit_bytes=8 * MIB
        ),
        name="stats",
    )(stats, tops, weight)


def finish_kernel(groups, shards, chunks, own, *refs):
    parts, rim, residual, gain, grad_in, out = refs[:shards], *refs[shards : shards + 5]
    slots, work, term_sems, from_rims, payload, full, rim_sems, row_sems, out_sems = refs[shards + 5 :]
    place, shard = lax.axis_index("dp"), lax.axis_index("tensor")
    half = groups // 2
    cols = out.shape[2]
    chunk = lax.rem(place, chunks)
    last = shard == shards - 1
    shard_peers = [(place, shard ^ off) for off in range(1, shards)]
    group_peers = [(place ^ off, shard) for off in range(1, groups)]
    barrier = pltpu.get_barrier_semaphore()

    def greet(device):
        pl.semaphore_signal(barrier, inc=1, device_id=device, device_id_type=pl.DeviceIdType.MESH)

    for peer in shard_peers + group_peers:
        greet(peer)

    @pl.when(jnp.logical_not(last))
    def _():
        greet((lax.rem(place + groups - 1, groups), shards - 1))

    @pl.when(last)
    def _():
        for other in range(shards - 1):
            greet((lax.rem(place + 1, groups), other))

    pl.semaphore_wait(barrier, shards + groups - 2 + jnp.where(last, shards - 1, 1))

    def rim_copy():
        return pltpu.make_async_remote_copy(
            src_ref=rim,
            dst_ref=from_rims.at[shard],
            send_sem=rim_sems.at[0, shard],
            recv_sem=rim_sems.at[1, shard],
            device_id=(place - 1, shards - 1),
            device_id_type=pl.DeviceIdType.MESH,
        )

    @pl.when(chunk > 0)
    def _():
        rim_copy().start()

    values = residual[...]
    inv = lax.rsqrt(jnp.mean(values * values, axis=-1, keepdims=True) + NORM_EPS)
    exchange_terms(parts, slots, work, term_sems)

    @pl.when(jnp.logical_and(chunk + 1 < chunks, last))
    def _():
        for other in range(shards):
            pltpu.make_async_remote_copy(
                src_ref=rim,
                dst_ref=from_rims.at[other],
                send_sem=rim_sems.at[0, other],
                recv_sem=rim_sems.at[1, other],
                device_id=(place + 1, other),
                device_id_type=pl.DeviceIdType.MESH,
            ).wait_recv()
        edge = from_rims[0].astype(F32)
        for other in range(1, shards):
            edge = edge + from_rims[other].astype(F32)
        work[own - RIM :, :] += edge

    @pl.when(chunk > 0)
    def _():
        rim_copy().wait_send()

    scaled = work[...] * gain[...]
    result = (
        grad_in[...]
        + inv * scaled
        - values * (inv * inv * inv) * jnp.mean(scaled * values, axis=-1, keepdims=True)
    ).astype(BF)
    payload[...] = result
    rows_out = [
        send(
            payload,
            full.at[off],
            row_sems.at[0, off],
            row_sems.at[1, off],
            shard_peers[off - 1],
        )
        for off in range(1, shards)
    ]
    full[0] = result

    def first_col(group):
        return pl.multiple_of(lax.rem(group, half) * cols, cols)

    cuts = []
    for off in range(shards):
        if off > 0:
            rows_out[off - 1].wait()
        at = pl.ds(pl.multiple_of((shard ^ off) * own, own), own)
        for other in range(1, groups):
            cuts.append(
                send(
                    full.at[off, :, pl.ds(first_col(place ^ other), cols)],
                    out.at[other, at, :],
                    out_sems.at[0, off, other],
                    out_sems.at[1, off, other],
                    group_peers[other - 1],
                )
            )
        out[0, at, :] = full[off, :, pl.ds(first_col(place), cols)]
    for cut in cuts:
        cut.wait()


def finish_rows(parts, rim, residual, gain, grad_in, groups, chunks):
    shards = len(parts)
    own = parts[0].shape[0]
    vmem = pl.BlockSpec(memory_space=pltpu.VMEM)
    args = (*parts, rim, residual, gain, grad_in)
    return pl.pallas_call(
        functools.partial(finish_kernel, groups, shards, chunks, own),
        out_shape=sds((groups, own * shards, 2 * D // groups), BF),
        in_specs=[vmem] * len(args),
        out_specs=vmem,
        scratch_shapes=[
            *term_scratch(shards, own, D),
            pltpu.VMEM((shards, RIM, D), BF),
            pltpu.VMEM((own, D), BF),
            pltpu.VMEM((shards, own, D), BF),
            pltpu.SemaphoreType.DMA((2, shards)),
            pltpu.SemaphoreType.DMA((2, shards)),
            pltpu.SemaphoreType.DMA((2, shards, groups)),
        ],
        compiler_params=pltpu.CompilerParams(
            collective_id=3, has_side_effects=True, vmem_limit_bytes=60 * MIB
        ),
        name="finish",
    )(*args)


def open_kernel(groups, shards, ids, piece, share, ids_out, pieces_out, share_out, middle, sends, gets):
    place, shard = lax.axis_index("dp"), lax.axis_index("tensor")
    near = [(place, shard ^ off) for off in range(1, shards)]
    far = [(place ^ off, shard) for off in range(1, groups)]
    barrier = pltpu.get_barrier_semaphore()
    for peer in near + far:
        pl.semaphore_signal(barrier, inc=1, device_id=peer, device_id_type=pl.DeviceIdType.MESH)
    pl.semaphore_wait(barrier, len(near) + len(far))
    shares, others = [], []
    for i, peer in enumerate(near):
        shares.append(send(share, middle.at[shard], sends.at[0, i], gets.at[0, i], peer))
    for i, peer in enumerate(far):
        others.append(send(ids, ids_out.at[place], sends.at[1, i], gets.at[1, i], peer))
    for i, peer in enumerate(near):
        others.append(send(piece, pieces_out.at[shard], sends.at[2, i], gets.at[2, i], peer))
    middle[shard] = share[...]
    ids_out[place] = ids[...]
    pieces_out[shard] = piece[...]
    for copy in shares:
        copy.wait()
    for i, peer in enumerate(far):
        others.append(send(middle, share_out.at[place], sends.at[3, i], gets.at[3, i], peer))
    share_out[place] = middle[...]
    for copy in others:
        copy.wait()


def open_exchange(ids, piece, share, groups, shards):
    count = max(groups, shards)
    vmem = pl.BlockSpec(memory_space=pltpu.VMEM)
    return pl.pallas_call(
        functools.partial(open_kernel, groups, shards),
        out_shape=[
            sds((groups, *ids.shape), jnp.int32),
            sds((shards, *piece.shape), BF),
            sds((groups, shards, *share.shape), BF),
        ],
        in_specs=[vmem] * 3,
        out_specs=[vmem] * 3,
        scratch_shapes=[
            pltpu.VMEM((shards, *share.shape), BF),
            pltpu.SemaphoreType.DMA((4, count)),
            pltpu.SemaphoreType.DMA((4, count)),
        ],
        compiler_params=pltpu.CompilerParams(
            collective_id=2, has_side_effects=True, vmem_limit_bytes=8 * MIB
        ),
        name="open",
    )(ids, piece, share)


def sum_kernel(groups, shards, once, split, *refs):
    loss = refs[0]
    refs = refs[1:]
    count = once + split
    ones, many, refs = refs[:once], refs[once:count], refs[count:]
    o_ref, start, mid, from_shards, from_groups, send, recv = refs
    place, shard = lax.axis_index("dp"), lax.axis_index("tensor")
    peers = [(place, shard ^ off) for off in range(1, shards)]
    peers += [(place ^ off, shard) for off in range(1, groups)]
    barrier = pltpu.get_barrier_semaphore()
    for peer in peers:
        pl.semaphore_signal(barrier, inc=1, device_id=peer, device_id_type=pl.DeviceIdType.MESH)

    def square(refs):
        total = jnp.zeros((1, 1), F32)
        for ref in refs:
            flat = jnp.sum(ref[...] * ref[...], axis=0, keepdims=True)
            total = total + jnp.sum(flat, axis=1, keepdims=True)
        return total

    first = (place == 0).astype(F32)
    part = square(many) + first * square(ones)
    start[...] = loss[...] + jnp.where(iota((8, LANES), 1) == LANES - 1, part, 0.0)
    pl.semaphore_wait(barrier, len(peers))

    def exchange(source, slots, first, some):
        copies = []
        for i, peer in enumerate(some):
            copy = pltpu.make_async_remote_copy(
                src_ref=source,
                dst_ref=slots.at[i],
                send_sem=send.at[first + i],
                recv_sem=recv.at[first + i],
                device_id=peer,
                device_id_type=pl.DeviceIdType.MESH,
            )
            copy.start()
            copies.append(copy)
        for copy in copies:
            copy.wait()
        total = source[...]
        for i in range(len(some)):
            total = total + slots[i]
        return total

    mid[...] = exchange(start, from_shards, 0, peers[: shards - 1])
    total = exchange(mid, from_groups, shards - 1, peers[shards - 1 :])
    norm = jnp.sqrt(total[0:1, LANES - 1 : LANES])
    factor = jnp.minimum(1.0, CLIP_LIMIT / (norm + 1e-06))
    row = iota((8, LANES), 0)
    o_ref[...] = jnp.where(row == 0, total, jnp.where(row == 1, norm, factor))


def sum_everywhere(loss, ones, many, groups, shards):
    count = groups + shards - 2
    args = (loss, *ones, *many)
    vmem = pl.BlockSpec(memory_space=pltpu.VMEM)
    return pl.pallas_call(
        functools.partial(sum_kernel, groups, shards, len(ones), len(many)),
        out_shape=sds((8, LANES), F32),
        in_specs=[vmem] * len(args),
        out_specs=vmem,
        scratch_shapes=[
            pltpu.VMEM((8, LANES), F32),
            pltpu.VMEM((8, LANES), F32),
            pltpu.VMEM((shards - 1, 8, LANES), F32),
            pltpu.VMEM((groups - 1, 8, LANES), F32),
            pltpu.SemaphoreType.DMA((count,)),
            pltpu.SemaphoreType.DMA((count,)),
        ],
        compiler_params=pltpu.CompilerParams(
            collective_id=1, has_side_effects=True, vmem_limit_bytes=8 * MIB
        ),
        name="sumall",
    )(*args)


def conv_sum(raw, params, rows, lanes):
    total = params[4:5, :] + params[0:1, :] * raw[pl.ds(RIM - 3, rows), lanes]
    for k in range(1, 4):
        total = total + params[k : k + 1, :] * raw[pl.ds(RIM - 3 + k, rows), lanes]
    return total


def front_kernel(normed, wzx, wside, chan, bcp, head, *rest):
    z_out, xr, side, yloc, final, c_out, cum_out, xs_scr = rest
    rows = normed.shape[0] - RIM
    inner = chan.shape[1]
    z_out[...] = nn(normed[RIM:, :], wzx[:, :inner])
    xr[...] = nn(normed[...], wzx[:, inner:])
    side[...] = nn(normed[...], wside[...])
    pre = conv_sum(xr, chan, rows, pl.ds(0, inner))
    xs_scr[...] = pre * sigmoid(pre)
    pre = conv_sum(side, bcp, rows, pl.ds(0, 2 * N))
    bc = (pre * sigmoid(pre)).astype(BF)
    c_out[...] = bc[:, N:]
    dt = softplus(side[RIM:, 2 * N :] + head[0:1, :])
    rate = -dt * jnp.exp(head[1:2, :])
    expand = head_map(inner)
    skip = widen(head[...], expand)[2:3, :]
    lower = (iota((SPAN, SPAN), 0) >= iota((SPAN, SPAN), 1)).astype(F32)
    lower_low = lower.astype(BF)
    first_half = iota((SPAN, LANES), 1) < P_SIZE
    state = None
    base = jnp.zeros((1, LANES), F32)
    for span in range(rows // SPAN):
        here = slice(span * SPAN, (span + 1) * SPAN)
        cum = tri_sum(lower_low, rate[here])
        cum_t = cum.T
        tot = cum[SPAN - 1 : SPAN, :]
        keys = bc[here, :N]
        queries = bc[here, N:]
        scores = nt_dot(queries, keys)
        xs = xs_scr[here, :]
        scaled = xs * widen(dt[here], expand)
        scaled_low = scaled.astype(BF)
        pieces = []
        for pair in range(inner // LANES):
            values = scaled_low[:, pair * LANES : (pair + 1) * LANES]
            both = []
            for h in (2 * pair, 2 * pair + 1):
                gap = cum[:, h : h + 1] - cum_t[h : h + 1, :]
                decay = jnp.exp(jnp.minimum(gap, 0.0)) * lower
                both.append(nn((scores * decay).astype(BF), values))
            pieces.append(jnp.where(first_half, both[0], both[1]))
        y = jnp.concatenate(pieces, axis=1) + skip * xs
        if state is not None:
            y = y + widen(jnp.exp(cum), expand) * nn(queries, state.astype(BF))
        yloc[here, :] = y
        tail = widen(jnp.exp(tot - cum), expand)
        fresh = tn(keys, (scaled * tail).astype(BF))
        if state is not None:
            fresh = fresh + widen(jnp.exp(tot), expand) * state
        state = fresh
        cum_out[here, :] = cum + base
        base = base + tot
    final[0:N, :] = state.astype(BF)
    final[N:, :] = rows3(base, inner)


def mixer_front(normed, wzx, wside, chan, bcp, head):
    rows = normed.shape[0] - RIM
    inner = chan.shape[1]
    return call(
        front_kernel,
        "front",
        [
            sds((rows, inner), F32),
            sds((rows + RIM, inner), F32),
            sds((rows + RIM, 2 * N + LANES), F32),
            sds((rows, inner), F32),
            sds((N + RIM, inner), BF),
            sds((rows, N), BF),
            sds((rows, LANES), F32),
        ],
        (normed, wzx, wside, chan, bcp, head),
        scratch=[pltpu.VMEM((rows, inner), F32)],
        flops=8 * rows * D * inner,
        moved=12 * MIB,
    )


def chain(parts, expand):
    total = None
    past = jnp.zeros((1, LANES), F32)
    for part in parts:
        term = widen(jnp.exp(past), expand) * part[0:N, :].astype(F32)
        total = term if total is None else total + term
        past = past + jnp.sum(part[N:, :LANES].astype(F32), axis=0, keepdims=True)
    return total


def middle_kernel(shards, own, hops, scal, *rest):
    states, rest = rest[:hops], rest[hops:]
    yloc, z_in, c_in, cum, wout, chan = rest[:6]
    y_out, s_out = rest[6:8]
    parts, work = rest[8 : 8 + shards], rest[-1]
    shard = scal[0]
    rows, inner = yloc.shape
    expand = head_map(inner)
    state = chain(states, expand)
    s_out[...] = state
    y = yloc[...] + widen(jnp.exp(cum[...]), expand) * nn(c_in[...], state.astype(BF))
    y_out[...] = y
    z = z_in[...]
    gated = y * (z * sigmoid(z))
    work[:, :D] = nn((gated * chan[5:6, :]).astype(BF), wout[...]).astype(BF)
    work[:, D:] = lanes3(jnp.sum(gated * gated, axis=1, keepdims=True))
    for off in range(shards):
        at = pl.multiple_of((shard ^ off) * own, own)
        parts[off][...] = work[pl.ds(at, own), :]


def mixer_middle(scal, states, yloc, z_in, c_in, cum, wout, chan, shards):
    rows, inner = yloc.shape
    own = rows // shards
    return call(
        functools.partial(middle_kernel, shards, own, len(states)),
        "middle",
        [sds((rows, inner), F32), sds((N, inner), F32)]
        + [sds((own, D + LANES), BF)] * shards,
        (scal, *states, yloc, z_in, c_in, cum, wout, chan),
        smem=(0,),
        scratch=[pltpu.VMEM((rows, D + LANES), BF)],
        flops=2 * rows * D * inner,
        moved=8 * MIB,
    )


def gate_back_kernel(grads, wout, y_in, z_in, c_in, cum, chan, *rest):
    u_out, dy_out, dz_out, state_out, gain_out = rest
    inner = chan.shape[1]
    du = nt_dot(grads[:, :D], wout[...])
    coef = column3(grads[:, D:].astype(F32))
    z = z_in[...]
    y = y_in[...]
    sig = sigmoid(z)
    silu = z * sig
    gated = y * silu
    gain_out[...] = jnp.sum(du * gated, axis=0, keepdims=True)
    gain = chan[5:6, :]
    u_out[...] = (gated * gain).astype(BF)
    dgated = du * gain - gated * coef
    dy = dgated * silu
    dy_out[...] = dy
    dz_out[...] = (dgated * y * (sig * (1.0 + z * (1.0 - sig)))).astype(BF)
    grown = widen(jnp.exp(cum[...]), head_map(inner))
    state_out[0:N, :] = tn(c_in[...], (dy * grown).astype(BF)).astype(BF)
    rows = dy.shape[0]
    state_out[N:, :] = rows3(cum[rows - 1 : rows, :], inner)


def gate_back(grads, wout, y, z_in, c_in, cum, chan):
    rows, inner = y.shape
    return call(
        gate_back_kernel,
        "gateback",
        [
            sds((rows, inner), BF),
            sds((rows, inner), F32),
            sds((rows, inner), BF),
            sds((N + RIM, inner), BF),
            sds((1, inner), F32),
        ],
        (grads, wout, y, z_in, c_in, cum, chan),
        flops=2 * rows * D * inner,
        moved=10 * MIB,
    )


def silu_slope(pre):
    sig = sigmoid(pre)
    return sig * (1.0 + pre * (1.0 - sig))


def conv_back(ds_scr, raw, params, rows, lanes, width, low_out, out_lanes):
    ext = rows + RIM
    total = params[0:1, :] * ds_scr[pl.ds(3, ext), :]
    for k in range(1, 4):
        total = total + params[k : k + 1, :] * ds_scr[pl.ds(3 - k, ext), :]
    low_out[:, out_lanes] = total.astype(BF)
    ds = ds_scr[pl.ds(RIM, rows), :]
    grads = [
        jnp.sum(ds * raw[pl.ds(RIM - 3 + k, rows), lanes], axis=0, keepdims=True) for k in range(4)
    ]
    grads.append(jnp.sum(ds, axis=0, keepdims=True))
    grads.append(jnp.zeros((3, width), F32))
    return jnp.concatenate(grads, axis=0)


def within_kernel(s_in, xr, side, dy_in, chan, bcp, head, *outs):
    xs_out, bc_out, cum_out, starts_out, dscaled_out, dbc_out = outs
    rows, inner = dy_in.shape
    expand = head_map(inner)
    pre_x = conv_sum(xr, chan, rows, pl.ds(0, inner))
    xs_out[...] = pre_x * sigmoid(pre_x)
    pre_bc = conv_sum(side, bcp, rows, pl.ds(0, 2 * N))
    bc = (pre_bc * sigmoid(pre_bc)).astype(BF)
    bc_out[...] = bc
    dt = softplus(side[RIM:, 2 * N :] + head[0:1, :])
    rate = -dt * jnp.exp(head[1:2, :])
    lower_low = (iota((SPAN, SPAN), 0) >= iota((SPAN, SPAN), 1)).astype(F32).astype(BF)
    upper = (iota((SPAN, SPAN), 0) <= iota((SPAN, SPAN), 1)).astype(F32)
    first_half = iota((SPAN, LANES), 1) < P_SIZE
    spans = rows // SPAN
    start = s_in[...]
    for span in range(spans):
        here = slice(span * SPAN, (span + 1) * SPAN)
        cum = tri_sum(lower_low, rate[here])
        cum_out[here, :] = cum
        cum_t = cum.T
        keys = bc[here, :N]
        queries = bc[here, N:]
        xs = xs_out[here, :]
        starts_out[span] = start
        start_low = start.astype(BF)
        if span + 1 < spans:
            tot = cum[SPAN - 1 : SPAN, :]
            scale = widen(dt[here] * jnp.exp(tot - cum), expand)
            fresh = tn(keys, (xs * scale).astype(BF))
            start = widen(jnp.exp(tot), expand) * start + fresh
        scores_t = nt_dot(keys, queries)
        dy = dy_in[here, :]
        dy_low = dy.astype(BF)
        scaled_low = (xs * widen(dt[here], expand)).astype(BF)
        dscores_t = jnp.zeros((SPAN, SPAN), F32)
        for pair in range(inner // LANES):
            lanes = slice(pair * LANES, (pair + 1) * LANES)
            values = scaled_low[:, lanes]
            dpair = dy_low[:, lanes]
            both = []
            for h in (2 * pair, 2 * pair + 1):
                gap = cum_t[h : h + 1, :] - cum[:, h : h + 1]
                decay = jnp.exp(jnp.minimum(gap, 0.0)) * upper
                mine = first_half if h % 2 == 0 else jnp.logical_not(first_half)
                outer = nt_dot(jnp.where(mine, values, jnp.zeros_like(values)), dpair)
                dscores_t = dscores_t + outer * decay
                both.append(nn((scores_t * decay).astype(BF), dpair))
            dscaled_out[here, lanes] = jnp.where(first_half, both[0], both[1])
        dscores_low = dscores_t.astype(BF)
        dy_grown = (dy * widen(jnp.exp(cum), expand)).astype(BF)
        dbc_out[here, :N] = nn(dscores_low, queries)
        dbc_out[here, N:] = tn(dscores_low, keys) + nt_dot(dy_grown, start_low)


def mixer_within(s_in, xr, side, dy, chan, bcp, head):
    rows, inner = dy.shape
    return call(
        within_kernel,
        "within",
        [
            sds((rows, inner), F32),
            sds((rows, 2 * N), BF),
            sds((rows, LANES), F32),
            sds((rows // SPAN, N, inner), F32),
            sds((rows, inner), F32),
            sds((rows, 2 * N), F32),
        ],
        (s_in, xr, side, dy, chan, bcp, head),
        flops=8 * rows * D * inner,
        moved=16 * MIB,
    )


def back_kernel(shards, own, hops, scal, *rest):
    states, rest = rest[:hops], rest[hops:]
    xs_in, bc_in, cum_in, starts, dscaled_in, dbc_in, rest = *rest[:6], rest[6:]
    xr, side, dy_in, dz_in, y_in, wzx, wside, chan, bcp, head = rest[:10]
    normed, gain = rest[10:12]
    dzx, dside, chan_out, bcp_out, head_out, rim_out, gain_out = rest[12:19]
    parts, rest = rest[19 : 19 + shards], rest[19 + shards :]
    dsx, dsbc, work = rest
    shard = scal[0]
    rows, inner = dy_in.shape
    expand = head_map(inner)
    raw_dt = side[RIM:, 2 * N :] + head[0:1, :]
    dt = softplus(raw_dt)
    grow = jnp.exp(head[1:2, :])
    rate = -dt * grow
    skip = widen(head[...], expand)[2:3, :]
    upper_low = (iota((SPAN, SPAN), 0) <= iota((SPAN, SPAN), 1)).astype(F32).astype(BF)
    spans = rows // SPAN
    dstate = chain(states, expand)
    dsx[0:RIM, :] = jnp.zeros((RIM, inner), F32)
    dsx[RIM + rows :, :] = jnp.zeros((RIM, inner), F32)
    dsbc[0:RIM, :] = jnp.zeros((RIM, 2 * N), F32)
    dsbc[RIM + rows :, :] = jnp.zeros((RIM, 2 * N), F32)
    dside[0:RIM, 2 * N :] = jnp.zeros((RIM, LANES), BF)
    dzx[0:RIM, :inner] = jnp.zeros((RIM, inner), BF)
    dzx[RIM:, :inner] = dz_in[...]
    dbias = jnp.zeros((1, LANES), F32)
    dgrow = jnp.zeros((1, LANES), F32)
    dskip = jnp.zeros((1, LANES), F32)
    for span in reversed(range(spans)):
        here = slice(span * SPAN, (span + 1) * SPAN)
        there = slice(RIM + span * SPAN, RIM + (span + 1) * SPAN)
        cum = cum_in[here, :]
        tot = cum[SPAN - 1 : SPAN, :]
        keys = bc_in[here, :N]
        queries = bc_in[here, N:]
        xs = xs_in[here, :]
        dy = dy_in[here, :]
        dy_low = dy.astype(BF)
        dt_wide = widen(dt[here], expand)
        scaled = xs * dt_wide
        scaled_low = scaled.astype(BF)
        tail = widen(jnp.exp(tot - cum), expand)
        dstate_low = dstate.astype(BF)
        through = tail * nn(keys, dstate_low)
        dscaled = dscaled_in[here, :] + through
        plain = y_in[here, :] - skip * xs
        held = scaled_low.astype(F32)
        dcum = narrow(dy_low.astype(F32) * plain - held * dscaled, expand)
        tot_wide = widen(jnp.exp(tot), expand)
        over = jnp.sum(held * through, axis=0, keepdims=True) + jnp.sum(
            tot_wide * dstate * starts[span], axis=0, keepdims=True
        )
        dtot = narrow(jnp.broadcast_to(over, (8, inner)), expand)[0:1, :]
        drate = tri_sum(upper_low, dcum) + dtot
        ddt = narrow(dscaled * xs, expand) - drate * grow
        dgrow = dgrow + jnp.sum(drate * rate[here], axis=0, keepdims=True)
        draw = ddt * sigmoid(raw_dt[here])
        dbias = dbias + jnp.sum(draw, axis=0, keepdims=True)
        dside[there, 2 * N :] = draw.astype(BF)
        over = jnp.sum(dy * xs, axis=0, keepdims=True)
        dskip = dskip + narrow(jnp.broadcast_to(over, (8, inner)), expand)[0:1, :]
        dsx[there, :] = dscaled * dt_wide + skip * dy
        dsbc[there, :N] = dbc_in[here, :N] + nt_dot((scaled * tail).astype(BF), dstate_low)
        dsbc[there, N:] = dbc_in[here, N:]
        if span > 0:
            grown = widen(jnp.exp(cum), expand)
            dstate = tot_wide * dstate + tn(queries, (dy * grown).astype(BF))
    body = pl.ds(RIM, rows)
    pre_x = conv_sum(xr, chan, rows, pl.ds(0, inner))
    dsx[body, :] = dsx[body, :] * silu_slope(pre_x)
    pre_bc = conv_sum(side, bcp, rows, pl.ds(0, 2 * N))
    dsbc[body, :] = dsbc[body, :] * silu_slope(pre_bc)
    chan_out[...] = conv_back(
        dsx, xr, chan, rows, pl.ds(0, inner), inner, dzx, pl.ds(inner, inner)
    )
    bcp_out[...] = conv_back(dsbc, side, bcp, rows, pl.ds(0, 2 * N), 2 * N, dside, pl.ds(0, 2 * N))
    head_out[...] = jnp.concatenate([dbias, dgrow, dskip, jnp.zeros((5, LANES), F32)], axis=0)
    dnormed = nt_dot(dzx[...], wzx[...]) + nt_dot(dside[...], wside[...])
    work[...] = dnormed.astype(BF)
    gain_out[...] = jnp.sum(dnormed * normed[...].astype(F32), axis=0, keepdims=True) / gain[...]
    rim_out[...] = work[0:RIM, :]
    for off in range(shards):
        at = pl.multiple_of(RIM + (shard ^ off) * own, RIM)
        parts[off][...] = work[pl.ds(at, own), :]


def mixer_back(
    scal, states, inside, xr, side, dy, dz, y, wzx, wside, chan, bcp, head, normed, gain, shards
):
    rows, inner = dy.shape
    own = rows // shards
    ext = rows + RIM
    return call(
        functools.partial(back_kernel, shards, own, len(states)),
        "back",
        [
            sds((ext, 2 * inner), BF),
            sds((ext, 2 * N + LANES), BF),
            sds((8, inner), F32),
            sds((8, 2 * N), F32),
            sds((8, LANES), F32),
            sds((RIM, D), BF),
            sds((1, D), F32),
        ]
        + [sds((own, D), BF)] * shards,
        (scal, *states, *inside, xr, side, dy, dz, y, wzx, wside, chan, bcp, head, normed, gain),
        smem=(0,),
        scratch=[
            pltpu.VMEM((ext + RIM, inner), F32),
            pltpu.VMEM((ext + RIM, 2 * N), F32),
            pltpu.VMEM((ext, D), BF),
        ],
        flops=8 * rows * D * inner,
        moved=16 * MIB,
    )


def logits_kernel(vrows, label, table, normed, *rest):
    p_out, tops, stats, rows_scr, top, total, target, plain = rest
    step = pl.program_id(0)
    rows = normed.shape[0] - RIM

    @pl.when(step == 0)
    def _():
        rows_scr[...] = normed[RIM:, :].T
        top[...] = jnp.full((1, rows), -1e30, F32)
        total[...] = jnp.zeros((1, rows), F32)
        target[...] = jnp.zeros((1, rows), F32)
        plain[...] = jnp.zeros((1, rows), F32)

    highest, summed, hit, whole = top[...], total[...], target[...], plain[...]
    line = 2 * iota((PART, rows), 0)
    for half in range(2):
        for part_at in range(PAIRS // PART):
            first = step * PAIRS + part_at * PART
            here = slice(part_at * PART, (part_at + 1) * PART)
            padding = jnp.where(first + iota((PART, LANES), 0) < vrows, 0.0, -1e30)
            padding = jnp.concatenate([padding] * (rows // LANES), axis=1)
            raw = nn(table[here, half * D : (half + 1) * D], rows_scr[...])
            shown = raw + padding
            before = highest
            highest = jnp.maximum(before, jnp.max(shown, axis=0, keepdims=True))
            part = jnp.exp(shown - highest)
            summed = summed * jnp.exp(before - highest) + jnp.sum(part, axis=0, keepdims=True)
            wanted = label[...] - 2 * first - half
            hit = hit + jnp.sum(jnp.where(line == wanted, raw, 0.0), axis=0, keepdims=True)
            whole = whole + jnp.sum(raw, axis=0, keepdims=True)
            p_out[half, here, :] = part.astype(BF)
            at = 8 * (half * (PAIRS // PART) + part_at)
            tops[0, at : at + 8, :] = jnp.broadcast_to(highest, (8, rows))
    top[...] = highest
    total[...] = summed
    target[...] = hit
    plain[...] = whole
    stats[...] = jnp.concatenate([highest, summed, hit, whole, jnp.zeros((4, rows), F32)], axis=0)


def vocab_logits(label, table, normed, vrows):
    rows = normed.shape[0] - RIM
    padded = table.shape[0]
    steps = padded // PAIRS
    whole = lambda i: (0, 0)
    return pl.pallas_call(
        functools.partial(logits_kernel, vrows),
        grid=(steps,),
        out_shape=[
            sds((2, padded, rows), BF),
            sds((steps, 16 * (PAIRS // PART), rows), F32),
            sds((8, rows), F32),
        ],
        in_specs=[
            pl.BlockSpec((1, rows), whole),
            pl.BlockSpec((PAIRS, 2 * D), lambda i: (i, 0)),
            pl.BlockSpec(normed.shape, whole),
        ],
        out_specs=[
            pl.BlockSpec((2, PAIRS, rows), lambda i: (0, i, 0)),
            pl.BlockSpec((1, 16 * (PAIRS // PART), rows), lambda i: (i, 0, 0)),
            pl.BlockSpec((8, rows), whole),
        ],
        scratch_shapes=[pltpu.VMEM((D, rows), BF)] + [pltpu.VMEM((1, rows), F32)] * 4,
        compiler_params=pltpu.CompilerParams(
            dimension_semantics=("arbitrary",), vmem_limit_bytes=56 * MIB
        ),
        cost_estimate=pl.CostEstimate(
            flops=4 * rows * D * padded, bytes_accessed=40 * MIB, transcendentals=2 * rows * padded
        ),
        name="logits",
    )(label, table, normed)


def logit_grads(step, label, scale, weight, p_in):
    pairs, rows = p_in.shape[1:]
    line = 2 * iota((PART, rows), 0)
    usual = (SMOOTHING / V) * weight[...]
    special = (1.0 - SMOOTHING + SMOOTHING / V) * weight[...]
    for half in range(2):
        pieces = []
        for part_at in range(pairs // PART):
            wanted = label[...] - 2 * (step * pairs + part_at * PART) - half
            share = jnp.where(line == wanted, special, usual)
            at = 8 * (half * (pairs // PART) + part_at)
            grown = p_in[half, part_at * PART : (part_at + 1) * PART, :].astype(F32)
            pieces.append((grown * scale[0, at : at + 1, :] - share).astype(BF))
        yield half, jnp.concatenate(pieces, axis=0)


def rows_kernel(shards, own, scal, label, scale, weight, p_in, table, *rest):
    parts, acc = rest[:shards], rest[-1]
    step = pl.program_id(0)

    @pl.when(step == 0)
    def _():
        acc[...] = jnp.zeros_like(acc)

    for half, q in logit_grads(step, label, scale, weight, p_in):
        acc[...] += tn(q, table[:, half * D : (half + 1) * D])

    @pl.when(step == pl.num_programs(0) - 1)
    def _():
        for off in range(shards):
            at = pl.ds(pl.multiple_of((scal[0] ^ off) * own, own), own)
            parts[off][...] = acc[at, :].astype(BF)


def vocab_specs(rows):
    whole = lambda i: (0, 0)
    return [
        pl.BlockSpec((1, rows), whole),
        pl.BlockSpec((1, 16 * (PAIRS // PART), rows), lambda i: (i, 0, 0)),
        pl.BlockSpec((1, rows), whole),
        pl.BlockSpec((2, PAIRS, rows), lambda i: (0, i, 0)),
    ]


def vocab_rows(scal, label, scale, weight, p_in, table, shards):
    _, padded, rows = p_in.shape
    own = rows // shards
    whole = lambda i: (0, 0)
    return pl.pallas_call(
        functools.partial(rows_kernel, shards, own),
        grid=(padded // PAIRS,),
        out_shape=[sds((own, D), BF)] * shards,
        in_specs=[pl.BlockSpec(memory_space=pltpu.SMEM)]
        + vocab_specs(rows)
        + [pl.BlockSpec((PAIRS, 2 * D), lambda i: (i, 0))],
        out_specs=[pl.BlockSpec((own, D), whole)] * shards,
        scratch_shapes=[pltpu.VMEM((rows, D), F32)],
        compiler_params=pltpu.CompilerParams(
            dimension_semantics=("arbitrary",), vmem_limit_bytes=56 * MIB
        ),
        cost_estimate=pl.CostEstimate(
            flops=4 * rows * D * padded, bytes_accessed=40 * MIB, transcendentals=0
        ),
        name="rowgrads",
    )(scal, label, scale, weight, p_in, table)


def table_kernel(label, scale, weight, p_in, normed, out, rows_scr):
    step = pl.program_id(0)

    @pl.when(step == 0)
    def _():
        rows_scr[...] = normed[RIM:, :]

    for half, q in logit_grads(step, label, scale, weight, p_in):
        out[:, half * D : (half + 1) * D] = nn(q, rows_scr[...]).astype(BF)


def vocab_table_grad(label, scale, weight, p_in, normed):
    _, padded, rows = p_in.shape
    whole = lambda i: (0, 0)
    return pl.pallas_call(
        table_kernel,
        grid=(padded // PAIRS,),
        out_shape=sds((padded, 2 * D), BF),
        in_specs=vocab_specs(rows) + [pl.BlockSpec(normed.shape, whole)],
        out_specs=pl.BlockSpec((PAIRS, 2 * D), lambda i: (i, 0)),
        scratch_shapes=[pltpu.VMEM((rows, D), BF)],
        compiler_params=pltpu.CompilerParams(
            dimension_semantics=("arbitrary",), vmem_limit_bytes=56 * MIB
        ),
        cost_estimate=pl.CostEstimate(
            flops=4 * rows * D * padded, bytes_accessed=40 * MIB, transcendentals=0
        ),
        name="tablegrads",
    )(label, scale, weight, p_in, normed)


def adam_update(weight_in, gradient, moment_one, moment_two, factor, fix_one, fix_two, decay_rate):
    gradient = gradient * factor
    one_next = BETA_FIRST * moment_one + (1.0 - BETA_FIRST) * gradient
    two_next = BETA_SECOND * moment_two + (1.0 - BETA_SECOND) * gradient * gradient
    direction = one_next / fix_one / (jnp.sqrt(two_next / fix_two) + ADAM_EPS)
    return (weight_in - LEARN_RATE * (direction + decay_rate * weight_in), one_next, two_next)


def turn_kernel(share, bases, turned, root):
    count = bases.shape[0]
    total = jnp.zeros((1, BLK), F32)

    def turn(at, total):
        grad = share[pl.ds(pl.multiple_of(at * BLK, BLK), BLK), :].astype(F32)
        half_turn = tn(bases[at, 0], grad, HIGHEST)
        turned[at] = nn(half_turn, bases[at, 1], HIGHEST)
        return total + jnp.sum(grad * grad, axis=0, keepdims=True)

    for at in range(count):
        total = turn(at, total)
    root[...] = jnp.sqrt(total)


def turn_tiles(share, bases):
    count = bases.shape[0]
    return call(
        turn_kernel,
        "turn",
        [sds((count, BLK, BLK), F32), sds((1, BLK), F32)],
        (share, bases),
        moved=6 * MIB,
    )


def last_kernel(small, fixes, sums, *refs):
    tiles, turned, bases, tile_one, tile_two = refs[:5]
    little, refs = refs[5 : 5 + 4 * small], refs[5 + 4 * small :]
    tiles_out, copy_out, tile_one_out, tile_two_out = refs[:4]
    little_out = refs[4:]
    factor, fix_one, fix_two = sums[2:3, 0:1], fixes[0], fixes[1]
    for at in range(tiles.shape[0]):
        rotated = turned[at] * factor
        one_next = BETA_FIRST * tile_one[at] + (1.0 - BETA_FIRST) * rotated
        two_next = BETA_SECOND * tile_two[at] + (1.0 - BETA_SECOND) * rotated * rotated
        direction = one_next / fix_one / (jnp.sqrt(two_next / fix_two) + ADAM_EPS)
        back_half = nn(bases[at, 0], direction, HIGHEST)
        back = nt_dot(back_half, bases[at, 1], HIGHEST)
        after = tiles[at] - LEARN_RATE * (back + WEIGHT_DECAY * tiles[at])
        tiles_out[at] = after
        copy_out[at] = after.astype(BF)
        tile_one_out[at] = one_next
        tile_two_out[at] = two_next

    @pl.when(pl.program_id(0) == 0)
    def _():
        for which in range(small):
            before, gradient, first, second = (ref[...] for ref in little[4 * which : 4 * which + 4])
            results = adam_update(
                before,
                gradient,
                first,
                second,
                factor,
                fix_one,
                fix_two,
                WEIGHT_DECAY if which == 0 else 0.0,
            )
            outs = little_out[3 * which : 3 * which + 3]
            outs[0][...] = results[0] if which == 0 else results[0] - before
            outs[1][...], outs[2][...] = results[1], results[2]


def last_update(fixes, sums, tiles, turned, bases, tile_one, tile_two, little):
    count = tiles.shape[0]
    each = 4 if count % 4 == 0 else 2
    tile_spec = pl.BlockSpec((each, BLK, BLK), lambda i: (i, 0, 0))
    base_spec = pl.BlockSpec((each, 2, BLK, BLK), lambda i: (i, 0, 0, 0))
    whole = [
        pl.BlockSpec(x.shape, lambda i, rank=x.ndim: (0,) * rank) for group in little for x in group
    ]
    return pl.pallas_call(
        functools.partial(last_kernel, len(little)),
        grid=(count // each,),
        out_shape=[sds(tiles.shape, F32), sds(tiles.shape, BF), sds(tiles.shape, F32), sds(tiles.shape, F32)]
        + [sds(group[0].shape, F32) for group in little for _ in range(3)],
        in_specs=[
            pl.BlockSpec(memory_space=pltpu.SMEM),
            pl.BlockSpec(sums.shape, lambda i: (0, 0)),
        ]
        + [tile_spec, tile_spec, base_spec, tile_spec, tile_spec]
        + whole,
        out_specs=[tile_spec] * 4
        + [spec for which in range(len(little)) for spec in whole[4 * which : 4 * which + 3]],
        compiler_params=pltpu.CompilerParams(
            dimension_semantics=("arbitrary",), vmem_limit_bytes=48 * MIB
        ),
        cost_estimate=pl.CostEstimate(
            flops=24 * count * BLK * BLK * BLK, bytes_accessed=16 * MIB, transcendentals=0
        ),
        name="update",
    )(
        fixes,
        sums,
        tiles,
        turned,
        bases,
        tile_one,
        tile_two,
        *[x for group in little for x in group],
    )


def total_over(x, axis):
    out = x
    for off in range(1, lax.axis_size(axis)):
        out = out + swap(x, axis, off)
    return out


def shards(
    token_ids,
    labels,
    seq_lengths,
    micro_batch,
    step_count,
    block_slot,
    vocab_table,
    vocab_first,
    vocab_second,
    layer_blocks,
    block_bases,
    block_first,
    block_second,
    side_proj,
    side_first,
    side_second,
    shared_params,
    shared_first,
    shared_second,
    channel_params,
    channel_first,
    channel_second,
    head_params,
    head_first,
    head_second,
):
    nt = lax.axis_size("tensor")
    nd = lax.axis_size("dp")
    shard = lax.axis_index("tensor")
    place = lax.axis_index("dp")
    seqs = token_ids.shape[0]
    length = token_ids.shape[1] * nd
    chunks = nd // seqs
    rows = seqs * length // nd
    own = rows // nt
    vrows = vocab_table.shape[0]
    padded = -(-vrows // PAIRS) * PAIRS
    half = nd // 2
    inner = channel_params.shape[2]
    heads = head_params.shape[2]
    tiles = block_slot.shape[1]
    zx_count = D * 2 * inner // (BLK * BLK)
    per_layer = 3 * D * inner // (BLK * BLK)
    stride = D + 10 * N
    both = ("dp", "tensor")
    side_rows = side_proj.shape[1]
    share_size = shared_params.shape[0]
    share_pad = -(-share_size // 2048) * 2048

    piece = jnp.pad(side_proj.astype(BF), ((0, 0), (0, 0), (0, LANES - H))).reshape(-1, LANES)
    share = jnp.pad(shared_params.astype(BF), (0, share_pad - share_size)).reshape(-1, LANES)
    side_part = piece.shape[0]
    piece_rows = side_part + share.shape[0]
    ids = jnp.pad(jnp.concatenate([token_ids, labels], axis=0), ((0, 8 - 2 * seqs), (0, 0)))
    ids_all, pieces, shared_all = open_exchange(ids, piece, share, nd, nt)
    shared_full = shared_all.reshape(nd * nt, share_pad)[:, :share_size].reshape(-1).astype(F32)
    ids_all = ids_all.transpose(1, 0, 2).reshape(8, length)
    all_ids = ids_all[:seqs].reshape(-1)
    local_row = all_ids // 2 - shard * vrows
    held = (local_row >= 0) & (local_row < vrows) & (all_ids % 2 == place // half)
    scal = jnp.stack([place, shard]).astype(jnp.int32)
    scal_shard = shard.astype(jnp.int32).reshape(1)
    code = jnp.concatenate([jnp.where(held, local_row, 0), jnp.zeros((8,), jnp.int32)])
    listed, count = list_held(held, nd * rows)
    own_tiles = layer_blocks.shape[2]
    gathered = lax.all_gather(
        jnp.concatenate(
            [layer_blocks.astype(BF).reshape(own_tiles * BLK, BLK), pieces.reshape(-1, LANES)], axis=0
        ),
        "dp",
        axis=0,
        tiled=False,
    )
    *parts, table_low = gather_rows(
        scal, code, listed, count, vocab_table, nd, rows, padded
    )
    residual, normed = forward_rows(
        parts, None, shared_full[None, :D], nd, chunks, True, 4, nt
    )
    table_low, normed = lax.optimization_barrier((table_low, normed))
    gathered, normed = lax.optimization_barrier((gathered, normed))
    side_full = (
        gathered[:, own_tiles * BLK :]
        .reshape(nd, nt, L, side_rows, 2 * N + LANES)
        .transpose(2, 0, 1, 3, 4)
        .reshape(L, D, 2 * N + LANES)
    )
    table_all = lax.all_gather(table_low, "dp", axis=1, tiled=True)

    def layer_mats(layer_index):
        dt_part = lax.dynamic_slice_in_dim(
            side_full[layer_index], 2 * N + shard * heads, heads, 1
        )
        side_here = jnp.concatenate(
            [
                side_full[layer_index][:, : 2 * N],
                jnp.pad(dt_part, ((0, 0), (0, LANES - heads))),
            ],
            axis=1,
        )
        base = layer_index * stride
        gain = shared_full[base : base + D]
        taps = shared_full[base + D : base + D + 8 * N].reshape(4, 2 * N)
        bias = shared_full[base + D + 8 * N : base + stride].reshape(1, 2 * N)
        bcp = jnp.concatenate([taps, bias, jnp.zeros((3, 2 * N), F32)], axis=0)
        chan = jnp.pad(channel_params[layer_index], ((0, 2), (0, 0)))
        head = jnp.pad(head_params[layer_index], ((0, 5), (0, LANES - heads)))
        return [None, None, side_here, gain, bcp, chan, head]

    def hop(x, distance):
        pairs = [
            (k, k + distance)
            for k in range(nd)
            if 0 <= k % chunks + distance < chunks
        ]
        return lax.ppermute(x, "dp", pairs)

    def returned(parts):
        return [parts[0]] + [swap(parts[off], "tensor", off) for off in range(1, nt)]

    hops = range(1, chunks)
    mats = [layer_mats(layer_index) for layer_index in range(L)]
    final_gain = shared_full[L * stride :][None, :]
    gains = [mats[layer_index][3][None, :] for layer_index in range(L)] + [final_gain]
    saved = []
    tiles_now = gathered
    for layer_index in range(L):
        mats[layer_index][:2] = place_tiles(
            block_slot, tiles_now, own_tiles, inner, zx_count, per_layer, layer_index
        )
        wzx, wout, wside, gain, bcp, chan, head = mats[layer_index]
        z, xr, side, yloc, final, c_out, cum = mixer_front(normed, wzx, wside, chan, bcp, head)
        final, tiles_now = lax.optimization_barrier((final, tiles_now))
        states = [hop(final, k) for k in hops]
        result = mixer_middle(scal_shard, states, yloc, z, c_out, cum, wout, chan, nt)
        y, s_in = result[:2]
        below = normed
        before = residual
        inside = layer_index + 1 < L
        residual, branch, factor, normed = forward_rows(
            result[2:], before, gains[layer_index + 1], nd, chunks, inside, 5 + layer_index
        )
        saved.append((before, below, z, xr, side, c_out, cum, y, s_in, factor, branch))

    member = micro_batch[:, None] == jnp.arange(MB, dtype=jnp.int32)[None, :]
    batch_tokens = jnp.sum(jnp.where(member, seq_lengths[:, None], 0), axis=0).astype(F32)
    seq_weight = 1.0 / (MB * jnp.sum(jnp.where(member, batch_tokens[None, :], 0.0), axis=1))
    row_at = place * rows + jnp.arange(rows, dtype=jnp.int32)
    my_seq = place // chunks
    weight = jnp.where(row_at % length < seq_lengths[my_seq], seq_weight[my_seq], 0.0)
    all_labels = ids_all[seqs : 2 * seqs].reshape(-1)
    label = (lax.dynamic_slice_in_dim(all_labels, place * rows, rows) - 2 * shard * vrows).reshape(
        1, rows
    )
    row_weight = weight.reshape(1, rows)
    p_low, tops, stats = vocab_logits(label, table_all, normed, vrows)
    scale, seq_part = merge_stats(stats, tops, row_weight, nt, chunks)
    sent = returned(vocab_rows(scal_shard, label, scale, row_weight, p_low, table_all, nt))
    table_grad = vocab_table_grad(label, scale, row_weight, p_low, normed)
    sent, table_grad = lax.optimization_barrier((sent, table_grad))
    table_share = lax.psum_scatter(table_grad, "dp", scatter_dimension=1, tiled=True)
    grad_res, payload, grad_final_gain = backward_rows(
        sent, None, residual, final_gain, None, saved[L - 1][10], saved[L - 1][9], nd, chunks, 10
    )

    block_pieces = [None] * (2 * L)
    side_pieces = [None] * L
    channel_pieces = [None] * L
    head_pieces = [None] * L
    shared_pieces = [None] * L
    for layer_index in reversed(range(L)):
        wzx, wout, wside, gain, bcp, chan, head = mats[layer_index]
        residual_in, normed, z, xr, side, c_out, cum, y, s_in, factor, branch = saved[layer_index]
        u_low, dy, dz, dstate, gain_grad = gate_back(payload, wout, y, z, c_out, cum, chan)
        states = [hop(dstate, -k) for k in hops]
        grad_out_w = tn(u_low, payload)
        inside = mixer_within(s_in, xr, side, dy, chan, bcp, head)
        result = mixer_back(
            scal_shard,
            states,
            inside,
            xr,
            side,
            dy,
            dz,
            y,
            wzx,
            wside,
            chan,
            bcp,
            head,
            normed,
            gains[layer_index],
            nt,
        )
        dzx, dside, chan_grad, bcp_grad, head_grad, rim_grad, grad_gain_in = result[:7]
        parts_out = result[7:]
        grad_zx_w = tn(normed, dzx)
        grad_side_w = tn(normed, dside)
        block_pieces[2 * layer_index] = grad_zx_w.astype(BF)
        block_pieces[2 * layer_index + 1] = grad_out_w.astype(BF)
        side_pieces[layer_index] = grad_side_w
        shared_pieces[layer_index] = jnp.concatenate(
            [grad_gain_in[0], bcp_grad[:4].reshape(-1), bcp_grad[4]]
        )
        channel_pieces[layer_index] = jnp.concatenate([chan_grad[:5], gain_grad], axis=0)
        head_pieces[layer_index] = head_grad[:3, :heads]
        if layer_index == 0:
            shared_grads = jnp.concatenate(shared_pieces + [grad_final_gain[0]]).astype(BF)
            shared_grads = jnp.pad(
                shared_grads.reshape(nd * nt, share_size), ((0, 0), (0, share_pad - share_size))
            ).reshape(nd, nt * share_pad // LANES, LANES)
            lines = jnp.concatenate(
                [
                    jnp.stack(channel_pieces).reshape(-1, LANES),
                    jnp.pad(jnp.stack(head_pieces).reshape(-1), (0, LANES - L * 3 * heads)).reshape(
                        1, LANES
                    ),
                ],
                axis=0,
            ).astype(BF)
            line_count = lines.shape[0]
            line_rows = -(-line_count // RIM) * RIM
            lines = jnp.pad(lines, ((0, line_rows - line_count), (0, 0)))
            tile_grads = pack_tiles(
                scal_shard,
                block_slot,
                block_pieces,
                side_pieces,
                shared_grads,
                lines,
                own_tiles,
                per_layer,
                nt,
                heads,
            )
            tile_grads, table_share, parts_out, rim_grad = lax.optimization_barrier(
                (tile_grads, table_share, parts_out, rim_grad)
            )
            block_share = lax.psum_scatter(tile_grads, "dp", scatter_dimension=0, tiled=True)[0]
        if layer_index:
            grad_res, payload = backward_rows(
                parts_out,
                rim_grad,
                residual_in,
                gains[layer_index],
                grad_res,
                saved[layer_index - 1][10],
                saved[layer_index - 1][9],
                nd,
                chunks,
                10 + layer_index,
            )
        else:
            embed = finish_rows(
                parts_out, rim_grad, residual_in, gains[0], grad_res, nd, chunks
            )

    side_count = nt * side_part
    small_share = jnp.concatenate(
        [
            block_share[own_tiles * BLK : own_tiles * BLK + side_count].reshape(nt, side_part, LANES),
            block_share[own_tiles * BLK + side_count : own_tiles * BLK + nt * piece_rows].reshape(
                nt, piece_rows - side_part, LANES
            ),
        ],
        axis=1,
    )
    mine = jnp.zeros((piece_rows, LANES), F32)
    for off in range(nt):
        piece = lax.dynamic_index_in_dim(small_share, shard ^ off, 0, False)
        mine = mine + (piece if off == 0 else swap(piece, "tensor", off)).astype(F32)
    side_share = (
        mine[:side_part]
        .reshape(L, 2 * N // LANES + 1, side_rows, LANES)
        .transpose(0, 2, 1, 3)
        .reshape(L * side_rows, 2 * N + LANES)[:, : 2 * N + H]
    )
    shared_share = mine[side_part:].reshape(1, -1)[:, :share_size]
    lines = block_share[own_tiles * BLK + nt * piece_rows :].astype(F32)
    channel_sum = lines[: line_count - 1].reshape(L * 6, inner)
    head_sum = lines[line_count - 1, : L * 3 * heads].reshape(L * 3, heads)
    rotated, tile_root = turn_tiles(block_share, block_bases.reshape(own_tiles, 2, BLK, BLK))
    grad_table, table_root = add_rows(scal, code, listed, count, table_share, embed, vrows)
    sums = sum_everywhere(
        seq_part,
        [channel_sum, head_sum],
        [table_root, tile_root, side_share, shared_share],
        nd,
        nt,
    )
    seq_loss = sums[0, :seqs]
    clip_norm = sums[1, 0]
    steps_done = step_count[0].astype(F32)
    fix_one = 1.0 - jnp.power(BETA_FIRST, steps_done)
    fix_two = 1.0 - jnp.power(BETA_SECOND, steps_done)
    tile_shape = layer_blocks.shape[2:]
    flat = lambda x: x.reshape((-1, x.shape[-1]))
    little = [
        [flat(side_proj), side_share, flat(side_first), flat(side_second)],
        [flat(shared_params), shared_share, flat(shared_first), flat(shared_second)],
        [
            x.reshape(channel_params.shape).transpose(1, 0, 2)
            for x in (channel_params, channel_sum, channel_first, channel_second)
        ],
        [
            x.reshape(head_params.shape).transpose(1, 0, 2)
            for x in (head_params, head_sum, head_first, head_second)
        ],
    ]
    updated = last_update(
        jnp.stack([fix_one, fix_two]),
        sums,
        layer_blocks.reshape(tile_shape),
        rotated,
        block_bases.reshape((own_tiles, 2, BLK, BLK)),
        block_first.reshape(tile_shape),
        block_second.reshape(tile_shape),
        little,
    )
    table_out = adam_update(
        vocab_table,
        grad_table.astype(F32),
        vocab_first,
        vocab_second,
        sums[2, 0],
        fix_one,
        fix_two,
        WEIGHT_DECAY,
    )
    block_out = [x.reshape(layer_blocks.shape) for x in updated[:4]]
    like = [side_proj] * 3 + [shared_params] * 3
    small_out = [x.reshape(y.shape) for x, y in zip(updated[4:10], like)]
    small_out += [x.transpose(1, 0, 2) for x in updated[10:]]
    return (
        seq_loss,
        clip_norm,
        table_out[0],
        table_out[1],
        table_out[2],
        block_out[0],
        block_out[1],
        block_out[2],
        block_out[3],
        *small_out,
    )


def solution(mesh):
    table = P("tensor", "dp")
    block = P("dp", "tensor", None, None, None)
    side = P(None, ("dp", "tensor"), None)
    shared = P(("dp", "tensor"))
    channel = P(None, None, "tensor")
    in_specs = (
        P(None, "dp"),
        P(None, "dp"),
        P(),
        P(),
        P(),
        P("tensor", None),
        *[table] * 3,
        block,
        P("dp", "tensor", None, None, None, None),
        block,
        block,
        *[side] * 3,
        *[shared] * 3,
        *[channel] * 6,
    )
    out_specs = (
        P(),
        P(),
        *[table] * 3,
        *[block] * 4,
        *[side] * 3,
        *[shared] * 3,
        *[channel] * 6,
    )
    return jax.shard_map(shards, mesh=mesh, in_specs=in_specs, out_specs=out_specs, check_vma=False)
```

```python
import functools

import jax
import jax.numpy as jnp
from jax import lax
from jax.experimental import pallas as pl
from jax.experimental.pallas import tpu as pltpu
from jax.sharding import PartitionSpec as P

D = 1024
DI = 2048
H = 32
P_SIZE = 64
N = 128
V = 50288
SPAN = 256
L = 2
MB = 2
BLK = 128
RIM = 16
PAIRS = 1280
PART = 320
LANES = 128

HIGHEST = lax.Precision.HIGHEST
NORM_EPS = 1e-05
SMOOTHING = 0.1
ZLOSS_WEIGHT = 0.005
CLIP_LIMIT = 0.02
BETA_FIRST = 0.9
BETA_SECOND = 0.95
ADAM_EPS = 1e-08
LEARN_RATE = 0.03
WEIGHT_DECAY = 0.01

BF = jnp.bfloat16
F32 = jnp.float32
MIB = 1 << 20


def nn(a, b, precision=None):
    return lax.dot_general(
        a, b, (((1,), (0,)), ((), ())), precision=precision, preferred_element_type=F32
    )


def nt_dot(a, b, precision=None):
    return lax.dot_general(
        a, b, (((1,), (1,)), ((), ())), precision=precision, preferred_element_type=F32
    )


def tn(a, b, precision=None):
    return lax.dot_general(
        a, b, (((0,), (0,)), ((), ())), precision=precision, preferred_element_type=F32
    )


def iota(shape, dim):
    return lax.broadcasted_iota(jnp.int32, shape, dim)


def head_map(inner):
    return (iota((LANES, inner), 0) == iota((LANES, inner), 1) // P_SIZE).astype(F32).astype(BF)


def swap(x, axis, offset):
    size = lax.axis_size(axis)
    return lax.ppermute(x, axis, [(i, i ^ offset) for i in range(size)])


def halves(x):
    high = x.astype(BF)
    return high, (x - high.astype(F32)).astype(BF)


def thirds(x):
    high = x.astype(BF)
    rest = x - high.astype(F32)
    mid = rest.astype(BF)
    return high, mid, (rest - mid.astype(F32)).astype(BF)


def widen(x, expand):
    high, low = halves(x)
    twice = jnp.concatenate([expand, expand], axis=0)
    return nn(jnp.concatenate([high, low], axis=1), twice)


def narrow(x, expand):
    high, low = halves(x)
    return nt_dot(high, expand) + nt_dot(low, expand)


def tri_sum(tri, x):
    wide = nn(tri, jnp.concatenate(thirds(x), axis=1))
    size = x.shape[1]
    return wide[:, :size] + wide[:, size : 2 * size] + wide[:, 2 * size :]


def lanes3(column):
    high, mid, low = thirds(column)
    lane = iota((column.shape[0], LANES), 1)
    zero = jnp.zeros((column.shape[0], LANES), F32)
    wide = jnp.where(lane == 0, high.astype(F32), zero)
    wide = jnp.where(lane == 1, mid.astype(F32), wide)
    return jnp.where(lane == 2, low.astype(F32), wide).astype(BF)


def column3(wide):
    return wide[:, 0:1] + wide[:, 1:2] + wide[:, 2:3]


def rows3(line, inner):
    high, mid, low = thirds(line)
    at = iota((RIM, LANES), 0)
    wide = jnp.where(at == 0, high.astype(F32), 0.0)
    wide = jnp.where(at == 1, mid.astype(F32), wide)
    wide = jnp.where(at == 2, low.astype(F32), wide)
    if inner > LANES:
        wide = jnp.concatenate([wide, jnp.zeros((RIM, inner - LANES), F32)], axis=1)
    return wide.astype(BF)


def sigmoid(x):
    return 1.0 / (1.0 + jnp.exp(-x))


def softplus(x):
    return jnp.maximum(x, 0.0) + jnp.log1p(jnp.exp(-jnp.abs(x)))


def call(kernel, name, out_shape, args, smem=(), scratch=(), mib=60, flops=0, moved=0, **extra):
    specs = [
        pl.BlockSpec(memory_space=pltpu.SMEM if i in smem else pltpu.VMEM)
        for i in range(len(args))
    ]
    return pl.pallas_call(
        kernel,
        out_shape=out_shape,
        in_specs=specs,
        out_specs=jax.tree.map(lambda _: pl.BlockSpec(memory_space=pltpu.VMEM), out_shape),
        scratch_shapes=list(scratch),
        compiler_params=pltpu.CompilerParams(vmem_limit_bytes=mib * MIB),
        cost_estimate=pl.CostEstimate(flops=flops, bytes_accessed=moved, transcendentals=0),
        name=name,
        **extra,
    )(*args)


def sds(shape, dtype):
    return jax.ShapeDtypeStruct(shape, dtype)


def list_held(held, total):
    runs = held.reshape(-1, LANES)
    upper = iota((LANES, LANES), 0) <= iota((LANES, LANES), 1)
    rank = nn(runs.astype(BF), upper.astype(BF)).astype(jnp.int32) - 1
    here = (rank[:, :, None] == iota((1, 1, LANES), 2)) & runs[:, :, None]
    at = jnp.sum(jnp.where(here, iota((1, LANES, 1), 1), 0), axis=1)
    counts = rank[:, -1] + 1
    first = iota(at.shape, 0) * LANES
    listed = jnp.where(iota(at.shape, 1) < counts[:, None], at + first, total)
    return listed.reshape(-1), counts


def over_listed(listed, count, body):
    def run(at_run, carry):
        def turn(step, inner_carry):
            for lane in range(8):
                body(listed[at_run * LANES + step * 8 + lane])
            return inner_carry

        lax.fori_loop(0, (count[at_run] + 7) // 8, turn, 0)
        return carry

    lax.fori_loop(0, count.shape[0], run, 0)


def look_kernel(groups, rows, scal, code, listed, count, table, *rest):
    outs, low, work = rest[:groups], rest[groups], rest[groups + 1]
    place = scal[0]
    vrows = table.shape[0]
    edge = vrows // RIM * RIM
    low[edge:, :] = jnp.zeros((low.shape[0] - edge, low.shape[1]), BF)
    low[0:vrows, :] = table[...].astype(BF)

    def fill(step, carry):
        work[pl.ds(pl.multiple_of(step * rows, rows), rows), :] = jnp.zeros((rows, table.shape[1]), F32)
        return carry

    lax.fori_loop(0, groups, fill, 0)

    def take(at):
        work[pl.ds(at, 1), :] = table[pl.ds(code[at], 1), :]

    over_listed(listed, count, take)
    for off in range(groups):
        base = pl.multiple_of((place ^ off) * rows, rows)
        outs[off][...] = work[pl.ds(base, rows), :].astype(BF)


def gather_rows(scal, code, listed, count, table, groups, rows, padded):
    cols = table.shape[1]
    return call(
        functools.partial(look_kernel, groups, rows),
        "look",
        [sds((rows, cols), BF)] * groups + [sds((padded, cols), BF)],
        (scal, code, listed, count, table),
        smem=(0, 1, 2, 3),
        scratch=[pltpu.VMEM((groups * rows + 8, cols), F32)],
        moved=30 * MIB,
    )


def add_kernel(groups, rows, vrows, scal, code, listed, count, share, parts, *rest):
    out, square, work, bins = rest
    place = scal[0]
    bins[...] = share[0:vrows, :].astype(F32)
    for off in range(groups):
        base = pl.multiple_of((place ^ off) * rows, rows)
        work[pl.ds(base, rows), :] = parts[off].astype(F32)
    work[groups * rows :, :] = jnp.zeros((8, work.shape[1]), F32)

    def add(at):
        to = pl.ds(code[at], 1)
        bins[to, :] = bins[to, :] + work[pl.ds(at, 1), :]

    over_listed(listed, count, add)
    total = bins[...]
    out[...] = total.astype(BF)
    square[...] = jnp.sqrt(jnp.sum(total * total, axis=0, keepdims=True))


def add_rows(scal, code, listed, count, share, parts, vrows):
    cols = share.shape[1]
    groups, rows, _ = parts.shape
    return call(
        functools.partial(add_kernel, groups, rows, vrows),
        "addrows",
        [sds((vrows, cols), BF), sds((1, cols), F32)],
        (scal, code, listed, count, share, parts),
        smem=(0, 1, 2, 3),
        scratch=[pltpu.VMEM((rows * groups + 8, cols), F32), pltpu.VMEM((vrows, cols), F32)],
        moved=30 * MIB,
    )


def tiles_kernel(slots_each, zx_count, per_layer, first_layer, slot, tiles, *outs):
    for layer in (first_layer,):
        for at in range(per_layer):
            where = slot[0, layer * per_layer + at]
            owner = where // slots_each
            first = pl.multiple_of((where % slots_each) * BLK, BLK)
            tile = tiles[owner, pl.ds(first, BLK), :]
            if at < zx_count:
                wide = outs[0].shape[1] // BLK
                row, col = at // wide, at % wide
                out = outs[0]
            else:
                wide = D // BLK
                row, col = (at - zx_count) // wide, (at - zx_count) % wide
                out = outs[1]
            out[row * BLK : (row + 1) * BLK, col * BLK : (col + 1) * BLK] = tile


def place_tiles(slot, tiles, slots_each, inner, zx_count, per_layer, layer):
    return call(
        functools.partial(tiles_kernel, slots_each, zx_count, per_layer, layer),
        "placetiles",
        [sds((D, 2 * inner), BF), sds((inner, D), BF)],
        (slot, tiles),
        smem=(0,),
        moved=14 * MIB,
    )


def pack_kernel(slots_each, per_layer, layers, shards, heads, scal, slot, *refs):
    mats, sides, refs = refs[: 2 * layers], refs[2 * layers : 3 * layers], refs[3 * layers :]
    shared, lines, out, work = refs
    for layer in range(layers):
        zx, wout = mats[2 * layer], mats[2 * layer + 1]
        zx_wide, out_wide = zx.shape[1] // BLK, D // BLK
        zx_count = zx.shape[0] // BLK * zx_wide
        for at in range(per_layer):
            where = slot[0, layer * per_layer + at]
            if at < zx_count:
                source, row, col = zx, at // zx_wide, at % zx_wide
            else:
                source = wout
                row, col = (at - zx_count) // out_wide, (at - zx_count) % out_wide
            first = pl.multiple_of((where % slots_each) * BLK, BLK)
            out[where // slots_each, pl.ds(first, BLK), :] = source[
                row * BLK : (row + 1) * BLK, col * BLK : (col + 1) * BLK
            ]
        work[layer, :, : 2 * N] = sides[layer][:, : 2 * N]
        work[layer, :, 2 * N :] = pltpu.roll(sides[layer][:, 2 * N :], scal[0] * heads, 1)
    groups = out.shape[0]
    each = work.shape[1] // (groups * shards)
    piece = layers * each * work.shape[2] // LANES
    base = slots_each * BLK
    for group in range(groups):
        for shard in range(shards):
            first = (group * shards + shard) * each
            blocks = [
                work[layer, first : first + each, col : col + LANES]
                for layer in range(layers)
                for col in range(0, work.shape[2], LANES)
            ]
            at = base + shard * piece
            out[group, at : at + piece, :] = jnp.concatenate(blocks, axis=0).astype(BF)
    base += shards * piece
    out[:, base : base + shared.shape[1], :] = shared[...]
    for group in range(groups):
        out[group, base + shared.shape[1] :, :] = lines[...]


def pack_tiles(scal, slot, mats, sides, shared, lines, slots_each, per_layer, shards, heads):
    groups = shared.shape[0]
    layers = len(sides)
    depth, width = sides[0].shape
    extra = layers * depth * width // (groups * LANES) + shared.shape[1] + lines.shape[0]
    return call(
        functools.partial(pack_kernel, slots_each, per_layer, layers, shards, heads),
        "packtiles",
        sds((groups, slots_each * BLK + extra, LANES), BF),
        (scal, slot, *mats, *sides, shared, lines),
        smem=(0, 1),
        scratch=[pltpu.VMEM((layers, depth, width), F32)],
        moved=14 * MIB,
    )


def norm_rows(values, gain):
    return values * lax.rsqrt(jnp.mean(values * values, axis=-1, keepdims=True) + NORM_EPS) * gain


def total_of(parts):
    total = parts[0][...].astype(F32)
    for part in parts[1:]:
        total = total + part[...].astype(F32)
    return total


def send(source, target, send_sem, recv_sem, device):
    copy = pltpu.make_async_remote_copy(
        src_ref=source,
        dst_ref=target,
        send_sem=send_sem,
        recv_sem=recv_sem,
        device_id=device,
        device_id_type=pl.DeviceIdType.MESH,
    )
    copy.start()
    return copy


def greet_shards(groups, shards, rims, wide=False):
    place, shard = lax.axis_index("dp"), lax.axis_index("tensor")
    last = shard == shards - 1
    barrier = pltpu.get_barrier_semaphore()

    def greet(device):
        pl.semaphore_signal(barrier, inc=1, device_id=device, device_id_type=pl.DeviceIdType.MESH)

    for off in range(1, shards):
        greet((place, shard ^ off))
    if not rims:
        pl.semaphore_wait(barrier, shards - 1)
        return
    if wide:
        for off in range(1, groups):
            greet((place ^ off, shard))

        @pl.when(jnp.logical_not(last))
        def _():
            greet((lax.rem(place + groups - 1, groups), shards - 1))

        @pl.when(last)
        def _():
            for other in range(shards - 1):
                greet((lax.rem(place + 1, groups), other))

        pl.semaphore_wait(barrier, shards + groups - 2 + jnp.where(last, shards - 1, 1))
        return
    greet((lax.rem(place + groups - 1, groups), shards - 1))

    @pl.when(last)
    def _():
        for other in range(shards):
            greet((lax.rem(place + 1, groups), other))

    pl.semaphore_wait(barrier, shards - 1 + jnp.where(last, shards + 1, 1))


def pass_along(rows, own, base, shards, sems):
    place, shard = lax.axis_index("dp"), lax.axis_index("tensor")

    def copy(way, hop, source, to):
        at = pl.ds(pl.multiple_of(base + source * own, RIM), own)
        return pltpu.make_async_remote_copy(
            src_ref=rows.at[at, :],
            dst_ref=rows.at[at, :],
            send_sem=sems.at[0, way, hop],
            recv_sem=sems.at[1, way, hop],
            device_id=(place, to),
            device_id_type=pl.DeviceIdType.MESH,
        )

    def up(hop):
        return copy(0, hop, shard - hop, shard + 1)

    def down(hop):
        return copy(1, hop, shard + hop, shard - 1)

    can_up, can_down = shard + 1 < shards, shard > 0
    for hop in range(shards):
        if hop > 0:

            @pl.when(shard - hop >= 0)
            def _():
                copy(0, hop - 1, shard - hop, shard - 1).wait_recv()

        if hop < shards - 1:

            @pl.when(jnp.logical_and(shard - hop >= 0, can_up))
            def _():
                up(hop).start()

        if hop > 0:

            @pl.when(shard + hop < shards)
            def _():
                copy(1, hop - 1, shard + hop, shard + 1).wait_recv()

        if hop < shards - 1:

            @pl.when(jnp.logical_and(shard + hop < shards, can_down))
            def _():
                down(hop).start()

    for hop in range(shards - 1):

        @pl.when(jnp.logical_and(shard - hop >= 0, can_up))
        def _():
            up(hop).wait_send()

        @pl.when(jnp.logical_and(shard + hop < shards, can_down))
        def _():
            down(hop).wait_send()


def exchange_terms(parts, slots, work, sems, ready=None):
    place, shard = lax.axis_index("dp"), lax.axis_index("tensor")
    shards = len(parts)

    def copy(off, source, to, slot):
        return pltpu.make_async_remote_copy(
            src_ref=source,
            dst_ref=slots.at[slot],
            send_sem=sems.at[0, off],
            recv_sem=sems.at[1, slot],
            device_id=(place, to),
            device_id_type=pl.DeviceIdType.MESH,
        )

    def direct(off):
        return copy(off, parts[off], shard ^ off, off)

    if shards != 4:
        for off in reversed(range(1, shards)):
            if ready:
                ready(off)
            direct(off).start()
        if ready:
            ready(0)
        for off in range(1, shards):
            direct(off).wait()
        total = parts[0][...].astype(F32)
        for off in range(1, shards):
            total = total + slots[off].astype(F32)
        work[...] = total
        return
    relay, added = 0, 4
    outer = jnp.logical_or(shard == 0, shard == shards - 1)
    inner = jnp.logical_not(outer)

    def pass_relayed():
        copy(0, parts[3], shard ^ 1, relay).wait_recv()
        slots[added] = (slots[relay].astype(F32) + parts[2][...].astype(F32)).astype(BF)
        copy(2, slots.at[added], shard ^ 2, 2).start()

    if ready:
        ready(3)

        @pl.when(outer)
        def _():
            copy(3, parts[3], shard ^ 1, relay).start()

        @pl.when(inner)
        def _():
            direct(3).start()

        ready(2)

        @pl.when(outer)
        def _():
            direct(2).start()

        @pl.when(inner)
        def _():
            pass_relayed()

        ready(1)
        direct(1).start()
        ready(0)
    else:

        @pl.when(outer)
        def _():
            copy(3, parts[3], shard ^ 1, relay).start()
            direct(2).start()
            direct(1).start()

        @pl.when(inner)
        def _():
            direct(3).start()
            direct(1).start()
            pass_relayed()

    direct(1).wait_recv()
    total = parts[0][...].astype(F32) + slots[1].astype(F32)
    direct(2).wait_recv()
    work[...] = total + slots[2].astype(F32)

    @pl.when(inner)
    def _():
        direct(3).wait_recv()
        work[...] += slots[3].astype(F32)

    for off in range(1, shards):
        direct(off).wait_send()


def term_scratch(shards, own, width):
    return [
        pltpu.VMEM((shards + 1, own, width), BF),
        pltpu.VMEM((own, width), F32),
        pltpu.SemaphoreType.DMA((2, shards + 1)),
    ]


def forward_kernel(groups, shards, chunks, packed, rims, *refs):
    ready = None
    place, shard = lax.axis_index("dp"), lax.axis_index("tensor")
    if packed:
        parts, refs = refs[:shards], refs[shards:]
        before, gain, residual, branch, factor, normed, *refs = refs
        slots, work, term_sems, row_sems, rim_sems = refs
        own = parts[0].shape[0]
        greet_shards(groups, shards, rims)
    else:
        looked, refs = refs[:groups], refs[groups:]
        gain, residual, normed, *refs = refs
        slots, work, term_sems, row_sems, rim_sems, arrived, terms, look_sems = refs
        own = terms.shape[1]
        half, cols = groups // 2, looked[0].shape[1]
        parts = [terms.at[off] for off in range(shards)]
        greet_shards(groups, shards, rims, True)

        def block(off):
            return pl.ds(pl.multiple_of((shard ^ off) * own, own), own)

        copies = {
            (off, other): send(
                looked[other].at[block(off), :],
                arrived.at[off, other],
                look_sems.at[0, off, other],
                look_sems.at[1, off, other],
                (place ^ other, shard),
            )
            for off in reversed(range(shards))
            for other in range(1, groups)
        }

        def ready(off):
            for other in range(1, groups):
                copies[off, other].wait()
            arrived[off, 0] = looked[0][block(off), :]
            for other in range(half):
                at = pl.multiple_of(lax.rem(place ^ other, half) * cols, cols)
                terms[off, :, pl.ds(at, cols)] = arrived[off, other] + arrived[off, other + half]

    rows = own * shards
    chunk = lax.rem(place, chunks)
    exchange_terms(parts, slots, work, term_sems, ready)
    total = work[...]
    if packed:
        scale = lax.rsqrt(column3(total[:, D:]) / DI + NORM_EPS)
        branch[...] = total[:, :D]
        factor[...] = scale
        total = before[...] + scale * total[:, :D]
    residual[...] = total
    at = pl.ds(pl.multiple_of(RIM + shard * own, RIM), own)
    normed[at, :] = norm_rows(total, gain[...]).astype(BF)

    def rim_copy(to, device):
        return pltpu.make_async_remote_copy(
            src_ref=normed.at[rows : rows + RIM, :],
            dst_ref=normed.at[0:RIM, :],
            send_sem=rim_sems.at[0, to],
            recv_sem=rim_sems.at[1, 0],
            device_id=device,
            device_id_type=pl.DeviceIdType.MESH,
        )

    gives = jnp.logical_and(shard == shards - 1, chunk + 1 < chunks)
    if rims:

        @pl.when(gives)
        def _():
            for to in range(shards):
                rim_copy(to, (place + 1, to)).start()

        @pl.when(chunk == 0)
        def _():
            normed[0:RIM, :] = jnp.zeros((RIM, D), BF)

    else:
        normed[0:RIM, :] = jnp.zeros((RIM, D), BF)
    pass_along(normed, own, RIM, shards, row_sems)
    if rims:

        @pl.when(chunk > 0)
        def _():
            rim_copy(0, (place - 1, shards - 1)).wait_recv()

        @pl.when(gives)
        def _():
            for to in range(shards):
                rim_copy(to, (place + 1, to)).wait_send()


def forward_rows(parts, before, gain, groups, chunks, rims, cid, entry=0):
    packed = before is not None
    if packed:
        shards = len(parts)
        own, width = parts[0].shape
        args = (*parts, before, gain)
        extra = []
    else:
        shards = entry
        own, width = parts[0].shape[0] // shards, D
        args = (*parts, gain)
        extra = [
            pltpu.VMEM((shards, groups, own, parts[0].shape[1]), BF),
            pltpu.VMEM((shards, own, D), BF),
            pltpu.SemaphoreType.DMA((2, shards, groups)),
        ]
    vmem = pl.BlockSpec(memory_space=pltpu.VMEM)
    outs = [sds((own, D), F32)]
    if packed:
        outs += [sds((own, D), F32), sds((own, 1), F32)]
    outs += [sds((RIM + own * shards, D), BF)]
    return pl.pallas_call(
        functools.partial(forward_kernel, groups, shards, chunks, packed, rims),
        out_shape=outs,
        in_specs=[vmem] * len(args),
        out_specs=[vmem] * len(outs),
        scratch_shapes=[
            *term_scratch(shards, own, width),
            pltpu.SemaphoreType.DMA((2, 2, shards)),
            pltpu.SemaphoreType.DMA((2, shards)),
            *extra,
        ],
        compiler_params=pltpu.CompilerParams(
            collective_id=cid, has_side_effects=True, vmem_limit_bytes=60 * MIB
        ),
        name="forward" if packed else "enter",
    )(*args)


def backward_kernel(groups, shards, chunks, exchanged, *refs):
    parts, refs = refs[:shards], refs[shards:]
    if exchanged:
        residual, gain, branch, factor, grad_out, rows_out, gain_grad, row_sems = refs
    else:
        rim, residual, gain, grad_in, branch, factor, grad_out, rows_out, refs = *refs[:8], refs[8:]
        slots, work, term_sems, from_rims, rim_sems, row_sems = refs
    own = parts[0].shape[0]
    place, shard = lax.axis_index("dp"), lax.axis_index("tensor")
    chunk = lax.rem(place, chunks)
    greet_shards(groups, shards, not exchanged)
    values = residual[...]
    inv = lax.rsqrt(jnp.mean(values * values, axis=-1, keepdims=True) + NORM_EPS)
    if exchanged:
        grad = total_of(parts)
        gain_grad[...] = jnp.sum(grad * values * inv, axis=0, keepdims=True)
    else:

        def rim_copy(slot, device):
            return pltpu.make_async_remote_copy(
                src_ref=rim,
                dst_ref=from_rims.at[slot],
                send_sem=rim_sems.at[0, slot],
                recv_sem=rim_sems.at[1, slot],
                device_id=device,
                device_id_type=pl.DeviceIdType.MESH,
            )

        @pl.when(chunk > 0)
        def _():
            rim_copy(shard, (place - 1, shards - 1)).start()

        exchange_terms(parts, slots, work, term_sems)

        @pl.when(jnp.logical_and(shard == shards - 1, chunk + 1 < chunks))
        def _():
            for other in range(shards):
                rim_copy(other, (place + 1, other)).wait_recv()
            edge = from_rims[0].astype(F32)
            for other in range(1, shards):
                edge = edge + from_rims[other].astype(F32)
            work[own - RIM :, :] += edge

        @pl.when(chunk > 0)
        def _():
            rim_copy(shard, (place - 1, shards - 1)).wait_send()

        grad = work[...]
    scaled = grad * gain[...]
    result = inv * scaled - values * (inv * inv * inv) * jnp.mean(
        scaled * values, axis=-1, keepdims=True
    )
    if not exchanged:
        result = grad_in[...] + result
    grad_out[...] = result
    scale = factor[...]
    at = pl.ds(pl.multiple_of(shard * own, RIM), own)
    rows_out[at, :D] = (scale * result).astype(BF)
    inner_rows = jnp.sum(result * branch[...], axis=-1, keepdims=True)
    rows_out[at, D:] = lanes3(scale * scale * scale * inner_rows / DI)
    pass_along(rows_out, own, 0, shards, row_sems)


def backward_rows(parts, rim, residual, gain, grad_in, branch, factor, groups, chunks, cid):
    shards = len(parts)
    own = residual.shape[0]
    exchanged = rim is None
    vmem = pl.BlockSpec(memory_space=pltpu.VMEM)
    outs = [sds((own, D), F32), sds((own * shards, D + LANES), BF)]
    row_sems = pltpu.SemaphoreType.DMA((2, 2, shards))
    if exchanged:
        args = (*parts, residual, gain, branch, factor)
        outs.append(sds((1, D), F32))
        scratch = [row_sems]
    else:
        args = (*parts, rim, residual, gain, grad_in, branch, factor)
        scratch = [
            *term_scratch(shards, own, D),
            pltpu.VMEM((shards, RIM, D), BF),
            pltpu.SemaphoreType.DMA((2, shards)),
            row_sems,
        ]
    return pl.pallas_call(
        functools.partial(backward_kernel, groups, shards, chunks, exchanged),
        out_shape=outs,
        in_specs=[vmem] * len(args),
        out_specs=[vmem] * len(outs),
        scratch_shapes=scratch,
        compiler_params=pltpu.CompilerParams(
            collective_id=cid, has_side_effects=True, vmem_limit_bytes=60 * MIB
        ),
        name="backward",
    )(*args)


def stats_kernel(shards, chunks, stats, tops, weight, scale_out, loss_out, slots, sems):
    place, shard = lax.axis_index("dp"), lax.axis_index("tensor")
    rows = weight.shape[1]
    own = rows // shards
    greet_shards(0, shards, False)
    copies = [
        send(stats, slots.at[off - 1], sems.at[0, off], sems.at[1, off], (place, shard ^ off))
        for off in range(1, shards)
    ]
    for copy in copies:
        copy.wait()
    others = [stats[...]] + [slots[off] for off in range(shards - 1)]
    best = others[0][0:1, :]
    for one in others[1:]:
        best = jnp.maximum(best, one[0:1, :])
    summed, target, plain = jnp.zeros((1, rows), F32), jnp.zeros((1, rows), F32), jnp.zeros((1, rows), F32)
    for one in others:
        summed = summed + one[1:2, :] * jnp.exp(one[0:1, :] - best)
        target = target + one[2:3, :]
        plain = plain + one[3:4, :]
    log_total = best + jnp.log(summed)
    token_loss = (
        log_total
        - (1.0 - SMOOTHING) * target
        - SMOOTHING / V * plain
        + ZLOSS_WEIGHT * log_total * log_total
    )
    lane = iota((1, rows), 1)
    mine = jnp.logical_and(lane >= shard * own, lane < (shard + 1) * own)
    loss = jnp.sum(jnp.where(mine, weight[...] * token_loss, 0.0), axis=1, keepdims=True)
    here = jnp.logical_and(iota((8, LANES), 0) == 0, iota((8, LANES), 1) == place // chunks)
    loss_out[...] = jnp.where(here, loss, 0.0)
    soft = weight[...] * (1.0 + 2.0 * ZLOSS_WEIGHT * log_total)
    for step in range(tops.shape[0]):
        scale_out[step] = soft * jnp.exp(tops[step] - log_total)


def merge_stats(stats, tops, weight, shards, chunks):
    vmem = pl.BlockSpec(memory_space=pltpu.VMEM)
    return pl.pallas_call(
        functools.partial(stats_kernel, shards, chunks),
        out_shape=[sds(tops.shape, F32), sds((8, LANES), F32)],
        in_specs=[vmem] * 3,
        out_specs=[vmem] * 2,
        scratch_shapes=[
            pltpu.VMEM((shards - 1, *stats.shape), F32),
            pltpu.SemaphoreType.DMA((2, shards)),
        ],
        compiler_params=pltpu.CompilerParams(
            collective_id=9, has_side_effects=True, vmem_limit_bytes=8 * MIB
        ),
        name="stats",
    )(stats, tops, weight)


def finish_kernel(groups, shards, chunks, own, *refs):
    parts, rim, residual, gain, grad_in, out = refs[:shards], *refs[shards : shards + 5]
    slots, work, term_sems, from_rims, payload, full, rim_sems, row_sems, out_sems = refs[shards + 5 :]
    place, shard = lax.axis_index("dp"), lax.axis_index("tensor")
    half = groups // 2
    cols = out.shape[2]
    chunk = lax.rem(place, chunks)
    last = shard == shards - 1
    shard_peers = [(place, shard ^ off) for off in range(1, shards)]
    group_peers = [(place ^ off, shard) for off in range(1, groups)]
    barrier = pltpu.get_barrier_semaphore()

    def greet(device):
        pl.semaphore_signal(barrier, inc=1, device_id=device, device_id_type=pl.DeviceIdType.MESH)

    for peer in shard_peers + group_peers:
        greet(peer)

    @pl.when(jnp.logical_not(last))
    def _():
        greet((lax.rem(place + groups - 1, groups), shards - 1))

    @pl.when(last)
    def _():
        for other in range(shards - 1):
            greet((lax.rem(place + 1, groups), other))

    pl.semaphore_wait(barrier, shards + groups - 2 + jnp.where(last, shards - 1, 1))

    def rim_copy():
        return pltpu.make_async_remote_copy(
            src_ref=rim,
            dst_ref=from_rims.at[shard],
            send_sem=rim_sems.at[0, shard],
            recv_sem=rim_sems.at[1, shard],
            device_id=(place - 1, shards - 1),
            device_id_type=pl.DeviceIdType.MESH,
        )

    @pl.when(chunk > 0)
    def _():
        rim_copy().start()

    values = residual[...]
    inv = lax.rsqrt(jnp.mean(values * values, axis=-1, keepdims=True) + NORM_EPS)
    exchange_terms(parts, slots, work, term_sems)

    @pl.when(jnp.logical_and(chunk + 1 < chunks, last))
    def _():
        for other in range(shards):
            pltpu.make_async_remote_copy(
                src_ref=rim,
                dst_ref=from_rims.at[other],
                send_sem=rim_sems.at[0, other],
                recv_sem=rim_sems.at[1, other],
                device_id=(place + 1, other),
                device_id_type=pl.DeviceIdType.MESH,
            ).wait_recv()
        edge = from_rims[0].astype(F32)
        for other in range(1, shards):
            edge = edge + from_rims[other].astype(F32)
        work[own - RIM :, :] += edge

    @pl.when(chunk > 0)
    def _():
        rim_copy().wait_send()

    scaled = work[...] * gain[...]
    result = (
        grad_in[...]
        + inv * scaled
        - values * (inv * inv * inv) * jnp.mean(scaled * values, axis=-1, keepdims=True)
    ).astype(BF)
    payload[...] = result
    rows_out = [
        send(
            payload,
            full.at[off],
            row_sems.at[0, off],
            row_sems.at[1, off],
            shard_peers[off - 1],
        )
        for off in range(1, shards)
    ]
    full[0] = result

    def first_col(group):
        return pl.multiple_of(lax.rem(group, half) * cols, cols)

    cuts = []
    for off in range(shards):
        if off > 0:
            rows_out[off - 1].wait()
        at = pl.ds(pl.multiple_of((shard ^ off) * own, own), own)
        for other in range(1, groups):
            cuts.append(
                send(
                    full.at[off, :, pl.ds(first_col(place ^ other), cols)],
                    out.at[other, at, :],
                    out_sems.at[0, off, other],
                    out_sems.at[1, off, other],
                    group_peers[other - 1],
                )
            )
        out[0, at, :] = full[off, :, pl.ds(first_col(place), cols)]
    for cut in cuts:
        cut.wait()


def finish_rows(parts, rim, residual, gain, grad_in, groups, chunks):
    shards = len(parts)
    own = parts[0].shape[0]
    vmem = pl.BlockSpec(memory_space=pltpu.VMEM)
    args = (*parts, rim, residual, gain, grad_in)
    return pl.pallas_call(
        functools.partial(finish_kernel, groups, shards, chunks, own),
        out_shape=sds((groups, own * shards, 2 * D // groups), BF),
        in_specs=[vmem] * len(args),
        out_specs=vmem,
        scratch_shapes=[
            *term_scratch(shards, own, D),
            pltpu.VMEM((shards, RIM, D), BF),
            pltpu.VMEM((own, D), BF),
            pltpu.VMEM((shards, own, D), BF),
            pltpu.SemaphoreType.DMA((2, shards)),
            pltpu.SemaphoreType.DMA((2, shards)),
            pltpu.SemaphoreType.DMA((2, shards, groups)),
        ],
        compiler_params=pltpu.CompilerParams(
            collective_id=3, has_side_effects=True, vmem_limit_bytes=60 * MIB
        ),
        name="finish",
    )(*args)


def open_kernel(groups, shards, ids, piece, share, ids_out, pieces_out, share_out, middle, sends, gets):
    place, shard = lax.axis_index("dp"), lax.axis_index("tensor")
    near = [(place, shard ^ off) for off in range(1, shards)]
    far = [(place ^ off, shard) for off in range(1, groups)]
    barrier = pltpu.get_barrier_semaphore()
    for peer in near + far:
        pl.semaphore_signal(barrier, inc=1, device_id=peer, device_id_type=pl.DeviceIdType.MESH)
    pl.semaphore_wait(barrier, len(near) + len(far))
    shares, others = [], []
    for i, peer in enumerate(near):
        shares.append(send(share, middle.at[shard], sends.at[0, i], gets.at[0, i], peer))
    for i, peer in enumerate(far):
        others.append(send(ids, ids_out.at[place], sends.at[1, i], gets.at[1, i], peer))
    for i, peer in enumerate(near):
        others.append(send(piece, pieces_out.at[shard], sends.at[2, i], gets.at[2, i], peer))
    middle[shard] = share[...]
    ids_out[place] = ids[...]
    pieces_out[shard] = piece[...]
    for copy in shares:
        copy.wait()
    for i, peer in enumerate(far):
        others.append(send(middle, share_out.at[place], sends.at[3, i], gets.at[3, i], peer))
    share_out[place] = middle[...]
    for copy in others:
        copy.wait()


def open_exchange(ids, piece, share, groups, shards):
    count = max(groups, shards)
    vmem = pl.BlockSpec(memory_space=pltpu.VMEM)
    return pl.pallas_call(
        functools.partial(open_kernel, groups, shards),
        out_shape=[
            sds((groups, *ids.shape), jnp.int32),
            sds((shards, *piece.shape), BF),
            sds((groups, shards, *share.shape), BF),
        ],
        in_specs=[vmem] * 3,
        out_specs=[vmem] * 3,
        scratch_shapes=[
            pltpu.VMEM((shards, *share.shape), BF),
            pltpu.SemaphoreType.DMA((4, count)),
            pltpu.SemaphoreType.DMA((4, count)),
        ],
        compiler_params=pltpu.CompilerParams(
            collective_id=2, has_side_effects=True, vmem_limit_bytes=8 * MIB
        ),
        name="open",
    )(ids, piece, share)


def sum_kernel(groups, shards, once, split, *refs):
    loss = refs[0]
    refs = refs[1:]
    count = once + split
    ones, many, refs = refs[:once], refs[once:count], refs[count:]
    o_ref, start, mid, from_shards, from_groups, send, recv = refs
    place, shard = lax.axis_index("dp"), lax.axis_index("tensor")
    peers = [(place, shard ^ off) for off in range(1, shards)]
    peers += [(place ^ off, shard) for off in range(1, groups)]
    barrier = pltpu.get_barrier_semaphore()
    for peer in peers:
        pl.semaphore_signal(barrier, inc=1, device_id=peer, device_id_type=pl.DeviceIdType.MESH)

    def square(refs):
        total = jnp.zeros((1, 1), F32)
        for ref in refs:
            flat = jnp.sum(ref[...] * ref[...], axis=0, keepdims=True)
            total = total + jnp.sum(flat, axis=1, keepdims=True)
        return total

    first = (place == 0).astype(F32)
    part = square(many) + first * square(ones)
    start[...] = loss[...] + jnp.where(iota((8, LANES), 1) == LANES - 1, part, 0.0)
    pl.semaphore_wait(barrier, len(peers))

    def exchange(source, slots, first, some):
        copies = []
        for i, peer in enumerate(some):
            copy = pltpu.make_async_remote_copy(
                src_ref=source,
                dst_ref=slots.at[i],
                send_sem=send.at[first + i],
                recv_sem=recv.at[first + i],
                device_id=peer,
                device_id_type=pl.DeviceIdType.MESH,
            )
            copy.start()
            copies.append(copy)
        for copy in copies:
            copy.wait()
        total = source[...]
        for i in range(len(some)):
            total = total + slots[i]
        return total

    mid[...] = exchange(start, from_shards, 0, peers[: shards - 1])
    total = exchange(mid, from_groups, shards - 1, peers[shards - 1 :])
    norm = jnp.sqrt(total[0:1, LANES - 1 : LANES])
    factor = jnp.minimum(1.0, CLIP_LIMIT / (norm + 1e-06))
    row = iota((8, LANES), 0)
    o_ref[...] = jnp.where(row == 0, total, jnp.where(row == 1, norm, factor))


def sum_everywhere(loss, ones, many, groups, shards):
    count = groups + shards - 2
    args = (loss, *ones, *many)
    vmem = pl.BlockSpec(memory_space=pltpu.VMEM)
    return pl.pallas_call(
        functools.partial(sum_kernel, groups, shards, len(ones), len(many)),
        out_shape=sds((8, LANES), F32),
        in_specs=[vmem] * len(args),
        out_specs=vmem,
        scratch_shapes=[
            pltpu.VMEM((8, LANES), F32),
            pltpu.VMEM((8, LANES), F32),
            pltpu.VMEM((shards - 1, 8, LANES), F32),
            pltpu.VMEM((groups - 1, 8, LANES), F32),
            pltpu.SemaphoreType.DMA((count,)),
            pltpu.SemaphoreType.DMA((count,)),
        ],
        compiler_params=pltpu.CompilerParams(
            collective_id=1, has_side_effects=True, vmem_limit_bytes=8 * MIB
        ),
        name="sumall",
    )(*args)


def conv_sum(raw, params, rows, lanes):
    total = params[4:5, :] + params[0:1, :] * raw[pl.ds(RIM - 3, rows), lanes]
    for k in range(1, 4):
        total = total + params[k : k + 1, :] * raw[pl.ds(RIM - 3 + k, rows), lanes]
    return total


def front_kernel(normed, wzx, wside, chan, bcp, head, *rest):
    z_out, xr, side, yloc, final, c_out, cum_out, xs_scr = rest
    rows = normed.shape[0] - RIM
    inner = chan.shape[1]
    z_out[...] = nn(normed[RIM:, :], wzx[:, :inner])
    xr[...] = nn(normed[...], wzx[:, inner:])
    side[...] = nn(normed[...], wside[...])
    pre = conv_sum(xr, chan, rows, pl.ds(0, inner))
    xs_scr[...] = pre * sigmoid(pre)
    pre = conv_sum(side, bcp, rows, pl.ds(0, 2 * N))
    bc = (pre * sigmoid(pre)).astype(BF)
    c_out[...] = bc[:, N:]
    dt = softplus(side[RIM:, 2 * N :] + head[0:1, :])
    rate = -dt * jnp.exp(head[1:2, :])
    expand = head_map(inner)
    skip = widen(head[...], expand)[2:3, :]
    lower = (iota((SPAN, SPAN), 0) >= iota((SPAN, SPAN), 1)).astype(F32)
    lower_low = lower.astype(BF)
    first_half = iota((SPAN, LANES), 1) < P_SIZE
    state = None
    base = jnp.zeros((1, LANES), F32)
    for span in range(rows // SPAN):
        here = slice(span * SPAN, (span + 1) * SPAN)
        cum = tri_sum(lower_low, rate[here])
        cum_t = cum.T
        tot = cum[SPAN - 1 : SPAN, :]
        keys = bc[here, :N]
        queries = bc[here, N:]
        scores = nt_dot(queries, keys)
        xs = xs_scr[here, :]
        scaled = xs * widen(dt[here], expand)
        scaled_low = scaled.astype(BF)
        pieces = []
        for pair in range(inner // LANES):
            values = scaled_low[:, pair * LANES : (pair + 1) * LANES]
            both = []
            for h in (2 * pair, 2 * pair + 1):
                gap = cum[:, h : h + 1] - cum_t[h : h + 1, :]
                decay = jnp.exp(jnp.minimum(gap, 0.0)) * lower
                both.append(nn((scores * decay).astype(BF), values))
            pieces.append(jnp.where(first_half, both[0], both[1]))
        y = jnp.concatenate(pieces, axis=1) + skip * xs
        if state is not None:
            y = y + widen(jnp.exp(cum), expand) * nn(queries, state.astype(BF))
        yloc[here, :] = y
        tail = widen(jnp.exp(tot - cum), expand)
        fresh = tn(keys, (scaled * tail).astype(BF))
        if state is not None:
            fresh = fresh + widen(jnp.exp(tot), expand) * state
        state = fresh
        cum_out[here, :] = cum + base
        base = base + tot
    final[0:N, :] = state.astype(BF)
    final[N:, :] = rows3(base, inner)


def mixer_front(normed, wzx, wside, chan, bcp, head):
    rows = normed.shape[0] - RIM
    inner = chan.shape[1]
    return call(
        front_kernel,
        "front",
        [
            sds((rows, inner), F32),
            sds((rows + RIM, inner), F32),
            sds((rows + RIM, 2 * N + LANES), F32),
            sds((rows, inner), F32),
            sds((N + RIM, inner), BF),
            sds((rows, N), BF),
            sds((rows, LANES), F32),
        ],
        (normed, wzx, wside, chan, bcp, head),
        scratch=[pltpu.VMEM((rows, inner), F32)],
        flops=8 * rows * D * inner,
        moved=12 * MIB,
    )


def chain(parts, expand):
    total = None
    past = jnp.zeros((1, LANES), F32)
    for part in parts:
        term = widen(jnp.exp(past), expand) * part[0:N, :].astype(F32)
        total = term if total is None else total + term
        past = past + jnp.sum(part[N:, :LANES].astype(F32), axis=0, keepdims=True)
    return total


def middle_kernel(shards, own, hops, scal, *rest):
    states, rest = rest[:hops], rest[hops:]
    yloc, z_in, c_in, cum, wout, chan = rest[:6]
    y_out, s_out = rest[6:8]
    parts, work = rest[8 : 8 + shards], rest[-1]
    shard = scal[0]
    rows, inner = yloc.shape
    expand = head_map(inner)
    state = chain(states, expand)
    s_out[...] = state
    y = yloc[...] + widen(jnp.exp(cum[...]), expand) * nn(c_in[...], state.astype(BF))
    y_out[...] = y
    z = z_in[...]
    gated = y * (z * sigmoid(z))
    work[:, :D] = nn((gated * chan[5:6, :]).astype(BF), wout[...]).astype(BF)
    work[:, D:] = lanes3(jnp.sum(gated * gated, axis=1, keepdims=True))
    for off in range(shards):
        at = pl.multiple_of((shard ^ off) * own, own)
        parts[off][...] = work[pl.ds(at, own), :]


def mixer_middle(scal, states, yloc, z_in, c_in, cum, wout, chan, shards):
    rows, inner = yloc.shape
    own = rows // shards
    return call(
        functools.partial(middle_kernel, shards, own, len(states)),
        "middle",
        [sds((rows, inner), F32), sds((N, inner), F32)]
        + [sds((own, D + LANES), BF)] * shards,
        (scal, *states, yloc, z_in, c_in, cum, wout, chan),
        smem=(0,),
        scratch=[pltpu.VMEM((rows, D + LANES), BF)],
        flops=2 * rows * D * inner,
        moved=8 * MIB,
    )


def gate_back_kernel(grads, wout, y_in, z_in, c_in, cum, chan, *rest):
    u_out, dy_out, dz_out, state_out, gain_out = rest
    inner = chan.shape[1]
    du = nt_dot(grads[:, :D], wout[...])
    coef = column3(grads[:, D:].astype(F32))
    z = z_in[...]
    y = y_in[...]
    sig = sigmoid(z)
    silu = z * sig
    gated = y * silu
    gain_out[...] = jnp.sum(du * gated, axis=0, keepdims=True)
    gain = chan[5:6, :]
    u_out[...] = (gated * gain).astype(BF)
    dgated = du * gain - gated * coef
    dy = dgated * silu
    dy_out[...] = dy
    dz_out[...] = (dgated * y * (sig * (1.0 + z * (1.0 - sig)))).astype(BF)
    grown = widen(jnp.exp(cum[...]), head_map(inner))
    state_out[0:N, :] = tn(c_in[...], (dy * grown).astype(BF)).astype(BF)
    rows = dy.shape[0]
    state_out[N:, :] = rows3(cum[rows - 1 : rows, :], inner)


def gate_back(grads, wout, y, z_in, c_in, cum, chan):
    rows, inner = y.shape
    return call(
        gate_back_kernel,
        "gateback",
        [
            sds((rows, inner), BF),
            sds((rows, inner), F32),
            sds((rows, inner), BF),
            sds((N + RIM, inner), BF),
            sds((1, inner), F32),
        ],
        (grads, wout, y, z_in, c_in, cum, chan),
        flops=2 * rows * D * inner,
        moved=10 * MIB,
    )


def silu_slope(pre):
    sig = sigmoid(pre)
    return sig * (1.0 + pre * (1.0 - sig))


def conv_back(ds_scr, raw, params, rows, lanes, width, low_out, out_lanes):
    ext = rows + RIM
    total = params[0:1, :] * ds_scr[pl.ds(3, ext), :]
    for k in range(1, 4):
        total = total + params[k : k + 1, :] * ds_scr[pl.ds(3 - k, ext), :]
    low_out[:, out_lanes] = total.astype(BF)
    ds = ds_scr[pl.ds(RIM, rows), :]
    grads = [
        jnp.sum(ds * raw[pl.ds(RIM - 3 + k, rows), lanes], axis=0, keepdims=True) for k in range(4)
    ]
    grads.append(jnp.sum(ds, axis=0, keepdims=True))
    grads.append(jnp.zeros((3, width), F32))
    return jnp.concatenate(grads, axis=0)


def within_kernel(s_in, xr, side, dy_in, chan, bcp, head, *outs):
    xs_out, bc_out, cum_out, starts_out, dscaled_out, dbc_out = outs
    rows, inner = dy_in.shape
    expand = head_map(inner)
    pre_x = conv_sum(xr, chan, rows, pl.ds(0, inner))
    xs_out[...] = pre_x * sigmoid(pre_x)
    pre_bc = conv_sum(side, bcp, rows, pl.ds(0, 2 * N))
    bc = (pre_bc * sigmoid(pre_bc)).astype(BF)
    bc_out[...] = bc
    dt = softplus(side[RIM:, 2 * N :] + head[0:1, :])
    rate = -dt * jnp.exp(head[1:2, :])
    lower_low = (iota((SPAN, SPAN), 0) >= iota((SPAN, SPAN), 1)).astype(F32).astype(BF)
    upper = (iota((SPAN, SPAN), 0) <= iota((SPAN, SPAN), 1)).astype(F32)
    first_half = iota((SPAN, LANES), 1) < P_SIZE
    spans = rows // SPAN
    start = s_in[...]
    for span in range(spans):
        here = slice(span * SPAN, (span + 1) * SPAN)
        cum = tri_sum(lower_low, rate[here])
        cum_out[here, :] = cum
        cum_t = cum.T
        keys = bc[here, :N]
        queries = bc[here, N:]
        xs = xs_out[here, :]
        starts_out[span] = start
        start_low = start.astype(BF)
        if span + 1 < spans:
            tot = cum[SPAN - 1 : SPAN, :]
            scale = widen(dt[here] * jnp.exp(tot - cum), expand)
            fresh = tn(keys, (xs * scale).astype(BF))
            start = widen(jnp.exp(tot), expand) * start + fresh
        scores_t = nt_dot(keys, queries)
        dy = dy_in[here, :]
        dy_low = dy.astype(BF)
        scaled_low = (xs * widen(dt[here], expand)).astype(BF)
        dscores_t = jnp.zeros((SPAN, SPAN), F32)
        for pair in range(inner // LANES):
            lanes = slice(pair * LANES, (pair + 1) * LANES)
            values = scaled_low[:, lanes]
            dpair = dy_low[:, lanes]
            both = []
            for h in (2 * pair, 2 * pair + 1):
                gap = cum_t[h : h + 1, :] - cum[:, h : h + 1]
                decay = jnp.exp(jnp.minimum(gap, 0.0)) * upper
                mine = first_half if h % 2 == 0 else jnp.logical_not(first_half)
                outer = nt_dot(jnp.where(mine, values, jnp.zeros_like(values)), dpair)
                dscores_t = dscores_t + outer * decay
                both.append(nn((scores_t * decay).astype(BF), dpair))
            dscaled_out[here, lanes] = jnp.where(first_half, both[0], both[1])
        dscores_low = dscores_t.astype(BF)
        dy_grown = (dy * widen(jnp.exp(cum), expand)).astype(BF)
        dbc_out[here, :N] = nn(dscores_low, queries)
        dbc_out[here, N:] = tn(dscores_low, keys) + nt_dot(dy_grown, start_low)


def mixer_within(s_in, xr, side, dy, chan, bcp, head):
    rows, inner = dy.shape
    return call(
        within_kernel,
        "within",
        [
            sds((rows, inner), F32),
            sds((rows, 2 * N), BF),
            sds((rows, LANES), F32),
            sds((rows // SPAN, N, inner), F32),
            sds((rows, inner), F32),
            sds((rows, 2 * N), F32),
        ],
        (s_in, xr, side, dy, chan, bcp, head),
        flops=8 * rows * D * inner,
        moved=16 * MIB,
    )


def back_kernel(shards, own, hops, scal, *rest):
    states, rest = rest[:hops], rest[hops:]
    xs_in, bc_in, cum_in, starts, dscaled_in, dbc_in, rest = *rest[:6], rest[6:]
    xr, side, dy_in, dz_in, y_in, wzx, wside, chan, bcp, head = rest[:10]
    normed, gain = rest[10:12]
    dzx, dside, chan_out, bcp_out, head_out, rim_out, gain_out = rest[12:19]
    parts, rest = rest[19 : 19 + shards], rest[19 + shards :]
    dsx, dsbc, work = rest
    shard = scal[0]
    rows, inner = dy_in.shape
    expand = head_map(inner)
    raw_dt = side[RIM:, 2 * N :] + head[0:1, :]
    dt = softplus(raw_dt)
    grow = jnp.exp(head[1:2, :])
    rate = -dt * grow
    skip = widen(head[...], expand)[2:3, :]
    upper_low = (iota((SPAN, SPAN), 0) <= iota((SPAN, SPAN), 1)).astype(F32).astype(BF)
    spans = rows // SPAN
    dstate = chain(states, expand)
    dsx[0:RIM, :] = jnp.zeros((RIM, inner), F32)
    dsx[RIM + rows :, :] = jnp.zeros((RIM, inner), F32)
    dsbc[0:RIM, :] = jnp.zeros((RIM, 2 * N), F32)
    dsbc[RIM + rows :, :] = jnp.zeros((RIM, 2 * N), F32)
    dside[0:RIM, 2 * N :] = jnp.zeros((RIM, LANES), BF)
    dzx[0:RIM, :inner] = jnp.zeros((RIM, inner), BF)
    dzx[RIM:, :inner] = dz_in[...]
    dbias = jnp.zeros((1, LANES), F32)
    dgrow = jnp.zeros((1, LANES), F32)
    dskip = jnp.zeros((1, LANES), F32)
    for span in reversed(range(spans)):
        here = slice(span * SPAN, (span + 1) * SPAN)
        there = slice(RIM + span * SPAN, RIM + (span + 1) * SPAN)
        cum = cum_in[here, :]
        tot = cum[SPAN - 1 : SPAN, :]
        keys = bc_in[here, :N]
        queries = bc_in[here, N:]
        xs = xs_in[here, :]
        dy = dy_in[here, :]
        dy_low = dy.astype(BF)
        dt_wide = widen(dt[here], expand)
        scaled = xs * dt_wide
        scaled_low = scaled.astype(BF)
        tail = widen(jnp.exp(tot - cum), expand)
        dstate_low = dstate.astype(BF)
        through = tail * nn(keys, dstate_low)
        dscaled = dscaled_in[here, :] + through
        plain = y_in[here, :] - skip * xs
        held = scaled_low.astype(F32)
        dcum = narrow(dy_low.astype(F32) * plain - held * dscaled, expand)
        tot_wide = widen(jnp.exp(tot), expand)
        over = jnp.sum(held * through, axis=0, keepdims=True) + jnp.sum(
            tot_wide * dstate * starts[span], axis=0, keepdims=True
        )
        dtot = narrow(jnp.broadcast_to(over, (8, inner)), expand)[0:1, :]
        drate = tri_sum(upper_low, dcum) + dtot
        ddt = narrow(dscaled * xs, expand) - drate * grow
        dgrow = dgrow + jnp.sum(drate * rate[here], axis=0, keepdims=True)
        draw = ddt * sigmoid(raw_dt[here])
        dbias = dbias + jnp.sum(draw, axis=0, keepdims=True)
        dside[there, 2 * N :] = draw.astype(BF)
        over = jnp.sum(dy * xs, axis=0, keepdims=True)
        dskip = dskip + narrow(jnp.broadcast_to(over, (8, inner)), expand)[0:1, :]
        dsx[there, :] = dscaled * dt_wide + skip * dy
        dsbc[there, :N] = dbc_in[here, :N] + nt_dot((scaled * tail).astype(BF), dstate_low)
        dsbc[there, N:] = dbc_in[here, N:]
        if span > 0:
            grown = widen(jnp.exp(cum), expand)
            dstate = tot_wide * dstate + tn(queries, (dy * grown).astype(BF))
    body = pl.ds(RIM, rows)
    pre_x = conv_sum(xr, chan, rows, pl.ds(0, inner))
    dsx[body, :] = dsx[body, :] * silu_slope(pre_x)
    pre_bc = conv_sum(side, bcp, rows, pl.ds(0, 2 * N))
    dsbc[body, :] = dsbc[body, :] * silu_slope(pre_bc)
    chan_out[...] = conv_back(
        dsx, xr, chan, rows, pl.ds(0, inner), inner, dzx, pl.ds(inner, inner)
    )
    bcp_out[...] = conv_back(dsbc, side, bcp, rows, pl.ds(0, 2 * N), 2 * N, dside, pl.ds(0, 2 * N))
    head_out[...] = jnp.concatenate([dbias, dgrow, dskip, jnp.zeros((5, LANES), F32)], axis=0)
    dnormed = nt_dot(dzx[...], wzx[...]) + nt_dot(dside[...], wside[...])
    work[...] = dnormed.astype(BF)
    gain_out[...] = jnp.sum(dnormed * normed[...].astype(F32), axis=0, keepdims=True) / gain[...]
    rim_out[...] = work[0:RIM, :]
    for off in range(shards):
        at = pl.multiple_of(RIM + (shard ^ off) * own, RIM)
        parts[off][...] = work[pl.ds(at, own), :]


def mixer_back(
    scal, states, inside, xr, side, dy, dz, y, wzx, wside, chan, bcp, head, normed, gain, shards
):
    rows, inner = dy.shape
    own = rows // shards
    ext = rows + RIM
    return call(
        functools.partial(back_kernel, shards, own, len(states)),
        "back",
        [
            sds((ext, 2 * inner), BF),
            sds((ext, 2 * N + LANES), BF),
            sds((8, inner), F32),
            sds((8, 2 * N), F32),
            sds((8, LANES), F32),
            sds((RIM, D), BF),
            sds((1, D), F32),
        ]
        + [sds((own, D), BF)] * shards,
        (scal, *states, *inside, xr, side, dy, dz, y, wzx, wside, chan, bcp, head, normed, gain),
        smem=(0,),
        scratch=[
            pltpu.VMEM((ext + RIM, inner), F32),
            pltpu.VMEM((ext + RIM, 2 * N), F32),
            pltpu.VMEM((ext, D), BF),
        ],
        flops=8 * rows * D * inner,
        moved=16 * MIB,
    )


def logits_kernel(vrows, label, table, normed, *rest):
    p_out, tops, stats, rows_scr, top, total, target, plain = rest
    step = pl.program_id(0)
    rows = normed.shape[0] - RIM

    @pl.when(step == 0)
    def _():
        rows_scr[...] = normed[RIM:, :].T
        top[...] = jnp.full((1, rows), -1e30, F32)
        total[...] = jnp.zeros((1, rows), F32)
        target[...] = jnp.zeros((1, rows), F32)
        plain[...] = jnp.zeros((1, rows), F32)

    highest, summed, hit, whole = top[...], total[...], target[...], plain[...]
    line = 2 * iota((PART, rows), 0)
    for half in range(2):
        for part_at in range(PAIRS // PART):
            first = step * PAIRS + part_at * PART
            here = slice(part_at * PART, (part_at + 1) * PART)
            padding = jnp.where(first + iota((PART, LANES), 0) < vrows, 0.0, -1e30)
            padding = jnp.concatenate([padding] * (rows // LANES), axis=1)
            raw = nn(table[here, half * D : (half + 1) * D], rows_scr[...])
            shown = raw + padding
            before = highest
            highest = jnp.maximum(before, jnp.max(shown, axis=0, keepdims=True))
            part = jnp.exp(shown - highest)
            summed = summed * jnp.exp(before - highest) + jnp.sum(part, axis=0, keepdims=True)
            wanted = label[...] - 2 * first - half
            hit = hit + jnp.sum(jnp.where(line == wanted, raw, 0.0), axis=0, keepdims=True)
            whole = whole + jnp.sum(raw, axis=0, keepdims=True)
            p_out[half, here, :] = part.astype(BF)
            at = 8 * (half * (PAIRS // PART) + part_at)
            tops[0, at : at + 8, :] = jnp.broadcast_to(highest, (8, rows))
    top[...] = highest
    total[...] = summed
    target[...] = hit
    plain[...] = whole
    stats[...] = jnp.concatenate([highest, summed, hit, whole, jnp.zeros((4, rows), F32)], axis=0)


def vocab_logits(label, table, normed, vrows):
    rows = normed.shape[0] - RIM
    padded = table.shape[0]
    steps = padded // PAIRS
    whole = lambda i: (0, 0)
    return pl.pallas_call(
        functools.partial(logits_kernel, vrows),
        grid=(steps,),
        out_shape=[
            sds((2, padded, rows), BF),
            sds((steps, 16 * (PAIRS // PART), rows), F32),
            sds((8, rows), F32),
        ],
        in_specs=[
            pl.BlockSpec((1, rows), whole),
            pl.BlockSpec((PAIRS, 2 * D), lambda i: (i, 0)),
            pl.BlockSpec(normed.shape, whole),
        ],
        out_specs=[
            pl.BlockSpec((2, PAIRS, rows), lambda i: (0, i, 0)),
            pl.BlockSpec((1, 16 * (PAIRS // PART), rows), lambda i: (i, 0, 0)),
            pl.BlockSpec((8, rows), whole),
        ],
        scratch_shapes=[pltpu.VMEM((D, rows), BF)] + [pltpu.VMEM((1, rows), F32)] * 4,
        compiler_params=pltpu.CompilerParams(
            dimension_semantics=("arbitrary",), vmem_limit_bytes=56 * MIB
        ),
        cost_estimate=pl.CostEstimate(
            flops=4 * rows * D * padded, bytes_accessed=40 * MIB, transcendentals=2 * rows * padded
        ),
        name="logits",
    )(label, table, normed)


def logit_grads(step, label, scale, weight, p_in):
    pairs, rows = p_in.shape[1:]
    line = 2 * iota((PART, rows), 0)
    usual = (SMOOTHING / V) * weight[...]
    special = (1.0 - SMOOTHING + SMOOTHING / V) * weight[...]
    for half in range(2):
        pieces = []
        for part_at in range(pairs // PART):
            wanted = label[...] - 2 * (step * pairs + part_at * PART) - half
            share = jnp.where(line == wanted, special, usual)
            at = 8 * (half * (pairs // PART) + part_at)
            grown = p_in[half, part_at * PART : (part_at + 1) * PART, :].astype(F32)
            pieces.append((grown * scale[0, at : at + 1, :] - share).astype(BF))
        yield half, jnp.concatenate(pieces, axis=0)


def rows_kernel(shards, own, scal, label, scale, weight, p_in, table, *rest):
    parts, acc = rest[:shards], rest[-1]
    step = pl.program_id(0)

    @pl.when(step == 0)
    def _():
        acc[...] = jnp.zeros_like(acc)

    for half, q in logit_grads(step, label, scale, weight, p_in):
        acc[...] += tn(q, table[:, half * D : (half + 1) * D])

    @pl.when(step == pl.num_programs(0) - 1)
    def _():
        for off in range(shards):
            at = pl.ds(pl.multiple_of((scal[0] ^ off) * own, own), own)
            parts[off][...] = acc[at, :].astype(BF)


def vocab_specs(rows):
    whole = lambda i: (0, 0)
    return [
        pl.BlockSpec((1, rows), whole),
        pl.BlockSpec((1, 16 * (PAIRS // PART), rows), lambda i: (i, 0, 0)),
        pl.BlockSpec((1, rows), whole),
        pl.BlockSpec((2, PAIRS, rows), lambda i: (0, i, 0)),
    ]


def vocab_rows(scal, label, scale, weight, p_in, table, shards):
    _, padded, rows = p_in.shape
    own = rows // shards
    whole = lambda i: (0, 0)
    return pl.pallas_call(
        functools.partial(rows_kernel, shards, own),
        grid=(padded // PAIRS,),
        out_shape=[sds((own, D), BF)] * shards,
        in_specs=[pl.BlockSpec(memory_space=pltpu.SMEM)]
        + vocab_specs(rows)
        + [pl.BlockSpec((PAIRS, 2 * D), lambda i: (i, 0))],
        out_specs=[pl.BlockSpec((own, D), whole)] * shards,
        scratch_shapes=[pltpu.VMEM((rows, D), F32)],
        compiler_params=pltpu.CompilerParams(
            dimension_semantics=("arbitrary",), vmem_limit_bytes=56 * MIB
        ),
        cost_estimate=pl.CostEstimate(
            flops=4 * rows * D * padded, bytes_accessed=40 * MIB, transcendentals=0
        ),
        name="rowgrads",
    )(scal, label, scale, weight, p_in, table)


def table_kernel(label, scale, weight, p_in, normed, out, rows_scr):
    step = pl.program_id(0)

    @pl.when(step == 0)
    def _():
        rows_scr[...] = normed[RIM:, :]

    for half, q in logit_grads(step, label, scale, weight, p_in):
        out[:, half * D : (half + 1) * D] = nn(q, rows_scr[...]).astype(BF)


def vocab_table_grad(label, scale, weight, p_in, normed):
    _, padded, rows = p_in.shape
    whole = lambda i: (0, 0)
    return pl.pallas_call(
        table_kernel,
        grid=(padded // PAIRS,),
        out_shape=sds((padded, 2 * D), BF),
        in_specs=vocab_specs(rows) + [pl.BlockSpec(normed.shape, whole)],
        out_specs=pl.BlockSpec((PAIRS, 2 * D), lambda i: (i, 0)),
        scratch_shapes=[pltpu.VMEM((rows, D), BF)],
        compiler_params=pltpu.CompilerParams(
            dimension_semantics=("arbitrary",), vmem_limit_bytes=56 * MIB
        ),
        cost_estimate=pl.CostEstimate(
            flops=4 * rows * D * padded, bytes_accessed=40 * MIB, transcendentals=0
        ),
        name="tablegrads",
    )(label, scale, weight, p_in, normed)


def adam_update(weight_in, gradient, moment_one, moment_two, factor, fix_one, fix_two, decay_rate):
    gradient = gradient * factor
    one_next = BETA_FIRST * moment_one + (1.0 - BETA_FIRST) * gradient
    two_next = BETA_SECOND * moment_two + (1.0 - BETA_SECOND) * gradient * gradient
    direction = one_next / fix_one / (jnp.sqrt(two_next / fix_two) + ADAM_EPS)
    return (weight_in - LEARN_RATE * (direction + decay_rate * weight_in), one_next, two_next)


def turn_kernel(share, bases, turned, root):
    count = bases.shape[0]
    total = jnp.zeros((1, BLK), F32)

    def turn(at, total):
        grad = share[pl.ds(pl.multiple_of(at * BLK, BLK), BLK), :].astype(F32)
        half_turn = tn(bases[at, 0], grad, HIGHEST)
        turned[at] = nn(half_turn, bases[at, 1], HIGHEST)
        return total + jnp.sum(grad * grad, axis=0, keepdims=True)

    for at in range(count):
        total = turn(at, total)
    root[...] = jnp.sqrt(total)


def turn_tiles(share, bases):
    count = bases.shape[0]
    return call(
        turn_kernel,
        "turn",
        [sds((count, BLK, BLK), F32), sds((1, BLK), F32)],
        (share, bases),
        moved=6 * MIB,
    )


def last_kernel(small, fixes, sums, *refs):
    tiles, turned, bases, tile_one, tile_two = refs[:5]
    little, refs = refs[5 : 5 + 4 * small], refs[5 + 4 * small :]
    tiles_out, copy_out, tile_one_out, tile_two_out = refs[:4]
    little_out = refs[4:]
    factor, fix_one, fix_two = sums[2:3, 0:1], fixes[0], fixes[1]
    for at in range(tiles.shape[0]):
        rotated = turned[at] * factor
        one_next = BETA_FIRST * tile_one[at] + (1.0 - BETA_FIRST) * rotated
        two_next = BETA_SECOND * tile_two[at] + (1.0 - BETA_SECOND) * rotated * rotated
        direction = one_next / fix_one / (jnp.sqrt(two_next / fix_two) + ADAM_EPS)
        back_half = nn(bases[at, 0], direction, HIGHEST)
        back = nt_dot(back_half, bases[at, 1], HIGHEST)
        after = tiles[at] - LEARN_RATE * (back + WEIGHT_DECAY * tiles[at])
        tiles_out[at] = after
        copy_out[at] = after.astype(BF)
        tile_one_out[at] = one_next
        tile_two_out[at] = two_next

    @pl.when(pl.program_id(0) == 0)
    def _():
        for which in range(small):
            before, gradient, first, second = (ref[...] for ref in little[4 * which : 4 * which + 4])
            results = adam_update(
                before,
                gradient,
                first,
                second,
                factor,
                fix_one,
                fix_two,
                WEIGHT_DECAY if which == 0 else 0.0,
            )
            outs = little_out[3 * which : 3 * which + 3]
            outs[0][...] = results[0] if which == 0 else results[0] - before
            outs[1][...], outs[2][...] = results[1], results[2]


def last_update(fixes, sums, tiles, turned, bases, tile_one, tile_two, little):
    count = tiles.shape[0]
    each = 6 if count % 6 == 0 else 2
    tile_spec = pl.BlockSpec((each, BLK, BLK), lambda i: (i, 0, 0))
    base_spec = pl.BlockSpec((each, 2, BLK, BLK), lambda i: (i, 0, 0, 0))
    whole = [
        pl.BlockSpec(x.shape, lambda i, rank=x.ndim: (0,) * rank) for group in little for x in group
    ]
    return pl.pallas_call(
        functools.partial(last_kernel, len(little)),
        grid=(count // each,),
        out_shape=[sds(tiles.shape, F32), sds(tiles.shape, BF), sds(tiles.shape, F32), sds(tiles.shape, F32)]
        + [sds(group[0].shape, F32) for group in little for _ in range(3)],
        in_specs=[
            pl.BlockSpec(memory_space=pltpu.SMEM),
            pl.BlockSpec(sums.shape, lambda i: (0, 0)),
        ]
        + [tile_spec, tile_spec, base_spec, tile_spec, tile_spec]
        + whole,
        out_specs=[tile_spec] * 4
        + [spec for which in range(len(little)) for spec in whole[4 * which : 4 * which + 3]],
        compiler_params=pltpu.CompilerParams(
            dimension_semantics=("arbitrary",), vmem_limit_bytes=48 * MIB
        ),
        cost_estimate=pl.CostEstimate(
            flops=24 * count * BLK * BLK * BLK, bytes_accessed=16 * MIB, transcendentals=0
        ),
        name="update",
    )(
        fixes,
        sums,
        tiles,
        turned,
        bases,
        tile_one,
        tile_two,
        *[x for group in little for x in group],
    )


def total_over(x, axis):
    out = x
    for off in range(1, lax.axis_size(axis)):
        out = out + swap(x, axis, off)
    return out


def shards(
    token_ids,
    labels,
    seq_lengths,
    micro_batch,
    step_count,
    block_slot,
    vocab_table,
    vocab_first,
    vocab_second,
    layer_blocks,
    block_bases,
    block_first,
    block_second,
    side_proj,
    side_first,
    side_second,
    shared_params,
    shared_first,
    shared_second,
    channel_params,
    channel_first,
    channel_second,
    head_params,
    head_first,
    head_second,
):
    nt = lax.axis_size("tensor")
    nd = lax.axis_size("dp")
    shard = lax.axis_index("tensor")
    place = lax.axis_index("dp")
    seqs = token_ids.shape[0]
    length = token_ids.shape[1] * nd
    chunks = nd // seqs
    rows = seqs * length // nd
    own = rows // nt
    vrows = vocab_table.shape[0]
    padded = -(-vrows // PAIRS) * PAIRS
    half = nd // 2
    inner = channel_params.shape[2]
    heads = head_params.shape[2]
    tiles = block_slot.shape[1]
    zx_count = D * 2 * inner // (BLK * BLK)
    per_layer = 3 * D * inner // (BLK * BLK)
    stride = D + 10 * N
    both = ("dp", "tensor")
    side_rows = side_proj.shape[1]
    share_size = shared_params.shape[0]
    share_pad = -(-share_size // 2048) * 2048

    piece = jnp.pad(side_proj.astype(BF), ((0, 0), (0, 0), (0, LANES - H))).reshape(-1, LANES)
    share = jnp.pad(shared_params.astype(BF), (0, share_pad - share_size)).reshape(-1, LANES)
    side_part = piece.shape[0]
    piece_rows = side_part + share.shape[0]
    ids = jnp.pad(jnp.concatenate([token_ids, labels], axis=0), ((0, 8 - 2 * seqs), (0, 0)))
    ids_all, pieces, shared_all = open_exchange(ids, piece, share, nd, nt)
    shared_full = shared_all.reshape(nd * nt, share_pad)[:, :share_size].reshape(-1).astype(F32)
    ids_all = ids_all.transpose(1, 0, 2).reshape(8, length)
    all_ids = ids_all[:seqs].reshape(-1)
    local_row = all_ids // 2 - shard * vrows
    held = (local_row >= 0) & (local_row < vrows) & (all_ids % 2 == place // half)
    scal = jnp.stack([place, shard]).astype(jnp.int32)
    scal_shard = shard.astype(jnp.int32).reshape(1)
    code = jnp.concatenate([jnp.where(held, local_row, 0), jnp.zeros((8,), jnp.int32)])
    listed, count = list_held(held, nd * rows)
    own_tiles = layer_blocks.shape[2]
    gathered = lax.all_gather(
        jnp.concatenate(
            [layer_blocks.astype(BF).reshape(own_tiles * BLK, BLK), pieces.reshape(-1, LANES)], axis=0
        ),
        "dp",
        axis=0,
        tiled=False,
    )
    *parts, table_low = gather_rows(
        scal, code, listed, count, vocab_table, nd, rows, padded
    )
    residual, normed = forward_rows(
        parts, None, shared_full[None, :D], nd, chunks, True, 4, nt
    )
    table_low, normed = lax.optimization_barrier((table_low, normed))
    gathered, normed = lax.optimization_barrier((gathered, normed))
    side_full = (
        gathered[:, own_tiles * BLK :]
        .reshape(nd, nt, L, side_rows, 2 * N + LANES)
        .transpose(2, 0, 1, 3, 4)
        .reshape(L, D, 2 * N + LANES)
    )
    table_all = lax.all_gather(table_low, "dp", axis=1, tiled=True)

    def layer_mats(layer_index):
        dt_part = lax.dynamic_slice_in_dim(
            side_full[layer_index], 2 * N + shard * heads, heads, 1
        )
        side_here = jnp.concatenate(
            [
                side_full[layer_index][:, : 2 * N],
                jnp.pad(dt_part, ((0, 0), (0, LANES - heads))),
            ],
            axis=1,
        )
        base = layer_index * stride
        gain = shared_full[base : base + D]
        taps = shared_full[base + D : base + D + 8 * N].reshape(4, 2 * N)
        bias = shared_full[base + D + 8 * N : base + stride].reshape(1, 2 * N)
        bcp = jnp.concatenate([taps, bias, jnp.zeros((3, 2 * N), F32)], axis=0)
        chan = jnp.pad(channel_params[layer_index], ((0, 2), (0, 0)))
        head = jnp.pad(head_params[layer_index], ((0, 5), (0, LANES - heads)))
        return [None, None, side_here, gain, bcp, chan, head]

    def hop(x, distance):
        pairs = [
            (k, k + distance)
            for k in range(nd)
            if 0 <= k % chunks + distance < chunks
        ]
        return lax.ppermute(x, "dp", pairs)

    def returned(parts):
        return [parts[0]] + [swap(parts[off], "tensor", off) for off in range(1, nt)]

    hops = range(1, chunks)
    mats = [layer_mats(layer_index) for layer_index in range(L)]
    final_gain = shared_full[L * stride :][None, :]
    gains = [mats[layer_index][3][None, :] for layer_index in range(L)] + [final_gain]
    saved = []
    tiles_now = gathered
    for layer_index in range(L):
        mats[layer_index][:2] = place_tiles(
            block_slot, tiles_now, own_tiles, inner, zx_count, per_layer, layer_index
        )
        wzx, wout, wside, gain, bcp, chan, head = mats[layer_index]
        z, xr, side, yloc, final, c_out, cum = mixer_front(normed, wzx, wside, chan, bcp, head)
        final, tiles_now = lax.optimization_barrier((final, tiles_now))
        states = [hop(final, k) for k in hops]
        result = mixer_middle(scal_shard, states, yloc, z, c_out, cum, wout, chan, nt)
        y, s_in = result[:2]
        below = normed
        before = residual
        inside = layer_index + 1 < L
        residual, branch, factor, normed = forward_rows(
            result[2:], before, gains[layer_index + 1], nd, chunks, inside, 5 + layer_index
        )
        saved.append((before, below, z, xr, side, c_out, cum, y, s_in, factor, branch))

    member = micro_batch[:, None] == jnp.arange(MB, dtype=jnp.int32)[None, :]
    batch_tokens = jnp.sum(jnp.where(member, seq_lengths[:, None], 0), axis=0).astype(F32)
    seq_weight = 1.0 / (MB * jnp.sum(jnp.where(member, batch_tokens[None, :], 0.0), axis=1))
    row_at = place * rows + jnp.arange(rows, dtype=jnp.int32)
    my_seq = place // chunks
    weight = jnp.where(row_at % length < seq_lengths[my_seq], seq_weight[my_seq], 0.0)
    all_labels = ids_all[seqs : 2 * seqs].reshape(-1)
    label = (lax.dynamic_slice_in_dim(all_labels, place * rows, rows) - 2 * shard * vrows).reshape(
        1, rows
    )
    row_weight = weight.reshape(1, rows)
    p_low, tops, stats = vocab_logits(label, table_all, normed, vrows)
    scale, seq_part = merge_stats(stats, tops, row_weight, nt, chunks)
    sent = returned(vocab_rows(scal_shard, label, scale, row_weight, p_low, table_all, nt))
    table_grad = vocab_table_grad(label, scale, row_weight, p_low, normed)
    sent, table_grad = lax.optimization_barrier((sent, table_grad))
    table_share = lax.psum_scatter(table_grad, "dp", scatter_dimension=1, tiled=True)
    grad_res, payload, grad_final_gain = backward_rows(
        sent, None, residual, final_gain, None, saved[L - 1][10], saved[L - 1][9], nd, chunks, 10
    )

    block_pieces = [None] * (2 * L)
    side_pieces = [None] * L
    channel_pieces = [None] * L
    head_pieces = [None] * L
    shared_pieces = [None] * L
    for layer_index in reversed(range(L)):
        wzx, wout, wside, gain, bcp, chan, head = mats[layer_index]
        residual_in, normed, z, xr, side, c_out, cum, y, s_in, factor, branch = saved[layer_index]
        u_low, dy, dz, dstate, gain_grad = gate_back(payload, wout, y, z, c_out, cum, chan)
        states = [hop(dstate, -k) for k in hops]
        grad_out_w = tn(u_low, payload)
        inside = mixer_within(s_in, xr, side, dy, chan, bcp, head)
        result = mixer_back(
            scal_shard,
            states,
            inside,
            xr,
            side,
            dy,
            dz,
            y,
            wzx,
            wside,
            chan,
            bcp,
            head,
            normed,
            gains[layer_index],
            nt,
        )
        dzx, dside, chan_grad, bcp_grad, head_grad, rim_grad, grad_gain_in = result[:7]
        parts_out = result[7:]
        grad_zx_w = tn(normed, dzx)
        grad_side_w = tn(normed, dside)
        block_pieces[2 * layer_index] = grad_zx_w.astype(BF)
        block_pieces[2 * layer_index + 1] = grad_out_w.astype(BF)
        side_pieces[layer_index] = grad_side_w
        shared_pieces[layer_index] = jnp.concatenate(
            [grad_gain_in[0], bcp_grad[:4].reshape(-1), bcp_grad[4]]
        )
        channel_pieces[layer_index] = jnp.concatenate([chan_grad[:5], gain_grad], axis=0)
        head_pieces[layer_index] = head_grad[:3, :heads]
        if layer_index == 0:
            shared_grads = jnp.concatenate(shared_pieces + [grad_final_gain[0]]).astype(BF)
            shared_grads = jnp.pad(
                shared_grads.reshape(nd * nt, share_size), ((0, 0), (0, share_pad - share_size))
            ).reshape(nd, nt * share_pad // LANES, LANES)
            lines = jnp.concatenate(
                [
                    jnp.stack(channel_pieces).reshape(-1, LANES),
                    jnp.pad(jnp.stack(head_pieces).reshape(-1), (0, LANES - L * 3 * heads)).reshape(
                        1, LANES
                    ),
                ],
                axis=0,
            ).astype(BF)
            line_count = lines.shape[0]
            line_rows = -(-line_count // RIM) * RIM
            lines = jnp.pad(lines, ((0, line_rows - line_count), (0, 0)))
            tile_grads = pack_tiles(
                scal_shard,
                block_slot,
                block_pieces,
                side_pieces,
                shared_grads,
                lines,
                own_tiles,
                per_layer,
                nt,
                heads,
            )
            tile_grads, table_share, parts_out, rim_grad = lax.optimization_barrier(
                (tile_grads, table_share, parts_out, rim_grad)
            )
            block_share = lax.psum_scatter(tile_grads, "dp", scatter_dimension=0, tiled=True)[0]
        if layer_index:
            grad_res, payload = backward_rows(
                parts_out,
                rim_grad,
                residual_in,
                gains[layer_index],
                grad_res,
                saved[layer_index - 1][10],
                saved[layer_index - 1][9],
                nd,
                chunks,
                10 + layer_index,
            )
        else:
            embed = finish_rows(
                parts_out, rim_grad, residual_in, gains[0], grad_res, nd, chunks
            )

    side_count = nt * side_part
    small_share = jnp.concatenate(
        [
            block_share[own_tiles * BLK : own_tiles * BLK + side_count].reshape(nt, side_part, LANES),
            block_share[own_tiles * BLK + side_count : own_tiles * BLK + nt * piece_rows].reshape(
                nt, piece_rows - side_part, LANES
            ),
        ],
        axis=1,
    )
    mine = jnp.zeros((piece_rows, LANES), F32)
    for off in range(nt):
        piece = lax.dynamic_index_in_dim(small_share, shard ^ off, 0, False)
        mine = mine + (piece if off == 0 else swap(piece, "tensor", off)).astype(F32)
    side_share = (
        mine[:side_part]
        .reshape(L, 2 * N // LANES + 1, side_rows, LANES)
        .transpose(0, 2, 1, 3)
        .reshape(L * side_rows, 2 * N + LANES)[:, : 2 * N + H]
    )
    shared_share = mine[side_part:].reshape(1, -1)[:, :share_size]
    lines = block_share[own_tiles * BLK + nt * piece_rows :].astype(F32)
    channel_sum = lines[: line_count - 1].reshape(L * 6, inner)
    head_sum = lines[line_count - 1, : L * 3 * heads].reshape(L * 3, heads)
    rotated, tile_root = turn_tiles(block_share, block_bases.reshape(own_tiles, 2, BLK, BLK))
    grad_table, table_root = add_rows(scal, code, listed, count, table_share, embed, vrows)
    sums = sum_everywhere(
        seq_part,
        [channel_sum, head_sum],
        [table_root, tile_root, side_share, shared_share],
        nd,
        nt,
    )
    seq_loss = sums[0, :seqs]
    clip_norm = sums[1, 0]
    steps_done = step_count[0].astype(F32)
    fix_one = 1.0 - jnp.power(BETA_FIRST, steps_done)
    fix_two = 1.0 - jnp.power(BETA_SECOND, steps_done)
    tile_shape = layer_blocks.shape[2:]
    flat = lambda x: x.reshape((-1, x.shape[-1]))
    little = [
        [flat(side_proj), side_share, flat(side_first), flat(side_second)],
        [flat(shared_params), shared_share, flat(shared_first), flat(shared_second)],
        [
            x.reshape(channel_params.shape).transpose(1, 0, 2)
            for x in (channel_params, channel_sum, channel_first, channel_second)
        ],
        [
            x.reshape(head_params.shape).transpose(1, 0, 2)
            for x in (head_params, head_sum, head_first, head_second)
        ],
    ]
    updated = last_update(
        jnp.stack([fix_one, fix_two]),
        sums,
        layer_blocks.reshape(tile_shape),
        rotated,
        block_bases.reshape((own_tiles, 2, BLK, BLK)),
        block_first.reshape(tile_shape),
        block_second.reshape(tile_shape),
        little,
    )
    table_out = adam_update(
        vocab_table,
        grad_table.astype(F32),
        vocab_first,
        vocab_second,
        sums[2, 0],
        fix_one,
        fix_two,
        WEIGHT_DECAY,
    )
    block_out = [x.reshape(layer_blocks.shape) for x in updated[:4]]
    like = [side_proj] * 3 + [shared_params] * 3
    small_out = [x.reshape(y.shape) for x, y in zip(updated[4:10], like)]
    small_out += [x.transpose(1, 0, 2) for x in updated[10:]]
    return (
        seq_loss,
        clip_norm,
        table_out[0],
        table_out[1],
        table_out[2],
        block_out[0],
        block_out[1],
        block_out[2],
        block_out[3],
        *small_out,
    )


def solution(mesh):
    table = P("tensor", "dp")
    block = P("dp", "tensor", None, None, None)
    side = P(None, ("dp", "tensor"), None)
    shared = P(("dp", "tensor"))
    channel = P(None, None, "tensor")
    in_specs = (
        P(None, "dp"),
        P(None, "dp"),
        P(),
        P(),
        P(),
        P("tensor", None),
        *[table] * 3,
        block,
        P("dp", "tensor", None, None, None, None),
        block,
        block,
        *[side] * 3,
        *[shared] * 3,
        *[channel] * 6,
    )
    out_specs = (
        P(),
        P(),
        *[table] * 3,
        *[block] * 4,
        *[side] * 3,
        *[shared] * 3,
        *[channel] * 6,
    )
    return jax.shard_map(shards, mesh=mesh, in_specs=in_specs, out_specs=out_specs, check_vma=False)
```
